32 devices in a mesh: wide: 8 (over z, y), narrow: 4 (over x, core).
Axes of the slice: x: 2, y: 2, z: 4, core: 2. Of those that a mesh axis runs over, the one named last changes fastest.
Arguments:
- byte_ids: int32 [32, 1488], P(('wide', 'narrow')), may hold values from 0 to 258
- lengths: int32 [32, 2], P(('wide', 'narrow')), may hold values from 186 to 744, as said below
- bucket: int32 [32], P(('wide', 'narrow')), may hold values 0 or 1
- out_grad: bfloat16 [32, 744, 768], P(('wide', 'narrow')), may hold values from -6 to 6
- embedding: bfloat16 [259, 768], P(None, 'wide')
- score_weight: bfloat16 [768], P('wide'), may hold values from -0.625 to 0.625
- gain_attn: bfloat16 [768], P('wide'), may hold values from 0.5 to 1.5
- w_query: bfloat16 [768, 768], P('wide'), may hold values from -0.02734375 to 0.02734375
- w_key: bfloat16 [768, 768], P('wide'), may hold values from -0.21875 to 0.21875
- w_value: bfloat16 [768, 768], P('wide'), may hold values from -0.21875 to 0.21875
- w_attn_out: bfloat16 [768, 768], P('wide'), may hold values from -0.875 to 0.875
- rel_bias: bfloat16 [32, 12], replicated, may hold values from -3 to 3
- gain_ff: bfloat16 [768], P('wide'), may hold values from 0.5 to 1.5
- w_gate: bfloat16 [768, 2048], P('wide'), may hold values from -0.21875 to 0.21875
- w_up: bfloat16 [768, 2048], P('wide'), may hold values from -0.21875 to 0.21875
- w_ff_out: bfloat16 [2048, 768], P('wide'), may hold values from -0.125 to 0.125
Outputs:
- encoded: bfloat16 [32, 744, 768], P(('wide', 'narrow'))
- grad_embedding: float32 [259, 768], P(None, 'wide')
- grad_score_weight: float32 [768], P('wide')
- grad_gain_attn: float32 [768], P('wide')
- grad_w_query: float32 [768, 768], P('wide')
- grad_w_key: float32 [768, 768], P('wide')
- grad_w_value: float32 [768, 768], P('wide')
- grad_w_attn_out: float32 [768, 768], P('wide')
- grad_rel_bias: float32 [32, 12], replicated
- grad_gain_ff: float32 [768], P('wide')
- grad_w_gate: float32 [768, 2048], P('wide')
- grad_w_up: float32 [768, 2048], P('wide')
- grad_w_ff_out: float32 [2048, 768], P('wide')
- block_share: float32 [4], replicated
The draws below stay inside these ranges and needn't reach their ends.
Inputs may be any that keep to these rules, and one draw needn't show every extreme that they name: Where bucket is 0 a group holds two sequences of lengths[g,0] and lengths[g,1] bytes in its two slots; where it is 1, one sequence of lengths[g,0] + lengths[g,1] bytes from the group's first byte. Some entry equals 744 and some equals 186.
All inputs are finite; a program needn't handle non-finite values. No bound on the sum of `bucket` on one device may be relied on, other than what follows from the above.
Results may differ from the reference program's by a relative error of at most 0.012.
Values may be sent and summed in bfloat16 or wider, within the bound.
A program may use at most 256 MiB of HBM per device.

```python
import jax
import jax.numpy as jnp
from jax import lax

D = 768
HEADS = 12
DH = 64
FF = 2048
VOCAB = 259
BUCKETS = 32
SLOT = 744
BUF = 1488
NTOK = 744
GROUPS = 32


def draw_lengths(key, part):
    drawn = jax.random.randint(key, (GROUPS, 2), SLOT // 4, SLOT + 1)
    drawn = drawn.at[0, 0].set(SLOT)
    drawn = drawn.at[0, 1].set(SLOT // 4)
    return drawn.astype(jnp.int32)


def draw_byte_ids(key, part):
    key = jax.random.fold_in(key, 11)
    base_key, first_key, second_key = jax.random.split(key, 3)
    group_index = jnp.arange(GROUPS, dtype=jnp.int32)
    base = group_index * (VOCAB - 32) // max(GROUPS - 1, 1) + jax.random.randint(base_key, (GROUPS,), 0, 8)
    first_offset = jax.random.randint(first_key, (GROUPS, BUF), 0, 24)
    second_offset = jax.random.randint(second_key, (GROUPS, BUF), 0, 24)
    drawn = base[:, None] + jnp.minimum(first_offset, second_offset)
    drawn = drawn.at[0, 0].set(0)
    drawn = drawn.at[GROUPS - 1, BUF - 1].set(VOCAB - 1)
    return drawn.astype(jnp.int32)


def draw_embedding(key, part):
    key = jax.random.fold_in(key, 23)
    entry_key, rough_key = jax.random.split(key, 2)
    position = jnp.arange(VOCAB, dtype=jnp.float32) / (VOCAB - 1)
    entries = jnp.clip(jax.random.normal(entry_key, (VOCAB, D), jnp.float32), -6.0, 6.0)
    low_scale = 0.15
    high_scale = 3.0
    rough = jnp.exp(jax.random.uniform(rough_key, (VOCAB,), jnp.float32, -0.223, 0.223))
    row_scale = low_scale * jnp.exp(position * jnp.log(high_scale / low_scale)) * rough
    return (entries * row_scale[:, None]).astype(jnp.bfloat16)


def touch_ends(values, key, least, largest):
    dims = values.shape
    index_at = [jax.random.randint(jax.random.fold_in(key, axis), (), 0, dims[axis]) for axis in range(len(dims))]
    values = values.at[tuple(index_at)].set(least)
    longest = dims.index(max(dims))
    index_at[longest] = (index_at[longest] + 1) % dims[longest]
    return values.at[tuple(index_at)].set(largest)


def level_of(own_key, extent, cuts, smallest, largest):
    def one(axis_at, blocks):
        steps = jax.random.uniform(jax.random.fold_in(jax.random.fold_in(own_key, 6), axis_at), (blocks,), jnp.float32, smallest / len(cuts), largest / len(cuts))
        return jnp.repeat(jnp.exp(steps), extent[axis_at] // blocks).reshape((-1,) + (1,) * (len(extent) - axis_at - 1))

    loudness = one(*cuts[0])
    for cut in cuts[1:]:
        loudness = loudness * one(*cut)
    return loudness


def normal_values(stream_key, extent, width, bound, shards=(), kind=jnp.bfloat16):
    gain = level_of(stream_key, extent, shards, -0.22, 0.18) if shards else 1.0
    values = jax.random.normal(stream_key, extent, jnp.float32) * width * gain
    return jnp.minimum(jnp.maximum(values, -bound), bound).astype(kind)


def setup_inputs(seed: int = 0) -> dict:
    key_list = jax.random.split(jax.random.key(seed), 17)
    byte_ids = draw_byte_ids(jax.random.fold_in(key_list[16], 71), 0)
    lengths = draw_lengths(jax.random.fold_in(key_list[16], 71), 0)
    bucket = touch_ends((jax.random.randint(key_list[2], (GROUPS,), 0, 3) < 1).astype(jnp.int32), jax.random.fold_in(key_list[2], 1), 0, 1)
    out_grad = normal_values(key_list[3], (GROUPS, NTOK, D), 1.0, 6.0, ((0, 32),))
    embedding = draw_embedding(jax.random.fold_in(key_list[16], 71), 0)
    score_weight = normal_values(key_list[5], (D,), (D // 8) ** -0.5, 0.625, ((0, 8),))
    gain_attn = jnp.clip(1.0 + 0.1 * jax.random.normal(key_list[6], (D,), jnp.float32), 0.5, 1.5).astype(jnp.bfloat16)
    w_query = normal_values(key_list[7], (D, D), (D * DH) ** -0.5, 0.02734375, ((0, 8),))
    w_key = normal_values(key_list[8], (D, D), D ** -0.5, 0.21875, ((0, 8),))
    w_value = normal_values(key_list[9], (D, D), D ** -0.5, 0.21875, ((0, 8),))
    w_attn_out = normal_values(key_list[10], (D, D), (D // 16) ** -0.5, 0.875, ((0, 8),))
    rel_bias = normal_values(key_list[11], (BUCKETS, HEADS), 0.5, 3.0)
    gain_ff = jnp.clip(1.0 + 0.1 * jax.random.normal(key_list[12], (D,), jnp.float32), 0.5, 1.5).astype(jnp.bfloat16)
    w_gate = normal_values(key_list[13], (D, FF), D ** -0.5, 0.21875, ((0, 8),))
    w_up = normal_values(key_list[14], (D, FF), D ** -0.5, 0.21875, ((0, 8),))
    w_ff_out = normal_values(key_list[15], (FF, D), FF ** -0.5, 0.125, ((0, 8),))
    return {"byte_ids": byte_ids, "lengths": lengths, "bucket": bucket, "out_grad": out_grad, "embedding": embedding, "score_weight": score_weight, "gain_attn": gain_attn, "w_query": w_query, "w_key": w_key, "w_value": w_value, "w_attn_out": w_attn_out, "rel_bias": rel_bias, "gain_ff": gain_ff, "w_gate": w_gate, "w_up": w_up, "w_ff_out": w_ff_out}


@jax.custom_vjp
def low(v):
    return lax.optimization_barrier(v.astype(jnp.bfloat16)).astype(jnp.float32)

@jax.custom_vjp
def low_back(v):
    return v

def low_keep(v):
    return (low(v), None)

def low_pass(kept, grad):
    return (grad,)

def back_keep(v):
    return (v, None)

def back_low(kept, grad):
    return (low(grad),)
low.defvjp(low_keep, low_pass)
low_back.defvjp(back_keep, back_low)
highest = lax.Precision.HIGHEST
thresholds = (12, 16, 23, 32, 46, 64, 91)
epsilon = 1e-06
block_sizes = (1, 2, 3, 4)

def bucket_of(relative):
    distance = jnp.abs(relative)
    far_bucket = 8 + sum(((distance >= threshold_edge).astype(jnp.int32) for threshold_edge in thresholds))
    near_far = jnp.where(distance < 8, distance, far_bucket)
    return near_far + 16 * (relative > 0).astype(jnp.int32)

def valid_masks(length_pair, joined_flag, slot_bytes):
    position = jnp.arange(2 * slot_bytes, dtype=jnp.int32)
    in_slot = position % slot_bytes
    slot_limit = jnp.where(position < slot_bytes, length_pair[0], length_pair[1])
    joined = joined_flag == 1
    byte_valid = jnp.where(joined, position < length_pair[0] + length_pair[1], in_slot < slot_limit)
    token_index = jnp.arange(slot_bytes, dtype=jnp.int32)
    segment = jnp.where(joined, 0, token_index // (slot_bytes // 2))
    token_valid = byte_valid[0::2]
    attend = (segment[:, None] == segment[None, :]) & token_valid[None, :]
    return (byte_valid.astype(jnp.float32), attend)

def gbst_mix(embedded, byte_valid, score_vector):
    nbytes, model_width = embedded.shape
    tile_count = nbytes // 12
    masked = (embedded * byte_valid[:, None]).reshape(tile_count, 12, model_width)
    counted = byte_valid.reshape(tile_count, 12)
    spread_blocks = []
    block_scores = []
    for block_size in block_sizes:
        groups_here = 12 // block_size
        summed = lax.optimization_barrier(jnp.sum(masked.reshape(tile_count, groups_here, block_size, model_width), axis=2))
        members = jnp.maximum(lax.optimization_barrier(jnp.sum(counted.reshape(tile_count, groups_here, block_size), axis=2)), 1.0)
        pooled = summed / members[..., None]
        rating = lax.optimization_barrier(jnp.sum(pooled * score_vector, axis=-1))
        spread_blocks.append(jnp.broadcast_to(pooled[:, :, None, :], (tile_count, groups_here, block_size, model_width)).reshape(nbytes, model_width))
        block_scores.append(jnp.broadcast_to(rating[:, :, None], (tile_count, groups_here, block_size)).reshape(nbytes))
    block_weights = jax.nn.softmax(jnp.stack(block_scores), axis=0)
    mixed = sum((block_weights[size_index][:, None] * spread_blocks[size_index] for size_index in range(4)))
    stream = lax.optimization_barrier(jnp.mean(mixed.reshape(nbytes // 2, 2, model_width), axis=1))
    return (stream, block_weights)

def rms_scale(activations, gain_vector):
    return activations * lax.rsqrt(lax.optimization_barrier(jnp.mean(activations * activations, axis=-1, keepdims=True)) + epsilon) * gain_vector

def one_group(weights, token_ids, length_pair, joined_flag):
    byte_table, score_vector, gain_one, query_full, key_full, value_full, out_full, bias_table, gain_two, gate_full, up_full, down_full = weights
    slot_bytes = token_ids.shape[0] // 2
    byte_valid, attend = valid_masks(length_pair, joined_flag, slot_bytes)
    onehot = (token_ids[:, None] == jnp.arange(VOCAB, dtype=jnp.int32)[None, :]).astype(jnp.float32)
    embedded = low_back(jnp.dot(onehot, byte_table, precision=highest))
    stream, block_weights = gbst_mix(embedded, byte_valid, score_vector)
    normed = low(rms_scale(stream, gain_one))
    queries = low_back(low(jnp.dot(normed, query_full, precision=highest))).reshape(slot_bytes, HEADS, DH)
    key_rows = low_back(low(jnp.dot(normed, key_full, precision=highest))).reshape(slot_bytes, HEADS, DH)
    value_rows = low_back(low(jnp.dot(normed, value_full, precision=highest))).reshape(slot_bytes, HEADS, DH)
    token_index = jnp.arange(slot_bytes, dtype=jnp.int32)
    bias_full = bias_table[bucket_of(token_index[None, :] - token_index[:, None])]
    scores = jnp.einsum('qhd,khd->hqk', queries, key_rows, precision=highest) + jnp.transpose(bias_full, (2, 0, 1))
    scores = low_back(scores)
    scores = jnp.where(attend[None], scores, -1e+30)
    softmax_rows = jax.nn.softmax(scores, axis=-1)
    mixed_heads = jnp.einsum('hqk,khd->qhd', low(softmax_rows), value_rows, precision=highest).reshape(slot_bytes, D)
    mixed_heads = low_back(low(mixed_heads))
    branch = low_back(jnp.dot(mixed_heads, out_full, precision=highest))
    middle = stream + branch
    normed_ff = low(rms_scale(middle, gain_two))
    gate_act = low_back(jnp.dot(normed_ff, gate_full, precision=highest))
    upward = low_back(jnp.dot(normed_ff, up_full, precision=highest))
    hidden = low(jax.nn.gelu(gate_act, approximate=True) * upward)
    result = middle + low_back(jnp.dot(hidden, down_full, precision=highest))
    totals = jnp.concatenate([lax.optimization_barrier(jnp.sum(block_weights * byte_valid[None, :], axis=1)), jnp.sum(byte_valid)[None]])
    return (result, totals)

def reference(byte_ids, lengths, bucket, out_grad, embedding, score_weight, gain_attn, w_query, w_key, w_value, w_attn_out, rel_bias, gain_ff, w_gate, w_up, w_ff_out):
    weights = tuple((weight_item.astype(jnp.float32) for weight_item in (embedding, score_weight, gain_attn, w_query, w_key, w_value, w_attn_out, rel_bias, gain_ff, w_gate, w_up, w_ff_out)))

    def forward(params):

        def scan_step(carry, group_row):
            result, totals = jax.checkpoint(one_group)(params, group_row[0], group_row[1], group_row[2])
            return (carry + totals, result)
        totals, results = lax.scan(scan_step, jnp.zeros((5,), jnp.float32), (byte_ids, lengths, bucket))
        return (results, totals)
    results, pullback, totals = jax.vjp(forward, weights, has_aux=True)
    gradients = pullback(out_grad.astype(jnp.float32))[0]
    block_share = totals[:4] / totals[4]
    return (results.astype(jnp.bfloat16), gradients[0], gradients[1], gradients[2], gradients[3], gradients[4], gradients[5], gradients[6], gradients[7], gradients[8], gradients[9], gradients[10], gradients[11], block_share)
```

```python
import functools

import jax
import jax.numpy as jnp
from jax import lax
from jax.experimental import pallas as pl
from jax.experimental.pallas import tpu as pltpu
from jax.sharding import PartitionSpec as P

f32 = jnp.float32
bf16 = jnp.bfloat16
TP = 768
BLK = 128
NB = TP // BLK
LEFT = TP - BLK
STRIP = 2 * TP - BLK
W0 = LEFT - 128
WN = 384

def nt(a, b):
    return lax.dot_general(a, b, (((1,), (1,)), ((), ())), preferred_element_type=f32)

def nn(a, b):
    return lax.dot_general(a, b, (((1,), (0,)), ((), ())), preferred_element_type=f32)

def build_masks(scal_ref, kaug, raug, ntok):
    joined = scal_ref[0] == 1
    l0 = scal_ref[1]; l1 = scal_ref[2]
    half = ntok // 2
    u = lax.broadcasted_iota(jnp.int32, (TP, 128), 0)
    lane = lax.broadcasted_iota(jnp.int32, (TP, 128), 1)
    seg = (u >= half).astype(jnp.int32)
    lim = jnp.where(seg == 1, l1, l0)
    start = seg * half
    lim = jnp.where(joined, l0 + l1, lim)
    start = jnp.where(joined, 0, start)
    valid = (2 * (u - start) < lim) & (u < ntok)
    segs = jnp.where(joined, 0, seg)
    ok = valid & (segs == lane)
    kaug[...] = jnp.where((lane < 2) & jnp.logical_not(ok), -1e30, 0.0).astype(bf16)
    t = u
    rows = jnp.where((lane == segs), 1.0, 0.0).astype(bf16)
    for b in range(NB):
        blk = rows[b * 128:(b + 1) * 128]
        raug[b] = jnp.concatenate([blk, blk], axis=0)

def build_strip(base_ref, row0, strip):
    for hh in range(2):
        row = base_ref[pl.ds(row0 + hh, 1), :]
        cl = row[:, 0:1]; cr = row[:, 383:384]
        sq = jnp.broadcast_to(row, (128, 512))
        sq = pltpu.roll(sq, 0, 1, stride=1, stride_axis=0)
        win = sq[:, :WN].T
        lanes = slice(hh * 128, hh * 128 + 128)
        strip[0:W0, lanes] = jnp.broadcast_to(cl, (W0, 128))
        strip[W0:W0 + WN, lanes] = win
        strip[W0 + WN:STRIP, lanes] = jnp.broadcast_to(cr, (STRIP - W0 - WN, 128))

def stacked(blk):
    lane = lax.broadcasted_iota(jnp.int32, blk.shape, 1)
    z = jnp.zeros_like(blk)
    return jnp.concatenate([jnp.where(lane < 64, blk, z), jnp.where(lane >= 64, blk, z)], axis=0)

def fwd_kernel(ntok, scal_ref, q_ref, k_ref, v_ref, base_ref, o_ref, lse_ref, kaug, raug, strip, vt):
    p = pl.program_id(0)
    @pl.when(p == 0)
    def _():
        build_masks(scal_ref, kaug, raug, ntok)
    build_strip(base_ref, 2 * p, strip)
    vt[...] = v_ref[...].T
    kcat = jnp.concatenate([k_ref[...], kaug[...]], axis=1)
    vtv = vt[...]
    rowsel = lax.broadcasted_iota(jnp.int32, (128, 128), 0) < 64
    for b in range(NB):
        rhs = jnp.concatenate([stacked(q_ref[b * 128:(b + 1) * 128, :]), raug[b]], axis=1)
        s = nt(kcat, rhs) + strip[LEFT - b * 128:LEFT - b * 128 + TP, :]
        mx = jnp.max(s, axis=0, keepdims=True)
        e = jnp.exp(s - mx)
        l = jnp.sum(e, axis=0, keepdims=True)
        ot = nn(vtv, e.astype(bf16)) * (1.0 / l)
        lse_ref[0, b:b + 1, :] = mx + jnp.log(l)
        o = jnp.where(rowsel, ot[:, :128], ot[:, 128:])
        o_ref[b * 128:(b + 1) * 128, :] = o.T.astype(bf16)

def attn_forward(scal, q, k, v, base2, ntok):
    heads = base2.shape[0]
    pairs = heads // 2
    col = pl.BlockSpec((TP, 128), lambda p: (0, p))
    return pl.pallas_call(
        functools.partial(fwd_kernel, ntok),
        grid=(pairs,),
        out_shape=(jax.ShapeDtypeStruct((TP, heads * 64), bf16), jax.ShapeDtypeStruct((pairs, 8, 256), f32)),
        in_specs=[pl.BlockSpec(memory_space=pltpu.SMEM), col, col, col, pl.BlockSpec(memory_space=pltpu.VMEM)],
        out_specs=(col, pl.BlockSpec((1, 8, 256), lambda p: (p, 0, 0))),
        scratch_shapes=[pltpu.VMEM((TP, 128), bf16), pltpu.VMEM((NB, 256, 128), bf16), pltpu.VMEM((STRIP, 256), f32), pltpu.VMEM((128, TP), bf16)],
        compiler_params=pltpu.CompilerParams(vmem_limit_bytes=48 << 20),
        name="attn_fwd",
    )(scal, q, k, v, base2)

def bwd_kernel(ntok, scal_ref, q_ref, k_ref, v_ref, g_ref, lse_ref, base_ref, dq_ref, dk_ref, dv_ref, db_ref, kaug, raug, strip, acc, kt, dk_s, dv_s):
    p = pl.program_id(0)
    @pl.when(p == 0)
    def _():
        build_masks(scal_ref, kaug, raug, ntok)
    build_strip(base_ref, 2 * p, strip)
    kt[...] = k_ref[...].T
    kcat = jnp.concatenate([k_ref[...], kaug[...]], axis=1)
    v = v_ref[...]
    ktv = kt[...]
    acc[...] = jnp.zeros_like(acc)
    dk_s[...] = jnp.zeros_like(dk_s)
    dv_s[...] = jnp.zeros_like(dv_s)
    rowsel = lax.broadcasted_iota(jnp.int32, (128, 128), 0) < 64
    for b in range(NB):
        qs = stacked(q_ref[b * 128:(b + 1) * 128, :])
        gs = stacked(g_ref[b * 128:(b + 1) * 128, :])
        rhs = jnp.concatenate([qs, raug[b]], axis=1)
        w = slice(LEFT - b * 128, LEFT - b * 128 + TP)
        s = nt(kcat, rhs) + strip[w, :]
        pr = jnp.exp(s - lse_ref[0, b:b + 1, :])
        dp = nt(v, gs)
        pdp = pr * dp
        delta = jnp.sum(pdp, axis=0, keepdims=True)
        ds = pdp - pr * delta
        acc[w, :] += ds
        dsb = ds.astype(bf16)
        dk_s[...] += nn(dsb, qs)
        dv_s[...] += nn(pr.astype(bf16), gs)
        dqt = nn(ktv, dsb)
        dq = jnp.where(rowsel, dqt[:, :128], dqt[:, 128:])
        dq_ref[b * 128:(b + 1) * 128, :] = dq.T.astype(bf16)
    dk_ref[...] = dk_s[...].astype(bf16)
    dv_ref[...] = dv_s[...].astype(bf16)
    fi = lax.broadcasted_iota(jnp.int32, (128, 128), 0)
    fj = lax.broadcasted_iota(jnp.int32, (128, 128), 1)
    flip = jnp.where(fi + fj == 127, 1.0, 0.0).astype(f32)
    for hh in range(2):
        lanes = slice(hh * 128, hh * 128 + 128)
        far_l = jnp.sum(acc[0:W0, lanes], keepdims=True)
        far_r = jnp.sum(acc[W0 + WN:STRIP, lanes], keepdims=True)
        win = acc[W0:W0 + WN, lanes]
        wt = lax.dot_general(flip, win, (((1,), (1,)), ((), ())), precision=lax.Precision.HIGHEST, preferred_element_type=f32)
        wt = jnp.concatenate([wt, jnp.zeros((128, 128), f32)], axis=1)
        wt = pltpu.roll(wt, 0, 1, stride=1, stride_axis=0)
        diag = jnp.sum(wt, axis=0, keepdims=True)
        lane = lax.broadcasted_iota(jnp.int32, (1, 512), 1)
        diag = diag + jnp.where(lane == 0, far_l, 0.0) + jnp.where(lane == 510, far_r, 0.0)
        db_ref[0, hh:hh + 1, :] = diag

def attn_backward(scal, q, k, v, g, lse, base2, ntok):
    heads = base2.shape[0]
    pairs = heads // 2
    col = pl.BlockSpec((TP, 128), lambda p: (0, p))
    sd = jax.ShapeDtypeStruct((TP, heads * 64), bf16)
    return pl.pallas_call(
        functools.partial(bwd_kernel, ntok),
        grid=(pairs,),
        out_shape=(sd, sd, sd, jax.ShapeDtypeStruct((pairs, 8, 512), f32)),
        in_specs=[pl.BlockSpec(memory_space=pltpu.SMEM), col, col, col, col, pl.BlockSpec((1, 8, 256), lambda p: (p, 0, 0)), pl.BlockSpec(memory_space=pltpu.VMEM)],
        out_specs=(col, col, col, pl.BlockSpec((1, 8, 512), lambda p: (p, 0, 0))),
        scratch_shapes=[pltpu.VMEM((TP, 128), bf16), pltpu.VMEM((NB, 256, 128), bf16), pltpu.VMEM((STRIP, 256), f32), pltpu.VMEM((STRIP, 256), f32), pltpu.VMEM((128, TP), bf16),
                        pltpu.VMEM((TP, 128), f32), pltpu.VMEM((TP, 128), f32)],
        compiler_params=pltpu.CompilerParams(vmem_limit_bytes=48 << 20),
        name="attn_bwd",
    )(scal, q, k, v, g, lse, base2)

def bucket_of(relative):
    distance = jnp.abs(relative)
    far = 8 + sum(((distance >= e).astype(jnp.int32) for e in (12, 16, 23, 32, 46, 64, 91)))
    near = jnp.where(distance < 8, distance, far)
    return near + 16 * (relative > 0).astype(jnp.int32)

def base_hot(nbuckets, grad=False):
    c = jnp.arange(512, dtype=jnp.int32)
    r = c - 255 if grad else jnp.where(c < 384, c - 128, c - 640)
    return (bucket_of(r)[:, None] == jnp.arange(nbuckets, dtype=jnp.int32)[None, :]).astype(f32)


ROWS = 128
VP = 384
VR = 272
EPS = 1e-6

def byte_valid_mat(scal_ref, nbytes):
    i = lax.broadcasted_iota(jnp.int32, (ROWS, 128), 0)
    j = lax.broadcasted_iota(jnp.int32, (ROWS, 128), 1)
    p = 12 * i + j
    slot = nbytes // 2
    joined = scal_ref[0] == 1
    l0 = scal_ref[1]; l1 = scal_ref[2]
    second = p >= slot
    start = jnp.where(joined, 0, jnp.where(second, slot, 0))
    lim = jnp.where(joined, l0 + l1, jnp.where(second, l1, l0))
    ok = (p - start < lim) & (p < nbytes) & (j < 12)
    return jnp.where(ok, 1.0, 0.0).astype(f32)

def inverse_counts(vm):
    v = [vm[:, j:j + 1] for j in range(12)]
    inv = {1: v}
    for b in (2, 3, 4):
        out = []
        for m in range(12 // b):
            tot = v[b * m]
            for t in range(1, b):
                tot = tot + v[b * m + t]
            out.append(1.0 / jnp.maximum(tot, 1.0))
        inv[b] = out
    return v, inv

def softmax_weights(e, inv):
    rate = {1: e}
    for b in (2, 3, 4):
        out = []
        for m in range(12 // b):
            tot = e[b * m]
            for t in range(1, b):
                tot = tot + e[b * m + t]
            out.append(tot * inv[b][m])
        rate[b] = out
    w = {b: [] for b in (1, 2, 3, 4)}
    for p in range(12):
        r = [rate[b][p // b] for b in (1, 2, 3, 4)]
        mx = jnp.maximum(jnp.maximum(r[0], r[1]), jnp.maximum(r[2], r[3]))
        ex = [jnp.exp(x - mx) for x in r]
        inv_t = 1.0 / (ex[0] + ex[1] + ex[2] + ex[3])
        for b in (1, 2, 3, 4):
            w[b].append(ex[b - 1] * inv_t)
    return w

def gbst_fwd_body(nbytes, scal_ref, ids_ref, table_ref, score_ref, gain_ref, stream_ref, normed_ref, emb_ref, wcol_ref, tot_ref, slabs):
    vm = byte_valid_mat(scal_ref, nbytes)
    v, inv = inverse_counts(vm)
    idt = ids_ref[...].astype(f32).T
    lane = lax.broadcasted_iota(jnp.int32, (ROWS, VP), 1).astype(f32)
    s = score_ref[...].astype(f32)
    e = []
    for j in range(12):
        hot = jnp.where((lane == idt[:, j:j + 1]) & (v[j] > 0.5), 1.0, 0.0).astype(bf16)
        ej = nn(hot, table_ref[...])
        emb_ref[j * ROWS:(j + 1) * ROWS, :] = ej.astype(bf16)
        e.append(jnp.sum(ej * s, axis=1, keepdims=True))
    w = softmax_weights(e, inv)
    l128 = lax.broadcasted_iota(jnp.int32, (ROWS, 128), 1)
    wc = jnp.zeros((ROWS, 128), f32)
    for b in (1, 2, 3, 4):
        for p in range(12):
            wc = jnp.where(l128 == (b - 1) * 12 + p, w[b][p], wc)
    wcol_ref[...] = wc
    tl = lax.broadcasted_iota(jnp.int32, (8, 128), 1)
    tot = jnp.zeros((8, 128), f32)
    for b in (1, 2, 3, 4):
        acc = w[b][0] * v[0]
        for p in range(1, 12):
            acc = acc + w[b][p] * v[p]
        tot = jnp.where(tl == b - 1, jnp.sum(acc, keepdims=True), tot)
    tot = jnp.where(tl == 4, jnp.sum(vm, keepdims=True), tot)
    tot_ref[...] = tot
    E = lambda j: emb_ref[j * ROWS:(j + 1) * ROWS, :].astype(f32)
    for k in range(6):
        p0, p1 = 2 * k, 2 * k + 1
        b2 = 0.5 * (w[2][p0] + w[2][p1]) * inv[2][k]
        acc = (0.5 * w[1][p0] + b2) * E(p0) + (0.5 * w[1][p1] + b2) * E(p1)
        n = k // 2
        d = 0.5 * (w[4][p0] + w[4][p1]) * inv[4][n]
        acc = acc + d * ((E(4 * n) + E(4 * n + 1)) + (E(4 * n + 2) + E(4 * n + 3)))
        m0, m1 = p0 // 3, p1 // 3
        s3 = lambda m: E(3 * m) + E(3 * m + 1) + E(3 * m + 2)
        if m0 == m1:
            acc = acc + (0.5 * (w[3][p0] + w[3][p1]) * inv[3][m0]) * s3(m0)
        else:
            acc = acc + (0.5 * w[3][p0] * inv[3][m0]) * s3(m0) + (0.5 * w[3][p1] * inv[3][m1]) * s3(m1)
        put_strided(slabs, k, acc)
    ntok = nbytes // 2
    for c in range(slabs.shape[0]):
        stream_ref[0:ntok, c * 128:(c + 1) * 128] = slabs[c, 0:ntok, :]
    stream_ref[ntok:TP, :] = jnp.zeros((TP - ntok, acc.shape[1]), f32)
    norm_rows(stream_ref, gain_ref, normed_ref)

def put_strided(ref, k, val):
    for c in range(val.shape[1] // 128):
        ref[c, pl.ds(k, 124, stride=6), :] = val[:124, c * 128:(c + 1) * 128]

def get_strided(ref, k):
    parts = [ref[c, pl.ds(k, 124, stride=6), :] for c in range(ref.shape[0])]
    x = jnp.concatenate(parts, axis=1)
    return jnp.concatenate([x, jnp.zeros((4, x.shape[1]), f32)], axis=0)

def norm_rows(x_ref, gain_ref, out_ref):
    g = gain_ref[...].astype(f32)
    for b in range(TP // 128):
        x = x_ref[b * 128:(b + 1) * 128, :]
        sc = lax.rsqrt(jnp.mean(x * x, axis=1, keepdims=True) + EPS)
        out_ref[b * 128:(b + 1) * 128, :] = (x * sc * g).astype(bf16)

def gbst_bwd_body(nbytes, scal_ref, ids_ref, emb_ref, wcol_ref, score_ref, gs_ref, gtable_ref, gscore_ref, de_ref, slabs):
    for c in range(slabs.shape[0]):
        slabs[c] = gs_ref[:, c * 128:(c + 1) * 128]
    vm = byte_valid_mat(scal_ref, nbytes)
    v, inv = inverse_counts(vm)
    wc = wcol_ref[...]
    w = {b: [wc[:, (b - 1) * 12 + p:(b - 1) * 12 + p + 1] for p in range(12)] for b in (1, 2, 3, 4)}
    s = score_ref[...].astype(f32)
    E = lambda j: emb_ref[j * ROWS:(j + 1) * ROWS, :].astype(f32)
    s3 = lambda m: E(3 * m) + E(3 * m + 1) + E(3 * m + 2)
    s4 = lambda n: (E(4 * n) + E(4 * n + 1)) + (E(4 * n + 2) + E(4 * n + 3))
    dot = lambda a, b: jnp.sum(a * b, axis=1, keepdims=True)
    dw = {b: [None] * 12 for b in (1, 2, 3, 4)}
    D = []
    for k in range(6):
        dk = 0.5 * get_strided(slabs, k)
        D.append(dk)
        p0, p1 = 2 * k, 2 * k + 1
        x0, x1 = dot(dk, E(p0)), dot(dk, E(p1))
        dw[1][p0], dw[1][p1] = x0, x1
        dw[2][p0] = dw[2][p1] = (x0 + x1) * inv[2][k]
        m0, m1 = p0 // 3, p1 // 3
        a0 = dot(dk, s3(m0)) * inv[3][m0]
        dw[3][p0] = a0
        dw[3][p1] = a0 if m0 == m1 else dot(dk, s3(m1)) * inv[3][m1]
        dw[4][p0] = dw[4][p1] = dot(dk, s4(k // 2)) * inv[4][k // 2]
    dr = {b: [] for b in (1, 2, 3, 4)}
    for p in range(12):
        mean = w[1][p] * dw[1][p] + w[2][p] * dw[2][p] + w[3][p] * dw[3][p] + w[4][p] * dw[4][p]
        for b in (1, 2, 3, 4):
            dr[b].append(w[b][p] * (dw[b][p] - mean))
    rb = {1: dr[1]}
    for b in (2, 3, 4):
        out = []
        for m in range(12 // b):
            tot = dr[b][b * m]
            for t in range(1, b):
                tot = tot + dr[b][b * m + t]
            out.append(tot * inv[b][m])
        rb[b] = out
    t3 = []
    for m in range(4):
        terms = {}
        for p in (3 * m, 3 * m + 1, 3 * m + 2):
            terms[p // 2] = terms[p // 2] + w[3][p] if p // 2 in terms else w[3][p]
        acc = None
        for k, coef in terms.items():
            t = (coef * inv[3][m]) * D[k]
            acc = t if acc is None else acc + t
        t3.append(acc)
    gscore = jnp.zeros((8, s.shape[1]), f32)
    for n in range(3):
        t4 = ((w[4][4 * n] + w[4][4 * n + 1]) * inv[4][n]) * D[2 * n] + ((w[4][4 * n + 2] + w[4][4 * n + 3]) * inv[4][n]) * D[2 * n + 1]
        for p in range(4 * n, 4 * n + 4):
            k = p // 2
            c = rb[1][p] + rb[2][k] + rb[3][p // 3] + rb[4][n]
            b2 = (w[2][2 * k] + w[2][2 * k + 1]) * inv[2][k]
            de = v[p] * ((w[1][p] + b2) * D[k] + t3[p // 3] + t4 + c * s)
            de_ref[p * ROWS:(p + 1) * ROWS, :] = de.astype(bf16)
            y = c * E(p)
            gscore = gscore + jnp.sum(y.reshape(ROWS // 8, 8, s.shape[1]), axis=0)
    gscore_ref[...] = jnp.sum(gscore, axis=0, keepdims=True)
    row = lax.broadcasted_iota(jnp.int32, (VR, ROWS), 0)
    hots = [jnp.where(row == ids_ref[j:j + 1, :], 1.0, 0.0).astype(bf16) for j in range(12)]
    hot = jnp.concatenate(hots, axis=1)
    gtable_ref[...] = nn(hot, de_ref[...])

def gbst_forward(scal, ids, table, score, gain, nbytes):
    d = table.shape[1]
    vm = pl.BlockSpec(memory_space=pltpu.VMEM)
    return pl.pallas_call(
        functools.partial(gbst_fwd_body, nbytes),
        out_shape=(jax.ShapeDtypeStruct((TP, d), f32), jax.ShapeDtypeStruct((TP, d), bf16), jax.ShapeDtypeStruct((12 * ROWS, d), bf16),
                   jax.ShapeDtypeStruct((ROWS, 128), f32), jax.ShapeDtypeStruct((8, 128), f32)),
        in_specs=[pl.BlockSpec(memory_space=pltpu.SMEM)] + [vm] * 4,
        out_specs=(vm,) * 5,
        scratch_shapes=[pltpu.VMEM((d // 128, TP, 128), f32)],
        compiler_params=pltpu.CompilerParams(vmem_limit_bytes=48 << 20),
        name="gbst_fwd",
    )(scal, ids, table, score, gain)

def gbst_backward(scal, ids, emb, wcol, score, gs, nbytes):
    d = emb.shape[1]
    vm = pl.BlockSpec(memory_space=pltpu.VMEM)
    return pl.pallas_call(
        functools.partial(gbst_bwd_body, nbytes),
        out_shape=(jax.ShapeDtypeStruct((VR, d), f32), jax.ShapeDtypeStruct((1, d), f32)),
        in_specs=[pl.BlockSpec(memory_space=pltpu.SMEM)] + [vm] * 5,
        out_specs=(vm, vm),
        scratch_shapes=[pltpu.VMEM((12 * ROWS, d), bf16), pltpu.VMEM((d // 128, TP, 128), f32)],
        compiler_params=pltpu.CompilerParams(vmem_limit_bytes=48 << 20),
        name="gbst_bwd",
    )(scal, ids, emb, wcol, score, gs)


def tn(a, b):
    return lax.dot_general(a, b, (((0,), (0,)), ((), ())), preferred_element_type=f32)


def norm_back(x, gain, gy):
    s = lax.rsqrt(jnp.mean(x * x, axis=1, keepdims=True) + EPS)
    t = gy * gain
    gx = s * t - x * (s * s * s) * jnp.mean(x * t, axis=1, keepdims=True)
    return gx, jnp.sum(gy * x * s, axis=0)


def layer(byte_ids, lengths, bucket, out_grad, table, score, gain_one, wq, wk, wv, wo, rel_bias, gain_two, wg, wu, wd):
    ids = byte_ids[0]
    nbytes = ids.shape[0]
    ntok = nbytes // 2
    d = table.shape[1]
    vocab = table.shape[0]
    scal = jnp.stack([bucket[0], lengths[0, 0], lengths[0, 1]])
    idp = jnp.pad(ids.reshape(nbytes // 12, 12).T, ((0, 4), (0, ROWS - nbytes // 12)), constant_values=-1)
    tp = jnp.pad(table, ((0, VP - vocab), (0, 0)))
    stream, normed, emb, wcol, tot = gbst_forward(scal, idp, tp, score[None], gain_one[None], nbytes)
    q = nn(normed, wq).astype(bf16)
    k = nn(normed, wk).astype(bf16)
    v = nn(normed, wv).astype(bf16)
    nb = rel_bias.shape[0]
    base2 = jnp.dot(base_hot(nb), rel_bias.astype(f32), precision=lax.Precision.HIGHEST).T
    mixed, lse = attn_forward(scal, q, k, v, base2, ntok)
    middle = stream + nn(mixed, wo)
    g2 = gain_two.astype(f32)
    s2 = lax.rsqrt(jnp.mean(middle * middle, axis=1, keepdims=True) + EPS)
    normed_ff = (middle * s2 * g2).astype(bf16)
    gate = nn(normed_ff, wg)
    up = nn(normed_ff, wu)
    c0 = 0.7978845608028654
    inner = c0 * (gate + 0.044715 * gate * gate * gate)
    th = jnp.tanh(inner)
    act = 0.5 * gate * (1.0 + th)
    hidden = (act * up).astype(bf16)
    encoded = (middle + nn(hidden, wd)).astype(bf16)[:ntok][None]
    og = jnp.pad(out_grad[0], ((0, TP - ntok), (0, 0)))
    g_wd = tn(hidden, og)
    gh = nt(og, wd)
    dact = 0.5 * (1.0 + th) + 0.5 * gate * (1.0 - th * th) * (c0 * (1.0 + 3 * 0.044715 * gate * gate))
    gg = (gh * up * dact).astype(bf16)
    gu = (gh * act).astype(bf16)
    g_wg = tn(normed_ff, gg)
    g_wu = tn(normed_ff, gu)
    g_nff = nt(gg, wg) + nt(gu, wu)
    gx2, g_gain2 = norm_back(middle, g2, g_nff)
    g_mid = og.astype(f32) + gx2
    g_br = g_mid.astype(bf16)
    g_wo = tn(mixed, g_br)
    g_heads = nt(g_br, wo).astype(bf16)
    dq, dk, dv, db = attn_backward(scal, q, k, v, g_heads, lse, base2, ntok)
    g_rel = jnp.dot(base_hot(nb, True).T, db[:, :2, :].reshape(rel_bias.shape[1], 512).T, precision=lax.Precision.HIGHEST)
    g_wq = tn(normed, dq)
    g_wk = tn(normed, dk)
    g_wv = tn(normed, dv)
    g_n = nt(dq, wq) + nt(dk, wk) + nt(dv, wv)
    gx1, g_gain1 = norm_back(stream, gain_one.astype(f32), g_n)
    g_stream = g_mid + gx1
    g_table, g_score = gbst_backward(scal, idp, emb, wcol, score[None], g_stream, nbytes)
    return encoded, g_table[:vocab], g_score[0], g_gain1, g_wq, g_wk, g_wv, g_wo, g_rel, g_gain2, g_wg, g_wu, g_wd, tot[0, :5]


def body(byte_ids, lengths, bucket, out_grad, *weights):
    axes = (1, 0, 0, 0, 0, 0, 0, None, 0, 0, 0, 0)
    full = [w if a is None else lax.all_gather(w, "wide", axis=a, tiled=True) for w, a in zip(weights, axes)]
    out = layer(byte_ids, lengths, bucket, out_grad, *full)
    encoded, grads, tot = out[0], out[1:13], out[13]
    final = [None] * 12
    grads = list(grads)
    scatter = {0: 1, 3: 0, 4: 0, 5: 0, 6: 0, 9: 0, 10: 0, 11: 0}
    for i, dim in scatter.items():
        part = lax.psum_scatter(grads[i].astype(bf16), "wide", scatter_dimension=dim, tiled=True)
        final[i] = lax.psum(part, "narrow").astype(f32)
    rel, score, gain1, gain2, tot = lax.psum((grads[7], grads[1], grads[2], grads[8], tot), ("wide", "narrow"))
    w = lax.axis_index("wide")
    n = weights[1].shape[0]
    cut = lambda x: lax.dynamic_slice(x, (w * n,), (n,))
    final[1], final[2], final[7], final[8] = cut(score), cut(gain1), rel, cut(gain2)
    return (encoded, *final, tot[:4] / tot[4])


def solution(mesh):
    both = ("wide", "narrow")
    rows = P("wide", None)
    vec = P("wide")
    placed = (P(both, None), P(both, None), P(both), P(both, None, None), P(None, "wide"), vec, vec, rows, rows, rows, rows, P(), vec, rows, rows, rows)
    outs = (P(both, None, None), P(None, "wide"), vec, vec, rows, rows, rows, rows, P(), vec, rows, rows, rows, P())
    return jax.shard_map(body, mesh=mesh, in_specs=placed, out_specs=outs, check_vma=False)
```

```python
import functools

import jax
import jax.numpy as jnp
from jax import lax
from jax.experimental import pallas as pl
from jax.experimental.pallas import tpu as pltpu
from jax.sharding import PartitionSpec as P

f32 = jnp.float32
bf16 = jnp.bfloat16
TP = 768
BLK = 128
NB = TP // BLK
LEFT = TP - BLK
STRIP = 2 * TP - BLK
W0 = LEFT - 128
WN = 384

def nt(a, b):
    return lax.dot_general(a, b, (((1,), (1,)), ((), ())), preferred_element_type=f32)

def nn(a, b):
    return lax.dot_general(a, b, (((1,), (0,)), ((), ())), preferred_element_type=f32)

def build_masks(scal_ref, kaug, raug, ntok):
    joined = scal_ref[0] == 1
    l0 = scal_ref[1]; l1 = scal_ref[2]
    half = ntok // 2
    u = lax.broadcasted_iota(jnp.int32, (TP, 128), 0)
    lane = lax.broadcasted_iota(jnp.int32, (TP, 128), 1)
    seg = (u >= half).astype(jnp.int32)
    lim = jnp.where(seg == 1, l1, l0)
    start = seg * half
    lim = jnp.where(joined, l0 + l1, lim)
    start = jnp.where(joined, 0, start)
    valid = (2 * (u - start) < lim) & (u < ntok)
    segs = jnp.where(joined, 0, seg)
    ok = valid & (segs == lane)
    kaug[...] = jnp.where((lane < 2) & jnp.logical_not(ok), -1e30, 0.0).astype(bf16)
    t = u
    rows = jnp.where((lane == segs), 1.0, 0.0).astype(bf16)
    for b in range(NB):
        blk = rows[b * 128:(b + 1) * 128]
        raug[b] = jnp.concatenate([blk, blk], axis=0)

def build_strip(base_ref, row0, strip):
    for hh in range(2):
        row = base_ref[pl.ds(row0 + hh, 1), :]
        cl = row[:, 0:1]; cr = row[:, 383:384]
        sq = jnp.broadcast_to(row, (128, 512))
        sq = pltpu.roll(sq, 0, 1, stride=1, stride_axis=0)
        win = sq[:, :WN].T
        lanes = slice(hh * 128, hh * 128 + 128)
        strip[0:W0, lanes] = jnp.broadcast_to(cl, (W0, 128))
        strip[W0:W0 + WN, lanes] = win
        strip[W0 + WN:STRIP, lanes] = jnp.broadcast_to(cr, (STRIP - W0 - WN, 128))

def stacked(blk):
    lane = lax.broadcasted_iota(jnp.int32, blk.shape, 1)
    z = jnp.zeros_like(blk)
    return jnp.concatenate([jnp.where(lane < 64, blk, z), jnp.where(lane >= 64, blk, z)], axis=0)

def fwd_kernel(ntok, scal_ref, q_ref, k_ref, v_ref, base_ref, o_ref, lse_ref, kaug, raug, strip, vt):
    p = pl.program_id(0)
    @pl.when(p == 0)
    def _():
        build_masks(scal_ref, kaug, raug, ntok)
    build_strip(base_ref, 2 * p, strip)
    vt[...] = v_ref[...].T
    kcat = jnp.concatenate([k_ref[...], kaug[...]], axis=1)
    vtv = vt[...]
    rowsel = lax.broadcasted_iota(jnp.int32, (128, 128), 0) < 64
    for b in range(NB):
        rhs = jnp.concatenate([stacked(q_ref[b * 128:(b + 1) * 128, :]), raug[b]], axis=1)
        s = nt(kcat, rhs) + strip[LEFT - b * 128:LEFT - b * 128 + TP, :]
        mx = jnp.max(s, axis=0, keepdims=True)
        e = jnp.exp(s - mx)
        l = jnp.sum(e, axis=0, keepdims=True)
        ot = nn(vtv, e.astype(bf16)) * (1.0 / l)
        lse_ref[0, b:b + 1, :] = mx + jnp.log(l)
        o = jnp.where(rowsel, ot[:, :128], ot[:, 128:])
        o_ref[b * 128:(b + 1) * 128, :] = o.T.astype(bf16)

def attn_forward(scal, q, k, v, base2, ntok):
    heads = base2.shape[0]
    pairs = heads // 2
    col = pl.BlockSpec((TP, 128), lambda p: (0, p))
    return pl.pallas_call(
        functools.partial(fwd_kernel, ntok),
        grid=(pairs,),
        out_shape=(jax.ShapeDtypeStruct((TP, heads * 64), bf16), jax.ShapeDtypeStruct((pairs, 8, 256), f32)),
        in_specs=[pl.BlockSpec(memory_space=pltpu.SMEM), col, col, col, pl.BlockSpec(memory_space=pltpu.VMEM)],
        out_specs=(col, pl.BlockSpec((1, 8, 256), lambda p: (p, 0, 0))),
        scratch_shapes=[pltpu.VMEM((TP, 128), bf16), pltpu.VMEM((NB, 256, 128), bf16), pltpu.VMEM((STRIP, 256), f32), pltpu.VMEM((128, TP), bf16)],
        compiler_params=pltpu.CompilerParams(vmem_limit_bytes=48 << 20),
        name="attn_fwd",
    )(scal, q, k, v, base2)

def bwd_kernel(ntok, scal_ref, q_ref, k_ref, v_ref, g_ref, lse_ref, base_ref, dq_ref, dk_ref, dv_ref, db_ref, kaug, raug, strip, acc, kt, dk_s, dv_s):
    p = pl.program_id(0)
    @pl.when(p == 0)
    def _():
        build_masks(scal_ref, kaug, raug, ntok)
    build_strip(base_ref, 2 * p, strip)
    kt[...] = k_ref[...].T
    kcat = jnp.concatenate([k_ref[...], kaug[...]], axis=1)
    v = v_ref[...]
    ktv = kt[...]
    acc[...] = jnp.zeros_like(acc)
    dk_s[...] = jnp.zeros_like(dk_s)
    dv_s[...] = jnp.zeros_like(dv_s)
    rowsel = lax.broadcasted_iota(jnp.int32, (128, 128), 0) < 64
    for b in range(NB):
        qs = stacked(q_ref[b * 128:(b + 1) * 128, :])
        gs = stacked(g_ref[b * 128:(b + 1) * 128, :])
        rhs = jnp.concatenate([qs, raug[b]], axis=1)
        w = slice(LEFT - b * 128, LEFT - b * 128 + TP)
        s = nt(kcat, rhs) + strip[w, :]
        pr = jnp.exp(s - lse_ref[0, b:b + 1, :])
        dp = nt(v, gs)
        pdp = pr * dp
        delta = jnp.sum(pdp, axis=0, keepdims=True)
        ds = pdp - pr * delta
        acc[w, :] += ds
        dsb = ds.astype(bf16)
        dk_s[...] += nn(dsb, qs)
        dv_s[...] += nn(pr.astype(bf16), gs)
        dqt = nn(ktv, dsb)
        dq = jnp.where(rowsel, dqt[:, :128], dqt[:, 128:])
        dq_ref[b * 128:(b + 1) * 128, :] = dq.T.astype(bf16)
    dk_ref[...] = dk_s[...].astype(bf16)
    dv_ref[...] = dv_s[...].astype(bf16)
    fi = lax.broadcasted_iota(jnp.int32, (128, 128), 0)
    fj = lax.broadcasted_iota(jnp.int32, (128, 128), 1)
    flip = jnp.where(fi + fj == 127, 1.0, 0.0).astype(f32)
    for hh in range(2):
        lanes = slice(hh * 128, hh * 128 + 128)
        far_l = jnp.sum(acc[0:W0, lanes], keepdims=True)
        far_r = jnp.sum(acc[W0 + WN:STRIP, lanes], keepdims=True)
        win = acc[W0:W0 + WN, lanes]
        wt = lax.dot_general(flip, win, (((1,), (1,)), ((), ())), precision=lax.Precision.HIGHEST, preferred_element_type=f32)
        wt = jnp.concatenate([wt, jnp.zeros((128, 128), f32)], axis=1)
        wt = pltpu.roll(wt, 0, 1, stride=1, stride_axis=0)
        diag = jnp.sum(wt, axis=0, keepdims=True)
        lane = lax.broadcasted_iota(jnp.int32, (1, 512), 1)
        diag = diag + jnp.where(lane == 0, far_l, 0.0) + jnp.where(lane == 510, far_r, 0.0)
        db_ref[0, hh:hh + 1, :] = diag

def attn_backward(scal, q, k, v, g, lse, base2, ntok):
    heads = base2.shape[0]
    pairs = heads // 2
    col = pl.BlockSpec((TP, 128), lambda p: (0, p))
    sd = jax.ShapeDtypeStruct((TP, heads * 64), bf16)
    return pl.pallas_call(
        functools.partial(bwd_kernel, ntok),
        grid=(pairs,),
        out_shape=(sd, sd, sd, jax.ShapeDtypeStruct((pairs, 8, 512), f32)),
        in_specs=[pl.BlockSpec(memory_space=pltpu.SMEM), col, col, col, col, pl.BlockSpec((1, 8, 256), lambda p: (p, 0, 0)), pl.BlockSpec(memory_space=pltpu.VMEM)],
        out_specs=(col, col, col, pl.BlockSpec((1, 8, 512), lambda p: (p, 0, 0))),
        scratch_shapes=[pltpu.VMEM((TP, 128), bf16), pltpu.VMEM((NB, 256, 128), bf16), pltpu.VMEM((STRIP, 256), f32), pltpu.VMEM((STRIP, 256), f32), pltpu.VMEM((128, TP), bf16),
                        pltpu.VMEM((TP, 128), f32), pltpu.VMEM((TP, 128), f32)],
        compiler_params=pltpu.CompilerParams(vmem_limit_bytes=48 << 20),
        name="attn_bwd",
    )(scal, q, k, v, g, lse, base2)

def bucket_of(relative):
    distance = jnp.abs(relative)
    far = 8 + sum(((distance >= e).astype(jnp.int32) for e in (12, 16, 23, 32, 46, 64, 91)))
    near = jnp.where(distance < 8, distance, far)
    return near + 16 * (relative > 0).astype(jnp.int32)

def base_hot(nbuckets, grad=False):
    c = jnp.arange(512, dtype=jnp.int32)
    r = c - 255 if grad else jnp.where(c < 384, c - 128, c - 640)
    return (bucket_of(r)[:, None] == jnp.arange(nbuckets, dtype=jnp.int32)[None, :]).astype(f32)


ROWS = 128
VP = 512
VR = 272
EPS = 1e-6

def byte_valid_mat(scal_ref, nbytes):
    i = lax.broadcasted_iota(jnp.int32, (ROWS, 128), 0)
    j = lax.broadcasted_iota(jnp.int32, (ROWS, 128), 1)
    p = 12 * i + j
    slot = nbytes // 2
    joined = scal_ref[0] == 1
    l0 = scal_ref[1]; l1 = scal_ref[2]
    second = p >= slot
    start = jnp.where(joined, 0, jnp.where(second, slot, 0))
    lim = jnp.where(joined, l0 + l1, jnp.where(second, l1, l0))
    ok = (p - start < lim) & (p < nbytes) & (j < 12)
    return jnp.where(ok, 1.0, 0.0).astype(f32)

def inverse_counts(vm):
    v = [vm[:, j:j + 1] for j in range(12)]
    inv = {1: v}
    for b in (2, 3, 4):
        out = []
        for m in range(12 // b):
            tot = v[b * m]
            for t in range(1, b):
                tot = tot + v[b * m + t]
            out.append(1.0 / jnp.maximum(tot, 1.0))
        inv[b] = out
    return v, inv

def softmax_weights(e, inv):
    rate = {1: e}
    for b in (2, 3, 4):
        out = []
        for m in range(12 // b):
            tot = e[b * m]
            for t in range(1, b):
                tot = tot + e[b * m + t]
            out.append(tot * inv[b][m])
        rate[b] = out
    w = {b: [] for b in (1, 2, 3, 4)}
    for p in range(12):
        r = [rate[b][p // b] for b in (1, 2, 3, 4)]
        mx = jnp.maximum(jnp.maximum(r[0], r[1]), jnp.maximum(r[2], r[3]))
        ex = [jnp.exp(x - mx) for x in r]
        inv_t = 1.0 / (ex[0] + ex[1] + ex[2] + ex[3])
        for b in (1, 2, 3, 4):
            w[b].append(ex[b - 1] * inv_t)
    return w

def gbst_fwd_body(nbytes, vocab, scal_ref, ids_ref, tt_ref, stream_ref, normed_ref, emb_ref, wcol_ref, tot_ref, vec_ref, slabs, table_ref):
    table_ref[...] = tt_ref[...].T
    base = vocab // 16 * 16
    tail = table_ref[base:base + 16, :].astype(f32)
    vec_ref[0:3, :] = tail[vocab - base:vocab - base + 3, :]
    vec_ref[3:8, :] = jnp.zeros((5, tail.shape[1]), f32)
    score_ref = vec_ref[0:1, :]
    gain_ref = vec_ref[1:2, :]
    vm = byte_valid_mat(scal_ref, nbytes)
    v, inv = inverse_counts(vm)
    idt = ids_ref[...].astype(f32).T
    lane = lax.broadcasted_iota(jnp.int32, (ROWS, VP), 1).astype(f32)
    s = score_ref
    e = []
    for j in range(12):
        hot = jnp.where((lane == idt[:, j:j + 1]) & (v[j] > 0.5), 1.0, 0.0).astype(bf16)
        ej = nn(hot, table_ref[...])
        emb_ref[j * ROWS:(j + 1) * ROWS, :] = ej.astype(bf16)
        e.append(jnp.sum(ej * s, axis=1, keepdims=True))
    w = softmax_weights(e, inv)
    l128 = lax.broadcasted_iota(jnp.int32, (ROWS, 128), 1)
    wc = jnp.zeros((ROWS, 128), f32)
    for b in (1, 2, 3, 4):
        for p in range(12):
            wc = jnp.where(l128 == (b - 1) * 12 + p, w[b][p], wc)
    wcol_ref[...] = wc
    tl = lax.broadcasted_iota(jnp.int32, (8, 128), 1)
    tot = jnp.zeros((8, 128), f32)
    for b in (1, 2, 3, 4):
        acc = w[b][0] * v[0]
        for p in range(1, 12):
            acc = acc + w[b][p] * v[p]
        tot = jnp.where(tl == b - 1, jnp.sum(acc, keepdims=True), tot)
    tot = jnp.where(tl == 4, jnp.sum(vm, keepdims=True), tot)
    tot_ref[...] = tot
    E = lambda j: emb_ref[j * ROWS:(j + 1) * ROWS, :].astype(f32)
    for k in range(6):
        p0, p1 = 2 * k, 2 * k + 1
        b2 = 0.5 * (w[2][p0] + w[2][p1]) * inv[2][k]
        acc = (0.5 * w[1][p0] + b2) * E(p0) + (0.5 * w[1][p1] + b2) * E(p1)
        n = k // 2
        d = 0.5 * (w[4][p0] + w[4][p1]) * inv[4][n]
        acc = acc + d * ((E(4 * n) + E(4 * n + 1)) + (E(4 * n + 2) + E(4 * n + 3)))
        m0, m1 = p0 // 3, p1 // 3
        s3 = lambda m: E(3 * m) + E(3 * m + 1) + E(3 * m + 2)
        if m0 == m1:
            acc = acc + (0.5 * (w[3][p0] + w[3][p1]) * inv[3][m0]) * s3(m0)
        else:
            acc = acc + (0.5 * w[3][p0] * inv[3][m0]) * s3(m0) + (0.5 * w[3][p1] * inv[3][m1]) * s3(m1)
        put_strided(slabs, k, acc)
    ntok = nbytes // 2
    for c in range(slabs.shape[0]):
        stream_ref[0:ntok, c * 128:(c + 1) * 128] = slabs[c, 0:ntok, :]
    stream_ref[ntok:TP, :] = jnp.zeros((TP - ntok, acc.shape[1]), f32)
    norm_rows(stream_ref, gain_ref, normed_ref)

def put_strided(ref, k, val):
    for c in range(val.shape[1] // 128):
        ref[c, pl.ds(k, 124, stride=6), :] = val[:124, c * 128:(c + 1) * 128]

def get_strided(ref, k):
    parts = [ref[c, pl.ds(k, 124, stride=6), :] for c in range(ref.shape[0])]
    x = jnp.concatenate(parts, axis=1)
    return jnp.concatenate([x, jnp.zeros((4, x.shape[1]), f32)], axis=0)

def norm_rows(x_ref, gain_ref, out_ref):
    g = gain_ref
    for b in range(TP // 128):
        x = x_ref[b * 128:(b + 1) * 128, :]
        sc = lax.rsqrt(jnp.mean(x * x, axis=1, keepdims=True) + EPS)
        out_ref[b * 128:(b + 1) * 128, :] = (x * sc * g).astype(bf16)

def gbst_bwd_body(nbytes, vocab, scal_ref, ids_ref, emb_ref, wcol_ref, score_ref, gs_ref, ggain_ref, gt_ref, de_ref, slabs):
    for c in range(slabs.shape[0]):
        slabs[c] = gs_ref[:, c * 128:(c + 1) * 128]
    vm = byte_valid_mat(scal_ref, nbytes)
    v, inv = inverse_counts(vm)
    wc = wcol_ref[...]
    w = {b: [wc[:, (b - 1) * 12 + p:(b - 1) * 12 + p + 1] for p in range(12)] for b in (1, 2, 3, 4)}
    s = score_ref[0:1, :]
    E = lambda j: emb_ref[j * ROWS:(j + 1) * ROWS, :].astype(f32)
    s3 = lambda m: E(3 * m) + E(3 * m + 1) + E(3 * m + 2)
    s4 = lambda n: (E(4 * n) + E(4 * n + 1)) + (E(4 * n + 2) + E(4 * n + 3))
    dot = lambda a, b: jnp.sum(a * b, axis=1, keepdims=True)
    dw = {b: [None] * 12 for b in (1, 2, 3, 4)}
    D = []
    for k in range(6):
        dk = 0.5 * get_strided(slabs, k)
        D.append(dk)
        p0, p1 = 2 * k, 2 * k + 1
        x0, x1 = dot(dk, E(p0)), dot(dk, E(p1))
        dw[1][p0], dw[1][p1] = x0, x1
        dw[2][p0] = dw[2][p1] = (x0 + x1) * inv[2][k]
        m0, m1 = p0 // 3, p1 // 3
        a0 = dot(dk, s3(m0)) * inv[3][m0]
        dw[3][p0] = a0
        dw[3][p1] = a0 if m0 == m1 else dot(dk, s3(m1)) * inv[3][m1]
        dw[4][p0] = dw[4][p1] = dot(dk, s4(k // 2)) * inv[4][k // 2]
    dr = {b: [] for b in (1, 2, 3, 4)}
    for p in range(12):
        mean = w[1][p] * dw[1][p] + w[2][p] * dw[2][p] + w[3][p] * dw[3][p] + w[4][p] * dw[4][p]
        for b in (1, 2, 3, 4):
            dr[b].append(w[b][p] * (dw[b][p] - mean))
    rb = {1: dr[1]}
    for b in (2, 3, 4):
        out = []
        for m in range(12 // b):
            tot = dr[b][b * m]
            for t in range(1, b):
                tot = tot + dr[b][b * m + t]
            out.append(tot * inv[b][m])
        rb[b] = out
    t3 = []
    for m in range(4):
        terms = {}
        for p in (3 * m, 3 * m + 1, 3 * m + 2):
            terms[p // 2] = terms[p // 2] + w[3][p] if p // 2 in terms else w[3][p]
        acc = None
        for k, coef in terms.items():
            t = (coef * inv[3][m]) * D[k]
            acc = t if acc is None else acc + t
        t3.append(acc)
    gscore = jnp.zeros((8, s.shape[1]), f32)
    for n in range(3):
        t4 = ((w[4][4 * n] + w[4][4 * n + 1]) * inv[4][n]) * D[2 * n] + ((w[4][4 * n + 2] + w[4][4 * n + 3]) * inv[4][n]) * D[2 * n + 1]
        for p in range(4 * n, 4 * n + 4):
            k = p // 2
            c = rb[1][p] + rb[2][k] + rb[3][p // 3] + rb[4][n]
            b2 = (w[2][2 * k] + w[2][2 * k + 1]) * inv[2][k]
            de = v[p] * ((w[1][p] + b2) * D[k] + t3[p // 3] + t4 + c * s)
            de_ref[p * ROWS:(p + 1) * ROWS, :] = de.astype(bf16)
            y = c * E(p)
            gscore = gscore + jnp.sum(y.reshape(ROWS // 8, 8, s.shape[1]), axis=0)
    gscore = jnp.sum(gscore, axis=0, keepdims=True)
    row = lax.broadcasted_iota(jnp.int32, (VR, ROWS), 0)
    hots = [jnp.where(row == ids_ref[j:j + 1, :], 1.0, 0.0).astype(bf16) for j in range(12)]
    hot = jnp.concatenate(hots, axis=1)
    gtable = nn(hot, de_ref[...])
    row = lax.broadcasted_iota(jnp.int32, gtable.shape, 0)
    for i, extra in enumerate((gscore, ggain_ref[0:1, :], ggain_ref[1:2, :])):
        gtable = jnp.where(row == vocab + i, extra, gtable)
    gt_ref[:, 0:VR] = gtable.T.astype(bf16)
    gt_ref[:, VR:VP] = jnp.zeros((gt_ref.shape[0], VP - VR), bf16)

def gbst_forward(scal, ids, tt, vocab, nbytes):
    d = tt.shape[0]
    vm = pl.BlockSpec(memory_space=pltpu.VMEM)
    return pl.pallas_call(
        functools.partial(gbst_fwd_body, nbytes, vocab),
        out_shape=(jax.ShapeDtypeStruct((TP, d), f32), jax.ShapeDtypeStruct((TP, d), bf16), jax.ShapeDtypeStruct((12 * ROWS, d), bf16),
                   jax.ShapeDtypeStruct((ROWS, 128), f32), jax.ShapeDtypeStruct((8, 128), f32), jax.ShapeDtypeStruct((8, d), f32)),
        in_specs=[pl.BlockSpec(memory_space=pltpu.SMEM), vm, vm],
        out_specs=(vm,) * 6,
        scratch_shapes=[pltpu.VMEM((d // 128, TP, 128), f32), pltpu.VMEM((VP, d), bf16)],
        compiler_params=pltpu.CompilerParams(vmem_limit_bytes=48 << 20),
        name="gbst_fwd",
    )(scal, ids, tt)


def gbst_backward(scal, ids, emb, wcol, vec, gs, ggain, vocab, nbytes):
    d = emb.shape[1]
    vm = pl.BlockSpec(memory_space=pltpu.VMEM)
    return pl.pallas_call(
        functools.partial(gbst_bwd_body, nbytes, vocab),
        out_shape=jax.ShapeDtypeStruct((d, VP), bf16),
        in_specs=[pl.BlockSpec(memory_space=pltpu.SMEM)] + [vm] * 6,
        out_specs=vm,
        scratch_shapes=[pltpu.VMEM((12 * ROWS, d), bf16), pltpu.VMEM((d // 128, TP, 128), f32)],
        compiler_params=pltpu.CompilerParams(vmem_limit_bytes=48 << 20),
        name="gbst_bwd",
    )(scal, ids, emb, wcol, vec, gs, ggain)


MESH = pl.DeviceIdType.MESH


def coords():
    w = lax.axis_index("wide")
    n = lax.axis_index("narrow")
    return w, w // 2, w % 2, n // 2, n % 2


def peer_ids():
    w, z, y, x, c = coords()
    n = 2 * x + c
    return {
        "y": (2 * z + 1 - y, n),
        "zp": (2 * ((z + 1) % 4) + y, n),
        "zm": (2 * ((z + 3) % 4) + y, n),
        "zo": (2 * ((z + 2) % 4) + y, n),
        "x": (w, 2 * (1 - x) + c),
        "c": (w, 2 * x + 1 - c),
    }


def enter(peers, names):
    barrier = pltpu.get_barrier_semaphore()
    for name in names:
        pl.semaphore_signal(barrier, inc=1, device_id=peers[name], device_id_type=MESH)
    pl.semaphore_wait(barrier, len(names))


class Gather:
    def __init__(self, shards, fulls, split, ssem, rsem, lsem):
        self.shards, self.fulls, self.split = shards, fulls, split
        self.ssem, self.rsem, self.lsem = ssem, rsem, lsem
        self.peers = peer_ids()
        self.w, self.z, self.y, self.x, self.c = coords()
        self.sent = []

    def enter(self):
        enter(self.peers, ("y", "zp", "zm", "x", "c"))

    def blocks(self):
        z, y = self.z, self.y
        up, down, far = (z + 1) % 4, (z + 3) % 4, (z + 2) % 4
        return (2 * z + 1 - y, 2 * down + y, 2 * down + 1 - y, 2 * up + y, 2 * up + 1 - y, 2 * far + y, 2 * far + 1 - y)

    def cols(self, i, half, quarter=None):
        width = self.fulls[i].shape[1] // 2
        start = half * width
        if quarter is not None:
            width = width // 2
            start = start + quarter * width
        return pl.ds(pl.multiple_of(start, 128), width)

    def mine(self, i):
        return self.cols(i, self.c, self.x if self.split[i] else None)

    def rows(self, i, owner):
        r = self.shards[i].shape[0]
        return pl.ds(pl.multiple_of(owner * r, 16), r)

    def copy(self, i, slot, src, owner, cols, to):
        return pltpu.make_async_remote_copy(
            src_ref=src, dst_ref=self.fulls[i].at[self.rows(i, owner), cols], send_sem=self.ssem.at[i, slot],
            recv_sem=self.rsem.at[i, slot], device_id=self.peers[to], device_id_type=MESH)

    def send(self, i, slot, src, owner, cols, to):
        cp = self.copy(i, slot, src, owner, cols, to)
        cp.start()
        self.sent.append(cp)

    def arrived(self, i, slot, cols):
        ref = self.fulls[i].at[self.rows(i, 0), cols]
        pltpu.make_async_remote_copy(
            src_ref=ref, dst_ref=ref, send_sem=self.ssem.at[i, slot], recv_sem=self.rsem.at[i, slot],
            device_id=self.peers["c"], device_id_type=MESH).wait_recv()

    def block(self, i, owner, cols):
        return self.fulls[i].at[self.rows(i, owner), cols]

    def start(self, i):
        own = self.shards[i].at[:, self.mine(i)]
        self.send(i, 0, own, self.w, self.mine(i), "y")
        self.send(i, 1, own, self.w, self.mine(i), "zp")
        self.send(i, 3, own, self.w, self.mine(i), "zm")
        cp = pltpu.make_async_copy(self.shards[i], self.fulls[i].at[self.rows(i, self.w), :], self.lsem.at[i])
        cp.start()
        self.local = getattr(self, "local", []) + [cp]

    def relay(self, i, slot):
        owner = self.blocks()[slot]
        src = self.block(i, owner, self.mine(i))
        self.send(i, 7 + slot, src, owner, self.mine(i), "c")
        if self.split[i]:
            self.send(i, 14 + slot, src, owner, self.mine(i), "x")

    def step_y(self, i):
        b = self.blocks()
        self.arrived(i, 0, self.mine(i))
        src = self.block(i, b[0], self.mine(i))
        self.send(i, 2, src, b[0], self.mine(i), "zp")
        self.send(i, 4, src, b[0], self.mine(i), "zm")
        self.relay(i, 0)

    def step_z(self, i):
        b = self.blocks()
        self.arrived(i, 1, self.mine(i))
        self.send(i, 5, self.block(i, b[1], self.mine(i)), b[1], self.mine(i), "zp")
        self.relay(i, 1)
        self.arrived(i, 4, self.mine(i))
        self.send(i, 6, self.block(i, b[4], self.mine(i)), b[4], self.mine(i), "zm")
        self.relay(i, 4)
        for slot in (2, 3):
            self.arrived(i, slot, self.mine(i))
            self.relay(i, slot)

    def step_far(self, i):
        for slot in (5, 6):
            self.arrived(i, slot, self.mine(i))
            self.relay(i, slot)

    def step_x(self, i):
        if self.split[i]:
            other = self.cols(i, self.c, 1 - self.x)
            for slot in range(7):
                owner = self.blocks()[slot]
                self.arrived(i, 14 + slot, other)
                self.send(i, 21 + slot, self.block(i, owner, other), owner, other, "c")

    def step_end(self, i):
        for slot in range(7):
            self.arrived(i, 7 + slot, self.mine(i))
            if self.split[i]:
                self.arrived(i, 21 + slot, self.mine(i))

    def finish(self):
        for cp in self.local:
            cp.wait()
        for cp in self.sent:
            cp.wait_send()


def gather_kernel(split, *refs):
    n = len(split)
    g = Gather(refs[:n], refs[n:2 * n], split, *refs[2 * n:])
    g.enter()
    for i in range(n):
        g.start(i)
    for step in (g.step_y, g.step_z, g.step_far, g.step_x, g.step_end):
        for i in range(n):
            step(i)
    g.finish()


def gather_all(shards, split, wide):
    n = len(shards)
    hbm = pl.BlockSpec(memory_space=pltpu.HBM)
    return pl.pallas_call(
        functools.partial(gather_kernel, split),
        out_shape=tuple(jax.ShapeDtypeStruct((wide * s.shape[0], s.shape[1]), s.dtype) for s in shards),
        in_specs=[hbm] * n,
        out_specs=(hbm,) * n,
        scratch_shapes=[pltpu.SemaphoreType.DMA((n, 28)), pltpu.SemaphoreType.DMA((n, 28)), pltpu.SemaphoreType.DMA((n,))],
        compiler_params=pltpu.CompilerParams(collective_id=1, has_side_effects=True),
        name="gather_weights",
    )(*shards)


class Reduce:
    STAGES = 9

    def __init__(self, terms, outs, order, own, rc, r1, r2, r3, ssem, rsem, lsem):
        self.terms, self.outs, self.order = terms, outs, order
        self.own, self.rc, self.r1, self.r2, self.r3 = own, rc, r1, r2, r3
        self.ssem, self.rsem, self.lsem = ssem, rsem, lsem
        self.peers = peer_ids()
        self.w, self.z, self.y, self.x, self.c = coords()
        self.sent = []

    def enter(self):
        enter(self.peers, ("y", "zp", "zm", "zo", "x", "c"))

    def send(self, i, slot, src, dst, to):
        cp = pltpu.make_async_remote_copy(
            src_ref=src, dst_ref=dst, send_sem=self.ssem.at[i, slot], recv_sem=self.rsem.at[i, slot],
            device_id=self.peers[to], device_id_type=MESH)
        cp.start()
        self.sent.append(cp)

    def arrived(self, i, slot, dst):
        pltpu.make_async_remote_copy(
            src_ref=dst, dst_ref=dst, send_sem=self.ssem.at[i, slot], recv_sem=self.rsem.at[i, slot],
            device_id=self.peers["c"], device_id_type=MESH).wait_recv()

    def half(self, i, c):
        width = self.terms[i].shape[4] // 2
        return pl.ds(pl.multiple_of(c * width, 128), width)

    def start(self, i):
        self.send(i, 0, self.terms[i].at[:, :, :, :, self.half(i, 1 - self.c)], self.rc[i], "c")
        cp = pltpu.make_async_copy(self.terms[i].at[:, :, :, :, self.half(i, self.c)], self.own[i], self.lsem.at[i])
        cp.start()
        self.local = getattr(self, "local", {})
        self.local[i] = cp

    def add(self, a, b):
        return (a.astype(f32) + b.astype(f32)).astype(bf16)

    def step_core(self, i):
        self.local[i].wait()
        self.arrived(i, 0, self.rc[i])

        def one(z, carry):
            self.own[i][z] = self.add(self.own[i][z], self.rc[i][z])
            return carry
        lax.fori_loop(0, 4, one, 0)
        if self.order[i] == "y":
            self.send(i, 1, self.own[i].at[:, 1 - self.y], self.r1[i], "y")
        else:
            self.send(i, 1, self.own[i].at[:, :, 1 - self.x], self.r1[i], "x")

    def step_one(self, i):
        self.arrived(i, 1, self.r1[i])

        def one(z, carry):
            if self.order[i] == "y":
                mine = self.own[i][z, self.y]
            else:
                mine = self.own[i][z, :, self.x]
            self.r1[i][z] = self.add(mine, self.r1[i][z])
            return carry
        lax.fori_loop(0, 4, one, 0)
        if self.order[i] == "y":
            self.send(i, 2, self.r1[i].at[:, 1 - self.x], self.r2[i], "x")
        else:
            self.send(i, 2, self.r1[i].at[:, 1 - self.y], self.r2[i], "y")

    def step_two(self, i):
        self.arrived(i, 2, self.r2[i])
        pick = self.x if self.order[i] == "y" else self.y

        def one(z, carry):
            self.r2[i][z] = self.add(self.r1[i][z, pick], self.r2[i][z])
            return carry
        lax.fori_loop(0, 4, one, 0)
        for dz, to in ((1, "zp"), (3, "zm"), (2, "zo")):
            self.send(i, 2 + dz, self.r2[i].at[(self.z + dz) % 4], self.r3[i].at[3 - dz], to)

    def step_z(self, i):
        total = self.r2[i][self.z].astype(f32)
        for dz in (1, 3, 2):
            self.arrived(i, 2 + dz, self.r3[i].at[3 - dz])
        for k in range(3):
            total = total + self.r3[i][k].astype(f32)
        out = self.outs[i]
        out[self.c, self.x] = total.astype(bf16)
        self.send(i, 6, out.at[self.c, self.x], out.at[self.c, self.x], "x")
        self.send(i, 7, out.at[self.c, self.x], out.at[self.c, self.x], "c")

    def step_x(self, i):
        out = self.outs[i]
        self.arrived(i, 6, out.at[self.c, 1 - self.x])
        self.send(i, 8, out.at[self.c, 1 - self.x], out.at[self.c, 1 - self.x], "c")

    def step_end(self, i):
        out = self.outs[i]
        self.arrived(i, 7, out.at[1 - self.c, self.x])
        self.arrived(i, 8, out.at[1 - self.c, 1 - self.x])

    def finish(self):
        for cp in self.sent:
            cp.wait_send()

    @staticmethod
    def scratch(shapes, order):
        own = [pltpu.VMEM((4, 2, 2, s[3], s[4] // 2), bf16) for s in shapes]
        rc = [pltpu.VMEM((4, 2, 2, s[3], s[4] // 2), bf16) for s in shapes]
        r1 = [pltpu.VMEM((4, 2, s[3], s[4] // 2), bf16) for s in shapes]
        r2 = [pltpu.VMEM((4, s[3], s[4] // 2), bf16) for s in shapes]
        r3 = [pltpu.VMEM((3, s[3], s[4] // 2), bf16) for s in shapes]
        n = len(shapes)
        return own + rc + r1 + r2 + r3 + [pltpu.SemaphoreType.DMA((n, 9)), pltpu.SemaphoreType.DMA((n, 9)), pltpu.SemaphoreType.DMA((n,))]

    @staticmethod
    def of(refs, order):
        n = len(order)
        cut = [refs[k * n:(k + 1) * n] for k in range(7)]
        return Reduce(cut[0], cut[1], order, *cut[2:7], *refs[7 * n:7 * n + 3])


SMALL = (16, 128)


def all_sum(value_ref, acc, slots, peers, ssem, rsem):
    acc[...] = value_ref[...]
    for k, to in enumerate(("c", "x", "y", "zn", "zo")):
        slots[5 + k] = acc[...]
        cp = pltpu.make_async_remote_copy(
            src_ref=slots.at[5 + k], dst_ref=slots.at[k], send_sem=ssem.at[k], recv_sem=rsem.at[k], device_id=peers[to], device_id_type=MESH)
        cp.start()
        cp.wait()
        acc[...] = acc[...] + slots[k]


def reduce_kernel(order, *refs):
    n = len(order)
    small_ref, small_out = refs[n], refs[2 * n + 1]
    rest = refs[2 * n + 2:]
    red = Reduce.of(refs[:n] + refs[n + 1:2 * n + 1] + rest[:5 * n + 3], order)
    acc, slots, ssem, rsem = rest[5 * n + 3:]
    red.peers["zn"] = near_z()
    red.enter()
    for i in range(n):
        red.start(i)
    all_sum(small_ref, acc, slots, red.peers, ssem, rsem)
    small_out[...] = acc[...]
    for step in (red.step_core, red.step_one, red.step_two, red.step_z, red.step_x, red.step_end):
        for i in range(n):
            step(i)
    red.finish()


def near_z():
    w, z, y, x, c = coords()
    return (2 * (z + 1 - 2 * (z % 2)) + y, 2 * x + c)


def reduce_all(terms, small, order):
    n = len(terms)
    hbm = pl.BlockSpec(memory_space=pltpu.HBM)
    vm = pl.BlockSpec(memory_space=pltpu.VMEM)
    shapes = [t.shape for t in terms]
    return pl.pallas_call(
        functools.partial(reduce_kernel, order),
        out_shape=tuple(jax.ShapeDtypeStruct((2, 2, s[3], s[4] // 2), bf16) for s in shapes) + (jax.ShapeDtypeStruct(SMALL, f32),),
        in_specs=[hbm] * n + [vm],
        out_specs=(vm,) * (n + 1),
        scratch_shapes=Reduce.scratch(shapes, order) + [pltpu.VMEM(SMALL, f32), pltpu.VMEM((10,) + SMALL, f32),
                                                        pltpu.SemaphoreType.DMA((5,)), pltpu.SemaphoreType.DMA((5,))],
        compiler_params=pltpu.CompilerParams(collective_id=2, has_side_effects=True, vmem_limit_bytes=56 << 20),
        name="reduce_grads",
    )(*terms, small)


def tn(a, b):
    return lax.dot_general(a, b, (((0,), (0,)), ((), ())), preferred_element_type=f32)


def norm_back(x, gain, gy):
    s = lax.rsqrt(jnp.mean(x * x, axis=1, keepdims=True) + EPS)
    t = gy * gain
    gx = s * t - x * (s * s * s) * jnp.mean(x * t, axis=1, keepdims=True)
    return gx, jnp.sum(gy * x * s, axis=0)


def layer(byte_ids, lengths, bucket, out_grad, rel_bias, vocab, tt, wq, wk, wv, wo, wg, wu, wd):
    ids = byte_ids[0]
    nbytes = ids.shape[0]
    ntok = nbytes // 2
    d = tt.shape[0]
    scal = jnp.stack([bucket[0], lengths[0, 0], lengths[0, 1]])
    idp = jnp.pad(ids.reshape(nbytes // 12, 12).T, ((0, 4), (0, ROWS - nbytes // 12)), constant_values=-1)
    stream, normed, emb, wcol, tot, vec = gbst_forward(scal, idp, tt, vocab, nbytes)
    q = nn(normed, wq).astype(bf16)
    k = nn(normed, wk).astype(bf16)
    v = nn(normed, wv).astype(bf16)
    nb = rel_bias.shape[0]
    base2 = jnp.dot(base_hot(nb), rel_bias.astype(f32), precision=lax.Precision.HIGHEST).T
    mixed, lse = attn_forward(scal, q, k, v, base2, ntok)
    middle = stream + nn(mixed, wo)
    g2 = vec[2]
    s2 = lax.rsqrt(jnp.mean(middle * middle, axis=1, keepdims=True) + EPS)
    normed_ff = (middle * s2 * g2).astype(bf16)
    gate = nn(normed_ff, wg)
    up = nn(normed_ff, wu)
    c0 = 0.7978845608028654
    th = jnp.tanh(c0 * (gate + 0.044715 * gate * gate * gate))
    act = 0.5 * gate * (1.0 + th)
    hidden = (act * up).astype(bf16)
    encoded = (middle + nn(hidden, wd)).astype(bf16)[:ntok][None]
    og = jnp.pad(out_grad[0], ((0, TP - ntok), (0, 0)))
    g_wd = tn(hidden, og).astype(bf16)
    gh = nt(og, wd)
    dact = 0.5 * (1.0 + th) + 0.5 * gate * (1.0 - th * th) * (c0 * (1.0 + 3 * 0.044715 * gate * gate))
    gg = (gh * up * dact).astype(bf16)
    gu = (gh * act).astype(bf16)
    g_wg = tn(normed_ff, gg).astype(bf16)
    g_wu = tn(normed_ff, gu).astype(bf16)
    g_nff = nt(gg, wg) + nt(gu, wu)
    gx2, g_gain2 = norm_back(middle, g2, g_nff)
    g_mid = og.astype(f32) + gx2
    g_br = g_mid.astype(bf16)
    g_wo = tn(mixed, g_br).astype(bf16)
    g_heads = nt(g_br, wo).astype(bf16)
    dq, dk, dv, db = attn_backward(scal, q, k, v, g_heads, lse, base2, ntok)
    g_rel = jnp.dot(base_hot(nb, True).T, db[:, :2, :].reshape(rel_bias.shape[1], 512).T, precision=lax.Precision.HIGHEST)
    g_wq = tn(normed, dq).astype(bf16)
    g_wk = tn(normed, dk).astype(bf16)
    g_wv = tn(normed, dv).astype(bf16)
    g_n = nt(dq, wq) + nt(dk, wk) + nt(dv, wv)
    gx1, g_gain1 = norm_back(stream, vec[1], g_n)
    g_stream = g_mid + gx1
    g_tt = gbst_backward(scal, idp, emb, wcol, vec, g_stream, jnp.stack([g_gain1, g_gain2]), vocab, nbytes)
    return encoded, (g_tt, g_wq, g_wk, g_wv, g_wo, g_wg, g_wu, g_wd), g_rel, tot[0, :5]


def body(byte_ids, lengths, bucket, out_grad, embedding, score_weight, gain_attn, w_query, w_key, w_value, w_attn_out, rel_bias, gain_ff, w_gate, w_up, w_ff_out):
    vocab, width = embedding.shape
    wide = lax.axis_size("wide")
    columns = jnp.concatenate([embedding.T, score_weight[:, None], gain_attn[:, None], gain_ff[:, None]], axis=1)
    tt = jnp.pad(columns, ((0, 0), (0, VP - columns.shape[1])))
    shards = (tt, w_query, w_key, w_value, w_attn_out, w_gate, w_up, w_ff_out)
    kernels = wide == 8 and lax.axis_size("narrow") == 4 and all(s.shape[0] % 32 == 0 for s in shards)
    if kernels:
        full = gather_all(shards, (False, False, False, False, False, True, True, False), wide)
    else:
        full = [lax.all_gather(s, "wide", axis=0, tiled=True) for s in shards]
    encoded, grads, g_rel, tot = layer(byte_ids, lengths, bucket, out_grad, rel_bias, vocab, *full)
    if kernels:
        small = jnp.pad(jnp.concatenate([g_rel.reshape(-1), tot]), (0, SMALL[0] * SMALL[1] - g_rel.size - 5)).reshape(SMALL)
        terms = [g.reshape(4, 2, 2, g.shape[0] // 16, g.shape[1]) for g in grads]
        outs = reduce_all(terms, small, ("x", "x", "y", "x", "y", "x", "y", "x"))
        small = outs[-1].reshape(-1)
        g_rel, tot = small[:g_rel.size].reshape(g_rel.shape), small[g_rel.size:g_rel.size + 5]
        sums = [o.transpose(1, 2, 0, 3).reshape(s.shape).astype(f32) for o, s in zip(outs, shards)]
    else:
        sums = [lax.psum(lax.psum_scatter(g, "wide", scatter_dimension=0, tiled=True), "narrow").astype(f32) for g in grads]
        g_rel, tot = lax.psum((g_rel, tot), ("wide", "narrow"))
    t = sums[0]
    return (encoded, t[:, :vocab].T, t[:, vocab], t[:, vocab + 1], *sums[1:5], g_rel, t[:, vocab + 2], *sums[5:], tot[:4] / tot[4])


def solution(mesh):
    both = ("wide", "narrow")
    rows = P("wide", None)
    vec = P("wide")
    placed = (P(both, None), P(both, None), P(both), P(both, None, None), P(None, "wide"), vec, vec, rows, rows, rows, rows, P(), vec, rows, rows, rows)
    outs = (P(both, None, None), P(None, "wide"), vec, vec, rows, rows, rows, rows, P(), vec, rows, rows, rows, P())
    return jax.shard_map(body, mesh=mesh, in_specs=placed, out_specs=outs, check_vma=False)
```

```python
import functools

import jax
import jax.numpy as jnp
from jax import lax
from jax.experimental import pallas as pl
from jax.experimental.pallas import tpu as pltpu
from jax.sharding import PartitionSpec as P

f32 = jnp.float32
bf16 = jnp.bfloat16
TP = 768
BLK = 128
NB = TP // BLK
LEFT = TP - BLK
STRIP = 2 * TP - BLK
W0 = LEFT - 128
WN = 384

def nt(a, b):
    return lax.dot_general(a, b, (((1,), (1,)), ((), ())), preferred_element_type=f32)

def nn(a, b):
    return lax.dot_general(a, b, (((1,), (0,)), ((), ())), preferred_element_type=f32)

def build_masks(scal_ref, kaug, raug, ntok):
    joined = scal_ref[0] == 1
    l0 = scal_ref[1]; l1 = scal_ref[2]
    half = ntok // 2
    u = lax.broadcasted_iota(jnp.int32, (TP, 128), 0)
    lane = lax.broadcasted_iota(jnp.int32, (TP, 128), 1)
    seg = (u >= half).astype(jnp.int32)
    lim = jnp.where(seg == 1, l1, l0)
    start = seg * half
    lim = jnp.where(joined, l0 + l1, lim)
    start = jnp.where(joined, 0, start)
    valid = (2 * (u - start) < lim) & (u < ntok)
    segs = jnp.where(joined, 0, seg)
    ok = valid & (segs == lane)
    kaug[...] = jnp.where((lane < 2) & jnp.logical_not(ok), -1e30, 0.0).astype(bf16)
    t = u
    rows = jnp.where((lane == segs), 1.0, 0.0).astype(bf16)
    for b in range(NB):
        blk = rows[b * 128:(b + 1) * 128]
        raug[b] = jnp.concatenate([blk, blk], axis=0)

def build_strip(base_ref, row0, strip):
    for hh in range(2):
        row = base_ref[pl.ds(row0 + hh, 1), :]
        cl = row[:, 0:1]; cr = row[:, 383:384]
        sq = jnp.broadcast_to(row, (128, 512))
        sq = pltpu.roll(sq, 0, 1, stride=1, stride_axis=0)
        win = sq[:, :WN].T
        lanes = slice(hh * 128, hh * 128 + 128)
        strip[0:W0, lanes] = jnp.broadcast_to(cl, (W0, 128))
        strip[W0:W0 + WN, lanes] = win
        strip[W0 + WN:STRIP, lanes] = jnp.broadcast_to(cr, (STRIP - W0 - WN, 128))

def stacked(blk):
    lane = lax.broadcasted_iota(jnp.int32, blk.shape, 1)
    z = jnp.zeros_like(blk)
    return jnp.concatenate([jnp.where(lane < 64, blk, z), jnp.where(lane >= 64, blk, z)], axis=0)

def fwd_pair(p, q_ref, k_ref, v_ref, base_ref, o_ref, lse_ref, kaug, raug, strip, vt):
    lanes = pl.ds(pl.multiple_of(p * 128, 128), 128)
    build_strip(base_ref, 2 * p, strip)
    vt[...] = v_ref[:, lanes].T
    kcat = jnp.concatenate([k_ref[:, lanes], kaug[...]], axis=1)
    vtv = vt[...]
    rowsel = lax.broadcasted_iota(jnp.int32, (128, 128), 0) < 64
    for b in range(NB):
        rhs = jnp.concatenate([stacked(q_ref[b * 128:(b + 1) * 128, lanes]), raug[b]], axis=1)
        s = nt(kcat, rhs) + strip[LEFT - b * 128:LEFT - b * 128 + TP, :]
        mx = jnp.max(s, axis=0, keepdims=True)
        e = jnp.exp(s - mx)
        l = jnp.sum(e, axis=0, keepdims=True)
        ot = nn(vtv, e.astype(bf16)) * (1.0 / l)
        lse_ref[p, b:b + 1, :] = mx + jnp.log(l)
        o = jnp.where(rowsel, ot[:, :128], ot[:, 128:])
        o_ref[b * 128:(b + 1) * 128, lanes] = o.T.astype(bf16)


def bwd_kernel(ntok, scal_ref, q_ref, k_ref, v_ref, g_ref, lse_ref, base_ref, dq_ref, dk_ref, dv_ref, db_ref, kaug, raug, strip, acc, kt, dk_s, dv_s):
    p = pl.program_id(0)
    @pl.when(p == 0)
    def _():
        build_masks(scal_ref, kaug, raug, ntok)
    build_strip(base_ref, 2 * p, strip)
    kt[...] = k_ref[...].T
    kcat = jnp.concatenate([k_ref[...], kaug[...]], axis=1)
    v = v_ref[...]
    ktv = kt[...]
    acc[...] = jnp.zeros_like(acc)
    dk_s[...] = jnp.zeros_like(dk_s)
    dv_s[...] = jnp.zeros_like(dv_s)
    rowsel = lax.broadcasted_iota(jnp.int32, (128, 128), 0) < 64
    for b in range(NB):
        qs = stacked(q_ref[b * 128:(b + 1) * 128, :])
        gs = stacked(g_ref[b * 128:(b + 1) * 128, :])
        rhs = jnp.concatenate([qs, raug[b]], axis=1)
        w = slice(LEFT - b * 128, LEFT - b * 128 + TP)
        s = nt(kcat, rhs) + strip[w, :]
        pr = jnp.exp(s - lse_ref[0, b:b + 1, :])
        dp = nt(v, gs)
        pdp = pr * dp
        delta = jnp.sum(pdp, axis=0, keepdims=True)
        ds = pdp - pr * delta
        acc[w, :] += ds
        dsb = ds.astype(bf16)
        dk_s[...] += nn(dsb, qs)
        dv_s[...] += nn(pr.astype(bf16), gs)
        dqt = nn(ktv, dsb)
        dq = jnp.where(rowsel, dqt[:, :128], dqt[:, 128:])
        dq_ref[b * 128:(b + 1) * 128, :] = dq.T.astype(bf16)
    dk_ref[...] = dk_s[...].astype(bf16)
    dv_ref[...] = dv_s[...].astype(bf16)
    fi = lax.broadcasted_iota(jnp.int32, (128, 128), 0)
    fj = lax.broadcasted_iota(jnp.int32, (128, 128), 1)
    flip = jnp.where(fi + fj == 127, 1.0, 0.0).astype(f32)
    for hh in range(2):
        lanes = slice(hh * 128, hh * 128 + 128)
        far_l = jnp.sum(acc[0:W0, lanes], keepdims=True)
        far_r = jnp.sum(acc[W0 + WN:STRIP, lanes], keepdims=True)
        win = acc[W0:W0 + WN, lanes]
        wt = lax.dot_general(flip, win, (((1,), (1,)), ((), ())), precision=lax.Precision.HIGHEST, preferred_element_type=f32)
        wt = jnp.concatenate([wt, jnp.zeros((128, 128), f32)], axis=1)
        wt = pltpu.roll(wt, 0, 1, stride=1, stride_axis=0)
        diag = jnp.sum(wt, axis=0, keepdims=True)
        lane = lax.broadcasted_iota(jnp.int32, (1, 512), 1)
        diag = diag + jnp.where(lane == 0, far_l, 0.0) + jnp.where(lane == 510, far_r, 0.0)
        db_ref[0, hh:hh + 1, :] = diag

def attn_backward(scal, q, k, v, g, lse, base2, ntok):
    heads = base2.shape[0]
    pairs = heads // 2
    col = pl.BlockSpec((TP, 128), lambda p: (0, p))
    sd = jax.ShapeDtypeStruct((TP, heads * 64), bf16)
    return pl.pallas_call(
        functools.partial(bwd_kernel, ntok),
        grid=(pairs,),
        out_shape=(sd, sd, sd, jax.ShapeDtypeStruct((pairs, 8, 512), f32)),
        in_specs=[pl.BlockSpec(memory_space=pltpu.SMEM), col, col, col, col, pl.BlockSpec((1, 8, 256), lambda p: (p, 0, 0)), pl.BlockSpec(memory_space=pltpu.VMEM)],
        out_specs=(col, col, col, pl.BlockSpec((1, 8, 512), lambda p: (p, 0, 0))),
        scratch_shapes=[pltpu.VMEM((TP, 128), bf16), pltpu.VMEM((NB, 256, 128), bf16), pltpu.VMEM((STRIP, 256), f32), pltpu.VMEM((STRIP, 256), f32), pltpu.VMEM((128, TP), bf16),
                        pltpu.VMEM((TP, 128), f32), pltpu.VMEM((TP, 128), f32)],
        compiler_params=pltpu.CompilerParams(vmem_limit_bytes=48 << 20),
        name="attn_bwd",
    )(scal, q, k, v, g, lse, base2)

def bucket_of(relative):
    distance = jnp.abs(relative)
    far = 8 + sum(((distance >= e).astype(jnp.int32) for e in (12, 16, 23, 32, 46, 64, 91)))
    near = jnp.where(distance < 8, distance, far)
    return near + 16 * (relative > 0).astype(jnp.int32)

def base_hot(nbuckets, grad=False):
    c = jnp.arange(512, dtype=jnp.int32)
    r = c - 255 if grad else jnp.where(c < 384, c - 128, c - 640)
    return (bucket_of(r)[:, None] == jnp.arange(nbuckets, dtype=jnp.int32)[None, :]).astype(f32)


ROWS = 128
VP = 384
VG = 512
VR = 272
EPS = 1e-6

def byte_valid_mat(scal_ref, nbytes):
    i = lax.broadcasted_iota(jnp.int32, (ROWS, 128), 0)
    j = lax.broadcasted_iota(jnp.int32, (ROWS, 128), 1)
    p = 12 * i + j
    slot = nbytes // 2
    joined = scal_ref[0] == 1
    l0 = scal_ref[1]; l1 = scal_ref[2]
    second = p >= slot
    start = jnp.where(joined, 0, jnp.where(second, slot, 0))
    lim = jnp.where(joined, l0 + l1, jnp.where(second, l1, l0))
    ok = (p - start < lim) & (p < nbytes) & (j < 12)
    return jnp.where(ok, 1.0, 0.0).astype(f32)

def inverse_counts(vm):
    v = [vm[:, j:j + 1] for j in range(12)]
    inv = {1: v}
    for b in (2, 3, 4):
        out = []
        for m in range(12 // b):
            tot = v[b * m]
            for t in range(1, b):
                tot = tot + v[b * m + t]
            out.append(1.0 / jnp.maximum(tot, 1.0))
        inv[b] = out
    return v, inv

def softmax_weights(e, inv):
    rate = {1: e}
    for b in (2, 3, 4):
        out = []
        for m in range(12 // b):
            tot = e[b * m]
            for t in range(1, b):
                tot = tot + e[b * m + t]
            out.append(tot * inv[b][m])
        rate[b] = out
    w = {b: [] for b in (1, 2, 3, 4)}
    for p in range(12):
        r = [rate[b][p // b] for b in (1, 2, 3, 4)]
        mx = jnp.maximum(jnp.maximum(r[0], r[1]), jnp.maximum(r[2], r[3]))
        ex = [jnp.exp(x - mx) for x in r]
        inv_t = 1.0 / (ex[0] + ex[1] + ex[2] + ex[3])
        for b in (1, 2, 3, 4):
            w[b].append(ex[b - 1] * inv_t)
    return w

def gbst_fwd_body(nbytes, vocab, scal_ref, ids_ref, tt_ref, stream_ref, normed_ref, emb_ref, wcol_ref, tot_ref, vec_ref, slabs, table_ref, hook):
    table_ref[...] = tt_ref[...].T
    base = vocab // 16 * 16
    tail = table_ref[base:base + 16, :].astype(f32)
    vec_ref[0:3, :] = tail[vocab - base:vocab - base + 3, :]
    vec_ref[3:8, :] = jnp.zeros((5, tail.shape[1]), f32)
    vm = byte_valid_mat(scal_ref, nbytes)
    v, inv = inverse_counts(vm)
    idt = ids_ref[...].astype(f32).T
    lane = lax.broadcasted_iota(jnp.int32, (ROWS, VP), 1).astype(f32)
    s = vec_ref[0:1, :]
    e = []
    for j in range(12):
        hot = jnp.where((lane == idt[:, j:j + 1]) & (v[j] > 0.5), 1.0, 0.0).astype(bf16)
        ej = nn(hot, table_ref[...])
        emb_ref[j * ROWS:(j + 1) * ROWS, :] = ej.astype(bf16)
        e.append(jnp.sum(ej * s, axis=1, keepdims=True))
        if j % 3 == 2:
            hook()
    w = softmax_weights(e, inv)
    l128 = lax.broadcasted_iota(jnp.int32, (ROWS, 128), 1)
    wc = jnp.zeros((ROWS, 128), f32)
    for b in (1, 2, 3, 4):
        for p in range(12):
            wc = jnp.where(l128 == (b - 1) * 12 + p, w[b][p], wc)
    wcol_ref[...] = wc
    tl = lax.broadcasted_iota(jnp.int32, (8, 128), 1)
    tot = jnp.zeros((8, 128), f32)
    for b in (1, 2, 3, 4):
        acc = w[b][0] * v[0]
        for p in range(1, 12):
            acc = acc + w[b][p] * v[p]
        tot = jnp.where(tl == b - 1, jnp.sum(acc, keepdims=True), tot)
    tot = jnp.where(tl == 4, jnp.sum(vm, keepdims=True), tot)
    tot_ref[...] = tot
    hook()
    E = lambda j: emb_ref[j * ROWS:(j + 1) * ROWS, :].astype(f32)
    s3 = lambda m: E(3 * m) + E(3 * m + 1) + E(3 * m + 2)
    for k in range(6):
        p0, p1 = 2 * k, 2 * k + 1
        b2 = 0.5 * (w[2][p0] + w[2][p1]) * inv[2][k]
        acc = (0.5 * w[1][p0] + b2) * E(p0) + (0.5 * w[1][p1] + b2) * E(p1)
        n = k // 2
        d = 0.5 * (w[4][p0] + w[4][p1]) * inv[4][n]
        acc = acc + d * ((E(4 * n) + E(4 * n + 1)) + (E(4 * n + 2) + E(4 * n + 3)))
        m0, m1 = p0 // 3, p1 // 3
        if m0 == m1:
            acc = acc + (0.5 * (w[3][p0] + w[3][p1]) * inv[3][m0]) * s3(m0)
        else:
            acc = acc + (0.5 * w[3][p0] * inv[3][m0]) * s3(m0) + (0.5 * w[3][p1] * inv[3][m1]) * s3(m1)
        put_strided(slabs, k, acc)
        if k % 2 == 1:
            hook()
    ntok = nbytes // 2
    for c in range(slabs.shape[0]):
        stream_ref[0:ntok, c * 128:(c + 1) * 128] = slabs[c, 0:ntok, :]
    stream_ref[ntok:TP, :] = jnp.zeros((TP - ntok, acc.shape[1]), f32)
    norm_rows(stream_ref, vec_ref[1:2, :], normed_ref)
    hook()


def put_strided(ref, k, val):
    for c in range(val.shape[1] // 128):
        ref[c, pl.ds(k, 124, stride=6), :] = val[:124, c * 128:(c + 1) * 128]

def get_strided(ref, k):
    parts = [ref[c, pl.ds(k, 124, stride=6), :] for c in range(ref.shape[0])]
    x = jnp.concatenate(parts, axis=1)
    return jnp.concatenate([x, jnp.zeros((4, x.shape[1]), f32)], axis=0)

def norm_rows(x_ref, gain_ref, out_ref):
    g = gain_ref
    for b in range(TP // 128):
        x = x_ref[b * 128:(b + 1) * 128, :]
        sc = lax.rsqrt(jnp.mean(x * x, axis=1, keepdims=True) + EPS)
        out_ref[b * 128:(b + 1) * 128, :] = (x * sc * g).astype(bf16)

def gbst_bwd_body(nbytes, vocab, scal_ref, ids_ref, emb_ref, wcol_ref, score_ref, gs_ref, ggain_ref, gt_ref, de_ref, slabs):
    for c in range(slabs.shape[0]):
        slabs[c] = gs_ref[:, c * 128:(c + 1) * 128]
    vm = byte_valid_mat(scal_ref, nbytes)
    v, inv = inverse_counts(vm)
    wc = wcol_ref[...]
    w = {b: [wc[:, (b - 1) * 12 + p:(b - 1) * 12 + p + 1] for p in range(12)] for b in (1, 2, 3, 4)}
    s = score_ref[0:1, :]
    E = lambda j: emb_ref[j * ROWS:(j + 1) * ROWS, :].astype(f32)
    s3 = lambda m: E(3 * m) + E(3 * m + 1) + E(3 * m + 2)
    s4 = lambda n: (E(4 * n) + E(4 * n + 1)) + (E(4 * n + 2) + E(4 * n + 3))
    dot = lambda a, b: jnp.sum(a * b, axis=1, keepdims=True)
    dw = {b: [None] * 12 for b in (1, 2, 3, 4)}
    D = []
    for k in range(6):
        dk = 0.5 * get_strided(slabs, k)
        D.append(dk)
        p0, p1 = 2 * k, 2 * k + 1
        x0, x1 = dot(dk, E(p0)), dot(dk, E(p1))
        dw[1][p0], dw[1][p1] = x0, x1
        dw[2][p0] = dw[2][p1] = (x0 + x1) * inv[2][k]
        m0, m1 = p0 // 3, p1 // 3
        a0 = dot(dk, s3(m0)) * inv[3][m0]
        dw[3][p0] = a0
        dw[3][p1] = a0 if m0 == m1 else dot(dk, s3(m1)) * inv[3][m1]
        dw[4][p0] = dw[4][p1] = dot(dk, s4(k // 2)) * inv[4][k // 2]
    dr = {b: [] for b in (1, 2, 3, 4)}
    for p in range(12):
        mean = w[1][p] * dw[1][p] + w[2][p] * dw[2][p] + w[3][p] * dw[3][p] + w[4][p] * dw[4][p]
        for b in (1, 2, 3, 4):
            dr[b].append(w[b][p] * (dw[b][p] - mean))
    rb = {1: dr[1]}
    for b in (2, 3, 4):
        out = []
        for m in range(12 // b):
            tot = dr[b][b * m]
            for t in range(1, b):
                tot = tot + dr[b][b * m + t]
            out.append(tot * inv[b][m])
        rb[b] = out
    t3 = []
    for m in range(4):
        terms = {}
        for p in (3 * m, 3 * m + 1, 3 * m + 2):
            terms[p // 2] = terms[p // 2] + w[3][p] if p // 2 in terms else w[3][p]
        acc = None
        for k, coef in terms.items():
            t = (coef * inv[3][m]) * D[k]
            acc = t if acc is None else acc + t
        t3.append(acc)
    gscore = jnp.zeros((8, s.shape[1]), f32)
    for n in range(3):
        t4 = ((w[4][4 * n] + w[4][4 * n + 1]) * inv[4][n]) * D[2 * n] + ((w[4][4 * n + 2] + w[4][4 * n + 3]) * inv[4][n]) * D[2 * n + 1]
        for p in range(4 * n, 4 * n + 4):
            k = p // 2
            c = rb[1][p] + rb[2][k] + rb[3][p // 3] + rb[4][n]
            b2 = (w[2][2 * k] + w[2][2 * k + 1]) * inv[2][k]
            de = v[p] * ((w[1][p] + b2) * D[k] + t3[p // 3] + t4 + c * s)
            de_ref[p * ROWS:(p + 1) * ROWS, :] = de.astype(bf16)
            y = c * E(p)
            gscore = gscore + jnp.sum(y.reshape(ROWS // 8, 8, s.shape[1]), axis=0)
    gscore = jnp.sum(gscore, axis=0, keepdims=True)
    row = lax.broadcasted_iota(jnp.int32, (VR, ROWS), 0)
    hots = [jnp.where(row == ids_ref[j:j + 1, :], 1.0, 0.0).astype(bf16) for j in range(12)]
    hot = jnp.concatenate(hots, axis=1)
    gtable = nn(hot, de_ref[...])
    row = lax.broadcasted_iota(jnp.int32, gtable.shape, 0)
    for i, extra in enumerate((gscore, ggain_ref[0:1, :], ggain_ref[1:2, :])):
        gtable = jnp.where(row == vocab + i, extra, gtable)
    gt_ref[:, 0:VR] = gtable.T.astype(bf16)
    gt_ref[:, VR:VG] = jnp.zeros((gt_ref.shape[0], VG - VR), bf16)

def gbst_backward(scal, ids, emb, wcol, vec, gs, ggain, vocab, nbytes):
    d = emb.shape[1]
    vm = pl.BlockSpec(memory_space=pltpu.VMEM)
    return pl.pallas_call(
        functools.partial(gbst_bwd_body, nbytes, vocab),
        out_shape=jax.ShapeDtypeStruct((d, VG), bf16),
        in_specs=[pl.BlockSpec(memory_space=pltpu.SMEM)] + [vm] * 6,
        out_specs=vm,
        scratch_shapes=[pltpu.VMEM((12 * ROWS, d), bf16), pltpu.VMEM((d // 128, TP, 128), f32)],
        compiler_params=pltpu.CompilerParams(vmem_limit_bytes=48 << 20),
        name="gbst_bwd",
    )(scal, ids, emb, wcol, vec, gs, ggain)


MESH = pl.DeviceIdType.MESH


def coords():
    w = lax.axis_index("wide")
    n = lax.axis_index("narrow")
    return w, w // 2, w % 2, n // 2, n % 2


def peer_ids():
    w, z, y, x, c = coords()
    n = 2 * x + c
    return {
        "y": (2 * z + 1 - y, n),
        "zp": (2 * ((z + 1) % 4) + y, n),
        "zm": (2 * ((z + 3) % 4) + y, n),
        "zo": (2 * ((z + 2) % 4) + y, n),
        "x": (w, 2 * (1 - x) + c),
        "c": (w, 2 * x + 1 - c),
    }


def enter(peers, names):
    barrier = pltpu.get_barrier_semaphore()
    for name in names:
        pl.semaphore_signal(barrier, inc=1, device_id=peers[name], device_id_type=MESH)
    pl.semaphore_wait(barrier, len(names))


class Gather:
    SENDS = 30
    SLOTS = 28

    def __init__(self, shards, fulls, split, ssem, rsem, lsem):
        self.shards, self.fulls, self.split = shards, fulls, split
        self.ssem, self.rsem, self.lsem = ssem, rsem, lsem
        self.peers = peer_ids()
        self.w, self.z, self.y, self.x, self.c = coords()
        z = self.z
        first = jnp.where(z == 3, 3, 1)
        second = jnp.where((z == 0) | (z == 3), 2, 3)
        self.order = (first, second, 6 - first - second)
        self.inner = (z == 1) | (z == 2)
        self.sent = []
        self.local = {}

    def enter(self):
        n = 2 * self.x + self.c
        barrier = pltpu.get_barrier_semaphore()
        near = [(owner, n) for _, owner in self.others()] + [self.peers["x"], self.peers["c"]]
        for peer in near:
            pl.semaphore_signal(barrier, inc=1, device_id=peer, device_id_type=MESH)
        pl.semaphore_wait(barrier, len(near))

    def cols(self, i, c):
        width = self.fulls[i].shape[1] // 2
        return pl.ds(pl.multiple_of(c * width, 128), width)

    def block(self, i, owner, part, ref=None):
        r = self.shards[i].shape[0]
        start = owner * r
        if self.split[i]:
            r = r // 2
            start = start + part[1] * r
        return (self.fulls[i] if ref is None else ref).at[pl.ds(pl.multiple_of(start, 16), r), self.cols(i, part[0])]

    @property
    def mine(self):
        return (self.c, self.x)

    def copy(self, i, out, slot, src, owner, part, device):
        return pltpu.make_async_remote_copy(
            src_ref=src, dst_ref=self.block(i, owner, part), send_sem=self.ssem.at[i, out],
            recv_sem=self.rsem.at[i, slot], device_id=device, device_id_type=MESH)

    def send(self, i, out, slot, owner, part, device, when=None, src=None):
        src = self.block(i, owner, part) if src is None else src
        cp = self.copy(i, out, slot, src, owner, part, device)
        if when is None:
            cp.start()
        else:
            pl.when(when)(cp.start)
        self.sent.append((i, out, when))

    def arrived(self, i, slot, owner, part):
        ref = self.block(i, owner, part)
        pltpu.make_async_remote_copy(
            src_ref=ref, dst_ref=ref, send_sem=self.ssem.at[i, 0], recv_sem=self.rsem.at[i, slot],
            device_id=self.peers["c"], device_id_type=MESH).wait_recv()

    def start_direct(self, i):
        n = 2 * self.x + self.c
        for k in range(1, 8):
            dz, dy = k // 2, k % 2
            to = (2 * lax.rem(self.z + dz, 4) + (1 - self.y if dy else self.y), n)
            self.send_rows(i, k, (4 - dz) % 4 * 2 + dy, self.w, self.c, to, self.half_rows(i, 0, self.c, self.shards[i]))
        r = self.shards[i].shape[0]
        cp = pltpu.make_async_copy(self.shards[i], self.fulls[i].at[pl.ds(pl.multiple_of(self.w * r, 16), r), :], self.lsem.at[i])
        cp.start()
        self.local[i] = cp

    def half_rows(self, i, owner, c, ref=None):
        r = self.shards[i].shape[0]
        return (self.fulls[i] if ref is None else ref).at[pl.ds(pl.multiple_of(owner * r + c * (r // 2), 16), r // 2), :]

    def send_rows(self, i, out, slot, owner, c, device, src=None):
        ref = self.half_rows(i, owner, c)
        cp = pltpu.make_async_remote_copy(
            src_ref=ref if src is None else src, dst_ref=ref, send_sem=self.ssem.at[i, out], recv_sem=self.rsem.at[i, slot],
            device_id=device, device_id_type=MESH)
        cp.start()
        self.sent.append((i, out, "rows"))

    def rows_arrived(self, i, slot, owner, c):
        ref = self.half_rows(i, owner, c)
        pltpu.make_async_remote_copy(
            src_ref=ref, dst_ref=ref, send_sem=self.ssem.at[i, 0], recv_sem=self.rsem.at[i, slot],
            device_id=self.peers["c"], device_id_type=MESH).wait_recv()

    def others(self):
        for k in range(1, 8):
            dz, dy = k // 2, k % 2
            yield k, 2 * lax.rem(self.z + dz, 4) + (1 - self.y if dy else self.y)

    def steps_direct(self, i):
        def relay():
            for k, owner in self.others():
                self.rows_arrived(i, k, owner, self.c)
                self.send_rows(i, 8 + k, 8 + k, owner, self.c, self.peers["c"])

        def end():
            for k, owner in self.others():
                self.rows_arrived(i, 8 + k, owner, 1 - self.c)
            self.local[i].wait()
        return [relay, end]

    def start(self, i):
        own = self.block(i, 0, self.mine, self.shards[i])
        n = 2 * self.x + self.c
        self.send(i, 0, 2, self.w, self.mine, (2 * jnp.minimum(self.z + 1, 3) + self.y, n), self.z < 3, own)
        self.send(i, 1, 0, self.w, self.mine, (2 * jnp.maximum(self.z - 1, 0) + self.y, n), self.z > 0, own)
        self.send(i, 5, 3, self.w, self.mine, self.peers["y"], None, own)
        r = self.shards[i].shape[0]
        cp = pltpu.make_async_copy(self.shards[i], self.fulls[i].at[pl.ds(pl.multiple_of(self.w * r, 16), r), :], self.lsem.at[i])
        cp.start()
        self.local[i] = cp

    def relay(self, i, s, n, owner):
        self.send(i, 9 + n, 7 + s, owner, self.mine, self.peers["c"])
        if self.split[i]:
            self.send(i, 16 + n, 14 + s, owner, self.mine, self.peers["x"])

    def step_z(self, i, j):
        d = self.order[j]
        o = lax.rem(self.z + d, 4)
        owner = 2 * o + self.y
        self.arrived(i, d - 1, owner, self.mine)
        to = jnp.where(self.inner, jnp.where(o < self.z, self.z + 1, self.z - 1), jnp.where(self.z == 0, 1, 2))
        slot = jnp.where(self.inner, lax.rem(o - to + 4, 4) - 1, 0)
        self.send(i, 2 + j, slot, owner, self.mine, (2 * to + self.y, 2 * self.x + self.c), self.inner)
        self.send(i, 6 + j, 3 + d, owner, self.mine, self.peers["y"])
        self.relay(i, d - 1, j, owner)

    def step_y(self, i, j):
        d = 0 if j < 0 else self.order[j]
        owner = 2 * lax.rem(self.z + d, 4) + 1 - self.y
        self.arrived(i, 3 + d, owner, self.mine)
        self.relay(i, 3 + d, 4 + j, owner)

    def each(self):
        for j in range(3):
            d = self.order[j]
            yield d - 1, j, 2 * lax.rem(self.z + d, 4) + self.y
        for j in range(-1, 3):
            d = 0 if j < 0 else self.order[j]
            yield 3 + d, 4 + j, 2 * lax.rem(self.z + d, 4) + 1 - self.y

    def step_x(self, i):
        if self.split[i]:
            other = (self.c, 1 - self.x)
            for s, n, owner in self.each():
                self.arrived(i, 14 + s, owner, other)
                self.send(i, 23 + n, 21 + s, owner, other, self.peers["c"])

    def step_end(self, i):
        for s, n, owner in self.each():
            self.arrived(i, 7 + s, owner, (1 - self.c, self.x))
            if self.split[i]:
                self.arrived(i, 21 + s, owner, (1 - self.c, 1 - self.x))
        self.local[i].wait()

    def finish(self):
        for i, out, when in self.sent:
            if isinstance(when, str):
                ref = self.half_rows(i, self.w, self.c)
                when = None
            else:
                ref = self.block(i, self.w, self.mine)
            cp = pltpu.make_async_remote_copy(
                src_ref=ref, dst_ref=ref, send_sem=self.ssem.at[i, out], recv_sem=self.rsem.at[i, 0],
                device_id=self.peers["c"], device_id_type=MESH)
            if when is None:
                cp.wait_send()
            else:
                pl.when(when)(cp.wait_send)

    def steps(self, i):
        return [functools.partial(self.step_y, i, -1)] + [functools.partial(f, i, j) for j in range(3) for f in (self.step_z, self.step_y)] + [
            functools.partial(self.step_x, i), functools.partial(self.step_end, i)]


class Reduce:
    STAGES = 9

    def __init__(self, terms, outs, order, own, rc, r1, r2, r3, ssem, rsem, lsem):
        self.terms, self.outs, self.order = terms, outs, order
        self.own, self.rc, self.r1, self.r2, self.r3 = own, rc, r1, r2, r3
        self.ssem, self.rsem, self.lsem = ssem, rsem, lsem
        self.peers = peer_ids()
        self.w, self.z, self.y, self.x, self.c = coords()
        self.sent = []

    def enter(self):
        enter(self.peers, ("y", "zp", "zm", "zo", "x", "c"))

    def send(self, i, slot, src, dst, to):
        cp = pltpu.make_async_remote_copy(
            src_ref=src, dst_ref=dst, send_sem=self.ssem.at[i, slot], recv_sem=self.rsem.at[i, slot],
            device_id=self.peers[to], device_id_type=MESH)
        cp.start()
        self.sent.append(cp)

    def arrived(self, i, slot, dst):
        pltpu.make_async_remote_copy(
            src_ref=dst, dst_ref=dst, send_sem=self.ssem.at[i, slot], recv_sem=self.rsem.at[i, slot],
            device_id=self.peers["c"], device_id_type=MESH).wait_recv()

    def half(self, i, c):
        width = self.terms[i].shape[4] // 2
        return pl.ds(pl.multiple_of(c * width, 128), width)

    def start(self, i):
        self.send(i, 0, self.terms[i].at[:, :, :, :, self.half(i, 1 - self.c)], self.rc[i], "c")
        cp = pltpu.make_async_copy(self.terms[i].at[:, :, :, :, self.half(i, self.c)], self.own[i], self.lsem.at[i])
        cp.start()
        self.local = getattr(self, "local", {})
        self.local[i] = cp

    def add(self, a, b):
        return (a.astype(f32) + b.astype(f32)).astype(bf16)

    def step_core(self, i):
        self.local[i].wait()
        self.arrived(i, 0, self.rc[i])

        def one(z, carry):
            self.own[i][z] = self.add(self.own[i][z], self.rc[i][z])
            return carry
        lax.fori_loop(0, 4, one, 0)
        if self.order[i] == "y":
            self.send(i, 1, self.own[i].at[:, 1 - self.y], self.r1[i], "y")
        else:
            self.send(i, 1, self.own[i].at[:, :, 1 - self.x], self.r1[i], "x")

    def step_one(self, i):
        self.arrived(i, 1, self.r1[i])

        def one(z, carry):
            if self.order[i] == "y":
                mine = self.own[i][z, self.y]
            else:
                mine = self.own[i][z, :, self.x]
            self.r1[i][z] = self.add(mine, self.r1[i][z])
            return carry
        lax.fori_loop(0, 4, one, 0)
        if self.order[i] == "y":
            self.send(i, 2, self.r1[i].at[:, 1 - self.x], self.r2[i], "x")
        else:
            self.send(i, 2, self.r1[i].at[:, 1 - self.y], self.r2[i], "y")

    def step_two(self, i):
        self.arrived(i, 2, self.r2[i])
        pick = self.x if self.order[i] == "y" else self.y

        def one(z, carry):
            self.r2[i][z] = self.add(self.r1[i][z, pick], self.r2[i][z])
            return carry
        lax.fori_loop(0, 4, one, 0)
        for dz, to in ((1, "zp"), (3, "zm"), (2, "zo")):
            self.send(i, 2 + dz, self.r2[i].at[(self.z + dz) % 4], self.r3[i].at[3 - dz], to)

    def step_z(self, i):
        total = self.r2[i][self.z].astype(f32)
        for dz in (1, 3, 2):
            self.arrived(i, 2 + dz, self.r3[i].at[3 - dz])
        for k in range(3):
            total = total + self.r3[i][k].astype(f32)
        out = self.outs[i]
        out[self.c, self.x] = total.astype(bf16)
        self.send(i, 6, out.at[self.c, self.x], out.at[self.c, self.x], "x")
        self.send(i, 7, out.at[self.c, self.x], out.at[self.c, self.x], "c")

    def step_x(self, i):
        out = self.outs[i]
        self.arrived(i, 6, out.at[self.c, 1 - self.x])
        self.send(i, 8, out.at[self.c, 1 - self.x], out.at[self.c, 1 - self.x], "c")

    def step_end(self, i):
        out = self.outs[i]
        self.arrived(i, 7, out.at[1 - self.c, self.x])
        self.arrived(i, 8, out.at[1 - self.c, 1 - self.x])

    def finish(self):
        for cp in self.sent:
            cp.wait_send()

    @staticmethod
    def scratch(shapes, order):
        own = [pltpu.VMEM((4, 2, 2, s[3], s[4] // 2), bf16) for s in shapes]
        rc = [pltpu.VMEM((4, 2, 2, s[3], s[4] // 2), bf16) for s in shapes]
        r1 = [pltpu.VMEM((4, 2, s[3], s[4] // 2), bf16) for s in shapes]
        r2 = [pltpu.VMEM((4, s[3], s[4] // 2), bf16) for s in shapes]
        r3 = [pltpu.VMEM((3, s[3], s[4] // 2), bf16) for s in shapes]
        n = len(shapes)
        return own + rc + r1 + r2 + r3 + [pltpu.SemaphoreType.DMA((n, 9)), pltpu.SemaphoreType.DMA((n, 9)), pltpu.SemaphoreType.DMA((n,))]

    @staticmethod
    def of(refs, order):
        n = len(order)
        cut = [refs[k * n:(k + 1) * n] for k in range(7)]
        return Reduce(cut[0], cut[1], order, *cut[2:7], *refs[7 * n:7 * n + 3])


SMALL = (16, 128)


def all_sum(value_ref, acc, slots, peers, ssem, rsem):
    acc[...] = value_ref[...]
    for k, to in enumerate(("c", "x", "y", "zn", "zo")):
        slots[5 + k] = acc[...]
        cp = pltpu.make_async_remote_copy(
            src_ref=slots.at[5 + k], dst_ref=slots.at[k], send_sem=ssem.at[k], recv_sem=rsem.at[k], device_id=peers[to], device_id_type=MESH)
        cp.start()
        cp.wait()
        acc[...] = acc[...] + slots[k]


def reduce_kernel(order, *refs):
    n = len(order)
    small_ref, small_out = refs[n], refs[2 * n + 1]
    rest = refs[2 * n + 2:]
    red = Reduce.of(refs[:n] + refs[n + 1:2 * n + 1] + rest[:5 * n + 3], order)
    acc, slots, ssem, rsem = rest[5 * n + 3:]
    red.peers["zn"] = near_z()
    red.enter()
    for i in range(n):
        red.start(i)
    all_sum(small_ref, acc, slots, red.peers, ssem, rsem)
    small_out[...] = acc[...]
    for step in (red.step_core, red.step_one, red.step_two, red.step_z, red.step_x, red.step_end):
        for i in range(n):
            step(i)
    red.finish()


def near_z():
    w, z, y, x, c = coords()
    return (2 * (z + 1 - 2 * (z % 2)) + y, 2 * x + c)


def reduce_all(terms, small, order):
    n = len(terms)
    hbm = pl.BlockSpec(memory_space=pltpu.HBM)
    vm = pl.BlockSpec(memory_space=pltpu.VMEM)
    shapes = [t.shape for t in terms]
    return pl.pallas_call(
        functools.partial(reduce_kernel, order),
        out_shape=tuple(jax.ShapeDtypeStruct((2, 2, s[3], s[4] // 2), bf16) for s in shapes) + (jax.ShapeDtypeStruct(SMALL, f32),),
        in_specs=[hbm] * n + [vm],
        out_specs=(vm,) * (n + 1),
        scratch_shapes=Reduce.scratch(shapes, order) + [pltpu.VMEM(SMALL, f32), pltpu.VMEM((10,) + SMALL, f32),
                                                        pltpu.SemaphoreType.DMA((5,)), pltpu.SemaphoreType.DMA((5,))],
        compiler_params=pltpu.CompilerParams(collective_id=2, has_side_effects=True, vmem_limit_bytes=56 << 20),
        name="reduce_grads",
    )(*terms, small)


def none():
    pass


class Feed:
    def __init__(self, steps, share=1):
        self.steps = list(steps)
        self.share = share

    def __call__(self):
        for _ in range(self.share):
            if self.steps:
                self.steps.pop(0)()

    def rest(self):
        while self.steps:
            self.steps.pop(0)()


def forward_kernel(nbytes, vocab, split, *refs):
    scal_ref, ids_ref, base_ref = refs[:3]
    shards = refs[3:11]
    outs = refs[11:28]
    fulls = list(outs[:7])
    stream_o, normed_o, emb_o, wcol_o, tot_o, vec_o, q_o, k_o, v_o, mixed_o = outs[7:17]
    lse_o = refs[28]
    (tt, wq, wk, wv, stream, normed, emb, wcol, tot, vec, q, k, v, mixed, lse, slabs, table, kaug, raug, strip, vt, osem, wsem) = refs[29:52]
    done = []

    def out(src, dst):
        cp = pltpu.make_async_copy(src, dst, osem.at[len(done)])
        cp.start()
        done.append(cp)

    ntok = nbytes // 2
    if split is not None:
        g = Gather(shards, [tt] + fulls, split, *refs[52:55])
        g.enter()
        g.start_direct(0)
        for i in range(1, 4):
            g.start(i)
        build_masks(scal_ref, kaug, raug, ntok)
        relay, end = g.steps_direct(0)
        relay()
        for i in range(4, 8):
            g.start(i)
        end()
        plans = [None] + [g.steps(i) for i in range(1, 8)]
        early = Feed([plans[i][s] for s in range(8) for i in (1, 2, 3)], 3)
        late = [plans[i][s] for s in range(8) for i in (4, 5, 6, 7)]
        per = -(-len(late) // 6)
        chunks = [late[j * per:(j + 1) * per] for j in range(6)]
    else:
        cp = pltpu.make_async_copy(shards[0], tt, wsem.at[3])
        cp.start()
        build_masks(scal_ref, kaug, raug, ntok)
        cp.wait()
        early = Feed([])
        chunks = [[]] * 6
    gbst_fwd_body(nbytes, vocab, scal_ref, ids_ref, tt, stream, normed, emb, wcol, tot, vec, slabs, table, early)
    early.rest()
    for src, dst in ((stream, stream_o), (normed, normed_o), (emb, emb_o), (wcol, wcol_o), (tot, tot_o), (vec, vec_o)):
        out(src, dst)
    loads = []
    for i, dst in enumerate((wq, wk, wv)):
        if split is not None:
            plans[i + 1][8]()
        cp = pltpu.make_async_copy(shards[i + 1] if split is None else fulls[i], dst, wsem.at[i])
        cp.start()
        loads.append(cp)
    for cp, w, dst, to in zip(loads, (wq, wk, wv), (q, k, v), (q_o, k_o, v_o)):
        cp.wait()

        def rows(b, carry):
            sl = pl.ds(pl.multiple_of(b * 256, 256), 256)
            dst[sl, :] = nn(normed[sl, :], w[...]).astype(bf16)
            return carry
        lax.fori_loop(0, TP // 256, rows, 0)
        out(dst, to)

    def pair(p, carry):
        for j in range(6):
            if chunks[j]:
                @pl.when(p == j)
                def _():
                    for step in chunks[j]:
                        step()
        fwd_pair(p, q, k, v, base_ref, mixed, lse, kaug, raug, strip, vt)
        return carry
    lax.fori_loop(0, q.shape[1] // 128, pair, 0)
    out(mixed, mixed_o)
    out(lse, lse_o)
    if split is not None:
        for i in range(4, 8):
            plans[i][8]()
        g.finish()
    for cp in done:
        cp.wait()


def forward_one(scal, ids, base2, shards, vocab, nbytes, wide, split):
    d = shards[1].shape[1]
    hbm = pl.BlockSpec(memory_space=pltpu.HBM)
    vm = pl.BlockSpec(memory_space=pltpu.VMEM)
    pairs = d // 128
    many = 1 if split is None else wide
    sd = jax.ShapeDtypeStruct
    acts = [((TP, d), f32), ((TP, d), bf16), ((12 * ROWS, d), bf16), ((ROWS, 128), f32), ((8, 128), f32), ((8, d), f32),
            ((TP, d), bf16), ((TP, d), bf16), ((TP, d), bf16), ((TP, d), bf16), ((pairs, 8, 256), f32)]
    wq = (d, d)
    scratch = [pltpu.VMEM((d, VP), bf16)] + [pltpu.VMEM(wq, bf16)] * 3 + [pltpu.VMEM(*a) for a in acts]
    scratch += [pltpu.VMEM((d // 128, TP, 128), f32), pltpu.VMEM((VP, d), bf16), pltpu.VMEM((TP, 128), bf16), pltpu.VMEM((NB, 256, 128), bf16),
                pltpu.VMEM((STRIP, 256), f32), pltpu.VMEM((128, TP), bf16), pltpu.SemaphoreType.DMA((11,)), pltpu.SemaphoreType.DMA((4,))]
    params = dict(vmem_limit_bytes=56 << 20)
    if split is not None:
        scratch += [pltpu.SemaphoreType.DMA((8, Gather.SENDS)), pltpu.SemaphoreType.DMA((8, Gather.SLOTS)), pltpu.SemaphoreType.DMA((8,))]
        params.update(collective_id=1, has_side_effects=True)
        whole = [sd((many * s.shape[0], s.shape[1]), bf16) for s in shards[1:]]
    else:
        whole = [sd((8, 128), bf16)] * 7
    return pl.pallas_call(
        functools.partial(forward_kernel, nbytes, vocab, split),
        out_shape=tuple(whole) + tuple(sd(*a) for a in acts),
        in_specs=[pl.BlockSpec(memory_space=pltpu.SMEM), vm, vm] + [hbm] * 8,
        out_specs=(hbm,) * 18,
        scratch_shapes=scratch,
        compiler_params=pltpu.CompilerParams(**params),
        name="forward_one",
    )(scal, ids, base2, *shards)


def tn(a, b):
    return lax.dot_general(a, b, (((0,), (0,)), ((), ())), preferred_element_type=f32)


def norm_back(x, gain, gy):
    s = lax.rsqrt(jnp.mean(x * x, axis=1, keepdims=True) + EPS)
    t = gy * gain
    gx = s * t - x * (s * s * s) * jnp.mean(x * t, axis=1, keepdims=True)
    return gx, jnp.sum(gy * x * s, axis=0)


def layer(byte_ids, lengths, bucket, out_grad, rel_bias, vocab, shards, wide, split):
    ids = byte_ids[0]
    nbytes = ids.shape[0]
    ntok = nbytes // 2
    scal = jnp.stack([bucket[0], lengths[0, 0], lengths[0, 1]])
    idp = jnp.pad(ids.reshape(nbytes // 12, 12).T, ((0, 4), (0, ROWS - nbytes // 12)), constant_values=-1)
    nb = rel_bias.shape[0]
    base2 = jnp.dot(base_hot(nb), rel_bias.astype(f32), precision=lax.Precision.HIGHEST).T
    done = forward_one(scal, idp, base2, shards, vocab, nbytes, wide, split)
    wq, wk, wv, wo, wg, wu, wd = shards[1:] if split is None else done[:7]
    stream, normed, emb, wcol, tot, vec, q, k, v, mixed, lse = done[7:]
    middle = stream + nn(mixed, wo)
    g2 = vec[2]
    s2 = lax.rsqrt(jnp.mean(middle * middle, axis=1, keepdims=True) + EPS)
    normed_ff = (middle * s2 * g2).astype(bf16)
    gate = nn(normed_ff, wg)
    up = nn(normed_ff, wu)
    c0 = 0.7978845608028654
    th = jnp.tanh(c0 * (gate + 0.044715 * gate * gate * gate))
    act = 0.5 * gate * (1.0 + th)
    hidden = (act * up).astype(bf16)
    encoded = (middle + nn(hidden, wd)).astype(bf16)[:ntok][None]
    og = jnp.pad(out_grad[0], ((0, TP - ntok), (0, 0)))
    g_wd = tn(hidden, og).astype(bf16)
    gh = nt(og, wd)
    dact = 0.5 * (1.0 + th) + 0.5 * gate * (1.0 - th * th) * (c0 * (1.0 + 3 * 0.044715 * gate * gate))
    gg = (gh * up * dact).astype(bf16)
    gu = (gh * act).astype(bf16)
    g_wg = tn(normed_ff, gg).astype(bf16)
    g_wu = tn(normed_ff, gu).astype(bf16)
    g_nff = nt(gg, wg) + nt(gu, wu)
    gx2, g_gain2 = norm_back(middle, g2, g_nff)
    g_mid = og.astype(f32) + gx2
    g_br = g_mid.astype(bf16)
    g_wo = tn(mixed, g_br).astype(bf16)
    g_heads = nt(g_br, wo).astype(bf16)
    dq, dk, dv, db = attn_backward(scal, q, k, v, g_heads, lse, base2, ntok)
    g_rel = jnp.dot(base_hot(nb, True).T, db[:, :2, :].reshape(rel_bias.shape[1], 512).T, precision=lax.Precision.HIGHEST)
    g_wq = tn(normed, dq).astype(bf16)
    g_wk = tn(normed, dk).astype(bf16)
    g_wv = tn(normed, dv).astype(bf16)
    g_n = nt(dq, wq) + nt(dk, wk) + nt(dv, wv)
    gx1, g_gain1 = norm_back(stream, vec[1], g_n)
    g_stream = g_mid + gx1
    g_tt = gbst_backward(scal, idp, emb, wcol, vec, g_stream, jnp.stack([g_gain1, g_gain2]), vocab, nbytes)
    return encoded, (g_tt, g_wq, g_wk, g_wv, g_wo, g_wg, g_wu, g_wd), g_rel, tot[0, :5]


def body(byte_ids, lengths, bucket, out_grad, embedding, score_weight, gain_attn, w_query, w_key, w_value, w_attn_out, rel_bias, gain_ff, w_gate, w_up, w_ff_out):
    vocab, width = embedding.shape
    wide = lax.axis_size("wide")
    columns = jnp.concatenate([embedding.T, score_weight[:, None], gain_attn[:, None], gain_ff[:, None]], axis=1)
    tt = jnp.pad(columns, ((0, 0), (0, VP - columns.shape[1])))
    rows = tt.shape[0]
    shards = (tt, w_query, w_key, w_value, w_attn_out, w_gate, w_up, w_ff_out)
    kernels = wide == 8 and lax.axis_size("narrow") == 4 and all(s.shape[0] % 32 == 0 for s in shards)
    split = (True, True, True, True, False, False, True, True) if kernels else None
    if not kernels:
        shards = tuple(lax.all_gather(s, "wide", axis=0, tiled=True) for s in shards)
    encoded, grads, g_rel, tot = layer(byte_ids, lengths, bucket, out_grad, rel_bias, vocab, shards, wide, split)
    if kernels:
        small = jnp.pad(jnp.concatenate([g_rel.reshape(-1), tot]), (0, SMALL[0] * SMALL[1] - g_rel.size - 5)).reshape(SMALL)
        terms = [g.reshape(4, 2, 2, g.shape[0] // 16, g.shape[1]) for g in grads]
        outs = reduce_all(terms, small, ("y", "x", "x", "y", "x", "x", "y", "y"))
        small = outs[-1].reshape(-1)
        g_rel, tot = small[:g_rel.size].reshape(g_rel.shape), small[g_rel.size:g_rel.size + 5]
        sums = [o.transpose(1, 2, 0, 3).reshape(2 * o.shape[1] * o.shape[2] // 2, 2 * o.shape[3]).astype(f32) for o in outs[:-1]]
    else:
        sums = [lax.psum(lax.psum_scatter(g, "wide", scatter_dimension=0, tiled=True), "narrow").astype(f32) for g in grads]
        g_rel, tot = lax.psum((g_rel, tot), ("wide", "narrow"))
    t = sums[0]
    return (encoded, t[:, :vocab].T, t[:, vocab], t[:, vocab + 1], *sums[1:5], g_rel, t[:, vocab + 2], *sums[5:], tot[:4] / tot[4])


def solution(mesh):
    both = ("wide", "narrow")
    rows = P("wide", None)
    vec = P("wide")
    placed = (P(both, None), P(both, None), P(both), P(both, None, None), P(None, "wide"), vec, vec, rows, rows, rows, rows, P(), vec, rows, rows, rows)
    outs = (P(both, None, None), P(None, "wide"), vec, vec, rows, rows, rows, rows, P(), vec, rows, rows, rows, P())
    return jax.shard_map(body, mesh=mesh, in_specs=placed, out_specs=outs, check_vma=False)
```

```python
import functools

import jax
import jax.numpy as jnp
from jax import lax
from jax.experimental import pallas as pl
from jax.experimental.pallas import tpu as pltpu
from jax.sharding import PartitionSpec as P

f32 = jnp.float32
bf16 = jnp.bfloat16
TP = 768
BLK = 128
NB = TP // BLK
LEFT = TP - BLK
STRIP = 2 * TP - BLK
W0 = LEFT - 128
WN = 384

def nt(a, b):
    return lax.dot_general(a, b, (((1,), (1,)), ((), ())), preferred_element_type=f32)

def nn(a, b):
    return lax.dot_general(a, b, (((1,), (0,)), ((), ())), preferred_element_type=f32)

def build_masks(scal_ref, kaug, raug, ntok):
    joined = scal_ref[0] == 1
    l0 = scal_ref[1]; l1 = scal_ref[2]
    half = ntok // 2
    u = lax.broadcasted_iota(jnp.int32, (TP, 128), 0)
    lane = lax.broadcasted_iota(jnp.int32, (TP, 128), 1)
    seg = (u >= half).astype(jnp.int32)
    lim = jnp.where(seg == 1, l1, l0)
    start = seg * half
    lim = jnp.where(joined, l0 + l1, lim)
    start = jnp.where(joined, 0, start)
    valid = (2 * (u - start) < lim) & (u < ntok)
    segs = jnp.where(joined, 0, seg)
    ok = valid & (segs == lane)
    kaug[...] = jnp.where((lane < 2) & jnp.logical_not(ok), -1e30, 0.0).astype(bf16)
    t = u
    rows = jnp.where((lane == segs), 1.0, 0.0).astype(bf16)
    for b in range(NB):
        blk = rows[b * 128:(b + 1) * 128]
        raug[b] = jnp.concatenate([blk, blk], axis=0)

def build_strip(base_ref, row0, strip):
    for hh in range(2):
        row = base_ref[pl.ds(row0 + hh, 1), :]
        cl = row[:, 0:1]; cr = row[:, 383:384]
        sq = jnp.broadcast_to(row, (128, 512))
        sq = pltpu.roll(sq, 0, 1, stride=1, stride_axis=0)
        win = sq[:, :WN].T
        lanes = slice(hh * 128, hh * 128 + 128)
        strip[0:W0, lanes] = jnp.broadcast_to(cl, (W0, 128))
        strip[W0:W0 + WN, lanes] = win
        strip[W0 + WN:STRIP, lanes] = jnp.broadcast_to(cr, (STRIP - W0 - WN, 128))

def stacked(blk):
    lane = lax.broadcasted_iota(jnp.int32, blk.shape, 1)
    z = jnp.zeros_like(blk)
    return jnp.concatenate([jnp.where(lane < 64, blk, z), jnp.where(lane >= 64, blk, z)], axis=0)

def fwd_pair(p, q_ref, k_ref, v_ref, base_ref, o_ref, lse_ref, kaug, raug, strip, vt):
    lanes = pl.ds(pl.multiple_of(p * 128, 128), 128)
    build_strip(base_ref, 2 * p, strip)
    vt[...] = v_ref[:, lanes].T
    kcat = jnp.concatenate([k_ref[:, lanes], kaug[...]], axis=1)
    vtv = vt[...]
    rowsel = lax.broadcasted_iota(jnp.int32, (128, 128), 0) < 64
    for b in range(NB):
        rhs = jnp.concatenate([stacked(q_ref[b * 128:(b + 1) * 128, lanes]), raug[b]], axis=1)
        s = nt(kcat, rhs) + strip[LEFT - b * 128:LEFT - b * 128 + TP, :]
        mx = jnp.max(s, axis=0, keepdims=True)
        e = jnp.exp(s - mx)
        l = jnp.sum(e, axis=0, keepdims=True)
        ot = nn(vtv, e.astype(bf16)) * (1.0 / l)
        lse_ref[p, b:b + 1, :] = mx + jnp.log(l)
        o = jnp.where(rowsel, ot[:, :128], ot[:, 128:])
        o_ref[b * 128:(b + 1) * 128, lanes] = o.T.astype(bf16)


def bwd_pair(p, q_ref, k_ref, v_ref, g_ref, lse_ref, base_ref, db_ref, kaug, raug, strip, acc, kt, dk_s, dv_s, hook=None):
    lanes = pl.ds(pl.multiple_of(p * 128, 128), 128)
    build_strip(base_ref, 2 * p, strip)
    kt[...] = k_ref[:, lanes].T
    kcat = jnp.concatenate([k_ref[:, lanes], kaug[...]], axis=1)
    v = v_ref[:, lanes]
    ktv = kt[...]
    acc[...] = jnp.zeros_like(acc)
    dk_s[...] = jnp.zeros_like(dk_s)
    dv_s[...] = jnp.zeros_like(dv_s)
    rowsel = lax.broadcasted_iota(jnp.int32, (128, 128), 0) < 64
    for b in range(NB):
        rows = slice(b * 128, (b + 1) * 128)
        qs = stacked(q_ref[rows, lanes])
        gs = stacked(g_ref[rows, lanes])
        rhs = jnp.concatenate([qs, raug[b]], axis=1)
        w = slice(LEFT - b * 128, LEFT - b * 128 + TP)
        s = nt(kcat, rhs) + strip[w, :]
        pr = jnp.exp(s - lse_ref[p, b:b + 1, :])
        dp = nt(v, gs)
        pdp = pr * dp
        delta = jnp.sum(pdp, axis=0, keepdims=True)
        ds = pdp - pr * delta
        acc[w, :] += ds
        dsb = ds.astype(bf16)
        dk_s[...] += nn(dsb, qs)
        dv_s[...] += nn(pr.astype(bf16), gs)
        dqt = nn(ktv, dsb)
        dq = jnp.where(rowsel, dqt[:, :128], dqt[:, 128:])
        q_ref[rows, lanes] = dq.T.astype(bf16)
    k_ref[:, lanes] = dk_s[...].astype(bf16)
    v_ref[:, lanes] = dv_s[...].astype(bf16)
    fi = lax.broadcasted_iota(jnp.int32, (128, 128), 0)
    fj = lax.broadcasted_iota(jnp.int32, (128, 128), 1)
    flip = jnp.where(fi + fj == 127, 1.0, 0.0).astype(f32)
    for hh in range(2):
        half = slice(hh * 128, hh * 128 + 128)
        far_l = jnp.sum(acc[0:W0, half], keepdims=True)
        far_r = jnp.sum(acc[W0 + WN:STRIP, half], keepdims=True)
        win = acc[W0:W0 + WN, half]
        wt = lax.dot_general(flip, win, (((1,), (1,)), ((), ())), precision=lax.Precision.HIGHEST, preferred_element_type=f32)
        wt = jnp.concatenate([wt, jnp.zeros((128, 128), f32)], axis=1)
        wt = pltpu.roll(wt, 0, 1, stride=1, stride_axis=0)
        diag = jnp.sum(wt, axis=0, keepdims=True)
        lane = lax.broadcasted_iota(jnp.int32, (1, 512), 1)
        diag = diag + jnp.where(lane == 0, far_l, 0.0) + jnp.where(lane == 510, far_r, 0.0)
        db_ref[pl.ds(2 * p + hh, 1), :] = diag


def bucket_of(relative):
    distance = jnp.abs(relative)
    far = 8 + sum(((distance >= e).astype(jnp.int32) for e in (12, 16, 23, 32, 46, 64, 91)))
    near = jnp.where(distance < 8, distance, far)
    return near + 16 * (relative > 0).astype(jnp.int32)

def base_hot(nbuckets, grad=False):
    c = jnp.arange(512, dtype=jnp.int32)
    r = c - 255 if grad else jnp.where(c < 384, c - 128, c - 640)
    return (bucket_of(r)[:, None] == jnp.arange(nbuckets, dtype=jnp.int32)[None, :]).astype(f32)


ROWS = 128
VP = 384
VG = 512
VR = 272
EPS = 1e-6

def byte_valid_mat(scal_ref, nbytes):
    i = lax.broadcasted_iota(jnp.int32, (ROWS, 128), 0)
    j = lax.broadcasted_iota(jnp.int32, (ROWS, 128), 1)
    p = 12 * i + j
    slot = nbytes // 2
    joined = scal_ref[0] == 1
    l0 = scal_ref[1]; l1 = scal_ref[2]
    second = p >= slot
    start = jnp.where(joined, 0, jnp.where(second, slot, 0))
    lim = jnp.where(joined, l0 + l1, jnp.where(second, l1, l0))
    ok = (p - start < lim) & (p < nbytes) & (j < 12)
    return jnp.where(ok, 1.0, 0.0).astype(f32)

def inverse_counts(vm):
    v = [vm[:, j:j + 1] for j in range(12)]
    inv = {1: v}
    for b in (2, 3, 4):
        out = []
        for m in range(12 // b):
            tot = v[b * m]
            for t in range(1, b):
                tot = tot + v[b * m + t]
            out.append(1.0 / jnp.maximum(tot, 1.0))
        inv[b] = out
    return v, inv

def softmax_weights(e, inv):
    rate = {1: e}
    for b in (2, 3, 4):
        out = []
        for m in range(12 // b):
            tot = e[b * m]
            for t in range(1, b):
                tot = tot + e[b * m + t]
            out.append(tot * inv[b][m])
        rate[b] = out
    w = {b: [] for b in (1, 2, 3, 4)}
    for p in range(12):
        r = [rate[b][p // b] for b in (1, 2, 3, 4)]
        mx = jnp.maximum(jnp.maximum(r[0], r[1]), jnp.maximum(r[2], r[3]))
        ex = [jnp.exp(x - mx) for x in r]
        inv_t = 1.0 / (ex[0] + ex[1] + ex[2] + ex[3])
        for b in (1, 2, 3, 4):
            w[b].append(ex[b - 1] * inv_t)
    return w

def gbst_fwd_body(nbytes, vocab, scal_ref, ids_ref, tt_ref, stream_ref, normed_ref, emb_ref, wcol_ref, tot_ref, vec_ref, slabs, table_ref, hook):
    table_ref[...] = tt_ref[...].T
    base = vocab // 16 * 16
    tail = table_ref[base:base + 16, :].astype(f32)
    vec_ref[0:3, :] = tail[vocab - base:vocab - base + 3, :]
    vec_ref[3:8, :] = jnp.zeros((5, tail.shape[1]), f32)
    vm = byte_valid_mat(scal_ref, nbytes)
    v, inv = inverse_counts(vm)
    idt = ids_ref[...].astype(f32).T
    lane = lax.broadcasted_iota(jnp.int32, (ROWS, VP), 1).astype(f32)
    s = vec_ref[0:1, :]
    e = []
    for j in range(12):
        hot = jnp.where((lane == idt[:, j:j + 1]) & (v[j] > 0.5), 1.0, 0.0).astype(bf16)
        ej = nn(hot, table_ref[...])
        emb_ref[j * ROWS:(j + 1) * ROWS, :] = ej.astype(bf16)
        e.append(jnp.sum(ej * s, axis=1, keepdims=True))
        if j % 3 == 2:
            hook()
    w = softmax_weights(e, inv)
    l128 = lax.broadcasted_iota(jnp.int32, (ROWS, 128), 1)
    wc = jnp.zeros((ROWS, 128), f32)
    for b in (1, 2, 3, 4):
        for p in range(12):
            wc = jnp.where(l128 == (b - 1) * 12 + p, w[b][p], wc)
    wcol_ref[...] = wc
    tl = lax.broadcasted_iota(jnp.int32, (8, 128), 1)
    tot = jnp.zeros((8, 128), f32)
    for b in (1, 2, 3, 4):
        acc = w[b][0] * v[0]
        for p in range(1, 12):
            acc = acc + w[b][p] * v[p]
        tot = jnp.where(tl == b - 1, jnp.sum(acc, keepdims=True), tot)
    tot = jnp.where(tl == 4, jnp.sum(vm, keepdims=True), tot)
    tot_ref[...] = tot
    hook()
    E = lambda j: emb_ref[j * ROWS:(j + 1) * ROWS, :].astype(f32)
    s3 = lambda m: E(3 * m) + E(3 * m + 1) + E(3 * m + 2)
    for k in range(6):
        p0, p1 = 2 * k, 2 * k + 1
        b2 = 0.5 * (w[2][p0] + w[2][p1]) * inv[2][k]
        acc = (0.5 * w[1][p0] + b2) * E(p0) + (0.5 * w[1][p1] + b2) * E(p1)
        n = k // 2
        d = 0.5 * (w[4][p0] + w[4][p1]) * inv[4][n]
        acc = acc + d * ((E(4 * n) + E(4 * n + 1)) + (E(4 * n + 2) + E(4 * n + 3)))
        m0, m1 = p0 // 3, p1 // 3
        if m0 == m1:
            acc = acc + (0.5 * (w[3][p0] + w[3][p1]) * inv[3][m0]) * s3(m0)
        else:
            acc = acc + (0.5 * w[3][p0] * inv[3][m0]) * s3(m0) + (0.5 * w[3][p1] * inv[3][m1]) * s3(m1)
        put_strided(slabs, k, acc)
        if k % 2 == 1:
            hook()
    ntok = nbytes // 2
    for c in range(slabs.shape[0]):
        stream_ref[0:ntok, c * 128:(c + 1) * 128] = slabs[c, 0:ntok, :]
    stream_ref[ntok:TP, :] = jnp.zeros((TP - ntok, acc.shape[1]), f32)
    norm_rows(stream_ref, vec_ref[1:2, :], normed_ref)
    hook()


def put_strided(ref, k, val):
    for c in range(val.shape[1] // 128):
        ref[c, pl.ds(k, 124, stride=6), :] = val[:124, c * 128:(c + 1) * 128]

def get_strided(ref, k):
    parts = [ref[c, pl.ds(k, 124, stride=6), :] for c in range(ref.shape[0])]
    x = jnp.concatenate(parts, axis=1)
    return jnp.concatenate([x, jnp.zeros((4, x.shape[1]), f32)], axis=0)

def norm_rows(x_ref, gain_ref, out_ref):
    g = gain_ref
    for b in range(TP // 128):
        x = x_ref[b * 128:(b + 1) * 128, :]
        sc = lax.rsqrt(jnp.mean(x * x, axis=1, keepdims=True) + EPS)
        out_ref[b * 128:(b + 1) * 128, :] = (x * sc * g).astype(bf16)

def gbst_bwd_body(nbytes, vocab, scal_ref, ids_ref, emb_ref, wcol_ref, score_ref, ggain_ref, put, de_ref, slabs, hook):
    vm = byte_valid_mat(scal_ref, nbytes)
    v, inv = inverse_counts(vm)
    wc = wcol_ref[...]
    w = {b: [wc[:, (b - 1) * 12 + p:(b - 1) * 12 + p + 1] for p in range(12)] for b in (1, 2, 3, 4)}
    s = score_ref[0:1, :]
    E = lambda j: emb_ref[j * ROWS:(j + 1) * ROWS, :].astype(f32)
    s3 = lambda m: E(3 * m) + E(3 * m + 1) + E(3 * m + 2)
    s4 = lambda n: (E(4 * n) + E(4 * n + 1)) + (E(4 * n + 2) + E(4 * n + 3))
    dot = lambda a, b: jnp.sum(a * b, axis=1, keepdims=True)
    dw = {b: [None] * 12 for b in (1, 2, 3, 4)}
    D = []
    for k in range(6):
        dk = 0.5 * get_strided(slabs, k)
        D.append(dk)
        p0, p1 = 2 * k, 2 * k + 1
        x0, x1 = dot(dk, E(p0)), dot(dk, E(p1))
        dw[1][p0], dw[1][p1] = x0, x1
        dw[2][p0] = dw[2][p1] = (x0 + x1) * inv[2][k]
        m0, m1 = p0 // 3, p1 // 3
        a0 = dot(dk, s3(m0)) * inv[3][m0]
        dw[3][p0] = a0
        dw[3][p1] = a0 if m0 == m1 else dot(dk, s3(m1)) * inv[3][m1]
        dw[4][p0] = dw[4][p1] = dot(dk, s4(k // 2)) * inv[4][k // 2]
        if k % 2 == 1:
            hook()
    hook()
    dr = {b: [] for b in (1, 2, 3, 4)}
    for p in range(12):
        mean = w[1][p] * dw[1][p] + w[2][p] * dw[2][p] + w[3][p] * dw[3][p] + w[4][p] * dw[4][p]
        for b in (1, 2, 3, 4):
            dr[b].append(w[b][p] * (dw[b][p] - mean))
    rb = {1: dr[1]}
    for b in (2, 3, 4):
        out = []
        for m in range(12 // b):
            tot = dr[b][b * m]
            for t in range(1, b):
                tot = tot + dr[b][b * m + t]
            out.append(tot * inv[b][m])
        rb[b] = out
    t3 = []
    for m in range(4):
        terms = {}
        for p in (3 * m, 3 * m + 1, 3 * m + 2):
            terms[p // 2] = terms[p // 2] + w[3][p] if p // 2 in terms else w[3][p]
        acc = None
        for k, coef in terms.items():
            t = (coef * inv[3][m]) * D[k]
            acc = t if acc is None else acc + t
        t3.append(acc)
    gscore = jnp.zeros((8, s.shape[1]), f32)
    for n in range(3):
        t4 = ((w[4][4 * n] + w[4][4 * n + 1]) * inv[4][n]) * D[2 * n] + ((w[4][4 * n + 2] + w[4][4 * n + 3]) * inv[4][n]) * D[2 * n + 1]
        for p in range(4 * n, 4 * n + 4):
            k = p // 2
            c = rb[1][p] + rb[2][k] + rb[3][p // 3] + rb[4][n]
            b2 = (w[2][2 * k] + w[2][2 * k + 1]) * inv[2][k]
            de = v[p] * ((w[1][p] + b2) * D[k] + t3[p // 3] + t4 + c * s)
            de_ref[p * ROWS:(p + 1) * ROWS, :] = de.astype(bf16)
            y = c * E(p)
            gscore = gscore + jnp.sum(y.reshape(ROWS // 8, 8, s.shape[1]), axis=0)
        hook()
    gscore = jnp.sum(gscore, axis=0, keepdims=True)
    row = lax.broadcasted_iota(jnp.int32, (VR, ROWS), 0)
    hots = [jnp.where(row == ids_ref[j:j + 1, :], 1.0, 0.0).astype(bf16) for j in range(12)]
    hot = jnp.concatenate(hots, axis=1)
    gtable = nn(hot, de_ref[...])
    row = lax.broadcasted_iota(jnp.int32, gtable.shape, 0)
    for i, extra in enumerate((gscore, ggain_ref[0:1, :], ggain_ref[1:2, :])):
        gtable = jnp.where(row == vocab + i, extra, gtable)
    put(gtable.T.astype(bf16))


MESH = pl.DeviceIdType.MESH


def coords():
    w = lax.axis_index("wide")
    n = lax.axis_index("narrow")
    return w, w // 2, w % 2, n // 2, n % 2


def peer_ids():
    w, z, y, x, c = coords()
    n = 2 * x + c
    return {
        "y": (2 * z + 1 - y, n),
        "zp": (2 * ((z + 1) % 4) + y, n),
        "zm": (2 * ((z + 3) % 4) + y, n),
        "zo": (2 * ((z + 2) % 4) + y, n),
        "x": (w, 2 * (1 - x) + c),
        "c": (w, 2 * x + 1 - c),
    }


def enter(peers, names):
    barrier = pltpu.get_barrier_semaphore()
    for name in names:
        pl.semaphore_signal(barrier, inc=1, device_id=peers[name], device_id_type=MESH)
    pl.semaphore_wait(barrier, len(names))


class Gather:
    SENDS = 30
    SLOTS = 28

    def __init__(self, shards, fulls, split, ssem, rsem, lsem):
        self.shards, self.fulls, self.split = shards, fulls, split
        self.ssem, self.rsem, self.lsem = ssem, rsem, lsem
        self.peers = peer_ids()
        self.w, self.z, self.y, self.x, self.c = coords()
        z = self.z
        first = jnp.where(z == 3, 3, 1)
        second = jnp.where((z == 0) | (z == 3), 2, 3)
        self.order = (first, second, 6 - first - second)
        self.inner = (z == 1) | (z == 2)
        self.sent = []
        self.local = {}

    def enter(self):
        n = 2 * self.x + self.c
        barrier = pltpu.get_barrier_semaphore()
        near = [(owner, n) for _, owner in self.others()] + [self.peers["x"], self.peers["c"]]
        for peer in near:
            pl.semaphore_signal(barrier, inc=1, device_id=peer, device_id_type=MESH)
        pl.semaphore_wait(barrier, len(near))

    def cols(self, i, c):
        width = self.fulls[i].shape[1] // 2
        return pl.ds(pl.multiple_of(c * width, 128), width)

    def block(self, i, owner, part, ref=None):
        r = self.shards[i].shape[0]
        start = owner * r
        if self.split[i]:
            r = r // 2
            start = start + part[1] * r
        return (self.fulls[i] if ref is None else ref).at[pl.ds(pl.multiple_of(start, 16), r), self.cols(i, part[0])]

    @property
    def mine(self):
        return (self.c, self.x)

    def copy(self, i, out, slot, src, owner, part, device):
        return pltpu.make_async_remote_copy(
            src_ref=src, dst_ref=self.block(i, owner, part), send_sem=self.ssem.at[i, out],
            recv_sem=self.rsem.at[i, slot], device_id=device, device_id_type=MESH)

    def send(self, i, out, slot, owner, part, device, when=None, src=None):
        src = self.block(i, owner, part) if src is None else src
        cp = self.copy(i, out, slot, src, owner, part, device)
        if when is None:
            cp.start()
        else:
            pl.when(when)(cp.start)
        self.sent.append((i, out, when))

    def arrived(self, i, slot, owner, part):
        ref = self.block(i, owner, part)
        pltpu.make_async_remote_copy(
            src_ref=ref, dst_ref=ref, send_sem=self.ssem.at[i, 0], recv_sem=self.rsem.at[i, slot],
            device_id=self.peers["c"], device_id_type=MESH).wait_recv()

    def start_direct(self, i):
        n = 2 * self.x + self.c
        for k in range(1, 8):
            dz, dy = k // 2, k % 2
            to = (2 * lax.rem(self.z + dz, 4) + (1 - self.y if dy else self.y), n)
            self.send_rows(i, k, (4 - dz) % 4 * 2 + dy, self.w, self.c, to, self.half_rows(i, 0, self.c, self.shards[i]))
        r = self.shards[i].shape[0]
        cp = pltpu.make_async_copy(self.shards[i], self.fulls[i].at[pl.ds(pl.multiple_of(self.w * r, 16), r), :], self.lsem.at[i])
        cp.start()
        self.local[i] = cp

    def half_rows(self, i, owner, c, ref=None):
        r = self.shards[i].shape[0]
        return (self.fulls[i] if ref is None else ref).at[pl.ds(pl.multiple_of(owner * r + c * (r // 2), 16), r // 2), :]

    def send_rows(self, i, out, slot, owner, c, device, src=None):
        ref = self.half_rows(i, owner, c)
        cp = pltpu.make_async_remote_copy(
            src_ref=ref if src is None else src, dst_ref=ref, send_sem=self.ssem.at[i, out], recv_sem=self.rsem.at[i, slot],
            device_id=device, device_id_type=MESH)
        cp.start()
        self.sent.append((i, out, "rows"))

    def rows_arrived(self, i, slot, owner, c):
        ref = self.half_rows(i, owner, c)
        pltpu.make_async_remote_copy(
            src_ref=ref, dst_ref=ref, send_sem=self.ssem.at[i, 0], recv_sem=self.rsem.at[i, slot],
            device_id=self.peers["c"], device_id_type=MESH).wait_recv()

    def others(self):
        for k in range(1, 8):
            dz, dy = k // 2, k % 2
            yield k, 2 * lax.rem(self.z + dz, 4) + (1 - self.y if dy else self.y)

    def steps_direct(self, i):
        def relay():
            for k, owner in self.others():
                self.rows_arrived(i, k, owner, self.c)
                self.send_rows(i, 8 + k, 8 + k, owner, self.c, self.peers["c"])

        def end():
            for k, owner in self.others():
                self.rows_arrived(i, 8 + k, owner, 1 - self.c)
            self.local[i].wait()
        return [relay, end]

    def start(self, i):
        own = self.block(i, 0, self.mine, self.shards[i])
        n = 2 * self.x + self.c
        self.send(i, 0, 2, self.w, self.mine, (2 * jnp.minimum(self.z + 1, 3) + self.y, n), self.z < 3, own)
        self.send(i, 1, 0, self.w, self.mine, (2 * jnp.maximum(self.z - 1, 0) + self.y, n), self.z > 0, own)
        self.send(i, 5, 3, self.w, self.mine, self.peers["y"], None, own)
        r = self.shards[i].shape[0]
        cp = pltpu.make_async_copy(self.shards[i], self.fulls[i].at[pl.ds(pl.multiple_of(self.w * r, 16), r), :], self.lsem.at[i])
        cp.start()
        self.local[i] = cp

    def relay(self, i, s, n, owner):
        self.send(i, 9 + n, 7 + s, owner, self.mine, self.peers["c"])
        if self.split[i]:
            self.send(i, 16 + n, 14 + s, owner, self.mine, self.peers["x"])

    def step_z(self, i, j):
        d = self.order[j]
        o = lax.rem(self.z + d, 4)
        owner = 2 * o + self.y
        self.arrived(i, d - 1, owner, self.mine)
        to = jnp.where(self.inner, jnp.where(o < self.z, self.z + 1, self.z - 1), jnp.where(self.z == 0, 1, 2))
        slot = jnp.where(self.inner, lax.rem(o - to + 4, 4) - 1, 0)
        self.send(i, 2 + j, slot, owner, self.mine, (2 * to + self.y, 2 * self.x + self.c), self.inner)
        self.send(i, 6 + j, 3 + d, owner, self.mine, self.peers["y"])
        self.relay(i, d - 1, j, owner)

    def step_y(self, i, j):
        d = 0 if j < 0 else self.order[j]
        owner = 2 * lax.rem(self.z + d, 4) + 1 - self.y
        self.arrived(i, 3 + d, owner, self.mine)
        self.relay(i, 3 + d, 4 + j, owner)

    def each(self):
        for j in range(3):
            d = self.order[j]
            yield d - 1, j, 2 * lax.rem(self.z + d, 4) + self.y
        for j in range(-1, 3):
            d = 0 if j < 0 else self.order[j]
            yield 3 + d, 4 + j, 2 * lax.rem(self.z + d, 4) + 1 - self.y

    def step_x(self, i):
        if self.split[i]:
            other = (self.c, 1 - self.x)
            for s, n, owner in self.each():
                self.arrived(i, 14 + s, owner, other)
                self.send(i, 23 + n, 21 + s, owner, other, self.peers["c"])

    def step_end(self, i):
        for s, n, owner in self.each():
            self.arrived(i, 7 + s, owner, (1 - self.c, self.x))
            if self.split[i]:
                self.arrived(i, 21 + s, owner, (1 - self.c, 1 - self.x))
        self.local[i].wait()

    def finish(self):
        for i, out, when in self.sent:
            if isinstance(when, str):
                ref = self.half_rows(i, self.w, self.c)
                when = None
            else:
                ref = self.block(i, self.w, self.mine)
            cp = pltpu.make_async_remote_copy(
                src_ref=ref, dst_ref=ref, send_sem=self.ssem.at[i, out], recv_sem=self.rsem.at[i, 0],
                device_id=self.peers["c"], device_id_type=MESH)
            if when is None:
                cp.wait_send()
            else:
                pl.when(when)(cp.wait_send)

    def steps(self, i):
        return [functools.partial(self.step_y, i, -1)] + [functools.partial(f, i, j) for j in range(3) for f in (self.step_z, self.step_y)] + [
            functools.partial(self.step_x, i), functools.partial(self.step_end, i)]


class Reduce:
    SLOTS = 9

    def __init__(self, terms, outs, order, own, rc, r1, r2, r3, ssem, rsem, lsem):
        self.terms, self.outs, self.order = terms, outs, order
        self.own, self.rc, self.r1, self.r2, self.r3 = own, rc, r1, r2, r3
        self.ssem, self.rsem, self.lsem = ssem, rsem, lsem
        self.peers = peer_ids()
        self.w, self.z, self.y, self.x, self.c = coords()
        self.sent = []

    def enter(self):
        enter(self.peers, ("y", "zp", "zm", "zo", "x", "c"))

    def transfer(self, i, slot, src, dst, to):
        return pltpu.make_async_remote_copy(
            src_ref=src, dst_ref=dst, send_sem=self.ssem.at[i, slot], recv_sem=self.rsem.at[i, slot],
            device_id=self.peers[to], device_id_type=MESH)

    def send(self, i, slot, src, dst, to):
        self.transfer(i, slot, src, dst, to).start()
        self.sent.append((i, slot))

    def arrived(self, i, slot, dst):
        self.transfer(i, slot, dst, dst, "c").wait_recv()

    def half(self, i, c):
        width = self.terms[i].shape[4] // 2
        return pl.ds(pl.multiple_of(c * width, 128), width)

    def local(self, i):
        return pltpu.make_async_copy(self.terms[i].at[:, :, :, :, self.half(i, self.c)], self.own[i], self.lsem.at[i])

    def start(self, i):
        self.send(i, 0, self.terms[i].at[:, :, :, :, self.half(i, 1 - self.c)], self.rc[i], "c")
        self.local(i).start()

    def add(self, a, b):
        return (a.astype(f32) + b.astype(f32)).astype(bf16)

    def step_core(self, i):
        self.local(i).wait()
        self.arrived(i, 0, self.rc[i])

        def one(z, carry):
            self.own[i][z] = self.add(self.own[i][z], self.rc[i][z])
            return carry
        lax.fori_loop(0, 4, one, 0)
        if self.order[i] == "y":
            self.send(i, 1, self.own[i].at[:, 1 - self.y], self.r1[i], "y")
        else:
            self.send(i, 1, self.own[i].at[:, :, 1 - self.x], self.r1[i], "x")

    def step_one(self, i):
        self.arrived(i, 1, self.r1[i])

        def one(z, carry):
            if self.order[i] == "y":
                mine = self.own[i][z, self.y]
            else:
                mine = self.own[i][z, :, self.x]
            self.r1[i][z] = self.add(mine, self.r1[i][z])
            return carry
        lax.fori_loop(0, 4, one, 0)
        if self.order[i] == "y":
            self.send(i, 2, self.r1[i].at[:, 1 - self.x], self.r2[i], "x")
        else:
            self.send(i, 2, self.r1[i].at[:, 1 - self.y], self.r2[i], "y")

    def step_two(self, i):
        self.arrived(i, 2, self.r2[i])
        pick = self.x if self.order[i] == "y" else self.y

        def one(z, carry):
            self.r2[i][z] = self.add(self.r1[i][z, pick], self.r2[i][z])
            return carry
        lax.fori_loop(0, 4, one, 0)
        for dz, to in ((1, "zp"), (3, "zm"), (2, "zo")):
            self.send(i, 2 + dz, self.r2[i].at[lax.rem(self.z + dz, 4)], self.r3[i].at[3 - dz], to)

    def step_z(self, i):
        total = self.r2[i][self.z].astype(f32)
        for dz in (1, 3, 2):
            self.arrived(i, 2 + dz, self.r3[i].at[3 - dz])
        for k in range(3):
            total = total + self.r3[i][k].astype(f32)
        out = self.outs[i]
        out[self.c, self.x] = total.astype(bf16)
        self.send(i, 6, out.at[self.c, self.x], out.at[self.c, self.x], "x")
        self.send(i, 7, out.at[self.c, self.x], out.at[self.c, self.x], "c")

    def step_x(self, i):
        out = self.outs[i]
        self.arrived(i, 6, out.at[self.c, 1 - self.x])
        self.send(i, 8, out.at[self.c, 1 - self.x], out.at[self.c, 1 - self.x], "c")

    def step_end(self, i):
        out = self.outs[i]
        self.arrived(i, 7, out.at[1 - self.c, self.x])
        self.arrived(i, 8, out.at[1 - self.c, 1 - self.x])

    def steps(self, i):
        return [functools.partial(f, i) for f in (self.step_core, self.step_one, self.step_two, self.step_z, self.step_x, self.step_end)]

    def finish(self):
        for i, slot in self.sent:
            block = self.r2[i].at[0]
            ref = {0: self.rc[i], 1: self.r1[i], 2: self.r2[i]}.get(slot, block)
            self.transfer(i, slot, ref, ref, "c").wait_send()

    @staticmethod
    def scratch(shapes):
        own = [pltpu.VMEM((4, 2, 2, s[3], s[4] // 2), bf16) for s in shapes]
        rc = [pltpu.VMEM((4, 2, 2, s[3], s[4] // 2), bf16) for s in shapes]
        r1 = [pltpu.VMEM((4, 2, s[3], s[4] // 2), bf16) for s in shapes]
        r2 = [pltpu.VMEM((4, s[3], s[4] // 2), bf16) for s in shapes]
        r3 = [pltpu.VMEM((3, s[3], s[4] // 2), bf16) for s in shapes]
        n = len(shapes)
        return own + rc + r1 + r2 + r3 + [pltpu.SemaphoreType.DMA((n, 9)), pltpu.SemaphoreType.DMA((n, 9)), pltpu.SemaphoreType.DMA((n,))]


SMALL = (16, 128)


class SmallSum:
    HOPS = ("c", "x", "y", "zn", "zo")

    def __init__(self, acc, slots, ssem, rsem):
        self.acc, self.slots, self.ssem, self.rsem = acc, slots, ssem, rsem
        self.peers = peer_ids()
        w, z, y, x, c = coords()
        self.peers["zn"] = (2 * (z + 1 - 2 * (z % 2)) + y, 2 * x + c)

    def copy(self, k):
        return pltpu.make_async_remote_copy(
            src_ref=self.slots.at[5 + k], dst_ref=self.slots.at[k], send_sem=self.ssem.at[k], recv_sem=self.rsem.at[k],
            device_id=self.peers[self.HOPS[k]], device_id_type=MESH)

    def step(self, k):
        if k:
            self.copy(k - 1).wait()
            self.acc[...] = self.acc[...] + self.slots[k - 1]
        if k < 5:
            self.slots[5 + k] = self.acc[...]
            self.copy(k).start()

    def steps(self):
        return [functools.partial(self.step, k) for k in range(6)]


def none():
    pass


class Feed:
    def __init__(self, steps, share=1):
        self.steps = list(steps)
        self.share = share

    def __call__(self):
        for _ in range(self.share):
            if self.steps:
                self.steps.pop(0)()

    def rest(self):
        while self.steps:
            self.steps.pop(0)()


def forward_kernel(nbytes, vocab, split, *refs):
    scal_ref, ids_ref, base_ref = refs[:3]
    shards = refs[3:11]
    outs = refs[11:28]
    fulls = list(outs[:7])
    stream_o, normed_o, emb_o, wcol_o, tot_o, vec_o, q_o, k_o, v_o, mixed_o = outs[7:17]
    lse_o = refs[28]
    (tt, wq, wk, wv, stream, normed, emb, wcol, tot, vec, q, k, v, mixed, lse, slabs, table, kaug, raug, strip, vt, osem, wsem) = refs[29:52]
    done = []

    def out(src, dst):
        cp = pltpu.make_async_copy(src, dst, osem.at[len(done)])
        cp.start()
        done.append(cp)

    ntok = nbytes // 2
    if split is not None:
        g = Gather(shards, [tt] + fulls, split, *refs[52:55])
        g.enter()
        g.start_direct(0)
        for i in range(1, 4):
            g.start(i)
        build_masks(scal_ref, kaug, raug, ntok)
        relay, end = g.steps_direct(0)
        relay()
        for i in range(4, 8):
            g.start(i)
        end()
        plans = [None] + [g.steps(i) for i in range(1, 8)]
        early = Feed([plans[i][s] for s in range(8) for i in (1, 2, 3)], 3)
        late = [plans[i][s] for s in range(8) for i in (4, 5, 6, 7)]
        per = -(-len(late) // 6)
        chunks = [late[j * per:(j + 1) * per] for j in range(6)]
    else:
        cp = pltpu.make_async_copy(shards[0], tt, wsem.at[3])
        cp.start()
        build_masks(scal_ref, kaug, raug, ntok)
        cp.wait()
        early = Feed([])
        chunks = [[]] * 6
    gbst_fwd_body(nbytes, vocab, scal_ref, ids_ref, tt, stream, normed, emb, wcol, tot, vec, slabs, table, early)
    early.rest()
    for src, dst in ((stream, stream_o), (normed, normed_o), (emb, emb_o), (wcol, wcol_o), (tot, tot_o), (vec, vec_o)):
        out(src, dst)
    loads = []
    for i, dst in enumerate((wq, wk, wv)):
        if split is not None:
            plans[i + 1][8]()
        cp = pltpu.make_async_copy(shards[i + 1] if split is None else fulls[i], dst, wsem.at[i])
        cp.start()
        loads.append(cp)
    for cp, w, dst, to in zip(loads, (wq, wk, wv), (q, k, v), (q_o, k_o, v_o)):
        cp.wait()

        def rows(b, carry):
            sl = pl.ds(pl.multiple_of(b * 256, 256), 256)
            dst[sl, :] = nn(normed[sl, :], w[...]).astype(bf16)
            return carry
        lax.fori_loop(0, TP // 256, rows, 0)
        out(dst, to)

    def pair(p, carry):
        for j in range(6):
            if chunks[j]:
                @pl.when(p == j)
                def _():
                    for step in chunks[j]:
                        step()
        fwd_pair(p, q, k, v, base_ref, mixed, lse, kaug, raug, strip, vt)
        return carry
    lax.fori_loop(0, q.shape[1] // 128, pair, 0)
    out(mixed, mixed_o)
    out(lse, lse_o)
    if split is not None:
        for i in range(4, 8):
            plans[i][8]()
        g.finish()
    for cp in done:
        cp.wait()


def forward_one(scal, ids, base2, shards, vocab, nbytes, wide, split):
    d = shards[1].shape[1]
    hbm = pl.BlockSpec(memory_space=pltpu.HBM)
    vm = pl.BlockSpec(memory_space=pltpu.VMEM)
    pairs = d // 128
    many = 1 if split is None else wide
    sd = jax.ShapeDtypeStruct
    acts = [((TP, d), f32), ((TP, d), bf16), ((12 * ROWS, d), bf16), ((ROWS, 128), f32), ((8, 128), f32), ((8, d), f32),
            ((TP, d), bf16), ((TP, d), bf16), ((TP, d), bf16), ((TP, d), bf16), ((pairs, 8, 256), f32)]
    wq = (d, d)
    scratch = [pltpu.VMEM((d, VP), bf16)] + [pltpu.VMEM(wq, bf16)] * 3 + [pltpu.VMEM(*a) for a in acts]
    scratch += [pltpu.VMEM((d // 128, TP, 128), f32), pltpu.VMEM((VP, d), bf16), pltpu.VMEM((TP, 128), bf16), pltpu.VMEM((NB, 256, 128), bf16),
                pltpu.VMEM((STRIP, 256), f32), pltpu.VMEM((128, TP), bf16), pltpu.SemaphoreType.DMA((11,)), pltpu.SemaphoreType.DMA((4,))]
    params = dict(vmem_limit_bytes=56 << 20)
    if split is not None:
        scratch += [pltpu.SemaphoreType.DMA((8, Gather.SENDS)), pltpu.SemaphoreType.DMA((8, Gather.SLOTS)), pltpu.SemaphoreType.DMA((8,))]
        params.update(collective_id=1, has_side_effects=True)
        whole = [sd((many * s.shape[0], s.shape[1]), bf16) for s in shards[1:]]
    else:
        whole = [sd((8, 128), bf16)] * 7
    return pl.pallas_call(
        functools.partial(forward_kernel, nbytes, vocab, split),
        out_shape=tuple(whole) + tuple(sd(*a) for a in acts),
        in_specs=[pl.BlockSpec(memory_space=pltpu.SMEM), vm, vm] + [hbm] * 8,
        out_specs=(hbm,) * 18,
        scratch_shapes=scratch,
        compiler_params=pltpu.CompilerParams(**params),
        name="forward_one",
    )(scal, ids, base2, *shards)


def backward_kernel(nbytes, vocab, order, *refs):
    scal_ref, ids_ref, base_ref, hot_ref, vec_ref, wcol_ref, tot_ref, gain2_ref, lse_ref = refs[:9]
    q_h, k_h, v_h, g_h, normed_h, stream_h, mid_h, emb_h, wq_h, wk_h, wv_h = refs[9:20]
    rest = refs[20:]
    (q, k, v, g, normed, nt_s, stream, mid, emb, wq, wk, wv, slabs, de, kaug, raug, strip, acc, kt, dk_s, dv_s, db, ggain, lsem) = rest[-24:]
    rest = rest[:-24]

    def load(n, src, dst):
        cp = pltpu.make_async_copy(src, dst, lsem.at[n])
        cp.start()
        return cp

    ntok = nbytes // 2
    d = q.shape[1]
    first = [load(n, s, t) for n, (s, t) in enumerate(((q_h, q), (k_h, k), (v_h, v), (g_h, g)))]
    if order is not None:
        ff, outs, small_o = rest[:4], rest[4:12], rest[12]
        rest = rest[13:]
        mine = rest[:4]
        rest = rest[4:]
        cut = [rest[n * 8:(n + 1) * 8] for n in range(5)]
        red = Reduce(list(mine) + list(ff), outs, order, *cut, *rest[40:43])
        small = SmallSum(rest[43], *rest[44:47])
        red.enter()
        for i in (6, 5, 7, 4):
            red.start(i)
    later = [load(4 + n, s, t) for n, (s, t) in enumerate(((normed_h, normed), (stream_h, stream), (mid_h, mid), (emb_h, emb), (wq_h, wq), (wk_h, wk), (wv_h, wv)))]
    build_masks(scal_ref, kaug, raug, ntok)
    for cp in first:
        cp.wait()
    if order is not None:
        st = {i: red.steps(i) for i in range(8)}
        chunks = [[], [st[6][0], st[5][0]], [st[7][0], st[4][0]], [], [], [st[6][1], st[5][1]]]
    else:
        chunks = [[]] * 6

    def pair(p, carry):
        for j in range(6):
            if chunks[j]:
                @pl.when(p == j)
                def _():
                    for step in chunks[j]:
                        step()
        bwd_pair(p, q, k, v, g, lse_ref, base_ref, db, kaug, raug, strip, acc, kt, dk_s, dv_s)
        return carry
    db[...] = jnp.zeros_like(db)
    lax.fori_loop(0, d // 128, pair, 0)
    for cp in later:
        cp.wait()
    if order is not None:
        tm = mine
        st[4][1]()
    else:
        tm, small_o = rest[:4], rest[4]
    nt_s[...] = normed[...].T
    block = tm[1].shape[3]
    for n, src in enumerate((q, k, v)):
        def rows(b, carry):
            r = nn(nt_s[pl.ds(pl.multiple_of(b * 4 * block, 16), 4 * block), :], src[...]).astype(bf16)
            for yy in range(2):
                for xx in range(2):
                    at = (2 * yy + xx) * block
                    tm[1 + n][b, yy, xx] = r[at:at + block]
            return carry
        lax.fori_loop(0, tm[1].shape[0], rows, 0)
        if order is not None:
            red.start(1 + n)
    relt = lax.dot_general(db[...], hot_ref[...], (((1,), (0,)), ((), ())), precision=lax.Precision.HIGHEST, preferred_element_type=f32)
    at = lax.broadcasted_iota(jnp.int32, SMALL, 0)
    total = jnp.where(at == SMALL[0] - 1, tot_ref[0:1, :], relt)
    if order is not None:
        small.acc[...] = total
        hook = Feed([small.steps()[0], st[7][1], st[6][2], small.steps()[1], st[1][0], st[2][0], st[3][0], st[5][2], small.steps()[2], st[4][2],
                     st[6][3], small.steps()[3], st[5][3], st[7][2], st[1][1], st[2][1], small.steps()[4], st[3][1], st[6][4], st[5][4], st[4][3]])
        hook()
    else:
        small_o[...] = total
        hook = none
    ggain[...] = jnp.zeros_like(ggain)
    gain = vec_ref[1:2, :]

    def rows(b, carry):
        sl = pl.ds(pl.multiple_of(b * 128, 128), 128)
        gy = nt(q[sl, :], wq[...]) + nt(k[sl, :], wk[...]) + nt(v[sl, :], wv[...])
        x = stream[sl, :]
        s = lax.rsqrt(jnp.mean(x * x, axis=1, keepdims=True) + EPS)
        t = gy * gain
        gs = mid[sl, :] + s * t - x * (s * s * s * jnp.mean(x * t, axis=1, keepdims=True))
        for c in range(d // 128):
            slabs[c, sl, :] = gs[:, c * 128:(c + 1) * 128]
        ggain[...] += jnp.sum((gy * x * s).reshape(16, 8, d), axis=0)
        return carry
    lax.fori_loop(0, TP // 128, rows, 0)
    ggain[0:2, :] = jnp.concatenate([jnp.sum(ggain[...], axis=0, keepdims=True), gain2_ref[...]], axis=0)
    hook()

    def put(gt):
        half = tm[0].shape[3]
        for zz in range(tm[0].shape[0]):
            for yy in range(2):
                for xx in range(2):
                    at = ((zz * 2 + yy) * 2 + xx) * half
                    tm[0][zz, yy, xx, :, 0:VR] = gt[at:at + half]
                    tm[0][zz, yy, xx, :, VR:VG] = jnp.zeros((half, VG - VR), bf16)
    gbst_bwd_body(nbytes, vocab, scal_ref, ids_ref, emb, wcol_ref, vec_ref, ggain, put, de, slabs, hook)
    if order is not None:
        red.start(0)
        hook.rest()
        st[0][0]()
        tail = [st[7][3], st[1][2], st[0][1], st[2][2], st[3][2], st[4][4], st[1][3], st[0][2], st[2][3], st[3][3], st[7][4], small.steps()[5], st[0][3]]
        tail += [st[1][4], st[2][4], st[3][4], st[0][4]] + [st[i][5] for i in (6, 5, 7, 4, 1, 2, 3, 0)]
        for f in tail:
            f()
        small_o[...] = small.acc[...]
        red.finish()


def backward_one(scal, ids, base2, hot, vec, wcol, tot, gain2, lse, acts, weights, terms, vocab, nbytes, order):
    d = acts[0].shape[1]
    hbm = pl.BlockSpec(memory_space=pltpu.HBM)
    vm = pl.BlockSpec(memory_space=pltpu.VMEM)
    sd = jax.ShapeDtypeStruct
    view = lambda r, c: (4, 2, 2, r // 16, c)
    mine = [view(d, VG), view(d, d), view(d, d), view(d, d)]
    shapes = mine + [t.shape for t in terms]
    wide = [(TP, d), bf16]
    scratch = []
    params = dict(vmem_limit_bytes=60 << 20)
    if order is not None:
        outs = [sd((2, 2, s[3], s[4] // 2), bf16) for s in shapes] + [sd(SMALL, f32)]
        scratch += [pltpu.VMEM(s, bf16) for s in mine] + Reduce.scratch(shapes)
        scratch += [pltpu.VMEM(SMALL, f32), pltpu.VMEM((10,) + SMALL, f32), pltpu.SemaphoreType.DMA((5,)), pltpu.SemaphoreType.DMA((5,))]
        params.update(collective_id=2, has_side_effects=True)
    else:
        outs = [sd(s, bf16) for s in mine] + [sd(SMALL, f32)]
    scratch += [pltpu.VMEM(*wide)] * 5 + [pltpu.VMEM((d, TP), bf16)] + [pltpu.VMEM((TP, d), f32)] * 2 + [pltpu.VMEM((12 * ROWS, d), bf16)]
    scratch += [pltpu.VMEM((d, d), bf16)] * 3 + [pltpu.VMEM((d // 128, TP, 128), f32), pltpu.VMEM((12 * ROWS, d), bf16)]
    scratch += [pltpu.VMEM((TP, 128), bf16), pltpu.VMEM((NB, 256, 128), bf16), pltpu.VMEM((STRIP, 256), f32), pltpu.VMEM((STRIP, 256), f32),
                pltpu.VMEM((128, TP), bf16), pltpu.VMEM((TP, 128), f32), pltpu.VMEM((TP, 128), f32), pltpu.VMEM((16, 512), f32), pltpu.VMEM((8, d), f32),
                pltpu.SemaphoreType.DMA((11,))]
    return pl.pallas_call(
        functools.partial(backward_kernel, nbytes, vocab, order),
        out_shape=tuple(outs),
        in_specs=[pl.BlockSpec(memory_space=pltpu.SMEM)] + [vm] * 8 + [hbm] * (11 + len(terms)),
        out_specs=(vm,) * len(outs),
        scratch_shapes=scratch,
        compiler_params=pltpu.CompilerParams(**params),
        name="backward_one",
    )(scal, ids, base2, hot, vec, wcol, tot, gain2, lse, *acts, *weights, *terms)


def tn(a, b):
    return lax.dot_general(a, b, (((0,), (0,)), ((), ())), preferred_element_type=f32)


def norm_back(x, gain, gy):
    s = lax.rsqrt(jnp.mean(x * x, axis=1, keepdims=True) + EPS)
    t = gy * gain
    gx = s * t - x * (s * s * s) * jnp.mean(x * t, axis=1, keepdims=True)
    return gx, jnp.sum(gy * x * s, axis=0)


def layer(byte_ids, lengths, bucket, out_grad, rel_bias, vocab, shards, wide, split):
    ids = byte_ids[0]
    nbytes = ids.shape[0]
    ntok = nbytes // 2
    scal = jnp.stack([bucket[0], lengths[0, 0], lengths[0, 1]])
    idp = jnp.pad(ids.reshape(nbytes // 12, 12).T, ((0, 4), (0, ROWS - nbytes // 12)), constant_values=-1)
    nb = rel_bias.shape[0]
    base2 = jnp.dot(base_hot(nb), rel_bias.astype(f32), precision=lax.Precision.HIGHEST).T
    done = forward_one(scal, idp, base2, shards, vocab, nbytes, wide, split)
    wq, wk, wv, wo, wg, wu, wd = shards[1:] if split is None else done[:7]
    stream, normed, emb, wcol, tot, vec, q, k, v, mixed, lse = done[7:]
    middle = stream + nn(mixed, wo)
    g2 = vec[2]
    s2 = lax.rsqrt(jnp.mean(middle * middle, axis=1, keepdims=True) + EPS)
    normed_ff = (middle * s2 * g2).astype(bf16)
    gate = nn(normed_ff, wg)
    up = nn(normed_ff, wu)
    c0 = 0.7978845608028654
    th = jnp.tanh(c0 * (gate + 0.044715 * gate * gate * gate))
    act = 0.5 * gate * (1.0 + th)
    hidden = (act * up).astype(bf16)
    encoded = (middle + nn(hidden, wd)).astype(bf16)[:ntok][None]
    og = jnp.pad(out_grad[0], ((0, TP - ntok), (0, 0)))
    g_wd = tn(hidden, og).astype(bf16)
    gh = nt(og, wd)
    dact = 0.5 * (1.0 + th) + 0.5 * gate * (1.0 - th * th) * (c0 * (1.0 + 3 * 0.044715 * gate * gate))
    gg = (gh * up * dact).astype(bf16)
    gu = (gh * act).astype(bf16)
    g_wg = tn(normed_ff, gg).astype(bf16)
    g_wu = tn(normed_ff, gu).astype(bf16)
    g_nff = nt(gg, wg) + nt(gu, wu)
    gx2, g_gain2 = norm_back(middle, g2, g_nff)
    g_mid = og.astype(f32) + gx2
    g_br = g_mid.astype(bf16)
    g_wo = tn(mixed, g_br).astype(bf16)
    g_heads = nt(g_br, wo).astype(bf16)
    order = None if split is None else ("y", "x", "x", "y", "x", "x", "y", "y")
    hot = jnp.pad(base_hot(nb, True), ((0, 0), (0, SMALL[1] - nb)))
    late = (g_wo, g_wg, g_wu, g_wd)
    terms = [] if split is None else [t.reshape(4, 2, 2, t.shape[0] // 16, t.shape[1]) for t in late]
    outs = backward_one(scal, idp, base2, hot, vec, wcol, tot, g_gain2[None], lse, (q, k, v, g_heads, normed, stream, g_mid, emb), (wq, wk, wv),
                        terms, vocab, nbytes, order)
    if split is None:
        outs = tuple(o.reshape(-1, o.shape[-1]) for o in outs[:4]) + late + (outs[4],)
    return encoded, outs


def body(byte_ids, lengths, bucket, out_grad, embedding, score_weight, gain_attn, w_query, w_key, w_value, w_attn_out, rel_bias, gain_ff, w_gate, w_up, w_ff_out):
    vocab, width = embedding.shape
    wide = lax.axis_size("wide")
    columns = jnp.concatenate([embedding.T, score_weight[:, None], gain_attn[:, None], gain_ff[:, None]], axis=1)
    tt = jnp.pad(columns, ((0, 0), (0, VP - columns.shape[1])))
    shards = (tt, w_query, w_key, w_value, w_attn_out, w_gate, w_up, w_ff_out)
    kernels = wide == 8 and lax.axis_size("narrow") == 4 and all(s.shape[0] % 32 == 0 for s in shards)
    split = (True, True, True, True, False, False, True, True) if kernels else None
    if not kernels:
        shards = tuple(lax.all_gather(s, "wide", axis=0, tiled=True) for s in shards)
    encoded, outs = layer(byte_ids, lengths, bucket, out_grad, rel_bias, vocab, shards, wide, split)
    small = outs[-1]
    if kernels:
        sums = [o.transpose(1, 2, 0, 3).reshape(o.shape[1] * o.shape[2], 2 * o.shape[3]).astype(f32) for o in outs[:-1]]
    else:
        sums = [lax.psum(lax.psum_scatter(g, "wide", scatter_dimension=0, tiled=True), "narrow").astype(f32) for g in outs[:-1]]
        small = lax.psum(small, ("wide", "narrow"))
    g_rel, tot = small[:rel_bias.shape[1], :rel_bias.shape[0]].T, small[-1, :5]
    t = sums[0]
    return (encoded, t[:, :vocab].T, t[:, vocab], t[:, vocab + 1], *sums[1:5], g_rel, t[:, vocab + 2], *sums[5:], tot[:4] / tot[4])


def solution(mesh):
    both = ("wide", "narrow")
    rows = P("wide", None)
    vec = P("wide")
    placed = (P(both, None), P(both, None), P(both), P(both, None, None), P(None, "wide"), vec, vec, rows, rows, rows, rows, P(), vec, rows, rows, rows)
    outs = (P(both, None, None), P(None, "wide"), vec, vec, rows, rows, rows, rows, P(), vec, rows, rows, rows, P())
    return jax.shard_map(body, mesh=mesh, in_specs=placed, out_specs=outs, check_vma=False)
```

```python
import functools

import jax
import jax.numpy as jnp
from jax import lax
from jax.experimental import pallas as pl
from jax.experimental.pallas import tpu as pltpu
from jax.sharding import PartitionSpec as P

f32 = jnp.float32
bf16 = jnp.bfloat16
TP = 768
BLK = 128
NB = TP // BLK
LEFT = TP - BLK
STRIP = 2 * TP - BLK
W0 = LEFT - 128
WN = 384

def nt(a, b):
    return lax.dot_general(a, b, (((1,), (1,)), ((), ())), preferred_element_type=f32)

def nn(a, b):
    return lax.dot_general(a, b, (((1,), (0,)), ((), ())), preferred_element_type=f32)

def build_masks(scal_ref, kaug, raug, ntok):
    joined = scal_ref[0] == 1
    l0 = scal_ref[1]; l1 = scal_ref[2]
    half = ntok // 2
    u = lax.broadcasted_iota(jnp.int32, (TP, 128), 0)
    lane = lax.broadcasted_iota(jnp.int32, (TP, 128), 1)
    seg = (u >= half).astype(jnp.int32)
    lim = jnp.where(seg == 1, l1, l0)
    start = seg * half
    lim = jnp.where(joined, l0 + l1, lim)
    start = jnp.where(joined, 0, start)
    valid = (2 * (u - start) < lim) & (u < ntok)
    segs = jnp.where(joined, 0, seg)
    ok = valid & (segs == lane)
    kaug[...] = jnp.where((lane < 2) & jnp.logical_not(ok), -1e30, 0.0).astype(bf16)
    t = u
    rows = jnp.where((lane == segs), 1.0, 0.0).astype(bf16)
    for b in range(NB):
        blk = rows[b * 128:(b + 1) * 128]
        raug[b] = jnp.concatenate([blk, blk], axis=0)

def build_strip(base_ref, row0, strip):
    for hh in range(2):
        row = base_ref[pl.ds(row0 + hh, 1), :]
        cl = row[:, 0:1]; cr = row[:, 383:384]
        sq = jnp.broadcast_to(row, (128, 512))
        sq = pltpu.roll(sq, 0, 1, stride=1, stride_axis=0)
        win = sq[:, :WN].T
        lanes = slice(hh * 128, hh * 128 + 128)
        strip[0:W0, lanes] = jnp.broadcast_to(cl, (W0, 128))
        strip[W0:W0 + WN, lanes] = win
        strip[W0 + WN:STRIP, lanes] = jnp.broadcast_to(cr, (STRIP - W0 - WN, 128))

def stacked(blk):
    lane = lax.broadcasted_iota(jnp.int32, blk.shape, 1)
    z = jnp.zeros_like(blk)
    return jnp.concatenate([jnp.where(lane < 64, blk, z), jnp.where(lane >= 64, blk, z)], axis=0)

def fwd_pair(p, q_ref, k_ref, v_ref, base_ref, o_ref, lse_ref, kaug, raug, strip, vt):
    lanes = pl.ds(pl.multiple_of(p * 128, 128), 128)
    build_strip(base_ref, 2 * p, strip)
    vt[...] = v_ref[:, lanes].T
    kcat = jnp.concatenate([k_ref[:, lanes], kaug[...]], axis=1)
    vtv = vt[...]
    rowsel = lax.broadcasted_iota(jnp.int32, (128, 128), 0) < 64
    for b in range(NB):
        rhs = jnp.concatenate([stacked(q_ref[b * 128:(b + 1) * 128, lanes]), raug[b]], axis=1)
        s = nt(kcat, rhs) + strip[LEFT - b * 128:LEFT - b * 128 + TP, :]
        mx = jnp.max(s, axis=0, keepdims=True)
        e = jnp.exp(s - mx)
        l = jnp.sum(e, axis=0, keepdims=True)
        ot = nn(vtv, e.astype(bf16)) * (1.0 / l)
        lse_ref[p, b:b + 1, :] = mx + jnp.log(l)
        o = jnp.where(rowsel, ot[:, :128], ot[:, 128:])
        o_ref[b * 128:(b + 1) * 128, lanes] = o.T.astype(bf16)


def bwd_pair(p, q_ref, k_ref, v_ref, g_ref, lse_ref, base_ref, db_ref, kaug, raug, strip, acc, kt, dk_s, dv_s, hook=None):
    lanes = pl.ds(pl.multiple_of(p * 128, 128), 128)
    build_strip(base_ref, 2 * p, strip)
    kt[...] = k_ref[:, lanes].T
    kcat = jnp.concatenate([k_ref[:, lanes], kaug[...]], axis=1)
    v = v_ref[:, lanes]
    ktv = kt[...]
    acc[...] = jnp.zeros_like(acc)
    dk_s[...] = jnp.zeros_like(dk_s)
    dv_s[...] = jnp.zeros_like(dv_s)
    rowsel = lax.broadcasted_iota(jnp.int32, (128, 128), 0) < 64
    for b in range(NB):
        if hook is not None:
            hook(b)
        rows = slice(b * 128, (b + 1) * 128)
        qs = stacked(q_ref[rows, lanes])
        gs = stacked(g_ref[rows, lanes])
        rhs = jnp.concatenate([qs, raug[b]], axis=1)
        w = slice(LEFT - b * 128, LEFT - b * 128 + TP)
        s = nt(kcat, rhs) + strip[w, :]
        pr = jnp.exp(s - lse_ref[p, b:b + 1, :])
        dp = nt(v, gs)
        pdp = pr * dp
        delta = jnp.sum(pdp, axis=0, keepdims=True)
        ds = pdp - pr * delta
        acc[w, :] += ds
        dsb = ds.astype(bf16)
        dk_s[...] += nn(dsb, qs)
        dv_s[...] += nn(pr.astype(bf16), gs)
        dqt = nn(ktv, dsb)
        dq = jnp.where(rowsel, dqt[:, :128], dqt[:, 128:])
        q_ref[rows, lanes] = dq.T.astype(bf16)
    k_ref[:, lanes] = dk_s[...].astype(bf16)
    v_ref[:, lanes] = dv_s[...].astype(bf16)
    fi = lax.broadcasted_iota(jnp.int32, (128, 128), 0)
    fj = lax.broadcasted_iota(jnp.int32, (128, 128), 1)
    flip = jnp.where(fi + fj == 127, 1.0, 0.0).astype(f32)
    for hh in range(2):
        half = slice(hh * 128, hh * 128 + 128)
        far_l = jnp.sum(acc[0:W0, half], keepdims=True)
        far_r = jnp.sum(acc[W0 + WN:STRIP, half], keepdims=True)
        win = acc[W0:W0 + WN, half]
        wt = lax.dot_general(flip, win, (((1,), (1,)), ((), ())), precision=lax.Precision.HIGHEST, preferred_element_type=f32)
        wt = jnp.concatenate([wt, jnp.zeros((128, 128), f32)], axis=1)
        wt = pltpu.roll(wt, 0, 1, stride=1, stride_axis=0)
        diag = jnp.sum(wt, axis=0, keepdims=True)
        lane = lax.broadcasted_iota(jnp.int32, (1, 512), 1)
        diag = diag + jnp.where(lane == 0, far_l, 0.0) + jnp.where(lane == 510, far_r, 0.0)
        db_ref[pl.ds(2 * p + hh, 1), :] = diag


def bucket_of(relative):
    distance = jnp.abs(relative)
    far = 8 + sum(((distance >= e).astype(jnp.int32) for e in (12, 16, 23, 32, 46, 64, 91)))
    near = jnp.where(distance < 8, distance, far)
    return near + 16 * (relative > 0).astype(jnp.int32)

def base_hot(nbuckets, grad=False):
    c = jnp.arange(512, dtype=jnp.int32)
    r = c - 255 if grad else jnp.where(c < 384, c - 128, c - 640)
    return (bucket_of(r)[:, None] == jnp.arange(nbuckets, dtype=jnp.int32)[None, :]).astype(f32)


ROWS = 128
VP = 384
VG = 512
VR = 272
EPS = 1e-6

def byte_valid_mat(scal_ref, nbytes):
    i = lax.broadcasted_iota(jnp.int32, (ROWS, 128), 0)
    j = lax.broadcasted_iota(jnp.int32, (ROWS, 128), 1)
    p = 12 * i + j
    slot = nbytes // 2
    joined = scal_ref[0] == 1
    l0 = scal_ref[1]; l1 = scal_ref[2]
    second = p >= slot
    start = jnp.where(joined, 0, jnp.where(second, slot, 0))
    lim = jnp.where(joined, l0 + l1, jnp.where(second, l1, l0))
    ok = (p - start < lim) & (p < nbytes) & (j < 12)
    return jnp.where(ok, 1.0, 0.0).astype(f32)

def inverse_counts(vm):
    v = [vm[:, j:j + 1] for j in range(12)]
    inv = {1: v}
    for b in (2, 3, 4):
        out = []
        for m in range(12 // b):
            tot = v[b * m]
            for t in range(1, b):
                tot = tot + v[b * m + t]
            out.append(1.0 / jnp.maximum(tot, 1.0))
        inv[b] = out
    return v, inv

def softmax_weights(e, inv):
    rate = {1: e}
    for b in (2, 3, 4):
        out = []
        for m in range(12 // b):
            tot = e[b * m]
            for t in range(1, b):
                tot = tot + e[b * m + t]
            out.append(tot * inv[b][m])
        rate[b] = out
    w = {b: [] for b in (1, 2, 3, 4)}
    for p in range(12):
        r = [rate[b][p // b] for b in (1, 2, 3, 4)]
        mx = jnp.maximum(jnp.maximum(r[0], r[1]), jnp.maximum(r[2], r[3]))
        ex = [jnp.exp(x - mx) for x in r]
        inv_t = 1.0 / (ex[0] + ex[1] + ex[2] + ex[3])
        for b in (1, 2, 3, 4):
            w[b].append(ex[b - 1] * inv_t)
    return w

def gbst_fwd_body(nbytes, vocab, scal_ref, ids_ref, tt_ref, stream_ref, normed_ref, emb_ref, wcol_ref, tot_ref, vec_ref, slabs, table_ref, hook):
    table_ref[...] = tt_ref[...].T
    base = vocab // 16 * 16
    tail = table_ref[base:base + 16, :].astype(f32)
    vec_ref[0:3, :] = tail[vocab - base:vocab - base + 3, :]
    vec_ref[3:8, :] = jnp.zeros((5, tail.shape[1]), f32)
    vm = byte_valid_mat(scal_ref, nbytes)
    v, inv = inverse_counts(vm)
    idt = ids_ref[...].astype(f32).T
    lane = lax.broadcasted_iota(jnp.int32, (ROWS, VP), 1).astype(f32)
    s = vec_ref[0:1, :]
    e = []
    for j in range(12):
        hot = jnp.where((lane == idt[:, j:j + 1]) & (v[j] > 0.5), 1.0, 0.0).astype(bf16)
        ej = nn(hot, table_ref[...])
        emb_ref[j * ROWS:(j + 1) * ROWS, :] = ej.astype(bf16)
        e.append(jnp.sum(ej * s, axis=1, keepdims=True))
        if j % 3 == 2:
            hook()
    w = softmax_weights(e, inv)
    l128 = lax.broadcasted_iota(jnp.int32, (ROWS, 128), 1)
    wc = jnp.zeros((ROWS, 128), f32)
    for b in (1, 2, 3, 4):
        for p in range(12):
            wc = jnp.where(l128 == (b - 1) * 12 + p, w[b][p], wc)
    wcol_ref[...] = wc
    tl = lax.broadcasted_iota(jnp.int32, (8, 128), 1)
    tot = jnp.zeros((8, 128), f32)
    for b in (1, 2, 3, 4):
        acc = w[b][0] * v[0]
        for p in range(1, 12):
            acc = acc + w[b][p] * v[p]
        tot = jnp.where(tl == b - 1, jnp.sum(acc, keepdims=True), tot)
    tot = jnp.where(tl == 4, jnp.sum(vm, keepdims=True), tot)
    tot_ref[...] = tot
    hook()
    E = lambda j: emb_ref[j * ROWS:(j + 1) * ROWS, :].astype(f32)
    s3 = lambda m: E(3 * m) + E(3 * m + 1) + E(3 * m + 2)
    for k in range(6):
        p0, p1 = 2 * k, 2 * k + 1
        b2 = 0.5 * (w[2][p0] + w[2][p1]) * inv[2][k]
        acc = (0.5 * w[1][p0] + b2) * E(p0) + (0.5 * w[1][p1] + b2) * E(p1)
        n = k // 2
        d = 0.5 * (w[4][p0] + w[4][p1]) * inv[4][n]
        acc = acc + d * ((E(4 * n) + E(4 * n + 1)) + (E(4 * n + 2) + E(4 * n + 3)))
        m0, m1 = p0 // 3, p1 // 3
        if m0 == m1:
            acc = acc + (0.5 * (w[3][p0] + w[3][p1]) * inv[3][m0]) * s3(m0)
        else:
            acc = acc + (0.5 * w[3][p0] * inv[3][m0]) * s3(m0) + (0.5 * w[3][p1] * inv[3][m1]) * s3(m1)
        put_strided(slabs, k, acc)
        if k % 2 == 1:
            hook()
    ntok = nbytes // 2
    for c in range(slabs.shape[0]):
        stream_ref[0:ntok, c * 128:(c + 1) * 128] = slabs[c, 0:ntok, :]
    stream_ref[ntok:TP, :] = jnp.zeros((TP - ntok, acc.shape[1]), f32)
    norm_rows(stream_ref, vec_ref[1:2, :], normed_ref)
    hook()


def put_strided(ref, k, val):
    for c in range(val.shape[1] // 128):
        ref[c, pl.ds(k, 124, stride=6), :] = val[:124, c * 128:(c + 1) * 128]

def get_strided(ref, k):
    parts = [ref[c, pl.ds(k, 124, stride=6), :] for c in range(ref.shape[0])]
    x = jnp.concatenate(parts, axis=1)
    return jnp.concatenate([x, jnp.zeros((4, x.shape[1]), f32)], axis=0)

def norm_rows(x_ref, gain_ref, out_ref):
    g = gain_ref
    for b in range(TP // 128):
        x = x_ref[b * 128:(b + 1) * 128, :]
        sc = lax.rsqrt(jnp.mean(x * x, axis=1, keepdims=True) + EPS)
        out_ref[b * 128:(b + 1) * 128, :] = (x * sc * g).astype(bf16)

def gbst_bwd_body(nbytes, vocab, scal_ref, ids_ref, emb_ref, wcol_ref, score_ref, ggain_ref, put, de_ref, slabs, hook):
    vm = byte_valid_mat(scal_ref, nbytes)
    v, inv = inverse_counts(vm)
    wc = wcol_ref[...]
    w = {b: [wc[:, (b - 1) * 12 + p:(b - 1) * 12 + p + 1] for p in range(12)] for b in (1, 2, 3, 4)}
    s = score_ref[0:1, :]
    E = lambda j: emb_ref[j * ROWS:(j + 1) * ROWS, :].astype(f32)
    s3 = lambda m: E(3 * m) + E(3 * m + 1) + E(3 * m + 2)
    s4 = lambda n: (E(4 * n) + E(4 * n + 1)) + (E(4 * n + 2) + E(4 * n + 3))
    dot = lambda a, b: jnp.sum(a * b, axis=1, keepdims=True)
    dw = {b: [None] * 12 for b in (1, 2, 3, 4)}
    D = []
    for k in range(6):
        dk = 0.5 * get_strided(slabs, k)
        D.append(dk)
        p0, p1 = 2 * k, 2 * k + 1
        x0, x1 = dot(dk, E(p0)), dot(dk, E(p1))
        dw[1][p0], dw[1][p1] = x0, x1
        dw[2][p0] = dw[2][p1] = (x0 + x1) * inv[2][k]
        m0, m1 = p0 // 3, p1 // 3
        a0 = dot(dk, s3(m0)) * inv[3][m0]
        dw[3][p0] = a0
        dw[3][p1] = a0 if m0 == m1 else dot(dk, s3(m1)) * inv[3][m1]
        dw[4][p0] = dw[4][p1] = dot(dk, s4(k // 2)) * inv[4][k // 2]
        if k % 2 == 1:
            hook()
    hook()
    dr = {b: [] for b in (1, 2, 3, 4)}
    for p in range(12):
        mean = w[1][p] * dw[1][p] + w[2][p] * dw[2][p] + w[3][p] * dw[3][p] + w[4][p] * dw[4][p]
        for b in (1, 2, 3, 4):
            dr[b].append(w[b][p] * (dw[b][p] - mean))
    rb = {1: dr[1]}
    for b in (2, 3, 4):
        out = []
        for m in range(12 // b):
            tot = dr[b][b * m]
            for t in range(1, b):
                tot = tot + dr[b][b * m + t]
            out.append(tot * inv[b][m])
        rb[b] = out
    t3 = []
    for m in range(4):
        terms = {}
        for p in (3 * m, 3 * m + 1, 3 * m + 2):
            terms[p // 2] = terms[p // 2] + w[3][p] if p // 2 in terms else w[3][p]
        acc = None
        for k, coef in terms.items():
            t = (coef * inv[3][m]) * D[k]
            acc = t if acc is None else acc + t
        t3.append(acc)
    gscore = jnp.zeros((8, s.shape[1]), f32)
    for n in range(3):
        t4 = ((w[4][4 * n] + w[4][4 * n + 1]) * inv[4][n]) * D[2 * n] + ((w[4][4 * n + 2] + w[4][4 * n + 3]) * inv[4][n]) * D[2 * n + 1]
        for p in range(4 * n, 4 * n + 4):
            k = p // 2
            c = rb[1][p] + rb[2][k] + rb[3][p // 3] + rb[4][n]
            b2 = (w[2][2 * k] + w[2][2 * k + 1]) * inv[2][k]
            de = v[p] * ((w[1][p] + b2) * D[k] + t3[p // 3] + t4 + c * s)
            de_ref[p * ROWS:(p + 1) * ROWS, :] = de.astype(bf16)
            y = c * E(p)
            gscore = gscore + jnp.sum(y.reshape(ROWS // 8, 8, s.shape[1]), axis=0)
        hook()
    gscore = jnp.sum(gscore, axis=0, keepdims=True)
    row = lax.broadcasted_iota(jnp.int32, (VR, ROWS), 0)
    hots = [jnp.where(row == ids_ref[j:j + 1, :], 1.0, 0.0).astype(bf16) for j in range(12)]
    hot = jnp.concatenate(hots, axis=1)
    gtable = nn(hot, de_ref[...])
    row = lax.broadcasted_iota(jnp.int32, gtable.shape, 0)
    for i, extra in enumerate((gscore, ggain_ref[0:1, :], ggain_ref[1:2, :])):
        gtable = jnp.where(row == vocab + i, extra, gtable)
    put(gtable.T.astype(bf16))


MESH = pl.DeviceIdType.MESH


def coords():
    w = lax.axis_index("wide")
    n = lax.axis_index("narrow")
    return w, w // 2, w % 2, n // 2, n % 2


def peer_ids():
    w, z, y, x, c = coords()
    n = 2 * x + c
    return {
        "y": (2 * z + 1 - y, n),
        "zp": (2 * ((z + 1) % 4) + y, n),
        "zm": (2 * ((z + 3) % 4) + y, n),
        "zo": (2 * ((z + 2) % 4) + y, n),
        "x": (w, 2 * (1 - x) + c),
        "c": (w, 2 * x + 1 - c),
        "xc": (w, 2 * (1 - x) + 1 - c),
    }


def enter(peers, names):
    barrier = pltpu.get_barrier_semaphore()
    for name in names:
        pl.semaphore_signal(barrier, inc=1, device_id=peers[name], device_id_type=MESH)
    pl.semaphore_wait(barrier, len(names))


class Gather:
    SENDS = 30
    SLOTS = 28

    def __init__(self, shards, fulls, split, ssem, rsem, lsem):
        self.shards, self.fulls, self.split = shards, fulls, split
        self.ssem, self.rsem, self.lsem = ssem, rsem, lsem
        self.peers = peer_ids()
        self.w, self.z, self.y, self.x, self.c = coords()
        z = self.z
        first = jnp.where(z == 3, 3, 1)
        second = jnp.where((z == 0) | (z == 3), 2, 3)
        self.order = (first, second, 6 - first - second)
        self.inner = (z == 1) | (z == 2)
        self.sent = []
        self.local = {}

    def enter(self):
        n = 2 * self.x + self.c
        barrier = pltpu.get_barrier_semaphore()
        near = [(owner, n) for _, owner in self.others()] + [self.peers["x"], self.peers["c"]]
        for peer in near:
            pl.semaphore_signal(barrier, inc=1, device_id=peer, device_id_type=MESH)
        pl.semaphore_wait(barrier, len(near))

    def cols(self, i, c):
        width = self.fulls[i].shape[1] // 2
        return pl.ds(pl.multiple_of(c * width, 128), width)

    def block(self, i, owner, part, ref=None):
        r = self.shards[i].shape[0]
        start = owner * r
        if self.split[i]:
            r = r // 2
            start = start + part[1] * r
        return (self.fulls[i] if ref is None else ref).at[pl.ds(pl.multiple_of(start, 16), r), self.cols(i, part[0])]

    @property
    def mine(self):
        return (self.c, self.x)

    def copy(self, i, out, slot, src, owner, part, device):
        return pltpu.make_async_remote_copy(
            src_ref=src, dst_ref=self.block(i, owner, part), send_sem=self.ssem.at[i, out],
            recv_sem=self.rsem.at[i, slot], device_id=device, device_id_type=MESH)

    def send(self, i, out, slot, owner, part, device, when=None, src=None):
        src = self.block(i, owner, part) if src is None else src
        cp = self.copy(i, out, slot, src, owner, part, device)
        if when is None:
            cp.start()
        else:
            pl.when(when)(cp.start)
        self.sent.append((i, out, when))

    def arrived(self, i, slot, owner, part):
        ref = self.block(i, owner, part)
        pltpu.make_async_remote_copy(
            src_ref=ref, dst_ref=ref, send_sem=self.ssem.at[i, 0], recv_sem=self.rsem.at[i, slot],
            device_id=self.peers["c"], device_id_type=MESH).wait_recv()

    def start_direct(self, i):
        n = 2 * self.x + self.c
        for k in range(1, 8):
            dz, dy = k // 2, k % 2
            to = (2 * lax.rem(self.z + dz, 4) + (1 - self.y if dy else self.y), n)
            self.send_rows(i, k, (4 - dz) % 4 * 2 + dy, self.w, self.c, to, self.half_rows(i, 0, self.c, self.shards[i]))
        r = self.shards[i].shape[0]
        cp = pltpu.make_async_copy(self.shards[i], self.fulls[i].at[pl.ds(pl.multiple_of(self.w * r, 16), r), :], self.lsem.at[i])
        cp.start()
        self.local[i] = cp

    def half_rows(self, i, owner, c, ref=None):
        r = self.shards[i].shape[0]
        return (self.fulls[i] if ref is None else ref).at[pl.ds(pl.multiple_of(owner * r + c * (r // 2), 16), r // 2), :]

    def send_rows(self, i, out, slot, owner, c, device, src=None):
        ref = self.half_rows(i, owner, c)
        cp = pltpu.make_async_remote_copy(
            src_ref=ref if src is None else src, dst_ref=ref, send_sem=self.ssem.at[i, out], recv_sem=self.rsem.at[i, slot],
            device_id=device, device_id_type=MESH)
        cp.start()
        self.sent.append((i, out, "rows"))

    def rows_arrived(self, i, slot, owner, c):
        ref = self.half_rows(i, owner, c)
        pltpu.make_async_remote_copy(
            src_ref=ref, dst_ref=ref, send_sem=self.ssem.at[i, 0], recv_sem=self.rsem.at[i, slot],
            device_id=self.peers["c"], device_id_type=MESH).wait_recv()

    def others(self):
        for k in range(1, 8):
            dz, dy = k // 2, k % 2
            yield k, 2 * lax.rem(self.z + dz, 4) + (1 - self.y if dy else self.y)

    def steps_direct(self, i):
        def relay():
            for k, owner in self.others():
                self.rows_arrived(i, k, owner, self.c)
                self.send_rows(i, 8 + k, 8 + k, owner, self.c, self.peers["c"])

        def end():
            for k, owner in self.others():
                self.rows_arrived(i, 8 + k, owner, 1 - self.c)
            self.local[i].wait()
        return [relay, end]

    def start(self, i):
        own = self.block(i, 0, self.mine, self.shards[i])
        n = 2 * self.x + self.c
        self.send(i, 0, 2, self.w, self.mine, (2 * jnp.minimum(self.z + 1, 3) + self.y, n), self.z < 3, own)
        self.send(i, 1, 0, self.w, self.mine, (2 * jnp.maximum(self.z - 1, 0) + self.y, n), self.z > 0, own)
        self.send(i, 5, 3, self.w, self.mine, self.peers["y"], None, own)
        r = self.shards[i].shape[0]
        cp = pltpu.make_async_copy(self.shards[i], self.fulls[i].at[pl.ds(pl.multiple_of(self.w * r, 16), r), :], self.lsem.at[i])
        cp.start()
        self.local[i] = cp

    def relay(self, i, s, n, owner):
        self.send(i, 9 + n, 7 + s, owner, self.mine, self.peers["c"])
        if self.split[i]:
            self.send(i, 16 + n, 14 + s, owner, self.mine, self.peers["x"])

    def step_z(self, i, j):
        d = self.order[j]
        o = lax.rem(self.z + d, 4)
        owner = 2 * o + self.y
        self.arrived(i, d - 1, owner, self.mine)
        to = jnp.where(self.inner, jnp.where(o < self.z, self.z + 1, self.z - 1), jnp.where(self.z == 0, 1, 2))
        slot = jnp.where(self.inner, lax.rem(o - to + 4, 4) - 1, 0)
        self.send(i, 2 + j, slot, owner, self.mine, (2 * to + self.y, 2 * self.x + self.c), self.inner)
        self.send(i, 6 + j, 3 + d, owner, self.mine, self.peers["y"])
        self.relay(i, d - 1, j, owner)

    def step_y(self, i, j):
        d = 0 if j < 0 else self.order[j]
        owner = 2 * lax.rem(self.z + d, 4) + 1 - self.y
        self.arrived(i, 3 + d, owner, self.mine)
        self.relay(i, 3 + d, 4 + j, owner)

    def each(self):
        for j in range(3):
            d = self.order[j]
            yield d - 1, j, 2 * lax.rem(self.z + d, 4) + self.y
        for j in range(-1, 3):
            d = 0 if j < 0 else self.order[j]
            yield 3 + d, 4 + j, 2 * lax.rem(self.z + d, 4) + 1 - self.y

    def step_x(self, i):
        if self.split[i]:
            other = (self.c, 1 - self.x)
            for s, n, owner in self.each():
                self.arrived(i, 14 + s, owner, other)
                self.send(i, 23 + n, 21 + s, owner, other, self.peers["c"])

    def step_end(self, i):
        for s, n, owner in self.each():
            self.arrived(i, 7 + s, owner, (1 - self.c, self.x))
            if self.split[i]:
                self.arrived(i, 21 + s, owner, (1 - self.c, 1 - self.x))
        self.local[i].wait()

    def finish(self):
        for i, out, when in self.sent:
            if isinstance(when, str):
                ref = self.half_rows(i, self.w, self.c)
                when = None
            else:
                ref = self.block(i, self.w, self.mine)
            cp = pltpu.make_async_remote_copy(
                src_ref=ref, dst_ref=ref, send_sem=self.ssem.at[i, out], recv_sem=self.rsem.at[i, 0],
                device_id=self.peers["c"], device_id_type=MESH)
            if when is None:
                cp.wait_send()
            else:
                pl.when(when)(cp.wait_send)

    def steps(self, i):
        return [functools.partial(self.step_y, i, -1)] + [functools.partial(f, i, j) for j in range(3) for f in (self.step_z, self.step_y)] + [
            functools.partial(self.step_x, i), functools.partial(self.step_end, i)]


class Reduce:
    SLOTS = 9

    def __init__(self, terms, outs, order, rc, r1, r2, r3, ssem, rsem):
        self.terms, self.outs, self.order = terms, outs, order
        self.rc, self.r1, self.r2, self.r3 = rc, r1, r2, r3
        self.ssem, self.rsem = ssem, rsem
        self.peers = peer_ids()
        self.w, self.z, self.y, self.x, self.c = coords()
        self.sent = []

    def enter(self):
        enter(self.peers, ("y", "zp", "zm", "zo", "x", "c", "xc"))

    def transfer(self, i, slot, src, dst, to):
        return pltpu.make_async_remote_copy(
            src_ref=src, dst_ref=dst, send_sem=self.ssem.at[i, slot], recv_sem=self.rsem.at[i, slot],
            device_id=self.peers[to], device_id_type=MESH)

    def send(self, i, slot, src, dst, to):
        self.transfer(i, slot, src, dst, to).start()
        self.sent.append((i, slot))

    def arrived(self, i, slot, dst):
        self.transfer(i, slot, dst, dst, "c").wait_recv()

    def half(self, i, c):
        width = self.terms[i].shape[4] // 2
        return pl.ds(pl.multiple_of(c * width, 128), width)

    def start(self, i):
        self.send(i, 0, self.terms[i].at[:, :, :, :, self.half(i, 1 - self.c)], self.rc[i], "c")

    def add(self, a, b):
        return a + b

    def step_core(self, i):
        self.arrived(i, 0, self.rc[i])

        def one(z, carry):
            self.rc[i][z] = self.add(self.terms[i][z, :, :, :, self.half(i, self.c)], self.rc[i][z])
            return carry
        lax.fori_loop(0, 4, one, 0)
        if self.order[i] == "y":
            self.send(i, 1, self.rc[i].at[:, 1 - self.y], self.r1[i], "y")
        else:
            self.send(i, 1, self.rc[i].at[:, :, 1 - self.x], self.r1[i], "x")

    def step_one(self, i):
        self.arrived(i, 1, self.r1[i])

        def one(z, carry):
            if self.order[i] == "y":
                mine = self.rc[i][z, self.y]
            else:
                mine = self.rc[i][z, :, self.x]
            self.r1[i][z] = self.add(mine, self.r1[i][z])
            return carry
        lax.fori_loop(0, 4, one, 0)
        if self.order[i] == "y":
            self.send(i, 2, self.r1[i].at[:, 1 - self.x], self.r2[i], "x")
        else:
            self.send(i, 2, self.r1[i].at[:, 1 - self.y], self.r2[i], "y")

    def step_two(self, i):
        self.arrived(i, 2, self.r2[i])
        pick = self.x if self.order[i] == "y" else self.y

        def one(z, carry):
            self.r2[i][z] = self.add(self.r1[i][z, pick], self.r2[i][z])
            return carry
        lax.fori_loop(0, 4, one, 0)
        for dz, to in ((1, "zp"), (3, "zm"), (2, "zo")):
            self.send(i, 2 + dz, self.r2[i].at[lax.rem(self.z + dz, 4)], self.r3[i].at[3 - dz], to)

    def step_z(self, i):
        total = self.r2[i][self.z].astype(f32)
        for dz in (1, 3, 2):
            self.arrived(i, 2 + dz, self.r3[i].at[3 - dz])
        for k in range(3):
            total = total + self.r3[i][k].astype(f32)
        out = self.outs[i]
        out[self.c, self.x] = total.astype(bf16)
        for slot, to in ((6, "x"), (7, "c"), (8, "xc")):
            self.send(i, slot, out.at[self.c, self.x], out.at[self.c, self.x], to)

    def step_end(self, i):
        out = self.outs[i]
        self.arrived(i, 6, out.at[self.c, 1 - self.x])
        self.arrived(i, 7, out.at[1 - self.c, self.x])
        self.arrived(i, 8, out.at[1 - self.c, 1 - self.x])

    def steps(self, i):
        return [functools.partial(f, i) for f in (self.step_core, self.step_one, self.step_two, self.step_z, self.step_end)]

    def finish(self):
        for i, slot in self.sent:
            block = self.r2[i].at[0]
            ref = {0: self.rc[i], 1: self.r1[i], 2: self.r2[i]}.get(slot, block)
            self.transfer(i, slot, ref, ref, "c").wait_send()

    @staticmethod
    def scratch(shapes):
        rc = [pltpu.VMEM((4, 2, 2, s[3], s[4] // 2), bf16) for s in shapes]
        r1 = [pltpu.VMEM((4, 2, s[3], s[4] // 2), bf16) for s in shapes]
        r2 = [pltpu.VMEM((4, s[3], s[4] // 2), bf16) for s in shapes]
        r3 = [pltpu.VMEM((3, s[3], s[4] // 2), bf16) for s in shapes]
        n = len(shapes)
        return rc + r1 + r2 + r3 + [pltpu.SemaphoreType.DMA((n, 9)), pltpu.SemaphoreType.DMA((n, 9))]


SMALL = (16, 128)


class SmallSum:
    HOPS = ("c", "x", "y", "zn", "zo")

    def __init__(self, acc, slots, ssem, rsem):
        self.acc, self.slots, self.ssem, self.rsem = acc, slots, ssem, rsem
        self.peers = peer_ids()
        w, z, y, x, c = coords()
        self.peers["zn"] = (2 * (z + 1 - 2 * (z % 2)) + y, 2 * x + c)

    def copy(self, k):
        return pltpu.make_async_remote_copy(
            src_ref=self.slots.at[5 + k], dst_ref=self.slots.at[k], send_sem=self.ssem.at[k], recv_sem=self.rsem.at[k],
            device_id=self.peers[self.HOPS[k]], device_id_type=MESH)

    def step(self, k):
        if k:
            self.copy(k - 1).wait()
            self.acc[...] = self.acc[...] + self.slots[k - 1]
        if k < 5:
            self.slots[5 + k] = self.acc[...]
            self.copy(k).start()

    def steps(self):
        return [functools.partial(self.step, k) for k in range(6)]


def none():
    pass


class Feed:
    def __init__(self, steps, share=1):
        self.steps = list(steps)
        self.share = share

    def __call__(self):
        for _ in range(self.share):
            if self.steps:
                self.steps.pop(0)()

    def rest(self):
        while self.steps:
            self.steps.pop(0)()


def forward_kernel(nbytes, vocab, split, *refs):
    scal_ref, ids_ref, base_ref = refs[:3]
    shards = refs[3:11]
    outs = refs[11:28]
    fulls = list(outs[:7])
    stream_o, normed_o, emb_o, wcol_o, tot_o, vec_o, q_o, k_o, v_o, mixed_o = outs[7:17]
    lse_o = refs[28]
    (tt, wq, wk, wv, stream, normed, emb, wcol, tot, vec, q, k, v, mixed, lse, slabs, table, kaug, raug, strip, vt, osem, wsem) = refs[29:52]
    done = []

    def out(src, dst):
        cp = pltpu.make_async_copy(src, dst, osem.at[len(done)])
        cp.start()
        done.append(cp)

    ntok = nbytes // 2
    if split is not None:
        g = Gather(shards, [tt] + fulls, split, *refs[52:55])
        g.enter()
        g.start_direct(0)
        for i in range(1, 4):
            g.start(i)
        build_masks(scal_ref, kaug, raug, ntok)
        relay, end = g.steps_direct(0)
        relay()
        for i in range(4, 8):
            g.start(i)
        end()
        plans = [None] + [g.steps(i) for i in range(1, 8)]
        early = Feed([plans[i][s] for s in range(8) for i in (1, 2, 3)], 3)
        late = [plans[i][s] for s in range(8) for i in (4, 5, 6, 7)]
        per = -(-len(late) // 6)
        chunks = [late[j * per:(j + 1) * per] for j in range(6)]
    else:
        cp = pltpu.make_async_copy(shards[0], tt, wsem.at[3])
        cp.start()
        build_masks(scal_ref, kaug, raug, ntok)
        cp.wait()
        early = Feed([])
        chunks = [[]] * 6
    gbst_fwd_body(nbytes, vocab, scal_ref, ids_ref, tt, stream, normed, emb, wcol, tot, vec, slabs, table, early)
    early.rest()
    for src, dst in ((stream, stream_o), (normed, normed_o), (emb, emb_o), (wcol, wcol_o), (tot, tot_o), (vec, vec_o)):
        out(src, dst)
    loads = []
    for i, dst in enumerate((wq, wk, wv)):
        if split is not None:
            plans[i + 1][8]()
        cp = pltpu.make_async_copy(shards[i + 1] if split is None else fulls[i], dst, wsem.at[i])
        cp.start()
        loads.append(cp)
    for cp, w, dst, to in zip(loads, (wq, wk, wv), (q, k, v), (q_o, k_o, v_o)):
        cp.wait()

        def rows(b, carry):
            sl = pl.ds(pl.multiple_of(b * 256, 256), 256)
            dst[sl, :] = nn(normed[sl, :], w[...]).astype(bf16)
            return carry
        lax.fori_loop(0, TP // 256, rows, 0)
        out(dst, to)

    def pair(p, carry):
        for j in range(6):
            if chunks[j]:
                @pl.when(p == j)
                def _():
                    for step in chunks[j]:
                        step()
        fwd_pair(p, q, k, v, base_ref, mixed, lse, kaug, raug, strip, vt)
        return carry
    lax.fori_loop(0, q.shape[1] // 128, pair, 0)
    out(mixed, mixed_o)
    out(lse, lse_o)
    if split is not None:
        for i in range(4, 8):
            plans[i][8]()
        g.finish()
    for cp in done:
        cp.wait()


def forward_one(scal, ids, base2, shards, vocab, nbytes, wide, split):
    d = shards[1].shape[1]
    hbm = pl.BlockSpec(memory_space=pltpu.HBM)
    vm = pl.BlockSpec(memory_space=pltpu.VMEM)
    pairs = d // 128
    many = 1 if split is None else wide
    sd = jax.ShapeDtypeStruct
    acts = [((TP, d), f32), ((TP, d), bf16), ((12 * ROWS, d), bf16), ((ROWS, 128), f32), ((8, 128), f32), ((8, d), f32),
            ((TP, d), bf16), ((TP, d), bf16), ((TP, d), bf16), ((TP, d), bf16), ((pairs, 8, 256), f32)]
    wq = (d, d)
    scratch = [pltpu.VMEM((d, VP), bf16)] + [pltpu.VMEM(wq, bf16)] * 3 + [pltpu.VMEM(*a) for a in acts]
    scratch += [pltpu.VMEM((d // 128, TP, 128), f32), pltpu.VMEM((VP, d), bf16), pltpu.VMEM((TP, 128), bf16), pltpu.VMEM((NB, 256, 128), bf16),
                pltpu.VMEM((STRIP, 256), f32), pltpu.VMEM((128, TP), bf16), pltpu.SemaphoreType.DMA((11,)), pltpu.SemaphoreType.DMA((4,))]
    params = dict(vmem_limit_bytes=56 << 20)
    if split is not None:
        scratch += [pltpu.SemaphoreType.DMA((8, Gather.SENDS)), pltpu.SemaphoreType.DMA((8, Gather.SLOTS)), pltpu.SemaphoreType.DMA((8,))]
        params.update(collective_id=1, has_side_effects=True)
        whole = [sd((many * s.shape[0], s.shape[1]), bf16) for s in shards[1:]]
    else:
        whole = [sd((8, 128), bf16)] * 7
    return pl.pallas_call(
        functools.partial(forward_kernel, nbytes, vocab, split),
        out_shape=tuple(whole) + tuple(sd(*a) for a in acts),
        in_specs=[pl.BlockSpec(memory_space=pltpu.SMEM), vm, vm] + [hbm] * 8,
        out_specs=(hbm,) * 18,
        scratch_shapes=scratch,
        compiler_params=pltpu.CompilerParams(**params),
        name="forward_one",
    )(scal, ids, base2, *shards)


FCH = 256
FRB = 256
GELU = 0.7978845608028654


def flat(ref, cs=slice(None)):
    return ref[:, :, :, :, cs].reshape(ref.shape[0] * 4 * ref.shape[3], -1)


def norm_scale(x):
    return lax.rsqrt(jnp.mean(x * x, axis=1, keepdims=True) + EPS)


def row_block(b):
    return pl.ds(pl.multiple_of(b * FRB, FRB), FRB)


def store_product(dst, tr, rhs):
    rows = dst.shape[0] * 4 * dst.shape[3]
    parts = -(-rows // 1024)
    size = dst.shape[0] // parts
    wide = 256
    for m in range(parts):
        left = tr[m * rows // parts:(m + 1) * rows // parts, :]
        for c in range(dst.shape[4] // wide):
            cs = slice(c * wide, (c + 1) * wide)
            r = nn(left, rhs[:, cs]).astype(bf16)
            dst[m * size:(m + 1) * size, :, :, :, cs] = r.reshape((size,) + dst.shape[1:4] + (wide,))


def ff_phase(weights_h, mixed_h, stream_h, og_h, enc_o, g2, wo, wf, wd, stream, mid, gh_out, ggain2, sems, ready, poll):
    d = mid.shape[1]
    halves = len(wf)
    part = wf[0].shape[4] // 2

    def scoped(hid, gg, gu, tr, mixed, og, nff, dacc):
        ins = []
        pairs = [(mixed_h, mixed), (weights_h[0], wo), (stream_h, stream), (og_h, og)]
        for h in range(halves):
            cs = slice(h * part, (h + 1) * part)
            pairs += [(weights_h[2].at[:, :, :, :, cs], wf[h].at[:, :, :, :, 0:part]), (weights_h[1].at[:, :, :, :, cs], wf[h].at[:, :, :, :, part:2 * part])]
            if h == 0:
                pairs.append((weights_h[3], wd))
        for n, (s, t) in enumerate(pairs):
            cp = pltpu.make_async_copy(s, t, sems.at[n])
            cp.start()
            ins.append(cp)
        for cp in ins[:3]:
            cp.wait()

        def first(b, carry):
            sl = row_block(b)
            middle = stream[sl, :] + nn(mixed[sl, :], flat(wo))
            dacc[sl, :] = middle
            nff[sl, :] = (middle * norm_scale(middle) * g2).astype(bf16)
            return carry
        lax.fori_loop(0, TP // FRB, first, 0)
        tr[0:d, :] = nff[...].T
        for cp in ins[3:7]:
            cp.wait()
        for h in range(halves):
            if h:
                for cp in ins[7:]:
                    cp.wait()

            for c in range(part // FCH):
                poll(h, c)
                cs = slice(c * FCH, (c + 1) * FCH)
                at = slice(h * part + c * FCH, h * part + (c + 1) * FCH)
                wuc, wgc = flat(wf[h], cs), flat(wf[h], slice(part + c * FCH, part + (c + 1) * FCH))
                wdc = wd[(h * part + c * FCH) // 512, c % 2].reshape(FCH, d)
                gate = nn(nff[...], wgc)
                up = nn(nff[...], wuc)
                gh = nt(og[...], wdc)
                sq = gate * gate
                th = jnp.tanh(gate * (GELU + (GELU * 0.044715) * sq))
                half = 0.5 + 0.5 * th
                act = gate * half
                hid[:, at] = (act * up).astype(bf16)
                dact = half + (0.5 * gate) * (1.0 - th * th) * (GELU + (3 * GELU * 0.044715) * sq)
                gg[:, cs] = (gh * up * dact).astype(bf16)
                gu[:, cs] = (gh * act).astype(bf16)
                dacc[...] += nn(hid[:, at], wdc)
                if h == 0 and c == 0:
                    mid[...] = nt(gg[:, cs], wgc)
                else:
                    mid[...] += nt(gg[:, cs], wgc)
                mid[...] += nt(gu[:, cs], wuc)
            store_product(wf[h].at[:, :, :, :, 0:part], tr.at[0:d], gu)
            store_product(wf[h].at[:, :, :, :, part:2 * part], tr.at[0:d], gg)
            ready("f%d" % h)

        tr[...] = hid[...].T
        store_product(wd, tr, og)
        ready("d")

        def last(b, carry):
            sl = row_block(b)
            nff[sl, :] = dacc[sl, :].astype(bf16)
            wo_all = flat(wo)
            middle = stream[sl, :] + nn(mixed[sl, :], wo_all)
            s2 = norm_scale(middle)
            back = mid[sl, :]
            t = back * g2
            xs = middle * s2
            grad = og[sl, :].astype(f32) + s2 * t - xs * (s2 * s2 * jnp.mean(middle * t, axis=1, keepdims=True))
            mid[sl, :] = grad
            low = grad.astype(bf16)
            gu[sl, 0:d] = low
            gh_out[sl, :] = nt(low, wo_all).astype(bf16)
            ggain2[...] += jnp.sum((back * xs).reshape(FRB // 8, 8, d), axis=0)
            return carry
        lax.fori_loop(0, TP // FRB, last, 0)
        cp = pltpu.make_async_copy(nff, enc_o, sems.at[0])
        cp.start()
        tr[0:d, :] = mixed[...].T
        store_product(wo, tr.at[0:d], gu)
        ready("o")
        cp.wait()
    act = lambda c: pltpu.VMEM((TP, c), bf16)
    pl.run_scoped(scoped, act(halves * part), act(part), act(part), pltpu.VMEM((halves * part, TP), bf16), act(d), act(d), act(d), pltpu.VMEM((TP, d), f32))


NAMES = ("t", "p0", "p1", "p2", "o", "f0", "f1", "d")
FIRST = {"t": "x", "p0": "x", "p1": "y", "p2": "x", "o": "x", "f0": "y", "f1": "x", "d": "y"}
STEPS = ("core", "one", "two", "z", "end")


def backward_kernel(nbytes, vocab, remote, *refs):
    n = len(NAMES)
    scal_ref, ids_ref, base_ref, hot_ref, vec_ref, wcol_ref, tot_ref, lse_ref = refs[:8]
    q_h, k_h, v_h, normed_h, stream_h, mixed_h, og_h, emb_h, wq_h, wk_h, wv_h = refs[8:19]
    big_h = refs[19:23]
    enc_o, outs, small_o = refs[23], refs[24:24 + n], refs[24 + n]
    refs = refs[25 + n:]
    stream, mid, g, ggain2, ggain, fsem, lsem = refs[:7]
    if remote:
        terms = refs[7:7 + n]
        rest = refs[7 + n:]
        red = Reduce(terms, outs, tuple(FIRST[k] for k in NAMES), *[rest[k * n:(k + 1) * n] for k in range(4)], *rest[4 * n:4 * n + 2])
        small = SmallSum(*rest[4 * n + 2:4 * n + 6])
        st = {k: dict(zip(STEPS, red.steps(i))) for i, k in enumerate(NAMES)}
        st["s"] = {k: f for k, f in enumerate(small.steps())}
        red.enter()
    else:
        terms = outs
    term = dict(zip(NAMES, terms))

    def run(words):
        if remote:
            for word in words:
                name, step = word.split(".")
                st[name][int(step) if name == "s" else step]()

    def point(key):
        run(TABLE.get(key, ()))

    def ready(name):
        if remote:
            red.start(NAMES.index(name))
            point(name)

    def point_at(index, keys):
        for j, key in enumerate(keys):
            if remote and TABLE.get(key):
                @pl.when(index == j)
                def _():
                    point(key)

    def poll(h, c):
        point("c%d%d" % (h, c))
    ggain2[...] = jnp.zeros_like(ggain2)
    ff_phase(big_h, mixed_h, stream_h, og_h, enc_o, vec_ref[2:3, :], term["o"], (term["f0"], term["f1"]), term["d"],
             stream, mid, g, ggain2, fsem, ready, poll)
    d = stream.shape[1]
    pairs = d // 128

    def scoped(q, k, v, nt_s, emb, wq, wk, wv):
        copies = []
        moves = ((q_h, q), (k_h, k), (v_h, v), (normed_h, nt_s), (emb_h, emb), (wq_h, wq), (wk_h, wk), (wv_h, wv))
        for m, (s, t) in enumerate(moves):
            cp = pltpu.make_async_copy(s, t, lsem.at[m])
            cp.start()
            copies.append(cp)
        for cp in copies[:4]:
            cp.wait()
        nt_s[...] = nt_s[...].T

        def attention(kaug, raug, strip, acc, kt, dk_s, dv_s, db):
            build_masks(scal_ref, kaug, raug, nbytes // 2)
            db[...] = jnp.zeros_like(db)
            def pair(p, carry):
                def hook(b):
                    if b % 3 == 0:
                        point_at(p, ["a%d%d" % (j, b // 3) for j in range(pairs)])
                bwd_pair(p, q, k, v, g, lse_ref, base_ref, db, kaug, raug, strip, acc, kt, dk_s, dv_s, hook)
                for j in range(pairs // 2):
                    @pl.when(p == 2 * j + 1)
                    def _():
                        dst = term["p%d" % j]
                        for m, src in enumerate((q, k, v)):
                            r = nn(nt_s[...], src[:, 256 * j:256 * (j + 1)]).astype(bf16)
                            dst[:, :, :, :, 256 * m:256 * (m + 1)] = r.reshape(dst.shape[:4] + (256,))
                        ready("p%d" % j)
                return carry
            lax.fori_loop(0, pairs, pair, 0)
            relt = lax.dot_general(db[...], hot_ref[...], (((1,), (0,)), ((), ())), precision=lax.Precision.HIGHEST, preferred_element_type=f32)
            row = lax.broadcasted_iota(jnp.int32, SMALL, 0)
            total = jnp.where(row == SMALL[0] - 1, tot_ref[0:1, :], relt)
            if remote:
                small.acc[...] = total
            else:
                small_o[...] = total
        strips = pltpu.VMEM((STRIP, 256), f32)
        pl.run_scoped(attention, pltpu.VMEM((TP, 128), bf16), pltpu.VMEM((NB, 256, 128), bf16), strips, strips, pltpu.VMEM((128, TP), bf16),
                      pltpu.VMEM((TP, 128), f32), pltpu.VMEM((TP, 128), f32), pltpu.VMEM((16, 512), f32))
        for cp in copies[4:]:
            cp.wait()

        def pooling(slabs, de):
            count = []

            def hook():
                point("h%d" % len(count))
                count.append(0)
            hook()
            ggain[...] = jnp.zeros_like(ggain)
            gain = vec_ref[1:2, :]

            def rows(b, carry):
                sl = row_block(b)
                gy = nt(q[sl, :], wq[...]) + nt(k[sl, :], wk[...]) + nt(v[sl, :], wv[...])
                x = stream[sl, :]
                s = norm_scale(x)
                t = gy * gain
                gs = mid[sl, :] + s * t - x * (s * s * s * jnp.mean(x * t, axis=1, keepdims=True))
                for c in range(d // 128):
                    slabs[c, sl, :] = gs[:, c * 128:(c + 1) * 128]
                ggain[...] += jnp.sum((gy * x * s).reshape(FRB // 8, 8, d), axis=0)
                return carry
            lax.fori_loop(0, TP // FRB, rows, 0)
            ggain[0:2, :] = jnp.concatenate([jnp.sum(ggain[...], axis=0, keepdims=True), jnp.sum(ggain2[...], axis=0, keepdims=True)], axis=0)
            hook()

            def put(gt):
                dst = term["t"]
                half = dst.shape[3]
                for zz in range(dst.shape[0]):
                    for yy in range(2):
                        for xx in range(2):
                            top = ((zz * 2 + yy) * 2 + xx) * half
                            dst[zz, yy, xx, :, 0:VR] = gt[top:top + half]
                            dst[zz, yy, xx, :, VR:VG] = jnp.zeros((half, VG - VR), bf16)
            gbst_bwd_body(nbytes, vocab, scal_ref, ids_ref, emb, wcol_ref, vec_ref, ggain, put, de, slabs, hook)
            if remote:
                ready("t")
        pl.run_scoped(pooling, pltpu.VMEM((d // 128, TP, 128), f32), pltpu.VMEM((12 * ROWS, d), bf16))
    act = pltpu.VMEM((TP, d), bf16)
    mat = pltpu.VMEM((d, d), bf16)
    pl.run_scoped(scoped, act, act, act, act, pltpu.VMEM((12 * ROWS, d), bf16), mat, mat, mat)
    if remote:
        point("end")
        small_o[...] = small.acc[...]
        red.finish()


TABLE = {
    "c13": ("f0.core",),
    "o": ("f1.core",),
    "a00": ("d.core", "o.core", "f0.one",),
    "a30": ("p0.core", "d.one", "f1.one",),
    "a31": ("o.one",),
    "a50": ("p1.core", "f0.two", "f1.two", "o.two",),
    "p2": ("p0.one",),
    "h0": ("p1.one",),
    "h1": ("p2.core", "s.0", "f0.z", "d.two", "p0.two",),
    "h2": ("s.1",),
    "h3": ("p1.two",),
    "h6": ("f1.z",),
    "h7": ("p2.one",),
    "h8": ("o.z",),
    "t": ("s.2",),
    "end": ("p2.two", "f0.end", "t.core", "s.3", "f1.end", "d.z", "o.end", "p0.z",
            "t.one", "p1.z", "t.two", "d.end", "s.4", "p2.z", "p0.end", "p1.end",
            "s.5", "t.z", "p2.end", "t.end",),
}


def backward_one(scal, ids, base2, hot, vec, wcol, tot, lse, acts, weights, vocab, nbytes, remote):
    d = acts[0].shape[1]
    hbm = pl.BlockSpec(memory_space=pltpu.HBM)
    vm = pl.BlockSpec(memory_space=pltpu.VMEM)
    sd = jax.ShapeDtypeStruct
    view = lambda r, c: (4, 2, 2, r // 16, c)
    big = [w.reshape(view(*w.shape)) for w in weights[3:]]
    ff = weights[4].shape[1]
    shapes = [view(d, VG)] + [view(d, d)] * 4 + [view(d, ff)] * 2 + [view(ff, d)]
    scratch = [pltpu.VMEM((TP, d), f32), pltpu.VMEM((TP, d), f32), pltpu.VMEM((TP, d), bf16), pltpu.VMEM((8, d), f32), pltpu.VMEM((8, d), f32),
               pltpu.SemaphoreType.DMA((9,)), pltpu.SemaphoreType.DMA((8,))]
    params = dict(vmem_limit_bytes=62 << 20)
    if remote:
        outs = [sd((2, 2, s[3], s[4] // 2), bf16) for s in shapes]
        scratch += [pltpu.VMEM(s, bf16) for s in shapes] + Reduce.scratch(shapes)
        scratch += [pltpu.VMEM(SMALL, f32), pltpu.VMEM((10,) + SMALL, f32), pltpu.SemaphoreType.DMA((5,)), pltpu.SemaphoreType.DMA((5,))]
        params.update(collective_id=2, has_side_effects=True)
    else:
        outs = [sd(s, bf16) for s in shapes]
    return pl.pallas_call(
        functools.partial(backward_kernel, nbytes, vocab, remote),
        out_shape=(sd((TP, d), bf16), *outs, sd(SMALL, f32)),
        in_specs=[pl.BlockSpec(memory_space=pltpu.SMEM)] + [vm] * 7 + [hbm] * 15,
        out_specs=(hbm,) + (vm,) * (len(outs) + 1),
        scratch_shapes=scratch,
        compiler_params=pltpu.CompilerParams(**params),
        name="backward_one",
    )(scal, ids, base2, hot, vec, wcol, tot, lse, *acts, *weights[:3], *big)


def finish_kernel(vocab, heads, buckets, *refs):
    ins, small_ref = dict(zip(NAMES, refs[:len(NAMES)])), refs[len(NAMES)]
    table_o, score_o, gain1_o, q_o, k_o, v_o, o_o, rel_o, gain2_o, gate_o, up_o, down_o, share_o = refs[len(NAMES) + 1:]

    def place(dst, src, left):
        half, width = src.shape[2], src.shape[3]
        for c in range(2):
            for x in range(2):
                dst[x * half:(x + 1) * half, left + c * width:left + (c + 1) * width] = src[c, x].astype(f32)
    place(o_o, ins["o"], 0)
    place(down_o, ins["d"], 0)
    for h in range(2):
        src = ins["f%d" % h]
        half, width = src.shape[2], src.shape[3]
        for c, dst in enumerate((up_o, gate_o)):
            for x in range(2):
                dst[x * half:(x + 1) * half, h * width:(h + 1) * width] = src[c, x].astype(f32)
    for j in range(3):
        src = ins["p%d" % j]
        half = src.shape[2]
        for piece in range(6):
            c, m = piece // 3, piece % 3
            dst = (q_o, k_o, v_o)[piece // 2]
            left = 256 * j + 128 * (piece % 2)
            for x in range(2):
                dst[x * half:(x + 1) * half, left:left + 128] = src[c, x, :, 128 * m:128 * (m + 1)].astype(f32)
    t = ins["t"]
    rows = jnp.concatenate([jnp.concatenate([t[c, x] for x in range(2)], axis=0) for c in range(2)], axis=1).astype(f32)
    turned = rows.T
    table_o[...] = turned[:vocab]
    score_o[...] = turned[vocab:vocab + 1]
    gain1_o[...] = turned[vocab + 1:vocab + 2]
    gain2_o[...] = turned[vocab + 2:vocab + 3]
    small = small_ref[...]
    rel_o[...] = small.T[:buckets, :heads]
    last = small[SMALL[0] - 1:SMALL[0], :]
    share_o[...] = last[:, 0:4] / last[:, 4:5]


def finish(outs, vocab, heads, buckets):
    vm = pl.BlockSpec(memory_space=pltpu.VMEM)
    sd = lambda *s: jax.ShapeDtypeStruct(s, f32)
    r = 2 * outs[1].shape[2]
    d = 2 * outs[1].shape[3]
    ff = 2 * outs[5].shape[3]
    return pl.pallas_call(
        functools.partial(finish_kernel, vocab, heads, buckets),
        out_shape=(sd(vocab, r), sd(1, r), sd(1, r), sd(r, d), sd(r, d), sd(r, d), sd(r, d), sd(buckets, heads), sd(1, r), sd(r, ff), sd(r, ff),
                   sd(2 * outs[7].shape[2], d), sd(1, 4)),
        in_specs=[vm] * len(outs),
        out_specs=(vm,) * 13,
        compiler_params=pltpu.CompilerParams(vmem_limit_bytes=32 << 20),
        name="finish",
    )(*outs)


def layer(byte_ids, lengths, bucket, out_grad, rel_bias, vocab, shards, wide, split):
    ids = byte_ids[0]
    nbytes = ids.shape[0]
    ntok = nbytes // 2
    scal = jnp.stack([bucket[0], lengths[0, 0], lengths[0, 1]])
    idp = jnp.pad(ids.reshape(nbytes // 12, 12).T, ((0, 4), (0, ROWS - nbytes // 12)), constant_values=-1)
    nb = rel_bias.shape[0]
    base2 = jnp.dot(base_hot(nb), rel_bias.astype(f32), precision=lax.Precision.HIGHEST).T
    done = forward_one(scal, idp, base2, shards, vocab, nbytes, wide, split)
    wq, wk, wv, wo, wg, wu, wd = shards[1:] if split is None else done[:7]
    stream, normed, emb, wcol, tot, vec, q, k, v, mixed, lse = done[7:]
    og = jnp.pad(out_grad[0], ((0, TP - ntok), (0, 0)))
    hot = jnp.pad(base_hot(nb, True), ((0, 0), (0, SMALL[1] - nb)))
    encoded, *outs = backward_one(scal, idp, base2, hot, vec, wcol, tot, lse, (q, k, v, normed, stream, mixed, og, emb), (wq, wk, wv, wo, wg, wu, wd), vocab, nbytes, split is not None)
    encoded = encoded[:ntok][None]
    if split is None:
        outs = [o.reshape(-1, o.shape[-1]) for o in outs]
    return encoded, outs


def body(byte_ids, lengths, bucket, out_grad, embedding, score_weight, gain_attn, w_query, w_key, w_value, w_attn_out, rel_bias, gain_ff, w_gate, w_up, w_ff_out):
    vocab, width = embedding.shape
    wide = lax.axis_size("wide")
    columns = jnp.concatenate([embedding.T, score_weight[:, None], gain_attn[:, None], gain_ff[:, None]], axis=1)
    tt = jnp.pad(columns, ((0, 0), (0, VP - columns.shape[1])))
    shards = (tt, w_query, w_key, w_value, w_attn_out, w_gate, w_up, w_ff_out)
    kernels = wide == 8 and lax.axis_size("narrow") == 4 and all(s.shape[0] % 32 == 0 for s in shards)
    split = (True, True, True, True, False, False, True, True) if kernels else None
    if not kernels:
        shards = tuple(lax.all_gather(s, "wide", axis=0, tiled=True) for s in shards)
    encoded, outs = layer(byte_ids, lengths, bucket, out_grad, rel_bias, vocab, shards, wide, split)
    if kernels:
        done = finish(outs, vocab, rel_bias.shape[1], rel_bias.shape[0])
        flat = lambda a: a.reshape(-1)
        return (encoded, done[0], flat(done[1]), flat(done[2]), *done[3:8], flat(done[8]), *done[9:12], flat(done[12]))
    t, p0, p1, p2, o, f0, f1, down, small = outs
    part = lambda m: jnp.concatenate([p[:, 256 * m:256 * (m + 1)] for p in (p0, p1, p2)], axis=1)
    half = lambda m: jnp.concatenate([f[:, m * f.shape[1] // 2:(m + 1) * f.shape[1] // 2] for f in (f0, f1)], axis=1)
    grads = (t, part(0), part(1), part(2), o, half(1), half(0), down)
    sums = [lax.psum(lax.psum_scatter(g, "wide", scatter_dimension=0, tiled=True), "narrow").astype(f32) for g in grads]
    small = lax.psum(small, ("wide", "narrow"))
    g_rel, tot = small[:rel_bias.shape[1], :rel_bias.shape[0]].T, small[-1, :5]
    t = sums[0]
    return (encoded, t[:, :vocab].T, t[:, vocab], t[:, vocab + 1], *sums[1:5], g_rel, t[:, vocab + 2], *sums[5:], tot[:4] / tot[4])


def solution(mesh):
    both = ("wide", "narrow")
    rows = P("wide", None)
    vec = P("wide")
    placed = (P(both, None), P(both, None), P(both), P(both, None, None), P(None, "wide"), vec, vec, rows, rows, rows, rows, P(), vec, rows, rows, rows)
    outs = (P(both, None, None), P(None, "wide"), vec, vec, rows, rows, rows, rows, P(), vec, rows, rows, rows, P())
    return jax.shard_map(body, mesh=mesh, in_specs=placed, out_specs=outs, check_vma=False)
```

```python
import functools

import jax
import jax.numpy as jnp
from jax import lax
from jax.experimental import pallas as pl
from jax.experimental.pallas import tpu as pltpu
from jax.sharding import PartitionSpec as P

f32 = jnp.float32
bf16 = jnp.bfloat16
TP = 768
BLK = 128
NB = TP // BLK
LEFT = TP - BLK
STRIP = 2 * TP - BLK
W0 = LEFT - 128
WN = 384

def nt(a, b):
    return lax.dot_general(a, b, (((1,), (1,)), ((), ())), preferred_element_type=f32)

def nn(a, b):
    return lax.dot_general(a, b, (((1,), (0,)), ((), ())), preferred_element_type=f32)

def build_masks(scal_ref, kaug, raug, ntok):
    joined = scal_ref[0] == 1
    l0 = scal_ref[1]; l1 = scal_ref[2]
    half = ntok // 2
    u = lax.broadcasted_iota(jnp.int32, (TP, 128), 0)
    lane = lax.broadcasted_iota(jnp.int32, (TP, 128), 1)
    seg = (u >= half).astype(jnp.int32)
    lim = jnp.where(seg == 1, l1, l0)
    start = seg * half
    lim = jnp.where(joined, l0 + l1, lim)
    start = jnp.where(joined, 0, start)
    valid = (2 * (u - start) < lim) & (u < ntok)
    segs = jnp.where(joined, 0, seg)
    ok = valid & (segs == lane)
    kaug[...] = jnp.where((lane < 2) & jnp.logical_not(ok), -1e30, 0.0).astype(bf16)
    t = u
    rows = jnp.where((lane == segs), 1.0, 0.0).astype(bf16)
    for b in range(NB):
        blk = rows[b * 128:(b + 1) * 128]
        raug[b] = jnp.concatenate([blk, blk], axis=0)

def bias_rows(rel_ref, base):
    c = lax.broadcasted_iota(jnp.int32, (rel_ref.shape[0], 512), 1)
    b = lax.broadcasted_iota(jnp.int32, (rel_ref.shape[0], 512), 0)
    hot = jnp.where(bucket_of(jnp.where(c < 384, c - 128, c - 640)) == b, 1.0, 0.0).astype(bf16)
    base[0:rel_ref.shape[1], :] = lax.dot_general(rel_ref[...], hot, (((0,), (0,)), ((), ())), preferred_element_type=f32)


def bucket_hot():
    m = lax.broadcasted_iota(jnp.int32, (512, 128), 0)
    b = lax.broadcasted_iota(jnp.int32, (512, 128), 1)
    return jnp.where(bucket_of(m - 255) == b, 1.0, 0.0).astype(f32)


class Flags:
    def __init__(self, bucket_ref, lengths_ref):
        self.refs = (bucket_ref, lengths_ref)

    def __getitem__(self, i):
        return self.refs[0][0] if i == 0 else self.refs[1][0, i - 1]


def build_strip(base_ref, row0, strip):
    for hh in range(2):
        row = base_ref[pl.ds(row0 + hh, 1), :]
        cl = row[:, 0:1]; cr = row[:, 383:384]
        sq = jnp.broadcast_to(row, (128, 512))
        sq = pltpu.roll(sq, 0, 1, stride=1, stride_axis=0)
        win = sq[:, :WN].T
        lanes = slice(hh * 128, hh * 128 + 128)
        strip[0:W0, lanes] = jnp.broadcast_to(cl, (W0, 128))
        strip[W0:W0 + WN, lanes] = win
        strip[W0 + WN:STRIP, lanes] = jnp.broadcast_to(cr, (STRIP - W0 - WN, 128))

def stacked(blk):
    lane = lax.broadcasted_iota(jnp.int32, blk.shape, 1)
    z = jnp.zeros_like(blk)
    return jnp.concatenate([jnp.where(lane < 64, blk, z), jnp.where(lane >= 64, blk, z)], axis=0)

def fwd_pair(p, q_ref, k_ref, v_ref, base_ref, o_ref, lse_ref, kaug, raug, strip, vt, hook):
    lanes = pl.ds(pl.multiple_of(p * 128, 128), 128)
    build_strip(base_ref, 2 * p, strip)
    vt[...] = v_ref[:, lanes].T
    kcat = jnp.concatenate([k_ref[:, lanes], kaug[...]], axis=1)
    vtv = vt[...]
    rowsel = lax.broadcasted_iota(jnp.int32, (128, 128), 0) < 64
    for b in range(NB):
        hook(b)
        rhs = jnp.concatenate([stacked(q_ref[b * 128:(b + 1) * 128, lanes]), raug[b]], axis=1)
        s = nt(kcat, rhs) + strip[LEFT - b * 128:LEFT - b * 128 + TP, :]
        mx = jnp.max(s, axis=0, keepdims=True)
        e = jnp.exp(s - mx)
        l = jnp.sum(e, axis=0, keepdims=True)
        ot = nn(vtv, e.astype(bf16)) * (1.0 / l)
        lse_ref[p, b:b + 1, :] = mx + jnp.log(l)
        o = jnp.where(rowsel, ot[:, :128], ot[:, 128:])
        o_ref[b * 128:(b + 1) * 128, lanes] = o.T.astype(bf16)


def bwd_pair(p, q_ref, k_ref, v_ref, g_ref, lse_ref, base_ref, db_ref, kaug, raug, strip, acc, kt, dk_s, dv_s, hook=None):
    lanes = pl.ds(pl.multiple_of(p * 128, 128), 128)
    build_strip(base_ref, 2 * p, strip)
    kt[...] = k_ref[:, lanes].T
    kcat = jnp.concatenate([k_ref[:, lanes], kaug[...]], axis=1)
    v = v_ref[:, lanes]
    ktv = kt[...]
    acc[...] = jnp.zeros_like(acc)
    dk_s[...] = jnp.zeros_like(dk_s)
    dv_s[...] = jnp.zeros_like(dv_s)
    rowsel = lax.broadcasted_iota(jnp.int32, (128, 128), 0) < 64
    for b in range(NB):
        if hook is not None:
            hook(b)
        rows = slice(b * 128, (b + 1) * 128)
        qs = stacked(q_ref[rows, lanes])
        gs = stacked(g_ref[rows, lanes])
        rhs = jnp.concatenate([qs, raug[b]], axis=1)
        w = slice(LEFT - b * 128, LEFT - b * 128 + TP)
        s = nt(kcat, rhs) + strip[w, :]
        pr = jnp.exp(s - lse_ref[p, b:b + 1, :])
        dp = nt(v, gs)
        pdp = pr * dp
        delta = jnp.sum(pdp, axis=0, keepdims=True)
        ds = pdp - pr * delta
        acc[w, :] += ds
        dsb = ds.astype(bf16)
        dk_s[...] += nn(dsb, qs)
        dv_s[...] += nn(pr.astype(bf16), gs)
        dqt = nn(ktv, dsb)
        dq = jnp.where(rowsel, dqt[:, :128], dqt[:, 128:])
        q_ref[rows, lanes] = dq.T.astype(bf16)
    k_ref[:, lanes] = dk_s[...].astype(bf16)
    v_ref[:, lanes] = dv_s[...].astype(bf16)
    fi = lax.broadcasted_iota(jnp.int32, (128, 128), 0)
    fj = lax.broadcasted_iota(jnp.int32, (128, 128), 1)
    flip = jnp.where(fi + fj == 127, 1.0, 0.0).astype(f32)
    for hh in range(2):
        half = slice(hh * 128, hh * 128 + 128)
        far_l = jnp.sum(acc[0:W0, half], keepdims=True)
        far_r = jnp.sum(acc[W0 + WN:STRIP, half], keepdims=True)
        win = acc[W0:W0 + WN, half]
        wt = lax.dot_general(flip, win, (((1,), (1,)), ((), ())), precision=lax.Precision.HIGHEST, preferred_element_type=f32)
        wt = jnp.concatenate([wt, jnp.zeros((128, 128), f32)], axis=1)
        wt = pltpu.roll(wt, 0, 1, stride=1, stride_axis=0)
        diag = jnp.sum(wt, axis=0, keepdims=True)
        lane = lax.broadcasted_iota(jnp.int32, (1, 512), 1)
        diag = diag + jnp.where(lane == 0, far_l, 0.0) + jnp.where(lane == 510, far_r, 0.0)
        db_ref[pl.ds(2 * p + hh, 1), :] = diag


def bucket_of(relative):
    distance = jnp.abs(relative)
    far = 8 + sum(((distance >= e).astype(jnp.int32) for e in (12, 16, 23, 32, 46, 64, 91)))
    near = jnp.where(distance < 8, distance, far)
    return near + 16 * (relative > 0).astype(jnp.int32)


ROWS = 128
VP = 384
VG = 512
VR = 272
EPS = 1e-6

def byte_valid_mat(scal_ref, nbytes):
    i = lax.broadcasted_iota(jnp.int32, (ROWS, 128), 0)
    j = lax.broadcasted_iota(jnp.int32, (ROWS, 128), 1)
    p = 12 * i + j
    slot = nbytes // 2
    joined = scal_ref[0] == 1
    l0 = scal_ref[1]; l1 = scal_ref[2]
    second = p >= slot
    start = jnp.where(joined, 0, jnp.where(second, slot, 0))
    lim = jnp.where(joined, l0 + l1, jnp.where(second, l1, l0))
    ok = (p - start < lim) & (p < nbytes) & (j < 12)
    return jnp.where(ok, 1.0, 0.0).astype(f32)

def inverse_counts(vm):
    v = [vm[:, j:j + 1] for j in range(12)]
    inv = {1: v}
    for b in (2, 3, 4):
        out = []
        for m in range(12 // b):
            tot = v[b * m]
            for t in range(1, b):
                tot = tot + v[b * m + t]
            out.append(1.0 / jnp.maximum(tot, 1.0))
        inv[b] = out
    return v, inv

def softmax_weights(e, inv):
    rate = {1: e}
    for b in (2, 3, 4):
        out = []
        for m in range(12 // b):
            tot = e[b * m]
            for t in range(1, b):
                tot = tot + e[b * m + t]
            out.append(tot * inv[b][m])
        rate[b] = out
    w = {b: [] for b in (1, 2, 3, 4)}
    for p in range(12):
        r = [rate[b][p // b] for b in (1, 2, 3, 4)]
        mx = jnp.maximum(jnp.maximum(r[0], r[1]), jnp.maximum(r[2], r[3]))
        ex = [jnp.exp(x - mx) for x in r]
        inv_t = 1.0 / (ex[0] + ex[1] + ex[2] + ex[3])
        for b in (1, 2, 3, 4):
            w[b].append(ex[b - 1] * inv_t)
    return w

def gbst_fwd_body(nbytes, vocab, scal_ref, ids_ref, tt_ref, stream_ref, normed_ref, emb_ref, wcol_ref, tot_ref, vec_ref, slabs, table_ref, hook):
    table_ref[...] = tt_ref[...].T
    base = vocab // 16 * 16
    tail = table_ref[base:base + 16, :].astype(f32)
    vec_ref[0:3, :] = tail[vocab - base:vocab - base + 3, :]
    vec_ref[3:8, :] = jnp.zeros((5, tail.shape[1]), f32)
    vm = byte_valid_mat(scal_ref, nbytes)
    v, inv = inverse_counts(vm)
    idt = ids_ref[...].astype(f32).T
    lane = lax.broadcasted_iota(jnp.int32, (ROWS, VP), 1).astype(f32)
    s = vec_ref[0:1, :]
    e = []
    for j in range(12):
        hot = jnp.where((lane == idt[:, j:j + 1]) & (v[j] > 0.5), 1.0, 0.0).astype(bf16)
        ej = nn(hot, table_ref[...])
        emb_ref[j * ROWS:(j + 1) * ROWS, :] = ej.astype(bf16)
        e.append(jnp.sum(ej * s, axis=1, keepdims=True))
        if j % 3 == 2:
            hook()
    w = softmax_weights(e, inv)
    l128 = lax.broadcasted_iota(jnp.int32, (ROWS, 128), 1)
    wc = jnp.zeros((ROWS, 128), f32)
    for b in (1, 2, 3, 4):
        for p in range(12):
            wc = jnp.where(l128 == (b - 1) * 12 + p, w[b][p], wc)
    wcol_ref[...] = wc
    tl = lax.broadcasted_iota(jnp.int32, (8, 128), 1)
    tot = jnp.zeros((8, 128), f32)
    for b in (1, 2, 3, 4):
        acc = w[b][0] * v[0]
        for p in range(1, 12):
            acc = acc + w[b][p] * v[p]
        tot = jnp.where(tl == b - 1, jnp.sum(acc, keepdims=True), tot)
    tot = jnp.where(tl == 4, jnp.sum(vm, keepdims=True), tot)
    tot_ref[...] = tot
    hook()
    E = lambda j: emb_ref[j * ROWS:(j + 1) * ROWS, :].astype(f32)
    s3 = lambda m: E(3 * m) + E(3 * m + 1) + E(3 * m + 2)
    for k in range(6):
        p0, p1 = 2 * k, 2 * k + 1
        b2 = 0.5 * (w[2][p0] + w[2][p1]) * inv[2][k]
        acc = (0.5 * w[1][p0] + b2) * E(p0) + (0.5 * w[1][p1] + b2) * E(p1)
        n = k // 2
        d = 0.5 * (w[4][p0] + w[4][p1]) * inv[4][n]
        acc = acc + d * ((E(4 * n) + E(4 * n + 1)) + (E(4 * n + 2) + E(4 * n + 3)))
        m0, m1 = p0 // 3, p1 // 3
        if m0 == m1:
            acc = acc + (0.5 * (w[3][p0] + w[3][p1]) * inv[3][m0]) * s3(m0)
        else:
            acc = acc + (0.5 * w[3][p0] * inv[3][m0]) * s3(m0) + (0.5 * w[3][p1] * inv[3][m1]) * s3(m1)
        put_strided(slabs, k, acc)
        if k % 2 == 1:
            hook()
    ntok = nbytes // 2
    for c in range(slabs.shape[0]):
        stream_ref[0:ntok, c * 128:(c + 1) * 128] = slabs[c, 0:ntok, :]
    stream_ref[ntok:TP, :] = jnp.zeros((TP - ntok, acc.shape[1]), f32)
    norm_rows(stream_ref, vec_ref[1:2, :], normed_ref)
    hook()


def put_strided(ref, k, val):
    for c in range(val.shape[1] // 128):
        ref[c, pl.ds(k, 124, stride=6), :] = val[:124, c * 128:(c + 1) * 128]

def get_strided(ref, k):
    parts = [ref[c, pl.ds(k, 124, stride=6), :] for c in range(ref.shape[0])]
    x = jnp.concatenate(parts, axis=1)
    return jnp.concatenate([x, jnp.zeros((4, x.shape[1]), f32)], axis=0)

def norm_rows(x_ref, gain_ref, out_ref):
    g = gain_ref
    for b in range(TP // 128):
        x = x_ref[b * 128:(b + 1) * 128, :]
        sc = lax.rsqrt(jnp.mean(x * x, axis=1, keepdims=True) + EPS)
        out_ref[b * 128:(b + 1) * 128, :] = (x * sc * g).astype(bf16)

def gbst_bwd_body(nbytes, vocab, scal_ref, ids_ref, emb_ref, wcol_ref, score_ref, ggain_ref, put, de_ref, slabs, hook):
    vm = byte_valid_mat(scal_ref, nbytes)
    v, inv = inverse_counts(vm)
    wc = wcol_ref[...]
    w = {b: [wc[:, (b - 1) * 12 + p:(b - 1) * 12 + p + 1] for p in range(12)] for b in (1, 2, 3, 4)}
    s = score_ref[0:1, :]
    E = lambda j: emb_ref[j * ROWS:(j + 1) * ROWS, :].astype(f32)
    s3 = lambda m: E(3 * m) + E(3 * m + 1) + E(3 * m + 2)
    s4 = lambda n: (E(4 * n) + E(4 * n + 1)) + (E(4 * n + 2) + E(4 * n + 3))
    dot = lambda a, b: jnp.sum(a * b, axis=1, keepdims=True)
    dw = {b: [None] * 12 for b in (1, 2, 3, 4)}
    D = []
    for k in range(6):
        dk = 0.5 * get_strided(slabs, k)
        D.append(dk)
        p0, p1 = 2 * k, 2 * k + 1
        x0, x1 = dot(dk, E(p0)), dot(dk, E(p1))
        dw[1][p0], dw[1][p1] = x0, x1
        dw[2][p0] = dw[2][p1] = (x0 + x1) * inv[2][k]
        m0, m1 = p0 // 3, p1 // 3
        a0 = dot(dk, s3(m0)) * inv[3][m0]
        dw[3][p0] = a0
        dw[3][p1] = a0 if m0 == m1 else dot(dk, s3(m1)) * inv[3][m1]
        dw[4][p0] = dw[4][p1] = dot(dk, s4(k // 2)) * inv[4][k // 2]
        if k % 2 == 1:
            hook()
    hook()
    dr = {b: [] for b in (1, 2, 3, 4)}
    for p in range(12):
        mean = w[1][p] * dw[1][p] + w[2][p] * dw[2][p] + w[3][p] * dw[3][p] + w[4][p] * dw[4][p]
        for b in (1, 2, 3, 4):
            dr[b].append(w[b][p] * (dw[b][p] - mean))
    rb = {1: dr[1]}
    for b in (2, 3, 4):
        out = []
        for m in range(12 // b):
            tot = dr[b][b * m]
            for t in range(1, b):
                tot = tot + dr[b][b * m + t]
            out.append(tot * inv[b][m])
        rb[b] = out
    t3 = []
    for m in range(4):
        terms = {}
        for p in (3 * m, 3 * m + 1, 3 * m + 2):
            terms[p // 2] = terms[p // 2] + w[3][p] if p // 2 in terms else w[3][p]
        acc = None
        for k, coef in terms.items():
            t = (coef * inv[3][m]) * D[k]
            acc = t if acc is None else acc + t
        t3.append(acc)
    gscore = jnp.zeros((8, s.shape[1]), f32)
    for n in range(3):
        t4 = ((w[4][4 * n] + w[4][4 * n + 1]) * inv[4][n]) * D[2 * n] + ((w[4][4 * n + 2] + w[4][4 * n + 3]) * inv[4][n]) * D[2 * n + 1]
        for p in range(4 * n, 4 * n + 4):
            k = p // 2
            c = rb[1][p] + rb[2][k] + rb[3][p // 3] + rb[4][n]
            b2 = (w[2][2 * k] + w[2][2 * k + 1]) * inv[2][k]
            de = v[p] * ((w[1][p] + b2) * D[k] + t3[p // 3] + t4 + c * s)
            de_ref[p * ROWS:(p + 1) * ROWS, :] = de.astype(bf16)
            y = c * E(p)
            gscore = gscore + jnp.sum(y.reshape(ROWS // 8, 8, s.shape[1]), axis=0)
        hook()
    gscore = jnp.sum(gscore, axis=0, keepdims=True)
    row = lax.broadcasted_iota(jnp.int32, (VR, ROWS), 0)
    hots = [jnp.where(row == ids_ref[j:j + 1, :], 1.0, 0.0).astype(bf16) for j in range(12)]
    hot = jnp.concatenate(hots, axis=1)
    gtable = nn(hot, de_ref[...])
    row = lax.broadcasted_iota(jnp.int32, gtable.shape, 0)
    for i, extra in enumerate((gscore, ggain_ref[0:1, :], ggain_ref[1:2, :])):
        gtable = jnp.where(row == vocab + i, extra, gtable)
    put(gtable.T.astype(bf16))


MESH = pl.DeviceIdType.MESH


def coords():
    w = lax.axis_index("wide")
    n = lax.axis_index("narrow")
    return w, w // 2, w % 2, n // 2, n % 2


def peer_ids():
    w, z, y, x, c = coords()
    n = 2 * x + c
    return {
        "y": (2 * z + 1 - y, n),
        "zp": (2 * ((z + 1) % 4) + y, n),
        "zm": (2 * ((z + 3) % 4) + y, n),
        "zo": (2 * ((z + 2) % 4) + y, n),
        "x": (w, 2 * (1 - x) + c),
        "c": (w, 2 * x + 1 - c),
        "xc": (w, 2 * (1 - x) + 1 - c),
    }


def enter(peers, names):
    barrier = pltpu.get_barrier_semaphore()
    for name in names:
        pl.semaphore_signal(barrier, inc=1, device_id=peers[name], device_id_type=MESH)
    pl.semaphore_wait(barrier, len(names))


class Gather:
    SENDS = 30
    SLOTS = 28

    def __init__(self, own, fulls, split, ssem, rsem, lsem):
        self.own, self.fulls, self.split = own, fulls, split
        self.r = [f.shape[0] // 8 for f in fulls]
        self.ssem, self.rsem, self.lsem = ssem, rsem, lsem
        self.peers = peer_ids()
        self.w, self.z, self.y, self.x, self.c = coords()
        z = self.z
        first = jnp.where(z == 3, 3, 1)
        second = jnp.where((z == 0) | (z == 3), 2, 3)
        self.order = (first, second, 6 - first - second)
        self.inner = (z == 1) | (z == 2)
        self.sent = []

    def enter(self):
        n = 2 * self.x + self.c
        barrier = pltpu.get_barrier_semaphore()
        near = [(owner, n) for _, owner in self.others()] + [self.peers["x"], self.peers["c"]]
        for peer in near:
            pl.semaphore_signal(barrier, inc=1, device_id=peer, device_id_type=MESH)
        pl.semaphore_wait(barrier, len(near))

    def cols(self, i, c):
        width = self.fulls[i].shape[1] // 2
        return pl.ds(pl.multiple_of(c * width, 128), width)

    def block(self, i, owner, part, ref=None):
        r = self.r[i]
        start = owner * r
        if self.split[i]:
            r = r // 2
            start = start + part[1] * r
        return (self.fulls[i] if ref is None else ref).at[pl.ds(pl.multiple_of(start, 16), r), self.cols(i, part[0])]

    @property
    def mine(self):
        return (self.c, self.x)

    def copy(self, i, out, slot, src, owner, part, device):
        return pltpu.make_async_remote_copy(
            src_ref=src, dst_ref=self.block(i, owner, part), send_sem=self.ssem.at[i, out],
            recv_sem=self.rsem.at[i, slot], device_id=device, device_id_type=MESH)

    def send(self, i, out, slot, owner, part, device, when=None, src=None):
        src = self.block(i, owner, part) if src is None else src
        cp = self.copy(i, out, slot, src, owner, part, device)
        if when is None:
            cp.start()
        else:
            pl.when(when)(cp.start)
        self.sent.append((i, out, when))

    def arrived(self, i, slot, owner, part):
        ref = self.block(i, owner, part)
        pltpu.make_async_remote_copy(
            src_ref=ref, dst_ref=ref, send_sem=self.ssem.at[i, 0], recv_sem=self.rsem.at[i, slot],
            device_id=self.peers["c"], device_id_type=MESH).wait_recv()

    def local(self, i):
        at = pl.ds(pl.multiple_of(self.w * self.r[i], 16), self.r[i])
        return pltpu.make_async_copy(self.own[i], self.fulls[i].at[at, :], self.lsem.at[i])

    def start_direct(self, i):
        n = 2 * self.x + self.c
        for k in range(1, 8):
            dz, dy = k // 2, k % 2
            to = (2 * lax.rem(self.z + dz, 4) + (1 - self.y if dy else self.y), n)
            self.send_rows(i, k, (4 - dz) % 4 * 2 + dy, self.w, self.c, to, self.half_rows(i, 0, self.c, self.own[i]))
        self.local(i).start()

    def half_rows(self, i, owner, c, ref=None):
        r = self.r[i]
        return (self.fulls[i] if ref is None else ref).at[pl.ds(pl.multiple_of(owner * r + c * (r // 2), 16), r // 2), :]

    def send_rows(self, i, out, slot, owner, c, device, src=None):
        ref = self.half_rows(i, owner, c)
        cp = pltpu.make_async_remote_copy(
            src_ref=ref if src is None else src, dst_ref=ref, send_sem=self.ssem.at[i, out], recv_sem=self.rsem.at[i, slot],
            device_id=device, device_id_type=MESH)
        cp.start()
        self.sent.append((i, out, "rows"))

    def rows_arrived(self, i, slot, owner, c):
        ref = self.half_rows(i, owner, c)
        pltpu.make_async_remote_copy(
            src_ref=ref, dst_ref=ref, send_sem=self.ssem.at[i, 0], recv_sem=self.rsem.at[i, slot],
            device_id=self.peers["c"], device_id_type=MESH).wait_recv()

    def others(self):
        for k in range(1, 8):
            dz, dy = k // 2, k % 2
            yield k, 2 * lax.rem(self.z + dz, 4) + (1 - self.y if dy else self.y)

    def steps_direct(self, i):
        def relay():
            for k, owner in self.others():
                self.rows_arrived(i, k, owner, self.c)
                self.send_rows(i, 8 + k, 8 + k, owner, self.c, self.peers["c"])

        def end():
            for k, owner in self.others():
                self.rows_arrived(i, 8 + k, owner, 1 - self.c)
            self.local(i).wait()
        return [relay, end]

    def start(self, i):
        n = 2 * self.x + self.c
        own = self.block(i, 0, self.mine, self.own[i])
        self.send(i, 0, 2, self.w, self.mine, (2 * jnp.minimum(self.z + 1, 3) + self.y, n), self.z < 3, own)
        self.send(i, 1, 0, self.w, self.mine, (2 * jnp.maximum(self.z - 1, 0) + self.y, n), self.z > 0, own)
        self.send(i, 5, 3, self.w, self.mine, self.peers["y"], None, own)
        self.local(i).start()

    def relay(self, i, s, n, owner):
        self.send(i, 9 + n, 7 + s, owner, self.mine, self.peers["c"])
        if self.split[i]:
            self.send(i, 16 + n, 14 + s, owner, self.mine, self.peers["x"])

    def step_z(self, i, j):
        d = self.order[j]
        o = lax.rem(self.z + d, 4)
        owner = 2 * o + self.y
        self.arrived(i, d - 1, owner, self.mine)
        to = jnp.where(self.inner, jnp.where(o < self.z, self.z + 1, self.z - 1), jnp.where(self.z == 0, 1, 2))
        slot = jnp.where(self.inner, lax.rem(o - to + 4, 4) - 1, 0)
        self.send(i, 2 + j, slot, owner, self.mine, (2 * to + self.y, 2 * self.x + self.c), self.inner)
        self.send(i, 6 + j, 3 + d, owner, self.mine, self.peers["y"])
        self.relay(i, d - 1, j, owner)

    def step_y(self, i, j):
        d = 0 if j < 0 else self.order[j]
        owner = 2 * lax.rem(self.z + d, 4) + 1 - self.y
        self.arrived(i, 3 + d, owner, self.mine)
        self.relay(i, 3 + d, 4 + j, owner)

    def each(self):
        for j in range(3):
            d = self.order[j]
            yield d - 1, j, 2 * lax.rem(self.z + d, 4) + self.y
        for j in range(-1, 3):
            d = 0 if j < 0 else self.order[j]
            yield 3 + d, 4 + j, 2 * lax.rem(self.z + d, 4) + 1 - self.y

    def step_x(self, i):
        if self.split[i]:
            other = (self.c, 1 - self.x)
            for s, n, owner in self.each():
                self.arrived(i, 14 + s, owner, other)
                self.send(i, 23 + n, 21 + s, owner, other, self.peers["c"])

    def step_end(self, i):
        for s, n, owner in self.each():
            self.arrived(i, 7 + s, owner, (1 - self.c, self.x))
            if self.split[i]:
                self.arrived(i, 21 + s, owner, (1 - self.c, 1 - self.x))
        self.local(i).wait()

    def finish(self):
        for i, out, when in self.sent:
            if isinstance(when, str):
                ref = self.half_rows(i, self.w, self.c)
                when = None
            else:
                ref = self.block(i, self.w, self.mine)
            cp = pltpu.make_async_remote_copy(
                src_ref=ref, dst_ref=ref, send_sem=self.ssem.at[i, out], recv_sem=self.rsem.at[i, 0],
                device_id=self.peers["c"], device_id_type=MESH)
            if when is None:
                cp.wait_send()
            else:
                pl.when(when)(cp.wait_send)

    def steps(self, i):
        return [functools.partial(self.step_y, i, -1)] + [functools.partial(f, i, j) for j in range(3) for f in (self.step_z, self.step_y)] + [
            functools.partial(self.step_x, i), functools.partial(self.step_end, i)]


class Reduce:
    SLOTS = 9

    def __init__(self, terms, outs, order, rc, r1, r2, r3, ssem, rsem):
        self.terms, self.outs, self.order = terms, outs, order
        self.rc, self.r1, self.r2, self.r3 = rc, r1, r2, r3
        self.ssem, self.rsem = ssem, rsem
        self.peers = peer_ids()
        self.w, self.z, self.y, self.x, self.c = coords()
        self.sent = []

    def enter(self):
        enter(self.peers, ("y", "zp", "zm", "zo", "x", "c", "xc"))

    def transfer(self, i, slot, src, dst, to):
        return pltpu.make_async_remote_copy(
            src_ref=src, dst_ref=dst, send_sem=self.ssem.at[i, slot], recv_sem=self.rsem.at[i, slot],
            device_id=self.peers[to], device_id_type=MESH)

    def send(self, i, slot, src, dst, to):
        self.transfer(i, slot, src, dst, to).start()
        self.sent.append((i, slot))

    def arrived(self, i, slot, dst):
        self.transfer(i, slot, dst, dst, "c").wait_recv()

    def half(self, i, c):
        width = self.terms[i].shape[4] // 2
        return pl.ds(pl.multiple_of(c * width, 128), width)

    def start(self, i):
        self.send(i, 0, self.terms[i].at[:, :, :, :, self.half(i, 1 - self.c)], self.rc[i], "c")

    def add(self, a, b):
        return a + b

    def step_core(self, i):
        self.arrived(i, 0, self.rc[i])

        def one(z, carry):
            self.rc[i][z] = self.add(self.terms[i][z, :, :, :, self.half(i, self.c)], self.rc[i][z])
            return carry
        lax.fori_loop(0, 4, one, 0)
        if self.order[i] == "y":
            self.send(i, 1, self.rc[i].at[:, 1 - self.y], self.r1[i], "y")
        else:
            self.send(i, 1, self.rc[i].at[:, :, 1 - self.x], self.r1[i], "x")

    def step_one(self, i):
        self.arrived(i, 1, self.r1[i])

        def one(z, carry):
            if self.order[i] == "y":
                mine = self.rc[i][z, self.y]
            else:
                mine = self.rc[i][z, :, self.x]
            self.r1[i][z] = self.add(mine, self.r1[i][z])
            return carry
        lax.fori_loop(0, 4, one, 0)
        if self.order[i] == "y":
            self.send(i, 2, self.r1[i].at[:, 1 - self.x], self.r2[i], "x")
        else:
            self.send(i, 2, self.r1[i].at[:, 1 - self.y], self.r2[i], "y")

    def step_two(self, i):
        self.arrived(i, 2, self.r2[i])
        pick = self.x if self.order[i] == "y" else self.y

        def one(z, carry):
            self.r2[i][z] = self.add(self.r1[i][z, pick], self.r2[i][z])
            return carry
        lax.fori_loop(0, 4, one, 0)
        for dz, to in ((1, "zp"), (3, "zm"), (2, "zo")):
            self.send(i, 2 + dz, self.r2[i].at[lax.rem(self.z + dz, 4)], self.r3[i].at[3 - dz], to)

    def step_z(self, i):
        total = self.r2[i][self.z].astype(f32)
        for dz in (1, 3, 2):
            self.arrived(i, 2 + dz, self.r3[i].at[3 - dz])
        for k in range(3):
            total = total + self.r3[i][k].astype(f32)
        out = self.outs[i]
        out[self.c, self.x] = total.astype(bf16)
        for slot, to in ((6, "x"), (7, "c"), (8, "xc")):
            self.send(i, slot, out.at[self.c, self.x], out.at[self.c, self.x], to)

    def step_end(self, i):
        out = self.outs[i]
        self.arrived(i, 6, out.at[self.c, 1 - self.x])
        self.arrived(i, 7, out.at[1 - self.c, self.x])
        self.arrived(i, 8, out.at[1 - self.c, 1 - self.x])

    def steps(self, i):
        return [functools.partial(f, i) for f in (self.step_core, self.step_one, self.step_two, self.step_z, self.step_end)]

    def finish(self):
        for i, slot in self.sent:
            block = self.r2[i].at[0]
            ref = {0: self.rc[i], 1: self.r1[i], 2: self.r2[i]}.get(slot, block)
            self.transfer(i, slot, ref, ref, "c").wait_send()

    @staticmethod
    def scratch(shapes):
        rc = [pltpu.VMEM((4, 2, 2, s[3], s[4] // 2), bf16) for s in shapes]
        r1 = [pltpu.VMEM((4, 2, s[3], s[4] // 2), bf16) for s in shapes]
        r2 = [pltpu.VMEM((4, s[3], s[4] // 2), bf16) for s in shapes]
        r3 = [pltpu.VMEM((3, s[3], s[4] // 2), bf16) for s in shapes]
        n = len(shapes)
        return rc + r1 + r2 + r3 + [pltpu.SemaphoreType.DMA((n, 9)), pltpu.SemaphoreType.DMA((n, 9))]


SMALL = (16, 128)


class SmallSum:
    HOPS = ("c", "x", "y", "zn", "zo")

    def __init__(self, acc, slots, ssem, rsem):
        self.acc, self.slots, self.ssem, self.rsem = acc, slots, ssem, rsem
        self.peers = peer_ids()
        w, z, y, x, c = coords()
        self.peers["zn"] = (2 * (z + 1 - 2 * (z % 2)) + y, 2 * x + c)

    def copy(self, k):
        return pltpu.make_async_remote_copy(
            src_ref=self.slots.at[5 + k], dst_ref=self.slots.at[k], send_sem=self.ssem.at[k], recv_sem=self.rsem.at[k],
            device_id=self.peers[self.HOPS[k]], device_id_type=MESH)

    def step(self, k):
        if k:
            self.copy(k - 1).wait()
            self.acc[...] = self.acc[...] + self.slots[k - 1]
        if k < 5:
            self.slots[5 + k] = self.acc[...]
            self.copy(k).start()

    def steps(self):
        return [functools.partial(self.step, k) for k in range(6)]


def none():
    pass


class Feed:
    def __init__(self, steps, share=1):
        self.steps = list(steps)
        self.share = share

    def __call__(self):
        for _ in range(self.share):
            if self.steps:
                self.steps.pop(0)()

    def rest(self):
        while self.steps:
            self.steps.pop(0)()


def forward_kernel(nbytes, vocab, split, *refs):
    bucket_ref, lengths_ref, ids_ref, rel_ref = refs[:4]
    scal_ref = Flags(bucket_ref, lengths_ref)
    n_in = 2 if split is None else 9
    given, refs = refs[4:4 + n_in], refs[4 + n_in:]
    fulls, outs = refs[:3], refs[3:14]
    stream_o, normed_o, emb_o, wcol_o, tot_o, vec_o, q_o, k_o, v_o, mixed_o, lse_o = outs
    (tt, wq, wk, wv, stream, normed, emb, wcol, tot, vec, q, k, v, mixed, lse, slabs, table, kaug, raug, strip, vt, base_ref, osem, wsem) = refs[14:38]
    done = []

    def out(src, dst):
        cp = pltpu.make_async_copy(src, dst, osem.at[len(done)])
        cp.start()
        done.append(cp)

    ntok = nbytes // 2
    d = q.shape[1]
    if split is not None:
        wide_t, own_t, own_p, own_f, own_d = refs[38:43]
        emb_ref, vecs_ref, sq, sk, sv, so, sg, su, sd = given
        rd = sd.shape[0]
        g = Gather([own_t, own_p, own_f, own_d], [tt] + list(fulls), split, *refs[43:46])
        r = own_t.shape[0]
        wide_t[...] = jnp.zeros_like(wide_t)
        wide_t[0:vocab, 0:r] = emb_ref[...].astype(f32)
        wide_t[vocab:vocab + 3, 0:r] = vecs_ref[...].astype(f32)
        own_t[...] = wide_t[...].T[0:r].astype(bf16)
        g.enter()
        g.start_direct(0)
        for m, part in enumerate((sq, sk, sv)):
            own_p[:, m * d:(m + 1) * d] = part[...]
        for m, part in enumerate((sg, su)):
            own_f[:, m * part.shape[1]:(m + 1) * part.shape[1]] = part[...]
        own_d[0:rd, :] = sd[...]
        own_d[rd:, :] = so[...]
        g.start(1)
        build_masks(scal_ref, kaug, raug, ntok)
        bias_rows(rel_ref, base_ref)
        relay, end = g.steps_direct(0)
        plans = [None] + [g.steps(i) for i in (1, 2, 3)]
        relay()
        for s in range(3):
            plans[1][s]()
        end()
        begin = [functools.partial(g.start, i) for i in (2, 3)]
        early = Feed(plans[1][3:6] + begin + plans[1][6:8] + [plans[i][s] for s in range(FEW) for i in (2, 3)], SHARE)
        late = [plans[i][s] for s in range(FEW, 8) for i in (2, 3)]
        per = -(-len(late) // 12)
        chunks = [late[j * per:(j + 1) * per] for j in range(12)]
    else:
        cp = pltpu.make_async_copy(given[0], tt, wsem.at[3])
        cp.start()
        build_masks(scal_ref, kaug, raug, ntok)
        bias_rows(rel_ref, base_ref)
        cp.wait()
        early = Feed([])
        chunks = [[]] * 12
    gbst_fwd_body(nbytes, vocab, scal_ref, ids_ref, tt, stream, normed, emb, wcol, tot, vec, slabs, table, early)
    early.rest()
    for src, dst in ((stream, stream_o), (normed, normed_o), (emb, emb_o), (wcol, wcol_o), (tot, tot_o), (vec, vec_o)):
        out(src, dst)
    loads = []
    for i, dst in enumerate((wq, wk, wv)):
        if split is not None and i == 0:
            plans[1][8]()
        cp = pltpu.make_async_copy((given[1] if split is None else fulls[0]).at[:, i * d:(i + 1) * d], dst, wsem.at[i])
        cp.start()
        loads.append(cp)
    for cp, w, dst, to in zip(loads, (wq, wk, wv), (q, k, v), (q_o, k_o, v_o)):
        cp.wait()
        for c in range(d // 256):
            cs = slice(c * 256, (c + 1) * 256)
            dst[:, cs] = nn(normed[...], w[:, cs]).astype(bf16)
        out(dst, to)

    def pair(p, carry):
        def hook(b):
            if b % 3 == 0:
                for j in range(6):
                    part = chunks[2 * j + b // 3]
                    if part:
                        @pl.when(p == j)
                        def _():
                            for step in part:
                                step()
        fwd_pair(p, q, k, v, base_ref, mixed, lse, kaug, raug, strip, vt, hook)
        return carry
    lax.fori_loop(0, d // 128, pair, 0)
    out(mixed, mixed_o)
    out(lse, lse_o)
    if split is not None:
        for i in (2, 3):
            plans[i][8]()
        g.finish()
    for cp in done:
        cp.wait()


FEW, SHARE = 3, 1


def forward_one(bucket, lengths, ids, rel, given, vocab, nbytes, wide, split):
    d = given[1].shape[0] if split is None else given[2].shape[1]
    hbm = pl.BlockSpec(memory_space=pltpu.HBM)
    vm = pl.BlockSpec(memory_space=pltpu.VMEM)
    sm = pl.BlockSpec(memory_space=pltpu.SMEM)
    pairs = d // 128
    sd = jax.ShapeDtypeStruct
    acts = [((TP, d), f32), ((TP, d), bf16), ((12 * ROWS, d), bf16), ((ROWS, 128), f32), ((8, 128), f32), ((8, d), f32),
            ((TP, d), bf16), ((TP, d), bf16), ((TP, d), bf16), ((TP, d), bf16), ((pairs, 8, 256), f32)]
    scratch = [pltpu.VMEM((d, VP), bf16)] + [pltpu.VMEM((d, d), bf16)] * 3 + [pltpu.VMEM(*a) for a in acts]
    scratch += [pltpu.VMEM((d // 128, TP, 128), f32), pltpu.VMEM((VP, d), bf16), pltpu.VMEM((TP, 128), bf16), pltpu.VMEM((NB, 256, 128), bf16),
                pltpu.VMEM((STRIP, 256), f32), pltpu.VMEM((128, TP), bf16), pltpu.VMEM((16, 512), f32), pltpu.SemaphoreType.DMA((11,)), pltpu.SemaphoreType.DMA((4,))]
    params = dict(vmem_limit_bytes=56 << 20)
    if split is not None:
        r, ff, rd = given[2].shape[0], given[6].shape[1], given[8].shape[0]
        scratch += [pltpu.VMEM((VP, 128), f32), pltpu.VMEM((r, VP), bf16), pltpu.VMEM((r, 3 * d), bf16), pltpu.VMEM((r, 2 * ff), bf16), pltpu.VMEM((rd + r, d), bf16)]
        scratch += [pltpu.SemaphoreType.DMA((4, Gather.SENDS)), pltpu.SemaphoreType.DMA((4, Gather.SLOTS)), pltpu.SemaphoreType.DMA((4,))]
        params.update(collective_id=1, has_side_effects=True)
        whole = [sd((wide * r, 3 * d), bf16), sd((wide * r, 2 * ff), bf16), sd((wide * (rd + r), d), bf16)]
    else:
        whole = [sd((16, 128), bf16)] * 3
    return pl.pallas_call(
        functools.partial(forward_kernel, nbytes, vocab, split),
        out_shape=tuple(whole) + tuple(sd(*a) for a in acts),
        in_specs=[sm, sm, vm, vm] + ([hbm] * 2 if split is None else [vm] * 9),
        out_specs=(hbm,) * 14,
        scratch_shapes=scratch,
        compiler_params=pltpu.CompilerParams(**params),
        name="forward_one",
    )(bucket, lengths, ids, rel, *given)


FCH = 256
FRB = 256
GELU = 0.7978845608028654


def flat(ref, cs=slice(None)):
    return ref[:, :, :, :, cs].reshape(ref.shape[0] * 4 * ref.shape[3], -1)


def norm_scale(x):
    return lax.rsqrt(jnp.mean(x * x, axis=1, keepdims=True) + EPS)


def row_block(b):
    return pl.ds(pl.multiple_of(b * FRB, FRB), FRB)


def store_product(dst, tr, rhs):
    rows = dst.shape[0] * 4 * dst.shape[3]
    parts = -(-rows // 1024)
    size = dst.shape[0] // parts
    wide = 256
    for m in range(parts):
        left = tr[m * rows // parts:(m + 1) * rows // parts, :]
        for c in range(dst.shape[4] // wide):
            cs = slice(c * wide, (c + 1) * wide)
            r = nn(left, rhs[:, cs]).astype(bf16)
            dst[m * size:(m + 1) * size, :, :, :, cs] = r.reshape((size,) + dst.shape[1:4] + (wide,))


def ff_phase(gu_h, do_h, mixed_h, stream_h, og_h, enc_o, g2, wo, wf, wd, stream, mid, gh_out, ggain2, sems, ready, poll):
    d = mid.shape[1]
    halves = len(wf)
    part = wf[0].shape[4] // 2

    def scoped(hid, gg, gu, tr, mixed, og, nff, dacc):
        ins = []
        ro, rd = wo.shape[3], wd.shape[3]
        ff = halves * part
        pairs = [(mixed_h, mixed)] + [(do_h.at[:, :, 2 * rd + x * ro:2 * rd + (x + 1) * ro], wo.at[:, :, x]) for x in range(2)]
        pairs += [(stream_h, stream), (og_h, og)]
        for h in range(halves):
            at = h * part
            pairs += [(gu_h.at[:, :, :, :, at:at + part], wf[h].at[:, :, :, :, part:2 * part]), (gu_h.at[:, :, :, :, ff + at:ff + at + part], wf[h].at[:, :, :, :, 0:part])]
            if h == 0:
                pairs += [(do_h.at[:, :, x * rd:(x + 1) * rd], wd.at[:, :, x]) for x in range(2)]
        for n, (s, t) in enumerate(pairs):
            cp = pltpu.make_async_copy(s, t, sems.at[n])
            cp.start()
            ins.append(cp)
        for cp in ins[:4]:
            cp.wait()

        def first(b, carry):
            sl = row_block(b)
            middle = stream[sl, :] + nn(mixed[sl, :], flat(wo))
            dacc[sl, :] = middle
            nff[sl, :] = (middle * norm_scale(middle) * g2).astype(bf16)
            return carry
        lax.fori_loop(0, TP // FRB, first, 0)
        tr[0:d, :] = nff[...].T
        for cp in ins[4:9]:
            cp.wait()
        for h in range(halves):
            if h:
                for cp in ins[9:]:
                    cp.wait()

            for c in range(part // FCH):
                poll(h, c)
                cs = slice(c * FCH, (c + 1) * FCH)
                at = slice(h * part + c * FCH, h * part + (c + 1) * FCH)
                wuc, wgc = flat(wf[h], cs), flat(wf[h], slice(part + c * FCH, part + (c + 1) * FCH))
                wdc = wd[(h * part + c * FCH) // 512, c % 2].reshape(FCH, d)
                gate = nn(nff[...], wgc)
                up = nn(nff[...], wuc)
                gh = nt(og[...], wdc)
                sq = gate * gate
                th = jnp.tanh(gate * (GELU + (GELU * 0.044715) * sq))
                half = 0.5 + 0.5 * th
                act = gate * half
                hid[:, at] = (act * up).astype(bf16)
                dact = half + (0.5 * gate) * (1.0 - th * th) * (GELU + (3 * GELU * 0.044715) * sq)
                gg[:, cs] = (gh * up * dact).astype(bf16)
                gu[:, cs] = (gh * act).astype(bf16)
                dacc[...] += nn(hid[:, at], wdc)
                if h == 0 and c == 0:
                    mid[...] = nt(gg[:, cs], wgc)
                else:
                    mid[...] += nt(gg[:, cs], wgc)
                mid[...] += nt(gu[:, cs], wuc)
            store_product(wf[h].at[:, :, :, :, 0:part], tr.at[0:d], gu)
            store_product(wf[h].at[:, :, :, :, part:2 * part], tr.at[0:d], gg)
            ready("f%d" % h)

        tr[...] = hid[...].T
        store_product(wd, tr, og)
        ready("d")

        def last(b, carry):
            sl = row_block(b)
            nff[sl, :] = dacc[sl, :].astype(bf16)
            wo_all = flat(wo)
            middle = stream[sl, :] + nn(mixed[sl, :], wo_all)
            s2 = norm_scale(middle)
            back = mid[sl, :]
            t = back * g2
            xs = middle * s2
            grad = og[sl, :].astype(f32) + s2 * t - xs * (s2 * s2 * jnp.mean(middle * t, axis=1, keepdims=True))
            mid[sl, :] = grad
            low = grad.astype(bf16)
            gu[sl, 0:d] = low
            gh_out[sl, :] = nt(low, wo_all).astype(bf16)
            ggain2[...] += jnp.sum((back * xs).reshape(FRB // 8, 8, d), axis=0)
            return carry
        lax.fori_loop(0, TP // FRB, last, 0)
        cp = pltpu.make_async_copy(nff, enc_o, sems.at[0])
        cp.start()
        tr[0:d, :] = mixed[...].T
        store_product(wo, tr.at[0:d], gu)
        ready("o")
        cp.wait()
    act = lambda c: pltpu.VMEM((TP, c), bf16)
    pl.run_scoped(scoped, act(halves * part), act(part), act(part), pltpu.VMEM((halves * part, TP), bf16), act(d), act(d), act(d), pltpu.VMEM((TP, d), f32))


NAMES = ("t", "p0", "p1", "p2", "o", "f0", "f1", "d")
FIRST = {"t": "x", "p0": "x", "p1": "y", "p2": "x", "o": "x", "f0": "y", "f1": "x", "d": "y"}
STEPS = ("core", "one", "two", "z", "end")


def backward_kernel(nbytes, vocab, remote, *refs):
    n = len(NAMES)
    bucket_ref, lengths_ref, ids_ref, rel_ref, vec_ref, wcol_ref, tot_ref, lse_ref = refs[:8]
    scal_ref = Flags(bucket_ref, lengths_ref)
    q_h, k_h, v_h, normed_h, stream_h, mixed_h, og_h, emb_h, qkv_h, gu_h, do_h = refs[8:19]
    enc_o, outs, small_o = refs[19], refs[20:20 + n], refs[20 + n]
    refs = refs[21 + n:]
    stream, mid, g, ggain2, ggain, base_ref, fsem, lsem = refs[:8]
    refs = refs[1:]
    bias_rows(rel_ref, base_ref)
    if remote:
        terms = refs[7:7 + n]
        rest = refs[7 + n:]
        red = Reduce(terms, outs, tuple(FIRST[k] for k in NAMES), *[rest[k * n:(k + 1) * n] for k in range(4)], *rest[4 * n:4 * n + 2])
        small = SmallSum(*rest[4 * n + 2:4 * n + 6])
        st = {k: dict(zip(STEPS, red.steps(i))) for i, k in enumerate(NAMES)}
        st["s"] = {k: f for k, f in enumerate(small.steps())}
        red.enter()
    else:
        terms = outs
    term = dict(zip(NAMES, terms))

    def run(words):
        if remote:
            for word in words:
                name, step = word.split(".")
                st[name][int(step) if name == "s" else step]()

    def point(key):
        run(TABLE.get(key, ()))

    def ready(name):
        if remote:
            red.start(NAMES.index(name))
            point(name)

    def point_at(index, keys):
        for j, key in enumerate(keys):
            if remote and TABLE.get(key):
                @pl.when(index == j)
                def _():
                    point(key)

    def poll(h, c):
        point("c%d%d" % (h, c))
    ggain2[...] = jnp.zeros_like(ggain2)
    ff_phase(gu_h, do_h, mixed_h, stream_h, og_h, enc_o, vec_ref[2:3, :], term["o"], (term["f0"], term["f1"]), term["d"],
             stream, mid, g, ggain2, fsem, ready, poll)
    d = stream.shape[1]
    pairs = d // 128

    def scoped(q, k, v, nt_s, emb, wq, wk, wv):
        copies = []
        moves = ((q_h, q), (k_h, k), (v_h, v), (normed_h, nt_s), (emb_h, emb), *((qkv_h.at[:, m * d:(m + 1) * d], w) for m, w in enumerate((wq, wk, wv))))
        for m, (s, t) in enumerate(moves):
            cp = pltpu.make_async_copy(s, t, lsem.at[m])
            cp.start()
            copies.append(cp)
        for cp in copies[:4]:
            cp.wait()
        nt_s[...] = nt_s[...].T

        def attention(kaug, raug, strip, acc, kt, dk_s, dv_s, db):
            build_masks(scal_ref, kaug, raug, nbytes // 2)
            db[...] = jnp.zeros_like(db)
            def pair(p, carry):
                def hook(b):
                    if b % 3 == 0:
                        point_at(p, ["a%d%d" % (j, b // 3) for j in range(pairs)])
                bwd_pair(p, q, k, v, g, lse_ref, base_ref, db, kaug, raug, strip, acc, kt, dk_s, dv_s, hook)
                for j in range(pairs // 2):
                    @pl.when(p == 2 * j + 1)
                    def _():
                        dst = term["p%d" % j]
                        for m, src in enumerate((q, k, v)):
                            r = nn(nt_s[...], src[:, 256 * j:256 * (j + 1)]).astype(bf16)
                            dst[:, :, :, :, 256 * m:256 * (m + 1)] = r.reshape(dst.shape[:4] + (256,))
                        ready("p%d" % j)
                return carry
            lax.fori_loop(0, pairs, pair, 0)
            relt = lax.dot_general(db[...], bucket_hot(), (((1,), (0,)), ((), ())), precision=lax.Precision.HIGHEST, preferred_element_type=f32)
            row = lax.broadcasted_iota(jnp.int32, SMALL, 0)
            total = jnp.where(row == SMALL[0] - 1, tot_ref[0:1, :], relt)
            if remote:
                small.acc[...] = total
            else:
                small_o[...] = total
        strips = pltpu.VMEM((STRIP, 256), f32)
        pl.run_scoped(attention, pltpu.VMEM((TP, 128), bf16), pltpu.VMEM((NB, 256, 128), bf16), strips, strips, pltpu.VMEM((128, TP), bf16),
                      pltpu.VMEM((TP, 128), f32), pltpu.VMEM((TP, 128), f32), pltpu.VMEM((16, 512), f32))
        for cp in copies[4:]:
            cp.wait()

        def pooling(slabs, de):
            count = []

            def hook():
                point("h%d" % len(count))
                count.append(0)
            hook()
            ggain[...] = jnp.zeros_like(ggain)
            gain = vec_ref[1:2, :]

            def rows(b, carry):
                sl = row_block(b)
                gy = nt(q[sl, :], wq[...]) + nt(k[sl, :], wk[...]) + nt(v[sl, :], wv[...])
                x = stream[sl, :]
                s = norm_scale(x)
                t = gy * gain
                gs = mid[sl, :] + s * t - x * (s * s * s * jnp.mean(x * t, axis=1, keepdims=True))
                for c in range(d // 128):
                    slabs[c, sl, :] = gs[:, c * 128:(c + 1) * 128]
                ggain[...] += jnp.sum((gy * x * s).reshape(FRB // 8, 8, d), axis=0)
                return carry
            lax.fori_loop(0, TP // FRB, rows, 0)
            ggain[0:2, :] = jnp.concatenate([jnp.sum(ggain[...], axis=0, keepdims=True), jnp.sum(ggain2[...], axis=0, keepdims=True)], axis=0)
            hook()

            def put(gt):
                dst = term["t"]
                half = dst.shape[3]
                for zz in range(dst.shape[0]):
                    for yy in range(2):
                        for xx in range(2):
                            top = ((zz * 2 + yy) * 2 + xx) * half
                            dst[zz, yy, xx, :, 0:VR] = gt[top:top + half]
                            dst[zz, yy, xx, :, VR:VG] = jnp.zeros((half, VG - VR), bf16)
            gbst_bwd_body(nbytes, vocab, scal_ref, ids_ref, emb, wcol_ref, vec_ref, ggain, put, de, slabs, hook)
            if remote:
                ready("t")
        pl.run_scoped(pooling, pltpu.VMEM((d // 128, TP, 128), f32), pltpu.VMEM((12 * ROWS, d), bf16))
    act = pltpu.VMEM((TP, d), bf16)
    mat = pltpu.VMEM((d, d), bf16)
    pl.run_scoped(scoped, act, act, act, act, pltpu.VMEM((12 * ROWS, d), bf16), mat, mat, mat)
    if remote:
        point("end")
        small_o[...] = small.acc[...]
        red.finish()


TABLE = {
    "c13": ("f0.core",),
    "o": ("f1.core",),
    "a00": ("d.core", "o.core", "f0.one",),
    "a30": ("p0.core", "d.one", "f1.one",),
    "a31": ("o.one",),
    "a50": ("p1.core", "f0.two", "f1.two", "o.two",),
    "p2": ("p0.one",),
    "h0": ("p1.one",),
    "h1": ("p2.core", "s.0", "f0.z", "d.two", "p0.two",),
    "h2": ("s.1",),
    "h3": ("p1.two",),
    "h6": ("f1.z",),
    "h7": ("p2.one",),
    "h8": ("o.z",),
    "t": ("s.2",),
    "end": ("p2.two", "f0.end", "t.core", "s.3", "f1.end", "d.z", "o.end", "p0.z",
            "t.one", "p1.z", "t.two", "d.end", "s.4", "p2.z", "p0.end", "p1.end",
            "s.5", "t.z", "p2.end", "t.end",),
}


def backward_one(bucket, lengths, ids, rel, vec, wcol, tot, lse, acts, weights, vocab, nbytes, remote):
    d = acts[0].shape[1]
    hbm = pl.BlockSpec(memory_space=pltpu.HBM)
    vm = pl.BlockSpec(memory_space=pltpu.VMEM)
    sd = jax.ShapeDtypeStruct
    view = lambda r, c: (4, 2, 2, r // 16, c)
    qkv, gu, do = weights
    ff = gu.shape[1] // 2
    sm = pl.BlockSpec(memory_space=pltpu.SMEM)
    shapes = [view(d, VG)] + [view(d, d)] * 4 + [view(d, ff)] * 2 + [view(ff, d)]
    scratch = [pltpu.VMEM((TP, d), f32), pltpu.VMEM((TP, d), f32), pltpu.VMEM((TP, d), bf16), pltpu.VMEM((8, d), f32), pltpu.VMEM((8, d), f32),
               pltpu.VMEM((16, 512), f32), pltpu.SemaphoreType.DMA((11,)), pltpu.SemaphoreType.DMA((8,))]
    params = dict(vmem_limit_bytes=62 << 20)
    if remote:
        outs = [sd((2, 2, s[3], s[4] // 2), bf16) for s in shapes]
        scratch += [pltpu.VMEM(s, bf16) for s in shapes] + Reduce.scratch(shapes)
        scratch += [pltpu.VMEM(SMALL, f32), pltpu.VMEM((10,) + SMALL, f32), pltpu.SemaphoreType.DMA((5,)), pltpu.SemaphoreType.DMA((5,))]
        params.update(collective_id=2, has_side_effects=True)
    else:
        outs = [sd(s, bf16) for s in shapes]
    return pl.pallas_call(
        functools.partial(backward_kernel, nbytes, vocab, remote),
        out_shape=(sd((TP, d), bf16), *outs, sd(SMALL, f32)),
        in_specs=[sm, sm] + [vm] * 6 + [hbm] * 11,
        out_specs=(hbm,) + (vm,) * (len(outs) + 1),
        scratch_shapes=scratch,
        compiler_params=pltpu.CompilerParams(**params),
        name="backward_one",
    )(bucket, lengths, ids, rel, vec, wcol, tot, lse, *acts, qkv, gu.reshape(view(*gu.shape)), do.reshape(4, 2, -1, d))


def finish_kernel(vocab, heads, buckets, *refs):
    ins, small_ref = dict(zip(NAMES, refs[:len(NAMES)])), refs[len(NAMES)]
    table_o, score_o, gain1_o, q_o, k_o, v_o, o_o, rel_o, gain2_o, gate_o, up_o, down_o, share_o = refs[len(NAMES) + 1:]

    def place(dst, src, left):
        half, width = src.shape[2], src.shape[3]
        for c in range(2):
            for x in range(2):
                dst[x * half:(x + 1) * half, left + c * width:left + (c + 1) * width] = src[c, x].astype(f32)
    place(o_o, ins["o"], 0)
    place(down_o, ins["d"], 0)
    for h in range(2):
        src = ins["f%d" % h]
        half, width = src.shape[2], src.shape[3]
        for c, dst in enumerate((up_o, gate_o)):
            for x in range(2):
                dst[x * half:(x + 1) * half, h * width:(h + 1) * width] = src[c, x].astype(f32)
    for j in range(3):
        src = ins["p%d" % j]
        half = src.shape[2]
        for piece in range(6):
            c, m = piece // 3, piece % 3
            dst = (q_o, k_o, v_o)[piece // 2]
            left = 256 * j + 128 * (piece % 2)
            for x in range(2):
                dst[x * half:(x + 1) * half, left:left + 128] = src[c, x, :, 128 * m:128 * (m + 1)].astype(f32)
    t = ins["t"]
    rows = jnp.concatenate([jnp.concatenate([t[c, x] for x in range(2)], axis=0) for c in range(2)], axis=1).astype(f32)
    turned = rows.T
    table_o[...] = turned[:vocab]
    score_o[...] = turned[vocab:vocab + 1]
    gain1_o[...] = turned[vocab + 1:vocab + 2]
    gain2_o[...] = turned[vocab + 2:vocab + 3]
    small = small_ref[...]
    rel_o[...] = small.T[:buckets, :heads]
    last = small[SMALL[0] - 1:SMALL[0], :]
    share_o[...] = last[:, 0:4] / last[:, 4:5]


def finish(outs, vocab, heads, buckets):
    vm = pl.BlockSpec(memory_space=pltpu.VMEM)
    sd = lambda *s: jax.ShapeDtypeStruct(s, f32)
    r = 2 * outs[1].shape[2]
    d = 2 * outs[1].shape[3]
    ff = 2 * outs[5].shape[3]
    return pl.pallas_call(
        functools.partial(finish_kernel, vocab, heads, buckets),
        out_shape=(sd(vocab, r), sd(1, r), sd(1, r), sd(r, d), sd(r, d), sd(r, d), sd(r, d), sd(buckets, heads), sd(1, r), sd(r, ff), sd(r, ff),
                   sd(2 * outs[7].shape[2], d), sd(1, 4)),
        in_specs=[vm] * len(outs),
        out_specs=(vm,) * 13,
        compiler_params=pltpu.CompilerParams(vmem_limit_bytes=32 << 20),
        name="finish",
    )(*outs)


def body(byte_ids, lengths, bucket, out_grad, embedding, score_weight, gain_attn, w_query, w_key, w_value, w_attn_out, rel_bias, gain_ff, w_gate, w_up, w_ff_out):
    vocab, width = embedding.shape
    wide = lax.axis_size("wide")
    ids = byte_ids[0]
    nbytes = ids.shape[0]
    ntok = nbytes // 2
    idp = jnp.pad(ids.reshape(nbytes // 12, 12).T, ((0, 4), (0, ROWS - nbytes // 12)), constant_values=-1)
    vecs = jnp.stack([score_weight, gain_attn, gain_ff])
    shards = (w_query, w_key, w_value, w_attn_out, w_gate, w_up, w_ff_out)
    kernels = wide == 8 and lax.axis_size("narrow") == 4 and all(s.shape[0] % 32 == 0 for s in shards)
    if kernels:
        split, given = (True, True, True, False), (embedding, vecs) + shards
    else:
        columns = jnp.concatenate([embedding.T, vecs.T], axis=1)
        tt = jnp.pad(columns, ((0, 0), (0, VP - columns.shape[1])))
        tt, wq, wk, wv, wo, wg, wu, wd = (lax.all_gather(s, "wide", axis=0, tiled=True) for s in (tt,) + shards)
        split, given = None, (tt, jnp.concatenate([wq, wk, wv], axis=1))
    *weights, stream, normed, emb, wcol, tot, vec, q, k, v, mixed, lse = forward_one(bucket, lengths, idp, rel_bias, given, vocab, nbytes, wide, split)
    if not kernels:
        eight = lambda w: w.reshape(8, -1, w.shape[1])
        weights = (given[1], jnp.concatenate([wg, wu], axis=1), jnp.concatenate([eight(wd), eight(wo)], axis=1).reshape(-1, wo.shape[1]))
    og = jnp.pad(out_grad[0], ((0, TP - ntok), (0, 0)))
    encoded, *outs = backward_one(bucket, lengths, idp, rel_bias, vec, wcol, tot, lse, (q, k, v, normed, stream, mixed, og, emb), weights, vocab, nbytes, kernels)
    encoded = encoded[:ntok][None]
    if kernels:
        done = finish(outs, vocab, rel_bias.shape[1], rel_bias.shape[0])
        line = lambda a: a.reshape(-1)
        return (encoded, done[0], line(done[1]), line(done[2]), *done[3:8], line(done[8]), *done[9:12], line(done[12]))
    small = outs[-1]
    t, p0, p1, p2, o, f0, f1, down = (a.reshape(-1, a.shape[-1]) for a in outs[:-1])
    part = lambda m: jnp.concatenate([p[:, 256 * m:256 * (m + 1)] for p in (p0, p1, p2)], axis=1)
    half = lambda m: jnp.concatenate([f[:, m * f.shape[1] // 2:(m + 1) * f.shape[1] // 2] for f in (f0, f1)], axis=1)
    grads = (t, part(0), part(1), part(2), o, half(1), half(0), down)
    sums = [lax.psum(lax.psum_scatter(g, "wide", scatter_dimension=0, tiled=True), "narrow").astype(f32) for g in grads]
    small = lax.psum(small, ("wide", "narrow"))
    g_rel, tot = small[:rel_bias.shape[1], :rel_bias.shape[0]].T, small[-1, :5]
    t = sums[0]
    return (encoded, t[:, :vocab].T, t[:, vocab], t[:, vocab + 1], *sums[1:5], g_rel, t[:, vocab + 2], *sums[5:], tot[:4] / tot[4])


def solution(mesh):
    both = ("wide", "narrow")
    rows = P("wide", None)
    vec = P("wide")
    placed = (P(both, None), P(both, None), P(both), P(both, None, None), P(None, "wide"), vec, vec, rows, rows, rows, rows, P(), vec, rows, rows, rows)
    outs = (P(both, None, None), P(None, "wide"), vec, vec, rows, rows, rows, rows, P(), vec, rows, rows, rows, P())
    return jax.shard_map(body, mesh=mesh, in_specs=placed, out_specs=outs, check_vma=False)
```

```python
import functools

import jax
import jax.numpy as jnp
from jax import lax
from jax.experimental import pallas as pl
from jax.experimental.pallas import tpu as pltpu
from jax.sharding import PartitionSpec as P

f32 = jnp.float32
bf16 = jnp.bfloat16
TP = 768
BLK = 128
NB = TP // BLK
LEFT = TP - BLK
STRIP = 2 * TP - BLK
W0 = LEFT - 128
WN = 384

def nt(a, b):
    return lax.dot_general(a, b, (((1,), (1,)), ((), ())), preferred_element_type=f32)

def nn(a, b):
    return lax.dot_general(a, b, (((1,), (0,)), ((), ())), preferred_element_type=f32)

def build_masks(scal_ref, kaug, raug, ntok):
    joined = scal_ref[0] == 1
    l0 = scal_ref[1]; l1 = scal_ref[2]
    half = ntok // 2
    u = lax.broadcasted_iota(jnp.int32, (TP, 128), 0)
    lane = lax.broadcasted_iota(jnp.int32, (TP, 128), 1)
    seg = (u >= half).astype(jnp.int32)
    lim = jnp.where(seg == 1, l1, l0)
    start = seg * half
    lim = jnp.where(joined, l0 + l1, lim)
    start = jnp.where(joined, 0, start)
    valid = (2 * (u - start) < lim) & (u < ntok)
    segs = jnp.where(joined, 0, seg)
    ok = valid & (segs == lane)
    kaug[...] = jnp.where((lane < 2) & jnp.logical_not(ok), -1e30, 0.0).astype(bf16)
    t = u
    rows = jnp.where((lane == segs), 1.0, 0.0).astype(bf16)
    for b in range(NB):
        blk = rows[b * 128:(b + 1) * 128]
        raug[b] = jnp.concatenate([blk, blk], axis=0)

def bias_rows(rel_ref, base):
    c = lax.broadcasted_iota(jnp.int32, (rel_ref.shape[0], 512), 1)
    b = lax.broadcasted_iota(jnp.int32, (rel_ref.shape[0], 512), 0)
    hot = jnp.where(bucket_of(jnp.where(c < 384, c - 128, c - 640)) == b, 1.0, 0.0).astype(bf16)
    base[0:rel_ref.shape[1], :] = lax.dot_general(rel_ref[...], hot, (((0,), (0,)), ((), ())), preferred_element_type=f32)


def bucket_hot():
    m = lax.broadcasted_iota(jnp.int32, (512, 128), 0)
    b = lax.broadcasted_iota(jnp.int32, (512, 128), 1)
    return jnp.where(bucket_of(m - 255) == b, 1.0, 0.0).astype(f32)


class Flags:
    def __init__(self, bucket_ref, lengths_ref):
        self.refs = (bucket_ref, lengths_ref)

    def __getitem__(self, i):
        return self.refs[0][0] if i == 0 else self.refs[1][0, i - 1]


def build_strip(base_ref, row0, strip):
    for hh in range(2):
        row = base_ref[pl.ds(row0 + hh, 1), :]
        cl = row[:, 0:1]; cr = row[:, 383:384]
        sq = jnp.broadcast_to(row, (128, 512))
        sq = pltpu.roll(sq, 0, 1, stride=1, stride_axis=0)
        win = sq[:, :WN].T
        lanes = slice(hh * 128, hh * 128 + 128)
        strip[0:W0, lanes] = jnp.broadcast_to(cl, (W0, 128))
        strip[W0:W0 + WN, lanes] = win
        strip[W0 + WN:STRIP, lanes] = jnp.broadcast_to(cr, (STRIP - W0 - WN, 128))

def stacked(blk):
    lane = lax.broadcasted_iota(jnp.int32, blk.shape, 1)
    z = jnp.zeros_like(blk)
    return jnp.concatenate([jnp.where(lane < 64, blk, z), jnp.where(lane >= 64, blk, z)], axis=0)

def fwd_pair(p, q_ref, k_ref, v_ref, base_ref, o_ref, lse_ref, kaug, raug, strip, vt, hook):
    lanes = pl.ds(pl.multiple_of(p * 128, 128), 128)
    build_strip(base_ref, 2 * p, strip)
    vt[...] = v_ref[:, lanes].T
    kcat = jnp.concatenate([k_ref[:, lanes], kaug[...]], axis=1)
    vtv = vt[...]
    rowsel = lax.broadcasted_iota(jnp.int32, (128, 128), 0) < 64
    for b in range(NB):
        hook(b)
        rhs = jnp.concatenate([stacked(q_ref[b * 128:(b + 1) * 128, lanes]), raug[b]], axis=1)
        s = nt(kcat, rhs) + strip[LEFT - b * 128:LEFT - b * 128 + TP, :]
        mx = jnp.max(s, axis=0, keepdims=True)
        e = jnp.exp(s - mx)
        l = jnp.sum(e, axis=0, keepdims=True)
        ot = nn(vtv, e.astype(bf16)) * (1.0 / l)
        lse_ref[p, b:b + 1, :] = mx + jnp.log(l)
        o = jnp.where(rowsel, ot[:, :128], ot[:, 128:])
        o_ref[b * 128:(b + 1) * 128, lanes] = o.T.astype(bf16)


def bwd_pair(p, q_ref, k_ref, v_ref, g_ref, lse_ref, base_ref, db_ref, kaug, raug, strip, acc, kt, dk_s, dv_s, hook=None):
    lanes = pl.ds(pl.multiple_of(p * 128, 128), 128)
    build_strip(base_ref, 2 * p, strip)
    kt[...] = k_ref[:, lanes].T
    kcat = jnp.concatenate([k_ref[:, lanes], kaug[...]], axis=1)
    v = v_ref[:, lanes]
    ktv = kt[...]
    acc[...] = jnp.zeros_like(acc)
    dk_s[...] = jnp.zeros_like(dk_s)
    dv_s[...] = jnp.zeros_like(dv_s)
    rowsel = lax.broadcasted_iota(jnp.int32, (128, 128), 0) < 64
    for b in range(NB):
        if hook is not None:
            hook(b)
        rows = slice(b * 128, (b + 1) * 128)
        qs = stacked(q_ref[rows, lanes])
        gs = stacked(g_ref[rows, lanes])
        rhs = jnp.concatenate([qs, raug[b]], axis=1)
        w = slice(LEFT - b * 128, LEFT - b * 128 + TP)
        s = nt(kcat, rhs) + strip[w, :]
        pr = jnp.exp(s - lse_ref[p, b:b + 1, :])
        dp = nt(v, gs)
        pdp = pr * dp
        delta = jnp.sum(pdp, axis=0, keepdims=True)
        ds = pdp - pr * delta
        acc[w, :] += ds
        dsb = ds.astype(bf16)
        dk_s[...] += nn(dsb, qs)
        dv_s[...] += nn(pr.astype(bf16), gs)
        dqt = nn(ktv, dsb)
        dq = jnp.where(rowsel, dqt[:, :128], dqt[:, 128:])
        q_ref[rows, lanes] = dq.T.astype(bf16)
    k_ref[:, lanes] = dk_s[...].astype(bf16)
    v_ref[:, lanes] = dv_s[...].astype(bf16)
    fi = lax.broadcasted_iota(jnp.int32, (128, 128), 0)
    fj = lax.broadcasted_iota(jnp.int32, (128, 128), 1)
    flip = jnp.where(fi + fj == 127, 1.0, 0.0).astype(f32)
    for hh in range(2):
        half = slice(hh * 128, hh * 128 + 128)
        far_l = jnp.sum(acc[0:W0, half], keepdims=True)
        far_r = jnp.sum(acc[W0 + WN:STRIP, half], keepdims=True)
        win = acc[W0:W0 + WN, half]
        wt = lax.dot_general(flip, win, (((1,), (1,)), ((), ())), precision=lax.Precision.HIGHEST, preferred_element_type=f32)
        wt = jnp.concatenate([wt, jnp.zeros((128, 128), f32)], axis=1)
        wt = pltpu.roll(wt, 0, 1, stride=1, stride_axis=0)
        diag = jnp.sum(wt, axis=0, keepdims=True)
        lane = lax.broadcasted_iota(jnp.int32, (1, 512), 1)
        diag = diag + jnp.where(lane == 0, far_l, 0.0) + jnp.where(lane == 510, far_r, 0.0)
        db_ref[pl.ds(2 * p + hh, 1), :] = diag


def bucket_of(relative):
    distance = jnp.abs(relative)
    far = 8 + sum(((distance >= e).astype(jnp.int32) for e in (12, 16, 23, 32, 46, 64, 91)))
    near = jnp.where(distance < 8, distance, far)
    return near + 16 * (relative > 0).astype(jnp.int32)


ROWS = 128
VP = 384
VG = 512
VR = 272
EPS = 1e-6

def byte_valid_mat(scal_ref, nbytes):
    i = lax.broadcasted_iota(jnp.int32, (ROWS, 128), 0)
    j = lax.broadcasted_iota(jnp.int32, (ROWS, 128), 1)
    p = 12 * i + j
    slot = nbytes // 2
    joined = scal_ref[0] == 1
    l0 = scal_ref[1]; l1 = scal_ref[2]
    second = p >= slot
    start = jnp.where(joined, 0, jnp.where(second, slot, 0))
    lim = jnp.where(joined, l0 + l1, jnp.where(second, l1, l0))
    ok = (p - start < lim) & (p < nbytes) & (j < 12)
    return jnp.where(ok, 1.0, 0.0).astype(f32)

def inverse_counts(vm):
    v = [vm[:, j:j + 1] for j in range(12)]
    inv = {1: v}
    for b in (2, 3, 4):
        out = []
        for m in range(12 // b):
            tot = v[b * m]
            for t in range(1, b):
                tot = tot + v[b * m + t]
            out.append(1.0 / jnp.maximum(tot, 1.0))
        inv[b] = out
    return v, inv

def softmax_weights(e, inv):
    rate = {1: e}
    for b in (2, 3, 4):
        out = []
        for m in range(12 // b):
            tot = e[b * m]
            for t in range(1, b):
                tot = tot + e[b * m + t]
            out.append(tot * inv[b][m])
        rate[b] = out
    w = {b: [] for b in (1, 2, 3, 4)}
    for p in range(12):
        r = [rate[b][p // b] for b in (1, 2, 3, 4)]
        mx = jnp.maximum(jnp.maximum(r[0], r[1]), jnp.maximum(r[2], r[3]))
        ex = [jnp.exp(x - mx) for x in r]
        inv_t = 1.0 / (ex[0] + ex[1] + ex[2] + ex[3])
        for b in (1, 2, 3, 4):
            w[b].append(ex[b - 1] * inv_t)
    return w

def gbst_fwd_body(nbytes, vocab, scal_ref, ids_ref, tt_ref, stream_ref, normed_ref, emb_ref, wcol_ref, tot_ref, vec_ref, slabs, table_ref, hook):
    table_ref[...] = tt_ref[...].T
    base = vocab // 16 * 16
    tail = table_ref[base:base + 16, :].astype(f32)
    vec_ref[0:3, :] = tail[vocab - base:vocab - base + 3, :]
    vec_ref[3:8, :] = jnp.zeros((5, tail.shape[1]), f32)
    vm = byte_valid_mat(scal_ref, nbytes)
    v, inv = inverse_counts(vm)
    idt = ids_ref[...].astype(f32).T
    lane = lax.broadcasted_iota(jnp.int32, (ROWS, VP), 1).astype(f32)
    s = vec_ref[0:1, :]
    e = []
    for j in range(12):
        hot = jnp.where((lane == idt[:, j:j + 1]) & (v[j] > 0.5), 1.0, 0.0).astype(bf16)
        ej = nn(hot, table_ref[...])
        emb_ref[j * ROWS:(j + 1) * ROWS, :] = ej.astype(bf16)
        e.append(jnp.sum(ej * s, axis=1, keepdims=True))
        if j % 3 == 2:
            hook()
    w = softmax_weights(e, inv)
    l128 = lax.broadcasted_iota(jnp.int32, (ROWS, 128), 1)
    wc = jnp.zeros((ROWS, 128), f32)
    for b in (1, 2, 3, 4):
        for p in range(12):
            wc = jnp.where(l128 == (b - 1) * 12 + p, w[b][p], wc)
    wcol_ref[...] = wc
    tl = lax.broadcasted_iota(jnp.int32, (8, 128), 1)
    tot = jnp.zeros((8, 128), f32)
    for b in (1, 2, 3, 4):
        acc = w[b][0] * v[0]
        for p in range(1, 12):
            acc = acc + w[b][p] * v[p]
        tot = jnp.where(tl == b - 1, jnp.sum(acc, keepdims=True), tot)
    tot = jnp.where(tl == 4, jnp.sum(vm, keepdims=True), tot)
    tot_ref[...] = tot
    hook()
    E = lambda j: emb_ref[j * ROWS:(j + 1) * ROWS, :].astype(f32)
    s3 = lambda m: E(3 * m) + E(3 * m + 1) + E(3 * m + 2)
    for k in range(6):
        p0, p1 = 2 * k, 2 * k + 1
        b2 = 0.5 * (w[2][p0] + w[2][p1]) * inv[2][k]
        acc = (0.5 * w[1][p0] + b2) * E(p0) + (0.5 * w[1][p1] + b2) * E(p1)
        n = k // 2
        d = 0.5 * (w[4][p0] + w[4][p1]) * inv[4][n]
        acc = acc + d * ((E(4 * n) + E(4 * n + 1)) + (E(4 * n + 2) + E(4 * n + 3)))
        m0, m1 = p0 // 3, p1 // 3
        if m0 == m1:
            acc = acc + (0.5 * (w[3][p0] + w[3][p1]) * inv[3][m0]) * s3(m0)
        else:
            acc = acc + (0.5 * w[3][p0] * inv[3][m0]) * s3(m0) + (0.5 * w[3][p1] * inv[3][m1]) * s3(m1)
        put_strided(slabs, k, acc)
        if k % 2 == 1:
            hook()
    ntok = nbytes // 2
    for c in range(slabs.shape[0]):
        stream_ref[0:ntok, c * 128:(c + 1) * 128] = slabs[c, 0:ntok, :]
    stream_ref[ntok:TP, :] = jnp.zeros((TP - ntok, acc.shape[1]), f32)
    norm_rows(stream_ref, vec_ref[1:2, :], normed_ref)
    hook()


def put_strided(ref, k, val):
    for c in range(val.shape[1] // 128):
        ref[c, pl.ds(k, 124, stride=6), :] = val[:124, c * 128:(c + 1) * 128]

def get_strided(ref, k):
    parts = [ref[c, pl.ds(k, 124, stride=6), :] for c in range(ref.shape[0])]
    x = jnp.concatenate(parts, axis=1)
    return jnp.concatenate([x, jnp.zeros((4, x.shape[1]), f32)], axis=0)

def norm_rows(x_ref, gain_ref, out_ref):
    g = gain_ref
    for b in range(TP // 128):
        x = x_ref[b * 128:(b + 1) * 128, :]
        sc = lax.rsqrt(jnp.mean(x * x, axis=1, keepdims=True) + EPS)
        out_ref[b * 128:(b + 1) * 128, :] = (x * sc * g).astype(bf16)

def gbst_bwd_body(nbytes, vocab, scal_ref, ids_ref, emb_ref, wcol_ref, score_ref, ggain_ref, put, de_ref, slabs, hook):
    vm = byte_valid_mat(scal_ref, nbytes)
    v, inv = inverse_counts(vm)
    wc = wcol_ref[...]
    w = {b: [wc[:, (b - 1) * 12 + p:(b - 1) * 12 + p + 1] for p in range(12)] for b in (1, 2, 3, 4)}
    s = score_ref[0:1, :]
    E = lambda j: emb_ref[j * ROWS:(j + 1) * ROWS, :].astype(f32)
    s3 = lambda m: E(3 * m) + E(3 * m + 1) + E(3 * m + 2)
    s4 = lambda n: (E(4 * n) + E(4 * n + 1)) + (E(4 * n + 2) + E(4 * n + 3))
    dot = lambda a, b: jnp.sum(a * b, axis=1, keepdims=True)
    dw = {b: [None] * 12 for b in (1, 2, 3, 4)}
    D = []
    for k in range(6):
        dk = 0.5 * get_strided(slabs, k)
        D.append(dk)
        p0, p1 = 2 * k, 2 * k + 1
        x0, x1 = dot(dk, E(p0)), dot(dk, E(p1))
        dw[1][p0], dw[1][p1] = x0, x1
        dw[2][p0] = dw[2][p1] = (x0 + x1) * inv[2][k]
        m0, m1 = p0 // 3, p1 // 3
        a0 = dot(dk, s3(m0)) * inv[3][m0]
        dw[3][p0] = a0
        dw[3][p1] = a0 if m0 == m1 else dot(dk, s3(m1)) * inv[3][m1]
        dw[4][p0] = dw[4][p1] = dot(dk, s4(k // 2)) * inv[4][k // 2]
        if k % 2 == 1:
            hook()
    hook()
    dr = {b: [] for b in (1, 2, 3, 4)}
    for p in range(12):
        mean = w[1][p] * dw[1][p] + w[2][p] * dw[2][p] + w[3][p] * dw[3][p] + w[4][p] * dw[4][p]
        for b in (1, 2, 3, 4):
            dr[b].append(w[b][p] * (dw[b][p] - mean))
    rb = {1: dr[1]}
    for b in (2, 3, 4):
        out = []
        for m in range(12 // b):
            tot = dr[b][b * m]
            for t in range(1, b):
                tot = tot + dr[b][b * m + t]
            out.append(tot * inv[b][m])
        rb[b] = out
    t3 = []
    for m in range(4):
        terms = {}
        for p in (3 * m, 3 * m + 1, 3 * m + 2):
            terms[p // 2] = terms[p // 2] + w[3][p] if p // 2 in terms else w[3][p]
        acc = None
        for k, coef in terms.items():
            t = (coef * inv[3][m]) * D[k]
            acc = t if acc is None else acc + t
        t3.append(acc)
    gscore = jnp.zeros((8, s.shape[1]), f32)
    for n in range(3):
        t4 = ((w[4][4 * n] + w[4][4 * n + 1]) * inv[4][n]) * D[2 * n] + ((w[4][4 * n + 2] + w[4][4 * n + 3]) * inv[4][n]) * D[2 * n + 1]
        for p in range(4 * n, 4 * n + 4):
            k = p // 2
            c = rb[1][p] + rb[2][k] + rb[3][p // 3] + rb[4][n]
            b2 = (w[2][2 * k] + w[2][2 * k + 1]) * inv[2][k]
            de = v[p] * ((w[1][p] + b2) * D[k] + t3[p // 3] + t4 + c * s)
            de_ref[p * ROWS:(p + 1) * ROWS, :] = de.astype(bf16)
            y = c * E(p)
            gscore = gscore + jnp.sum(y.reshape(ROWS // 8, 8, s.shape[1]), axis=0)
        hook()
    gscore = jnp.sum(gscore, axis=0, keepdims=True)
    row = lax.broadcasted_iota(jnp.int32, (VR, ROWS), 0)
    hots = [jnp.where(row == ids_ref[j:j + 1, :], 1.0, 0.0).astype(bf16) for j in range(12)]
    hot = jnp.concatenate(hots, axis=1)
    gtable = nn(hot, de_ref[...])
    row = lax.broadcasted_iota(jnp.int32, gtable.shape, 0)
    for i, extra in enumerate((gscore, ggain_ref[0:1, :], ggain_ref[1:2, :])):
        gtable = jnp.where(row == vocab + i, extra, gtable)
    put(gtable.T.astype(bf16))


MESH = pl.DeviceIdType.MESH


def coords():
    w = lax.axis_index("wide")
    n = lax.axis_index("narrow")
    return w, w // 2, w % 2, n // 2, n % 2


def peer_ids():
    w, z, y, x, c = coords()
    n = 2 * x + c
    return {
        "y": (2 * z + 1 - y, n),
        "zp": (2 * ((z + 1) % 4) + y, n),
        "zm": (2 * ((z + 3) % 4) + y, n),
        "zo": (2 * ((z + 2) % 4) + y, n),
        "x": (w, 2 * (1 - x) + c),
        "c": (w, 2 * x + 1 - c),
        "xc": (w, 2 * (1 - x) + 1 - c),
    }


def enter(peers, names):
    barrier = pltpu.get_barrier_semaphore()
    for name in names:
        pl.semaphore_signal(barrier, inc=1, device_id=peers[name], device_id_type=MESH)
    pl.semaphore_wait(barrier, len(names))


class Gather:
    SENDS = 30
    SLOTS = 28

    def __init__(self, own, fulls, split, ssem, rsem, lsem):
        self.own, self.fulls, self.split = own, fulls, split
        self.r = [f.shape[0] // 8 for f in fulls]
        self.ssem, self.rsem, self.lsem = ssem, rsem, lsem
        self.peers = peer_ids()
        self.w, self.z, self.y, self.x, self.c = coords()
        z = self.z
        first = jnp.where(z == 3, 3, 1)
        second = jnp.where((z == 0) | (z == 3), 2, 3)
        self.order = (first, second, 6 - first - second)
        self.inner = (z == 1) | (z == 2)
        self.sent = []

    def enter(self):
        n = 2 * self.x + self.c
        barrier = pltpu.get_barrier_semaphore()
        near = [(owner, n) for _, owner in self.others()] + [self.peers["x"], self.peers["c"]]
        for peer in near:
            pl.semaphore_signal(barrier, inc=1, device_id=peer, device_id_type=MESH)
        pl.semaphore_wait(barrier, len(near))

    def cols(self, i, c):
        width = self.fulls[i].shape[1] // 2
        return pl.ds(pl.multiple_of(c * width, 128), width)

    def block(self, i, owner, part, ref=None):
        r = self.r[i]
        start = owner * r
        if self.split[i]:
            r = r // 2
            start = start + part[1] * r
        return (self.fulls[i] if ref is None else ref).at[pl.ds(pl.multiple_of(start, 16), r), self.cols(i, part[0])]

    @property
    def mine(self):
        return (self.c, self.x)

    def copy(self, i, out, slot, src, owner, part, device):
        return pltpu.make_async_remote_copy(
            src_ref=src, dst_ref=self.block(i, owner, part), send_sem=self.ssem.at[i, out],
            recv_sem=self.rsem.at[i, slot], device_id=device, device_id_type=MESH)

    def send(self, i, out, slot, owner, part, device, when=None, src=None):
        src = self.block(i, owner, part) if src is None else src
        cp = self.copy(i, out, slot, src, owner, part, device)
        if when is None:
            cp.start()
        else:
            pl.when(when)(cp.start)
        self.sent.append((i, out, when))

    def arrived(self, i, slot, owner, part):
        ref = self.block(i, owner, part)
        pltpu.make_async_remote_copy(
            src_ref=ref, dst_ref=ref, send_sem=self.ssem.at[i, 0], recv_sem=self.rsem.at[i, slot],
            device_id=self.peers["c"], device_id_type=MESH).wait_recv()

    def local(self, i):
        at = pl.ds(pl.multiple_of(self.w * self.r[i], 16), self.r[i])
        return pltpu.make_async_copy(self.own[i], self.fulls[i].at[at, :], self.lsem.at[i])

    def start_direct(self, i):
        n = 2 * self.x + self.c
        for k in range(1, 8):
            dz, dy = k // 2, k % 2
            to = (2 * lax.rem(self.z + dz, 4) + (1 - self.y if dy else self.y), n)
            self.send_rows(i, k, (4 - dz) % 4 * 2 + dy, self.w, self.c, to, self.half_rows(i, 0, self.c, self.own[i]))
        self.local(i).start()

    def half_rows(self, i, owner, c, ref=None):
        r = self.r[i]
        return (self.fulls[i] if ref is None else ref).at[pl.ds(pl.multiple_of(owner * r + c * (r // 2), 16), r // 2), :]

    def send_rows(self, i, out, slot, owner, c, device, src=None):
        ref = self.half_rows(i, owner, c)
        cp = pltpu.make_async_remote_copy(
            src_ref=ref if src is None else src, dst_ref=ref, send_sem=self.ssem.at[i, out], recv_sem=self.rsem.at[i, slot],
            device_id=device, device_id_type=MESH)
        cp.start()
        self.sent.append((i, out, "rows"))

    def rows_arrived(self, i, slot, owner, c):
        ref = self.half_rows(i, owner, c)
        pltpu.make_async_remote_copy(
            src_ref=ref, dst_ref=ref, send_sem=self.ssem.at[i, 0], recv_sem=self.rsem.at[i, slot],
            device_id=self.peers["c"], device_id_type=MESH).wait_recv()

    def others(self):
        for k in range(1, 8):
            dz, dy = k // 2, k % 2
            yield k, 2 * lax.rem(self.z + dz, 4) + (1 - self.y if dy else self.y)

    def steps_direct(self, i):
        def relay():
            for k, owner in self.others():
                self.rows_arrived(i, k, owner, self.c)
                self.send_rows(i, 8 + k, 8 + k, owner, self.c, self.peers["c"])

        def end():
            for k, owner in self.others():
                self.rows_arrived(i, 8 + k, owner, 1 - self.c)
            self.local(i).wait()
        return [relay, end]

    def start(self, i):
        n = 2 * self.x + self.c
        own = self.block(i, 0, self.mine, self.own[i])
        self.send(i, 0, 2, self.w, self.mine, (2 * jnp.minimum(self.z + 1, 3) + self.y, n), self.z < 3, own)
        self.send(i, 1, 0, self.w, self.mine, (2 * jnp.maximum(self.z - 1, 0) + self.y, n), self.z > 0, own)
        self.send(i, 5, 3, self.w, self.mine, self.peers["y"], None, own)
        self.local(i).start()

    def relay(self, i, s, n, owner):
        self.send(i, 9 + n, 7 + s, owner, self.mine, self.peers["c"])
        if self.split[i]:
            self.send(i, 16 + n, 14 + s, owner, self.mine, self.peers["x"])

    def step_z(self, i, j):
        d = self.order[j]
        o = lax.rem(self.z + d, 4)
        owner = 2 * o + self.y
        self.arrived(i, d - 1, owner, self.mine)
        to = jnp.where(self.inner, jnp.where(o < self.z, self.z + 1, self.z - 1), jnp.where(self.z == 0, 1, 2))
        slot = jnp.where(self.inner, lax.rem(o - to + 4, 4) - 1, 0)
        self.send(i, 2 + j, slot, owner, self.mine, (2 * to + self.y, 2 * self.x + self.c), self.inner)
        self.send(i, 6 + j, 3 + d, owner, self.mine, self.peers["y"])
        self.relay(i, d - 1, j, owner)

    def step_y(self, i, j):
        d = 0 if j < 0 else self.order[j]
        owner = 2 * lax.rem(self.z + d, 4) + 1 - self.y
        self.arrived(i, 3 + d, owner, self.mine)
        self.relay(i, 3 + d, 4 + j, owner)

    def each(self):
        for j in range(3):
            d = self.order[j]
            yield d - 1, j, 2 * lax.rem(self.z + d, 4) + self.y
        for j in range(-1, 3):
            d = 0 if j < 0 else self.order[j]
            yield 3 + d, 4 + j, 2 * lax.rem(self.z + d, 4) + 1 - self.y

    def step_x(self, i):
        if self.split[i]:
            other = (self.c, 1 - self.x)
            for s, n, owner in self.each():
                self.arrived(i, 14 + s, owner, other)
                self.send(i, 23 + n, 21 + s, owner, other, self.peers["c"])

    def step_end(self, i):
        for s, n, owner in self.each():
            self.arrived(i, 7 + s, owner, (1 - self.c, self.x))
            if self.split[i]:
                self.arrived(i, 21 + s, owner, (1 - self.c, 1 - self.x))
        self.local(i).wait()

    def finish(self):
        for i, out, when in self.sent:
            if isinstance(when, str):
                ref = self.half_rows(i, self.w, self.c)
                when = None
            else:
                ref = self.block(i, self.w, self.mine)
            cp = pltpu.make_async_remote_copy(
                src_ref=ref, dst_ref=ref, send_sem=self.ssem.at[i, out], recv_sem=self.rsem.at[i, 0],
                device_id=self.peers["c"], device_id_type=MESH)
            if when is None:
                cp.wait_send()
            else:
                pl.when(when)(cp.wait_send)

    def steps(self, i):
        return [functools.partial(self.step_y, i, -1)] + [functools.partial(f, i, j) for j in range(3) for f in (self.step_z, self.step_y)] + [
            functools.partial(self.step_x, i), functools.partial(self.step_end, i)]


class Reduce:
    SLOTS = 9

    def __init__(self, terms, outs, order, rc, r1, r2, r3, ssem, rsem):
        self.terms, self.outs, self.order = terms, outs, order
        self.rc, self.r1, self.r2, self.r3 = rc, r1, r2, r3
        self.ssem, self.rsem = ssem, rsem
        self.peers = peer_ids()
        self.w, self.z, self.y, self.x, self.c = coords()
        self.sent = []

    def enter(self):
        enter(self.peers, ("y", "zp", "zm", "zo", "x", "c", "xc"))

    def transfer(self, i, slot, src, dst, to):
        return pltpu.make_async_remote_copy(
            src_ref=src, dst_ref=dst, send_sem=self.ssem.at[i, slot], recv_sem=self.rsem.at[i, slot],
            device_id=self.peers[to], device_id_type=MESH)

    def send(self, i, slot, src, dst, to):
        self.transfer(i, slot, src, dst, to).start()
        self.sent.append((i, slot))

    def arrived(self, i, slot, dst):
        self.transfer(i, slot, dst, dst, "c").wait_recv()

    def half(self, i, c):
        width = self.terms[i].shape[4] // 2
        return pl.ds(pl.multiple_of(c * width, 128), width)

    def start(self, i):
        self.send(i, 0, self.terms[i].at[:, :, :, :, self.half(i, 1 - self.c)], self.rc[i], "c")

    def add(self, a, b):
        return a + b

    def step_core(self, i):
        self.arrived(i, 0, self.rc[i])

        def one(z, carry):
            self.rc[i][z] = self.add(self.terms[i][z, :, :, :, self.half(i, self.c)], self.rc[i][z])
            return carry
        lax.fori_loop(0, 4, one, 0)
        if self.order[i] == "y":
            self.send(i, 1, self.rc[i].at[:, 1 - self.y], self.r1[i], "y")
        else:
            self.send(i, 1, self.rc[i].at[:, :, 1 - self.x], self.r1[i], "x")

    def step_one(self, i):
        self.arrived(i, 1, self.r1[i])

        def one(z, carry):
            if self.order[i] == "y":
                mine = self.rc[i][z, self.y]
            else:
                mine = self.rc[i][z, :, self.x]
            self.r1[i][z] = self.add(mine, self.r1[i][z])
            return carry
        lax.fori_loop(0, 4, one, 0)
        if self.order[i] == "y":
            self.send(i, 2, self.r1[i].at[:, 1 - self.x], self.r2[i], "x")
        else:
            self.send(i, 2, self.r1[i].at[:, 1 - self.y], self.r2[i], "y")

    def step_two(self, i):
        self.arrived(i, 2, self.r2[i])
        pick = self.x if self.order[i] == "y" else self.y

        def one(z, carry):
            self.r2[i][z] = self.add(self.r1[i][z, pick], self.r2[i][z])
            return carry
        lax.fori_loop(0, 4, one, 0)
        for dz, to in ((1, "zp"), (3, "zm"), (2, "zo")):
            self.send(i, 2 + dz, self.r2[i].at[lax.rem(self.z + dz, 4)], self.r3[i].at[3 - dz], to)

    def step_z(self, i):
        total = self.r2[i][self.z].astype(f32)
        for dz in (1, 3, 2):
            self.arrived(i, 2 + dz, self.r3[i].at[3 - dz])
        for k in range(3):
            total = total + self.r3[i][k].astype(f32)
        out = self.outs[i]
        out[self.c, self.x] = total.astype(bf16)
        for slot, to in ((6, "x"), (7, "c"), (8, "xc")):
            self.send(i, slot, out.at[self.c, self.x], out.at[self.c, self.x], to)

    def step_end(self, i):
        out = self.outs[i]
        self.arrived(i, 6, out.at[self.c, 1 - self.x])
        self.arrived(i, 7, out.at[1 - self.c, self.x])
        self.arrived(i, 8, out.at[1 - self.c, 1 - self.x])

    def steps(self, i):
        return [functools.partial(f, i) for f in (self.step_core, self.step_one, self.step_two, self.step_z, self.step_end)]

    def finish(self):
        for i, slot in self.sent:
            block = self.r2[i].at[0]
            ref = {0: self.rc[i], 1: self.r1[i], 2: self.r2[i]}.get(slot, block)
            self.transfer(i, slot, ref, ref, "c").wait_send()

    @staticmethod
    def scratch(shapes):
        rc = [pltpu.VMEM((4, 2, 2, s[3], s[4] // 2), bf16) for s in shapes]
        r1 = [pltpu.VMEM((4, 2, s[3], s[4] // 2), bf16) for s in shapes]
        r2 = [pltpu.VMEM((4, s[3], s[4] // 2), bf16) for s in shapes]
        r3 = [pltpu.VMEM((3, s[3], s[4] // 2), bf16) for s in shapes]
        n = len(shapes)
        return rc + r1 + r2 + r3 + [pltpu.SemaphoreType.DMA((n, 9)), pltpu.SemaphoreType.DMA((n, 9))]


SMALL = (16, 128)


class SmallSum:
    HOPS = ("c", "x", "y", "zn", "zo")

    def __init__(self, acc, slots, ssem, rsem):
        self.acc, self.slots, self.ssem, self.rsem = acc, slots, ssem, rsem
        self.peers = peer_ids()
        w, z, y, x, c = coords()
        self.peers["zn"] = (2 * (z + 1 - 2 * (z % 2)) + y, 2 * x + c)

    def copy(self, k):
        return pltpu.make_async_remote_copy(
            src_ref=self.slots.at[5 + k], dst_ref=self.slots.at[k], send_sem=self.ssem.at[k], recv_sem=self.rsem.at[k],
            device_id=self.peers[self.HOPS[k]], device_id_type=MESH)

    def step(self, k):
        if k:
            self.copy(k - 1).wait()
            self.acc[...] = self.acc[...] + self.slots[k - 1]
        if k < 5:
            self.slots[5 + k] = self.acc[...]
            self.copy(k).start()

    def steps(self):
        return [functools.partial(self.step, k) for k in range(6)]


def none():
    pass


class Feed:
    def __init__(self, steps, share=1):
        self.steps = list(steps)
        self.share = share

    def __call__(self):
        for _ in range(self.share):
            if self.steps:
                self.steps.pop(0)()

    def rest(self):
        while self.steps:
            self.steps.pop(0)()


def forward_kernel(nbytes, vocab, split, *refs):
    bucket_ref, lengths_ref, ids_ref, rel_ref = refs[:4]
    scal_ref = Flags(bucket_ref, lengths_ref)
    n_in = 2 if split is None else 9
    given, refs = refs[4:4 + n_in], refs[4 + n_in:]
    fulls, outs = refs[:3], refs[3:14]
    stream_o, normed_o, emb_o, wcol_o, tot_o, vec_o, q_o, k_o, v_o, mixed_o, lse_o = outs
    (tt, wq, wk, wv, stream, normed, emb, wcol, tot, vec, q, k, v, mixed, lse, slabs, table, kaug, raug, strip, vt, base_ref, osem, wsem) = refs[14:38]
    done = []

    def out(src, dst):
        cp = pltpu.make_async_copy(src, dst, osem.at[len(done)])
        cp.start()
        done.append(cp)

    ntok = nbytes // 2
    d = q.shape[1]
    if split is not None:
        wide_t, own_t, own_p, own_f, own_d = refs[38:43]
        emb_ref, vecs_ref, sq, sk, sv, so, sg, su, sd = given
        rd = sd.shape[0]
        g = Gather([own_t, own_p, own_f, own_d], [tt] + list(fulls), split, *refs[43:46])
        r = own_t.shape[0]
        wide_t[...] = jnp.zeros_like(wide_t)
        wide_t[0:vocab, 0:r] = emb_ref[...].astype(f32)
        wide_t[vocab:vocab + 3, 0:r] = vecs_ref[...].astype(f32)
        own_t[...] = wide_t[...].T[0:r].astype(bf16)
        g.enter()
        g.start_direct(0)
        for m, part in enumerate((sq, sk, sv)):
            own_p[:, m * d:(m + 1) * d] = part[...]
        for m, part in enumerate((sg, su)):
            own_f[:, m * part.shape[1]:(m + 1) * part.shape[1]] = part[...]
        own_d[0:rd, :] = sd[...]
        own_d[rd:, :] = so[...]
        g.start(1)
        build_masks(scal_ref, kaug, raug, ntok)
        bias_rows(rel_ref, base_ref)
        relay, end = g.steps_direct(0)
        plans = [None] + [g.steps(i) for i in (1, 2, 3)]
        relay()
        for s in range(3):
            plans[1][s]()
        end()
        begin = [functools.partial(g.start, i) for i in (2, 3)]
        early = Feed(plans[1][3:6] + begin + plans[1][6:8] + [plans[i][s] for s in range(FEW) for i in (2, 3)], SHARE)
        late = [plans[i][s] for s in range(FEW, 8) for i in (2, 3)]
        per = -(-len(late) // 12)
        chunks = [late[j * per:(j + 1) * per] for j in range(12)]
    else:
        cp = pltpu.make_async_copy(given[0], tt, wsem.at[3])
        cp.start()
        build_masks(scal_ref, kaug, raug, ntok)
        bias_rows(rel_ref, base_ref)
        cp.wait()
        early = Feed([])
        chunks = [[]] * 12
    gbst_fwd_body(nbytes, vocab, scal_ref, ids_ref, tt, stream, normed, emb, wcol, tot, vec, slabs, table, early)
    early.rest()
    for src, dst in ((stream, stream_o), (normed, normed_o), (emb, emb_o), (wcol, wcol_o), (tot, tot_o), (vec, vec_o)):
        out(src, dst)
    loads = []
    for i, dst in enumerate((wq, wk, wv)):
        if split is not None and i == 0:
            plans[1][8]()
        cp = pltpu.make_async_copy((given[1] if split is None else fulls[0]).at[:, i * d:(i + 1) * d], dst, wsem.at[i])
        cp.start()
        loads.append(cp)
    for cp, w, dst, to in zip(loads, (wq, wk, wv), (q, k, v), (q_o, k_o, v_o)):
        cp.wait()
        for c in range(d // 256):
            cs = slice(c * 256, (c + 1) * 256)
            dst[:, cs] = nn(normed[...], w[:, cs]).astype(bf16)
        out(dst, to)

    def pair(p, carry):
        def hook(b):
            if b % 3 == 0:
                for j in range(6):
                    part = chunks[2 * j + b // 3]
                    if part:
                        @pl.when(p == j)
                        def _():
                            for step in part:
                                step()
        fwd_pair(p, q, k, v, base_ref, mixed, lse, kaug, raug, strip, vt, hook)
        return carry
    lax.fori_loop(0, d // 128, pair, 0)
    out(mixed, mixed_o)
    out(lse, lse_o)
    if split is not None:
        for i in (2, 3):
            plans[i][8]()
        g.finish()
    for cp in done:
        cp.wait()


FEW, SHARE = 3, 1


def forward_one(bucket, lengths, ids, rel, given, vocab, nbytes, wide, split):
    d = given[1].shape[0] if split is None else given[2].shape[1]
    hbm = pl.BlockSpec(memory_space=pltpu.HBM)
    vm = pl.BlockSpec(memory_space=pltpu.VMEM)
    sm = pl.BlockSpec(memory_space=pltpu.SMEM)
    pairs = d // 128
    sd = jax.ShapeDtypeStruct
    acts = [((TP, d), f32), ((TP, d), bf16), ((12 * ROWS, d), bf16), ((ROWS, 128), f32), ((8, 128), f32), ((8, d), f32),
            ((TP, d), bf16), ((TP, d), bf16), ((TP, d), bf16), ((TP, d), bf16), ((pairs, 8, 256), f32)]
    scratch = [pltpu.VMEM((d, VP), bf16)] + [pltpu.VMEM((d, d), bf16)] * 3 + [pltpu.VMEM(*a) for a in acts]
    scratch += [pltpu.VMEM((d // 128, TP, 128), f32), pltpu.VMEM((VP, d), bf16), pltpu.VMEM((TP, 128), bf16), pltpu.VMEM((NB, 256, 128), bf16),
                pltpu.VMEM((STRIP, 256), f32), pltpu.VMEM((128, TP), bf16), pltpu.VMEM((16, 512), f32), pltpu.SemaphoreType.DMA((11,)), pltpu.SemaphoreType.DMA((4,))]
    params = dict(vmem_limit_bytes=56 << 20)
    if split is not None:
        r, ff, rd = given[2].shape[0], given[6].shape[1], given[8].shape[0]
        scratch += [pltpu.VMEM((VP, 128), f32), pltpu.VMEM((r, VP), bf16), pltpu.VMEM((r, 3 * d), bf16), pltpu.VMEM((r, 2 * ff), bf16), pltpu.VMEM((rd + r, d), bf16)]
        scratch += [pltpu.SemaphoreType.DMA((4, Gather.SENDS)), pltpu.SemaphoreType.DMA((4, Gather.SLOTS)), pltpu.SemaphoreType.DMA((4,))]
        params.update(collective_id=1, has_side_effects=True)
        whole = [sd((wide * r, 3 * d), bf16), sd((wide * r, 2 * ff), bf16), sd((wide * (rd + r), d), bf16)]
    else:
        whole = [sd((16, 128), bf16)] * 3
    return pl.pallas_call(
        functools.partial(forward_kernel, nbytes, vocab, split),
        out_shape=tuple(whole) + tuple(sd(*a) for a in acts),
        in_specs=[sm, sm, vm, vm] + ([hbm] * 2 if split is None else [vm] * 9),
        out_specs=(hbm,) * 14,
        scratch_shapes=scratch,
        compiler_params=pltpu.CompilerParams(**params),
        name="forward_one",
    )(bucket, lengths, ids, rel, *given)


FCH = 256
FRB = 256
GELU = 0.7978845608028654


def flat(ref, cs=slice(None)):
    return ref[:, :, :, :, cs].reshape(ref.shape[0] * 4 * ref.shape[3], -1)


def norm_scale(x):
    return lax.rsqrt(jnp.mean(x * x, axis=1, keepdims=True) + EPS)


def row_block(b):
    return pl.ds(pl.multiple_of(b * FRB, FRB), FRB)


def store_product(dst, tr, rhs):
    rows = dst.shape[0] * 4 * dst.shape[3]
    parts = -(-rows // 1024)
    size = dst.shape[0] // parts
    wide = 256
    for m in range(parts):
        left = tr[m * rows // parts:(m + 1) * rows // parts, :]
        for c in range(dst.shape[4] // wide):
            cs = slice(c * wide, (c + 1) * wide)
            r = nn(left, rhs[:, cs]).astype(bf16)
            dst[m * size:(m + 1) * size, :, :, :, cs] = r.reshape((size,) + dst.shape[1:4] + (wide,))


def ff_phase(gu_h, do_h, mixed_h, stream_h, og_h, enc_o, g2, wo, wf, wd, stream, mid, gh_out, ggain2, sems, ready, poll):
    d = mid.shape[1]
    halves = len(wf)
    part = wf[0].shape[4] // 2

    def scoped(hid, gg, gu, tr, mixed, og, nff, dacc):
        ins = []
        ro, rd = wo.shape[3], wd.shape[3]
        ff = halves * part
        pairs = [(mixed_h, mixed)] + [(do_h.at[:, :, 2 * rd + x * ro:2 * rd + (x + 1) * ro], wo.at[:, :, x]) for x in range(2)]
        pairs += [(stream_h, stream)]
        for h in range(halves):
            at = h * part
            pairs += [(gu_h.at[:, :, :, :, at:at + part], wf[h].at[:, :, :, :, part:2 * part]), (gu_h.at[:, :, :, :, ff + at:ff + at + part], wf[h].at[:, :, :, :, 0:part])]
            if h == 0:
                pairs += [(do_h.at[:, :, x * rd:(x + 1) * rd], wd.at[:, :, x]) for x in range(2)]
        for n, (s, t) in enumerate(pairs):
            cp = pltpu.make_async_copy(s, t, sems.at[n])
            cp.start()
            ins.append(cp)
        for cp in ins[:4]:
            cp.wait()

        def first(b, carry):
            sl = row_block(b)
            middle = stream[sl, :] + nn(mixed[sl, :], flat(wo))
            dacc[sl, :] = middle
            nff[sl, :] = (middle * norm_scale(middle) * g2).astype(bf16)
            return carry
        lax.fori_loop(0, TP // FRB, first, 0)
        tr[0:d, :] = nff[...].T
        ntok = og_h.shape[0]
        og[...] = jnp.concatenate([og_h[...].astype(f32), jnp.zeros((TP - ntok, d), f32)], axis=0).astype(bf16)
        for cp in ins[4:8]:
            cp.wait()
        for h in range(halves):
            if h:
                for cp in ins[8:]:
                    cp.wait()

            for c in range(part // FCH):
                poll(h, c)
                cs = slice(c * FCH, (c + 1) * FCH)
                at = slice(h * part + c * FCH, h * part + (c + 1) * FCH)
                wuc, wgc = flat(wf[h], cs), flat(wf[h], slice(part + c * FCH, part + (c + 1) * FCH))
                wdc = wd[(h * part + c * FCH) // 512, c % 2].reshape(FCH, d)
                gate = nn(nff[...], wgc)
                up = nn(nff[...], wuc)
                gh = nt(og[...], wdc)
                sq = gate * gate
                th = jnp.tanh(gate * (GELU + (GELU * 0.044715) * sq))
                half = 0.5 + 0.5 * th
                act = gate * half
                hid[:, at] = (act * up).astype(bf16)
                dact = half + (0.5 * gate) * (1.0 - th * th) * (GELU + (3 * GELU * 0.044715) * sq)
                gg[:, cs] = (gh * up * dact).astype(bf16)
                gu[:, cs] = (gh * act).astype(bf16)
                dacc[...] += nn(hid[:, at], wdc)
                if h == 0 and c == 0:
                    mid[...] = nt(gg[:, cs], wgc)
                else:
                    mid[...] += nt(gg[:, cs], wgc)
                mid[...] += nt(gu[:, cs], wuc)
            store_product(wf[h].at[:, :, :, :, 0:part], tr.at[0:d], gu)
            store_product(wf[h].at[:, :, :, :, part:2 * part], tr.at[0:d], gg)
            ready("f%d" % h)

        tr[...] = hid[...].T
        store_product(wd, tr, og)
        ready("d")

        def last(b, carry):
            sl = row_block(b)
            wo_all = flat(wo)
            middle = stream[sl, :] + nn(mixed[sl, :], wo_all)
            s2 = norm_scale(middle)
            back = mid[sl, :]
            t = back * g2
            xs = middle * s2
            grad = og[sl, :].astype(f32) + s2 * t - xs * (s2 * s2 * jnp.mean(middle * t, axis=1, keepdims=True))
            mid[sl, :] = grad
            low = grad.astype(bf16)
            gu[sl, 0:d] = low
            gh_out[sl, :] = nt(low, wo_all).astype(bf16)
            ggain2[...] += jnp.sum((back * xs).reshape(FRB // 8, 8, d), axis=0)
            return carry
        lax.fori_loop(0, TP // FRB, last, 0)
        enc_o[...] = dacc[0:enc_o.shape[0], :].astype(bf16)
        tr[0:d, :] = mixed[...].T
        store_product(wo, tr.at[0:d], gu)
        ready("o")
    act = lambda c: pltpu.VMEM((TP, c), bf16)
    pl.run_scoped(scoped, act(halves * part), act(part), act(part), pltpu.VMEM((halves * part, TP), bf16), act(d), act(d), act(d), pltpu.VMEM((TP, d), f32))


NAMES = ("t", "p0", "p1", "p2", "o", "f0", "f1", "d")
FIRST = {"t": "x", "p0": "x", "p1": "y", "p2": "x", "o": "x", "f0": "y", "f1": "x", "d": "y"}
STEPS = ("core", "one", "two", "z", "end")


def backward_kernel(nbytes, vocab, remote, *refs):
    n = len(NAMES)
    bucket_ref, lengths_ref, ids_ref, rel_ref, vec_ref, wcol_ref, tot_ref, lse_ref = refs[:8]
    scal_ref = Flags(bucket_ref, lengths_ref)
    q_h, k_h, v_h, normed_h, stream_h, mixed_h, og_h, emb_h, qkv_h, gu_h, do_h = refs[8:19]
    enc_o, outs, small_o = refs[19], refs[20:20 + n], refs[20 + n]
    refs = refs[21 + n:]
    stream, mid, g, ggain2, ggain, base_ref, fsem, lsem = refs[:8]
    refs = refs[1:]
    bias_rows(rel_ref, base_ref)
    if remote:
        terms = refs[7:7 + n]
        rest = refs[7 + n:]
        red = Reduce(terms, outs, tuple(FIRST[k] for k in NAMES), *[rest[k * n:(k + 1) * n] for k in range(4)], *rest[4 * n:4 * n + 2])
        small = SmallSum(*rest[4 * n + 2:4 * n + 6])
        st = {k: dict(zip(STEPS, red.steps(i))) for i, k in enumerate(NAMES)}
        st["s"] = {k: f for k, f in enumerate(small.steps())}
        red.enter()
    else:
        terms = outs
    term = dict(zip(NAMES, terms))

    def run(words):
        if remote:
            for word in words:
                name, step = word.split(".")
                st[name][int(step) if name == "s" else step]()

    def point(key):
        run(TABLE.get(key, ()))

    def ready(name):
        if remote:
            red.start(NAMES.index(name))
            point(name)

    def point_at(index, keys):
        for j, key in enumerate(keys):
            if remote and TABLE.get(key):
                @pl.when(index == j)
                def _():
                    point(key)

    def poll(h, c):
        point("c%d%d" % (h, c))
    ggain2[...] = jnp.zeros_like(ggain2)
    ff_phase(gu_h, do_h, mixed_h, stream_h, og_h, enc_o, vec_ref[2:3, :], term["o"], (term["f0"], term["f1"]), term["d"],
             stream, mid, g, ggain2, fsem, ready, poll)
    d = stream.shape[1]
    pairs = d // 128

    def scoped(q, k, v, nt_s, emb, wq, wk, wv):
        copies = []
        moves = ((q_h, q), (k_h, k), (v_h, v), (normed_h, nt_s), (emb_h, emb), *((qkv_h.at[:, m * d:(m + 1) * d], w) for m, w in enumerate((wq, wk, wv))))
        for m, (s, t) in enumerate(moves):
            cp = pltpu.make_async_copy(s, t, lsem.at[m])
            cp.start()
            copies.append(cp)
        for cp in copies[:4]:
            cp.wait()
        nt_s[...] = nt_s[...].T

        def attention(kaug, raug, strip, acc, kt, dk_s, dv_s, db):
            build_masks(scal_ref, kaug, raug, nbytes // 2)
            db[...] = jnp.zeros_like(db)
            def pair(p, carry):
                def hook(b):
                    if b % 3 == 0:
                        point_at(p, ["a%d%d" % (j, b // 3) for j in range(pairs)])
                bwd_pair(p, q, k, v, g, lse_ref, base_ref, db, kaug, raug, strip, acc, kt, dk_s, dv_s, hook)
                for j in range(pairs // 2):
                    @pl.when(p == 2 * j + 1)
                    def _():
                        dst = term["p%d" % j]
                        for m, src in enumerate((q, k, v)):
                            r = nn(nt_s[...], src[:, 256 * j:256 * (j + 1)]).astype(bf16)
                            dst[:, :, :, :, 256 * m:256 * (m + 1)] = r.reshape(dst.shape[:4] + (256,))
                        ready("p%d" % j)
                return carry
            lax.fori_loop(0, pairs, pair, 0)
            relt = lax.dot_general(db[...], bucket_hot(), (((1,), (0,)), ((), ())), precision=lax.Precision.HIGHEST, preferred_element_type=f32)
            row = lax.broadcasted_iota(jnp.int32, SMALL, 0)
            total = jnp.where(row == SMALL[0] - 1, tot_ref[0:1, :], relt)
            if remote:
                small.acc[...] = total
            else:
                small_o[...] = total
        strips = pltpu.VMEM((STRIP, 256), f32)
        pl.run_scoped(attention, pltpu.VMEM((TP, 128), bf16), pltpu.VMEM((NB, 256, 128), bf16), strips, strips, pltpu.VMEM((128, TP), bf16),
                      pltpu.VMEM((TP, 128), f32), pltpu.VMEM((TP, 128), f32), pltpu.VMEM((16, 512), f32))
        for cp in copies[4:]:
            cp.wait()

        def pooling(slabs, de):
            count = []

            def hook():
                point("h%d" % len(count))
                count.append(0)
            hook()
            ggain[...] = jnp.zeros_like(ggain)
            gain = vec_ref[1:2, :]

            def rows(b, carry):
                sl = row_block(b)
                gy = nt(q[sl, :], wq[...]) + nt(k[sl, :], wk[...]) + nt(v[sl, :], wv[...])
                x = stream[sl, :]
                s = norm_scale(x)
                t = gy * gain
                gs = mid[sl, :] + s * t - x * (s * s * s * jnp.mean(x * t, axis=1, keepdims=True))
                for c in range(d // 128):
                    slabs[c, sl, :] = gs[:, c * 128:(c + 1) * 128]
                ggain[...] += jnp.sum((gy * x * s).reshape(FRB // 8, 8, d), axis=0)
                return carry
            lax.fori_loop(0, TP // FRB, rows, 0)
            ggain[0:2, :] = jnp.concatenate([jnp.sum(ggain[...], axis=0, keepdims=True), jnp.sum(ggain2[...], axis=0, keepdims=True)], axis=0)
            hook()

            def put(gt):
                dst = term["t"]
                half = dst.shape[3]
                for zz in range(dst.shape[0]):
                    for yy in range(2):
                        for xx in range(2):
                            top = ((zz * 2 + yy) * 2 + xx) * half
                            dst[zz, yy, xx, :, 0:VR] = gt[top:top + half]
                            dst[zz, yy, xx, :, VR:VG] = jnp.zeros((half, VG - VR), bf16)
            gbst_bwd_body(nbytes, vocab, scal_ref, ids_ref, emb, wcol_ref, vec_ref, ggain, put, de, slabs, hook)
            if remote:
                ready("t")
        pl.run_scoped(pooling, pltpu.VMEM((d // 128, TP, 128), f32), pltpu.VMEM((12 * ROWS, d), bf16))
    act = pltpu.VMEM((TP, d), bf16)
    mat = pltpu.VMEM((d, d), bf16)
    pl.run_scoped(scoped, act, act, act, act, pltpu.VMEM((12 * ROWS, d), bf16), mat, mat, mat)
    if remote:
        point("end")
        small_o[...] = small.acc[...]
        red.finish()


TABLE = {
    "c13": ("f0.core",),
    "o": ("f1.core",),
    "a00": ("d.core", "o.core", "f0.one",),
    "a30": ("p0.core", "d.one", "f1.one",),
    "a31": ("o.one",),
    "a50": ("p1.core", "f0.two", "f1.two", "o.two",),
    "p2": ("p0.one",),
    "h0": ("p1.one",),
    "h1": ("p2.core", "s.0", "f0.z", "d.two", "p0.two",),
    "h2": ("s.1",),
    "h3": ("p1.two",),
    "h6": ("f1.z",),
    "h7": ("p2.one",),
    "h8": ("o.z",),
    "t": ("s.2",),
    "end": ("p2.two", "f0.end", "t.core", "s.3", "f1.end", "d.z", "o.end", "p0.z",
            "t.one", "p1.z", "t.two", "d.end", "s.4", "p2.z", "p0.end", "p1.end",
            "s.5", "t.z", "p2.end", "t.end",),
}


def backward_one(bucket, lengths, ids, rel, vec, wcol, tot, lse, acts, weights, vocab, nbytes, remote):
    d = acts[0].shape[1]
    hbm = pl.BlockSpec(memory_space=pltpu.HBM)
    vm = pl.BlockSpec(memory_space=pltpu.VMEM)
    sd = jax.ShapeDtypeStruct
    view = lambda r, c: (4, 2, 2, r // 16, c)
    qkv, gu, do = weights
    ff = gu.shape[1] // 2
    sm = pl.BlockSpec(memory_space=pltpu.SMEM)
    shapes = [view(d, VG)] + [view(d, d)] * 4 + [view(d, ff)] * 2 + [view(ff, d)]
    scratch = [pltpu.VMEM((TP, d), f32), pltpu.VMEM((TP, d), f32), pltpu.VMEM((TP, d), bf16), pltpu.VMEM((8, d), f32), pltpu.VMEM((8, d), f32),
               pltpu.VMEM((16, 512), f32), pltpu.SemaphoreType.DMA((11,)), pltpu.SemaphoreType.DMA((8,))]
    params = dict(vmem_limit_bytes=62 << 20)
    if remote:
        outs = [sd((2, 2, s[3], s[4] // 2), bf16) for s in shapes]
        scratch += [pltpu.VMEM(s, bf16) for s in shapes] + Reduce.scratch(shapes)
        scratch += [pltpu.VMEM(SMALL, f32), pltpu.VMEM((10,) + SMALL, f32), pltpu.SemaphoreType.DMA((5,)), pltpu.SemaphoreType.DMA((5,))]
        params.update(collective_id=2, has_side_effects=True)
    else:
        outs = [sd(s, bf16) for s in shapes]
    return pl.pallas_call(
        functools.partial(backward_kernel, nbytes, vocab, remote),
        out_shape=(sd(acts[6].shape, bf16), *outs, sd(SMALL, f32)),
        in_specs=[sm, sm] + [vm] * 6 + [hbm] * 6 + [vm] + [hbm] * 4,
        out_specs=(vm,) * (len(outs) + 2),
        scratch_shapes=scratch,
        compiler_params=pltpu.CompilerParams(**params),
        name="backward_one",
    )(bucket, lengths, ids, rel, vec, wcol, tot, lse, *acts, qkv, gu.reshape(view(*gu.shape)), do.reshape(4, 2, -1, d))


def finish_kernel(vocab, heads, buckets, *refs):
    ins, small_ref = dict(zip(NAMES, refs[:len(NAMES)])), refs[len(NAMES)]
    table_o, score_o, gain1_o, q_o, k_o, v_o, o_o, rel_o, gain2_o, gate_o, up_o, down_o, share_o = refs[len(NAMES) + 1:]

    def place(dst, src, left):
        half, width = src.shape[2], src.shape[3]
        for c in range(2):
            for x in range(2):
                dst[x * half:(x + 1) * half, left + c * width:left + (c + 1) * width] = src[c, x].astype(f32)
    place(o_o, ins["o"], 0)
    place(down_o, ins["d"], 0)
    for h in range(2):
        src = ins["f%d" % h]
        half, width = src.shape[2], src.shape[3]
        for c, dst in enumerate((up_o, gate_o)):
            for x in range(2):
                dst[x * half:(x + 1) * half, h * width:(h + 1) * width] = src[c, x].astype(f32)
    for j in range(3):
        src = ins["p%d" % j]
        half = src.shape[2]
        for piece in range(6):
            c, m = piece // 3, piece % 3
            dst = (q_o, k_o, v_o)[piece // 2]
            left = 256 * j + 128 * (piece % 2)
            for x in range(2):
                dst[x * half:(x + 1) * half, left:left + 128] = src[c, x, :, 128 * m:128 * (m + 1)].astype(f32)
    t = ins["t"]
    rows = jnp.concatenate([jnp.concatenate([t[c, x] for x in range(2)], axis=0) for c in range(2)], axis=1).astype(f32)
    turned = rows.T
    table_o[...] = turned[:vocab]
    score_o[...] = turned[vocab:vocab + 1]
    gain1_o[...] = turned[vocab + 1:vocab + 2]
    gain2_o[...] = turned[vocab + 2:vocab + 3]
    small = small_ref[...]
    rel_o[...] = small.T[:buckets, :heads]
    last = small[SMALL[0] - 1:SMALL[0], :]
    share_o[...] = last[:, 0:4] / last[:, 4:5]


def finish(outs, vocab, heads, buckets):
    vm = pl.BlockSpec(memory_space=pltpu.VMEM)
    sd = lambda *s: jax.ShapeDtypeStruct(s, f32)
    r = 2 * outs[1].shape[2]
    d = 2 * outs[1].shape[3]
    ff = 2 * outs[5].shape[3]
    return pl.pallas_call(
        functools.partial(finish_kernel, vocab, heads, buckets),
        out_shape=(sd(vocab, r), sd(1, r), sd(1, r), sd(r, d), sd(r, d), sd(r, d), sd(r, d), sd(buckets, heads), sd(1, r), sd(r, ff), sd(r, ff),
                   sd(2 * outs[7].shape[2], d), sd(1, 4)),
        in_specs=[vm] * len(outs),
        out_specs=(vm,) * 13,
        compiler_params=pltpu.CompilerParams(vmem_limit_bytes=32 << 20),
        name="finish",
    )(*outs)


def body(byte_ids, lengths, bucket, out_grad, embedding, score_weight, gain_attn, w_query, w_key, w_value, w_attn_out, rel_bias, gain_ff, w_gate, w_up, w_ff_out):
    vocab, width = embedding.shape
    wide = lax.axis_size("wide")
    ids = byte_ids[0]
    nbytes = ids.shape[0]
    idp = jnp.pad(ids.reshape(nbytes // 12, 12).T, ((0, 4), (0, ROWS - nbytes // 12)), constant_values=-1)
    vecs = jnp.stack([score_weight, gain_attn, gain_ff])
    shards = (w_query, w_key, w_value, w_attn_out, w_gate, w_up, w_ff_out)
    kernels = wide == 8 and lax.axis_size("narrow") == 4 and all(s.shape[0] % 32 == 0 for s in shards)
    if kernels:
        split, given = (True, True, True, False), (embedding, vecs) + shards
    else:
        columns = jnp.concatenate([embedding.T, vecs.T], axis=1)
        tt = jnp.pad(columns, ((0, 0), (0, VP - columns.shape[1])))
        tt, wq, wk, wv, wo, wg, wu, wd = (lax.all_gather(s, "wide", axis=0, tiled=True) for s in (tt,) + shards)
        split, given = None, (tt, jnp.concatenate([wq, wk, wv], axis=1))
    *weights, stream, normed, emb, wcol, tot, vec, q, k, v, mixed, lse = forward_one(bucket, lengths, idp, rel_bias, given, vocab, nbytes, wide, split)
    if not kernels:
        eight = lambda w: w.reshape(8, -1, w.shape[1])
        weights = (given[1], jnp.concatenate([wg, wu], axis=1), jnp.concatenate([eight(wd), eight(wo)], axis=1).reshape(-1, wo.shape[1]))
    encoded, *outs = backward_one(bucket, lengths, idp, rel_bias, vec, wcol, tot, lse, (q, k, v, normed, stream, mixed, out_grad[0], emb), weights, vocab, nbytes, kernels)
    encoded = encoded[None]
    if kernels:
        done = finish(outs, vocab, rel_bias.shape[1], rel_bias.shape[0])
        line = lambda a: a.reshape(-1)
        return (encoded, done[0], line(done[1]), line(done[2]), *done[3:8], line(done[8]), *done[9:12], line(done[12]))
    small = outs[-1]
    t, p0, p1, p2, o, f0, f1, down = (a.reshape(-1, a.shape[-1]) for a in outs[:-1])
    part = lambda m: jnp.concatenate([p[:, 256 * m:256 * (m + 1)] for p in (p0, p1, p2)], axis=1)
    half = lambda m: jnp.concatenate([f[:, m * f.shape[1] // 2:(m + 1) * f.shape[1] // 2] for f in (f0, f1)], axis=1)
    grads = (t, part(0), part(1), part(2), o, half(1), half(0), down)
    sums = [lax.psum(lax.psum_scatter(g, "wide", scatter_dimension=0, tiled=True), "narrow").astype(f32) for g in grads]
    small = lax.psum(small, ("wide", "narrow"))
    g_rel, tot = small[:rel_bias.shape[1], :rel_bias.shape[0]].T, small[-1, :5]
    t = sums[0]
    return (encoded, t[:, :vocab].T, t[:, vocab], t[:, vocab + 1], *sums[1:5], g_rel, t[:, vocab + 2], *sums[5:], tot[:4] / tot[4])


def solution(mesh):
    both = ("wide", "narrow")
    rows = P("wide", None)
    vec = P("wide")
    placed = (P(both, None), P(both, None), P(both), P(both, None, None), P(None, "wide"), vec, vec, rows, rows, rows, rows, P(), vec, rows, rows, rows)
    outs = (P(both, None, None), P(None, "wide"), vec, vec, rows, rows, rows, rows, P(), vec, rows, rows, rows, P())
    return jax.shard_map(body, mesh=mesh, in_specs=placed, out_specs=outs, check_vma=False)
```

```python
import functools

import jax
import jax.numpy as jnp
from jax import lax
from jax.experimental import pallas as pl
from jax.experimental.pallas import tpu as pltpu
from jax.sharding import PartitionSpec as P

f32 = jnp.float32
bf16 = jnp.bfloat16
TP = 768
BLK = 128
NB = TP // BLK
LEFT = TP - BLK
STRIP = 2 * TP - BLK
W0 = LEFT - 128
WN = 384

def nt(a, b):
    return lax.dot_general(a, b, (((1,), (1,)), ((), ())), preferred_element_type=f32)

def nn(a, b):
    return lax.dot_general(a, b, (((1,), (0,)), ((), ())), preferred_element_type=f32)

def build_masks(scal_ref, kaug, raug, ntok):
    joined = scal_ref[0] == 1
    l0 = scal_ref[1]; l1 = scal_ref[2]
    half = ntok // 2
    u = lax.broadcasted_iota(jnp.int32, (TP, 128), 0)
    lane = lax.broadcasted_iota(jnp.int32, (TP, 128), 1)
    seg = (u >= half).astype(jnp.int32)
    lim = jnp.where(seg == 1, l1, l0)
    start = seg * half
    lim = jnp.where(joined, l0 + l1, lim)
    start = jnp.where(joined, 0, start)
    valid = (2 * (u - start) < lim) & (u < ntok)
    segs = jnp.where(joined, 0, seg)
    ok = valid & (segs == lane)
    kaug[...] = jnp.where((lane < 2) & jnp.logical_not(ok), -1e30, 0.0).astype(bf16)
    t = u
    rows = jnp.where((lane == segs), 1.0, 0.0).astype(bf16)
    for b in range(NB):
        blk = rows[b * 128:(b + 1) * 128]
        raug[b] = jnp.concatenate([blk, blk], axis=0)

def bias_rows(rel_ref, base):
    c = lax.broadcasted_iota(jnp.int32, (rel_ref.shape[0], 512), 1)
    b = lax.broadcasted_iota(jnp.int32, (rel_ref.shape[0], 512), 0)
    hot = jnp.where(bucket_of(jnp.where(c < 384, c - 128, c - 640)) == b, 1.0, 0.0).astype(bf16)
    base[0:rel_ref.shape[1], :] = lax.dot_general(rel_ref[...], hot, (((0,), (0,)), ((), ())), preferred_element_type=f32)


def bucket_hot():
    m = lax.broadcasted_iota(jnp.int32, (512, 128), 0)
    b = lax.broadcasted_iota(jnp.int32, (512, 128), 1)
    return jnp.where(bucket_of(m - 255) == b, 1.0, 0.0).astype(f32)


class Flags:
    def __init__(self, bucket_ref, lengths_ref):
        self.refs = (bucket_ref, lengths_ref)

    def __getitem__(self, i):
        return self.refs[0][0] if i == 0 else self.refs[1][0, i - 1]


def build_strip(base_ref, row0, strip):
    for hh in range(2):
        row = base_ref[pl.ds(row0 + hh, 1), :]
        cl = row[:, 0:1]; cr = row[:, 383:384]
        sq = jnp.broadcast_to(row, (128, 512))
        sq = pltpu.roll(sq, 0, 1, stride=1, stride_axis=0)
        win = sq[:, :WN].T
        lanes = slice(hh * 128, hh * 128 + 128)
        strip[0:W0, lanes] = jnp.broadcast_to(cl, (W0, 128))
        strip[W0:W0 + WN, lanes] = win
        strip[W0 + WN:STRIP, lanes] = jnp.broadcast_to(cr, (STRIP - W0 - WN, 128))

def stacked(blk):
    lane = lax.broadcasted_iota(jnp.int32, blk.shape, 1)
    z = jnp.zeros_like(blk)
    return jnp.concatenate([jnp.where(lane < 64, blk, z), jnp.where(lane >= 64, blk, z)], axis=0)

def fwd_pair(p, q_ref, k_ref, v_ref, base_ref, o_ref, lse_ref, kaug, raug, strip, vt, hook):
    lanes = pl.ds(pl.multiple_of(p * 128, 128), 128)
    build_strip(base_ref, 2 * p, strip)
    vt[...] = v_ref[:, lanes].T
    kcat = jnp.concatenate([k_ref[:, lanes], kaug[...]], axis=1)
    vtv = vt[...]
    rowsel = lax.broadcasted_iota(jnp.int32, (128, 128), 0) < 64
    for b in range(NB):
        hook(b)
        rhs = jnp.concatenate([stacked(q_ref[b * 128:(b + 1) * 128, lanes]), raug[b]], axis=1)
        s = nt(kcat, rhs) + strip[LEFT - b * 128:LEFT - b * 128 + TP, :]
        mx = jnp.max(s, axis=0, keepdims=True)
        e = jnp.exp(s - mx)
        l = jnp.sum(e, axis=0, keepdims=True)
        ot = nn(vtv, e.astype(bf16)) * (1.0 / l)
        lse_ref[p, b:b + 1, :] = mx + jnp.log(l)
        o = jnp.where(rowsel, ot[:, :128], ot[:, 128:])
        o_ref[b * 128:(b + 1) * 128, lanes] = o.T.astype(bf16)


def bwd_pair(p, q_ref, k_ref, v_ref, g_ref, lse_ref, base_ref, db_ref, kaug, raug, strip, acc, kt, dk_s, dv_s, hook=None):
    lanes = pl.ds(pl.multiple_of(p * 128, 128), 128)
    build_strip(base_ref, 2 * p, strip)
    kt[...] = k_ref[:, lanes].T
    kcat = jnp.concatenate([k_ref[:, lanes], kaug[...]], axis=1)
    v = v_ref[:, lanes]
    ktv = kt[...]
    acc[...] = jnp.zeros_like(acc)
    dk_s[...] = jnp.zeros_like(dk_s)
    dv_s[...] = jnp.zeros_like(dv_s)
    rowsel = lax.broadcasted_iota(jnp.int32, (128, 128), 0) < 64
    for b in range(NB):
        if hook is not None:
            hook(b)
        rows = slice(b * 128, (b + 1) * 128)
        qs = stacked(q_ref[rows, lanes])
        gs = stacked(g_ref[rows, lanes])
        rhs = jnp.concatenate([qs, raug[b]], axis=1)
        w = slice(LEFT - b * 128, LEFT - b * 128 + TP)
        s = nt(kcat, rhs) + strip[w, :]
        pr = jnp.exp(s - lse_ref[p, b:b + 1, :])
        dp = nt(v, gs)
        pdp = pr * dp
        delta = jnp.sum(pdp, axis=0, keepdims=True)
        ds = pdp - pr * delta
        acc[w, :] += ds
        dsb = ds.astype(bf16)
        dk_s[...] += nn(dsb, qs)
        dv_s[...] += nn(pr.astype(bf16), gs)
        dqt = nn(ktv, dsb)
        dq = jnp.where(rowsel, dqt[:, :128], dqt[:, 128:])
        q_ref[rows, lanes] = dq.T.astype(bf16)
    k_ref[:, lanes] = dk_s[...].astype(bf16)
    v_ref[:, lanes] = dv_s[...].astype(bf16)
    fi = lax.broadcasted_iota(jnp.int32, (128, 128), 0)
    fj = lax.broadcasted_iota(jnp.int32, (128, 128), 1)
    flip = jnp.where(fi + fj == 127, 1.0, 0.0).astype(f32)
    for hh in range(2):
        half = slice(hh * 128, hh * 128 + 128)
        far_l = jnp.sum(acc[0:W0, half], keepdims=True)
        far_r = jnp.sum(acc[W0 + WN:STRIP, half], keepdims=True)
        win = acc[W0:W0 + WN, half]
        wt = lax.dot_general(flip, win, (((1,), (1,)), ((), ())), precision=lax.Precision.HIGHEST, preferred_element_type=f32)
        wt = jnp.concatenate([wt, jnp.zeros((128, 128), f32)], axis=1)
        wt = pltpu.roll(wt, 0, 1, stride=1, stride_axis=0)
        diag = jnp.sum(wt, axis=0, keepdims=True)
        lane = lax.broadcasted_iota(jnp.int32, (1, 512), 1)
        diag = diag + jnp.where(lane == 0, far_l, 0.0) + jnp.where(lane == 510, far_r, 0.0)
        db_ref[pl.ds(2 * p + hh, 1), :] = diag


def bucket_of(relative):
    distance = jnp.abs(relative)
    far = 8 + sum(((distance >= e).astype(jnp.int32) for e in (12, 16, 23, 32, 46, 64, 91)))
    near = jnp.where(distance < 8, distance, far)
    return near + 16 * (relative > 0).astype(jnp.int32)


ROWS = 128
VP = 384
VG = 512
VR = 272
EPS = 1e-6

def byte_valid_mat(scal_ref, nbytes):
    i = lax.broadcasted_iota(jnp.int32, (ROWS, 128), 0)
    j = lax.broadcasted_iota(jnp.int32, (ROWS, 128), 1)
    p = 12 * i + j
    slot = nbytes // 2
    joined = scal_ref[0] == 1
    l0 = scal_ref[1]; l1 = scal_ref[2]
    second = p >= slot
    start = jnp.where(joined, 0, jnp.where(second, slot, 0))
    lim = jnp.where(joined, l0 + l1, jnp.where(second, l1, l0))
    ok = (p - start < lim) & (p < nbytes) & (j < 12)
    return jnp.where(ok, 1.0, 0.0).astype(f32)

def inverse_counts(vm):
    v = [vm[:, j:j + 1] for j in range(12)]
    inv = {1: v}
    for b in (2, 3, 4):
        out = []
        for m in range(12 // b):
            tot = v[b * m]
            for t in range(1, b):
                tot = tot + v[b * m + t]
            out.append(1.0 / jnp.maximum(tot, 1.0))
        inv[b] = out
    return v, inv

def softmax_weights(e, inv):
    rate = {1: e}
    for b in (2, 3, 4):
        out = []
        for m in range(12 // b):
            tot = e[b * m]
            for t in range(1, b):
                tot = tot + e[b * m + t]
            out.append(tot * inv[b][m])
        rate[b] = out
    w = {b: [] for b in (1, 2, 3, 4)}
    for p in range(12):
        r = [rate[b][p // b] for b in (1, 2, 3, 4)]
        mx = jnp.maximum(jnp.maximum(r[0], r[1]), jnp.maximum(r[2], r[3]))
        ex = [jnp.exp(x - mx) for x in r]
        inv_t = 1.0 / (ex[0] + ex[1] + ex[2] + ex[3])
        for b in (1, 2, 3, 4):
            w[b].append(ex[b - 1] * inv_t)
    return w

def gbst_fwd_body(nbytes, vocab, scal_ref, ids_ref, tt_ref, stream_ref, normed_ref, emb_ref, wcol_ref, tot_ref, vec_ref, slabs, table_ref, hook):
    table_ref[...] = tt_ref[...].T
    base = vocab // 16 * 16
    tail = table_ref[base:base + 16, :].astype(f32)
    vec_ref[0:3, :] = tail[vocab - base:vocab - base + 3, :]
    vec_ref[3:8, :] = jnp.zeros((5, tail.shape[1]), f32)
    vm = byte_valid_mat(scal_ref, nbytes)
    v, inv = inverse_counts(vm)
    idt = ids_ref[...].astype(f32).T
    lane = lax.broadcasted_iota(jnp.int32, (ROWS, VP), 1).astype(f32)
    s = vec_ref[0:1, :]
    e = []
    for j in range(12):
        hot = jnp.where((lane == idt[:, j:j + 1]) & (v[j] > 0.5), 1.0, 0.0).astype(bf16)
        ej = nn(hot, table_ref[...])
        emb_ref[j * ROWS:(j + 1) * ROWS, :] = ej.astype(bf16)
        e.append(jnp.sum(ej * s, axis=1, keepdims=True))
        if j % 3 == 2:
            hook()
    w = softmax_weights(e, inv)
    l128 = lax.broadcasted_iota(jnp.int32, (ROWS, 128), 1)
    wc = jnp.zeros((ROWS, 128), f32)
    for b in (1, 2, 3, 4):
        for p in range(12):
            wc = jnp.where(l128 == (b - 1) * 12 + p, w[b][p], wc)
    wcol_ref[...] = wc
    tl = lax.broadcasted_iota(jnp.int32, (8, 128), 1)
    tot = jnp.zeros((8, 128), f32)
    for b in (1, 2, 3, 4):
        acc = w[b][0] * v[0]
        for p in range(1, 12):
            acc = acc + w[b][p] * v[p]
        tot = jnp.where(tl == b - 1, jnp.sum(acc, keepdims=True), tot)
    tot = jnp.where(tl == 4, jnp.sum(vm, keepdims=True), tot)
    tot_ref[...] = tot
    hook()
    E = lambda j: emb_ref[j * ROWS:(j + 1) * ROWS, :].astype(f32)
    s3 = lambda m: E(3 * m) + E(3 * m + 1) + E(3 * m + 2)
    for k in range(6):
        p0, p1 = 2 * k, 2 * k + 1
        b2 = 0.5 * (w[2][p0] + w[2][p1]) * inv[2][k]
        acc = (0.5 * w[1][p0] + b2) * E(p0) + (0.5 * w[1][p1] + b2) * E(p1)
        n = k // 2
        d = 0.5 * (w[4][p0] + w[4][p1]) * inv[4][n]
        acc = acc + d * ((E(4 * n) + E(4 * n + 1)) + (E(4 * n + 2) + E(4 * n + 3)))
        m0, m1 = p0 // 3, p1 // 3
        if m0 == m1:
            acc = acc + (0.5 * (w[3][p0] + w[3][p1]) * inv[3][m0]) * s3(m0)
        else:
            acc = acc + (0.5 * w[3][p0] * inv[3][m0]) * s3(m0) + (0.5 * w[3][p1] * inv[3][m1]) * s3(m1)
        put_strided(slabs, k, acc)
        if k % 2 == 1:
            hook()
    ntok = nbytes // 2
    for c in range(slabs.shape[0]):
        stream_ref[0:ntok, c * 128:(c + 1) * 128] = slabs[c, 0:ntok, :]
    stream_ref[ntok:TP, :] = jnp.zeros((TP - ntok, acc.shape[1]), f32)
    norm_rows(stream_ref, vec_ref[1:2, :], normed_ref)
    hook()


def put_strided(ref, k, val):
    for c in range(val.shape[1] // 128):
        ref[c, pl.ds(k, 124, stride=6), :] = val[:124, c * 128:(c + 1) * 128]

def get_strided(ref, k):
    parts = [ref[c, pl.ds(k, 124, stride=6), :] for c in range(ref.shape[0])]
    x = jnp.concatenate(parts, axis=1)
    return jnp.concatenate([x, jnp.zeros((4, x.shape[1]), f32)], axis=0)

def norm_rows(x_ref, gain_ref, out_ref):
    g = gain_ref
    for b in range(TP // 128):
        x = x_ref[b * 128:(b + 1) * 128, :]
        sc = lax.rsqrt(jnp.mean(x * x, axis=1, keepdims=True) + EPS)
        out_ref[b * 128:(b + 1) * 128, :] = (x * sc * g).astype(bf16)

def gbst_bwd_body(nbytes, vocab, scal_ref, ids_ref, emb_ref, wcol_ref, score_ref, ggain_ref, put, de_ref, slabs, hook):
    vm = byte_valid_mat(scal_ref, nbytes)
    v, inv = inverse_counts(vm)
    wc = wcol_ref[...]
    w = {b: [wc[:, (b - 1) * 12 + p:(b - 1) * 12 + p + 1] for p in range(12)] for b in (1, 2, 3, 4)}
    s = score_ref[0:1, :]
    E = lambda j: emb_ref[j * ROWS:(j + 1) * ROWS, :].astype(f32)
    s3 = lambda m: E(3 * m) + E(3 * m + 1) + E(3 * m + 2)
    s4 = lambda n: (E(4 * n) + E(4 * n + 1)) + (E(4 * n + 2) + E(4 * n + 3))
    dot = lambda a, b: jnp.sum(a * b, axis=1, keepdims=True)
    dw = {b: [None] * 12 for b in (1, 2, 3, 4)}
    D = []
    for k in range(6):
        dk = 0.5 * get_strided(slabs, k)
        D.append(dk)
        p0, p1 = 2 * k, 2 * k + 1
        x0, x1 = dot(dk, E(p0)), dot(dk, E(p1))
        dw[1][p0], dw[1][p1] = x0, x1
        dw[2][p0] = dw[2][p1] = (x0 + x1) * inv[2][k]
        m0, m1 = p0 // 3, p1 // 3
        a0 = dot(dk, s3(m0)) * inv[3][m0]
        dw[3][p0] = a0
        dw[3][p1] = a0 if m0 == m1 else dot(dk, s3(m1)) * inv[3][m1]
        dw[4][p0] = dw[4][p1] = dot(dk, s4(k // 2)) * inv[4][k // 2]
        if k % 2 == 1:
            hook()
    hook()
    dr = {b: [] for b in (1, 2, 3, 4)}
    for p in range(12):
        mean = w[1][p] * dw[1][p] + w[2][p] * dw[2][p] + w[3][p] * dw[3][p] + w[4][p] * dw[4][p]
        for b in (1, 2, 3, 4):
            dr[b].append(w[b][p] * (dw[b][p] - mean))
    rb = {1: dr[1]}
    for b in (2, 3, 4):
        out = []
        for m in range(12 // b):
            tot = dr[b][b * m]
            for t in range(1, b):
                tot = tot + dr[b][b * m + t]
            out.append(tot * inv[b][m])
        rb[b] = out
    t3 = []
    for m in range(4):
        terms = {}
        for p in (3 * m, 3 * m + 1, 3 * m + 2):
            terms[p // 2] = terms[p // 2] + w[3][p] if p // 2 in terms else w[3][p]
        acc = None
        for k, coef in terms.items():
            t = (coef * inv[3][m]) * D[k]
            acc = t if acc is None else acc + t
        t3.append(acc)
    gscore = jnp.zeros((8, s.shape[1]), f32)
    for n in range(3):
        t4 = ((w[4][4 * n] + w[4][4 * n + 1]) * inv[4][n]) * D[2 * n] + ((w[4][4 * n + 2] + w[4][4 * n + 3]) * inv[4][n]) * D[2 * n + 1]
        for p in range(4 * n, 4 * n + 4):
            k = p // 2
            c = rb[1][p] + rb[2][k] + rb[3][p // 3] + rb[4][n]
            b2 = (w[2][2 * k] + w[2][2 * k + 1]) * inv[2][k]
            de = v[p] * ((w[1][p] + b2) * D[k] + t3[p // 3] + t4 + c * s)
            de_ref[p * ROWS:(p + 1) * ROWS, :] = de.astype(bf16)
            y = c * E(p)
            gscore = gscore + jnp.sum(y.reshape(ROWS // 8, 8, s.shape[1]), axis=0)
        hook()
    gscore = jnp.sum(gscore, axis=0, keepdims=True)
    row = lax.broadcasted_iota(jnp.int32, (VR, ROWS), 0)
    hots = [jnp.where(row == ids_ref[j:j + 1, :], 1.0, 0.0).astype(bf16) for j in range(12)]
    hot = jnp.concatenate(hots, axis=1)
    gtable = nn(hot, de_ref[...])
    row = lax.broadcasted_iota(jnp.int32, gtable.shape, 0)
    for i, extra in enumerate((gscore, ggain_ref[0:1, :], ggain_ref[1:2, :])):
        gtable = jnp.where(row == vocab + i, extra, gtable)
    put(gtable.T.astype(bf16))


MESH = pl.DeviceIdType.MESH


def coords():
    w = lax.axis_index("wide")
    n = lax.axis_index("narrow")
    return w, w // 2, w % 2, n // 2, n % 2


def peer_ids():
    w, z, y, x, c = coords()
    n = 2 * x + c
    return {
        "y": (2 * z + 1 - y, n),
        "zp": (2 * ((z + 1) % 4) + y, n),
        "zm": (2 * ((z + 3) % 4) + y, n),
        "zo": (2 * ((z + 2) % 4) + y, n),
        "x": (w, 2 * (1 - x) + c),
        "c": (w, 2 * x + 1 - c),
        "xc": (w, 2 * (1 - x) + 1 - c),
    }


def enter(peers, names):
    barrier = pltpu.get_barrier_semaphore()
    for name in names:
        pl.semaphore_signal(barrier, inc=1, device_id=peers[name], device_id_type=MESH)
    pl.semaphore_wait(barrier, len(names))


class Gather:
    SENDS = 30
    SLOTS = 28

    def __init__(self, own, fulls, split, ssem, rsem, lsem):
        self.own, self.fulls, self.split = own, fulls, split
        self.r = [f.shape[0] // 8 for f in fulls]
        self.ssem, self.rsem, self.lsem = ssem, rsem, lsem
        self.peers = peer_ids()
        self.w, self.z, self.y, self.x, self.c = coords()
        z = self.z
        first = jnp.where(z == 3, 3, 1)
        second = jnp.where((z == 0) | (z == 3), 2, 3)
        self.order = (first, second, 6 - first - second)
        self.inner = (z == 1) | (z == 2)
        self.sent = []

    def enter(self):
        n = 2 * self.x + self.c
        barrier = pltpu.get_barrier_semaphore()
        near = [(owner, n) for _, owner in self.others()] + [self.peers["x"], self.peers["c"]]
        for peer in near:
            pl.semaphore_signal(barrier, inc=1, device_id=peer, device_id_type=MESH)
        pl.semaphore_wait(barrier, len(near))

    def cols(self, i, c):
        width = self.fulls[i].shape[1] // 2
        return pl.ds(pl.multiple_of(c * width, 128), width)

    def block(self, i, owner, part, ref=None):
        r = self.r[i]
        start = owner * r
        if self.split[i]:
            r = r // 2
            start = start + part[1] * r
        return (self.fulls[i] if ref is None else ref).at[pl.ds(pl.multiple_of(start, 16), r), self.cols(i, part[0])]

    @property
    def mine(self):
        return (self.c, self.x)

    def copy(self, i, out, slot, src, owner, part, device):
        return pltpu.make_async_remote_copy(
            src_ref=src, dst_ref=self.block(i, owner, part), send_sem=self.ssem.at[i, out],
            recv_sem=self.rsem.at[i, slot], device_id=device, device_id_type=MESH)

    def send(self, i, out, slot, owner, part, device, when=None, src=None):
        src = self.block(i, owner, part) if src is None else src
        cp = self.copy(i, out, slot, src, owner, part, device)
        if when is None:
            cp.start()
        else:
            pl.when(when)(cp.start)
        self.sent.append((i, out, when))

    def arrived(self, i, slot, owner, part):
        ref = self.block(i, owner, part)
        pltpu.make_async_remote_copy(
            src_ref=ref, dst_ref=ref, send_sem=self.ssem.at[i, 0], recv_sem=self.rsem.at[i, slot],
            device_id=self.peers["c"], device_id_type=MESH).wait_recv()

    def local(self, i):
        at = pl.ds(pl.multiple_of(self.w * self.r[i], 16), self.r[i])
        return pltpu.make_async_copy(self.own[i], self.fulls[i].at[at, :], self.lsem.at[i])

    def start_direct(self, i):
        n = 2 * self.x + self.c
        for k in range(1, 8):
            dz, dy = k // 2, k % 2
            to = (2 * lax.rem(self.z + dz, 4) + (1 - self.y if dy else self.y), n)
            self.send_rows(i, k, (4 - dz) % 4 * 2 + dy, self.w, self.c, to, self.half_rows(i, 0, self.c, self.own[i]))
        self.local(i).start()

    def half_rows(self, i, owner, c, ref=None):
        r = self.r[i]
        return (self.fulls[i] if ref is None else ref).at[pl.ds(pl.multiple_of(owner * r + c * (r // 2), 16), r // 2), :]

    def send_rows(self, i, out, slot, owner, c, device, src=None):
        ref = self.half_rows(i, owner, c)
        cp = pltpu.make_async_remote_copy(
            src_ref=ref if src is None else src, dst_ref=ref, send_sem=self.ssem.at[i, out], recv_sem=self.rsem.at[i, slot],
            device_id=device, device_id_type=MESH)
        cp.start()
        self.sent.append((i, out, "rows"))

    def rows_arrived(self, i, slot, owner, c):
        ref = self.half_rows(i, owner, c)
        pltpu.make_async_remote_copy(
            src_ref=ref, dst_ref=ref, send_sem=self.ssem.at[i, 0], recv_sem=self.rsem.at[i, slot],
            device_id=self.peers["c"], device_id_type=MESH).wait_recv()

    def others(self):
        for k in range(1, 8):
            dz, dy = k // 2, k % 2
            yield k, 2 * lax.rem(self.z + dz, 4) + (1 - self.y if dy else self.y)

    def steps_direct(self, i):
        def relay():
            for k, owner in self.others():
                self.rows_arrived(i, k, owner, self.c)
                self.send_rows(i, 8 + k, 8 + k, owner, self.c, self.peers["c"])

        def end():
            for k, owner in self.others():
                self.rows_arrived(i, 8 + k, owner, 1 - self.c)
            self.local(i).wait()
        return [relay, end]

    def start(self, i):
        n = 2 * self.x + self.c
        own = self.block(i, 0, self.mine, self.own[i])
        self.send(i, 0, 2, self.w, self.mine, (2 * jnp.minimum(self.z + 1, 3) + self.y, n), self.z < 3, own)
        self.send(i, 1, 0, self.w, self.mine, (2 * jnp.maximum(self.z - 1, 0) + self.y, n), self.z > 0, own)
        self.send(i, 5, 3, self.w, self.mine, self.peers["y"], None, own)
        self.local(i).start()

    def relay(self, i, s, n, owner):
        self.send(i, 9 + n, 7 + s, owner, self.mine, self.peers["c"])
        if self.split[i]:
            self.send(i, 16 + n, 14 + s, owner, self.mine, self.peers["x"])

    def step_z(self, i, j):
        d = self.order[j]
        o = lax.rem(self.z + d, 4)
        owner = 2 * o + self.y
        self.arrived(i, d - 1, owner, self.mine)
        to = jnp.where(self.inner, jnp.where(o < self.z, self.z + 1, self.z - 1), jnp.where(self.z == 0, 1, 2))
        slot = jnp.where(self.inner, lax.rem(o - to + 4, 4) - 1, 0)
        self.send(i, 2 + j, slot, owner, self.mine, (2 * to + self.y, 2 * self.x + self.c), self.inner)
        self.send(i, 6 + j, 3 + d, owner, self.mine, self.peers["y"])
        self.relay(i, d - 1, j, owner)

    def step_y(self, i, j):
        d = 0 if j < 0 else self.order[j]
        owner = 2 * lax.rem(self.z + d, 4) + 1 - self.y
        self.arrived(i, 3 + d, owner, self.mine)
        self.relay(i, 3 + d, 4 + j, owner)

    def each(self):
        for j in range(3):
            d = self.order[j]
            yield d - 1, j, 2 * lax.rem(self.z + d, 4) + self.y
        for j in range(-1, 3):
            d = 0 if j < 0 else self.order[j]
            yield 3 + d, 4 + j, 2 * lax.rem(self.z + d, 4) + 1 - self.y

    def step_x(self, i):
        if self.split[i]:
            other = (self.c, 1 - self.x)
            for s, n, owner in self.each():
                self.arrived(i, 14 + s, owner, other)
                self.send(i, 23 + n, 21 + s, owner, other, self.peers["c"])

    def step_end(self, i):
        for s, n, owner in self.each():
            self.arrived(i, 7 + s, owner, (1 - self.c, self.x))
            if self.split[i]:
                self.arrived(i, 21 + s, owner, (1 - self.c, 1 - self.x))
        self.local(i).wait()

    def finish(self):
        for i, out, when in self.sent:
            if isinstance(when, str):
                ref = self.half_rows(i, self.w, self.c)
                when = None
            else:
                ref = self.block(i, self.w, self.mine)
            cp = pltpu.make_async_remote_copy(
                src_ref=ref, dst_ref=ref, send_sem=self.ssem.at[i, out], recv_sem=self.rsem.at[i, 0],
                device_id=self.peers["c"], device_id_type=MESH)
            if when is None:
                cp.wait_send()
            else:
                pl.when(when)(cp.wait_send)

    def steps(self, i):
        return [functools.partial(self.step_y, i, -1)] + [functools.partial(f, i, j) for j in range(3) for f in (self.step_z, self.step_y)] + [
            functools.partial(self.step_x, i), functools.partial(self.step_end, i)]


class Reduce:
    SLOTS = 9

    def __init__(self, terms, outs, order, rc, r1, r2, r3, ssem, rsem):
        self.terms, self.outs, self.order = terms, outs, order
        self.rc, self.r1, self.r2, self.r3 = rc, r1, r2, r3
        self.ssem, self.rsem = ssem, rsem
        self.peers = peer_ids()
        self.w, self.z, self.y, self.x, self.c = coords()
        self.sent = []

    def enter(self):
        enter(self.peers, ("y", "zp", "zm", "zo", "x", "c", "xc"))

    def transfer(self, i, slot, src, dst, to):
        return pltpu.make_async_remote_copy(
            src_ref=src, dst_ref=dst, send_sem=self.ssem.at[i, slot], recv_sem=self.rsem.at[i, slot],
            device_id=self.peers[to], device_id_type=MESH)

    def send(self, i, slot, src, dst, to):
        self.transfer(i, slot, src, dst, to).start()
        self.sent.append((i, slot))

    def arrived(self, i, slot, dst):
        self.transfer(i, slot, dst, dst, "c").wait_recv()

    def half(self, i, c):
        width = self.terms[i].shape[4] // 2
        return pl.ds(pl.multiple_of(c * width, 128), width)

    def start(self, i):
        self.send(i, 0, self.terms[i].at[:, :, :, :, self.half(i, 1 - self.c)], self.rc[i], "c")

    def add(self, a, b):
        return a + b

    def step_core(self, i):
        self.arrived(i, 0, self.rc[i])

        def one(z, carry):
            self.rc[i][z] = self.add(self.terms[i][z, :, :, :, self.half(i, self.c)], self.rc[i][z])
            return carry
        lax.fori_loop(0, 4, one, 0)
        if self.order[i] == "y":
            self.send(i, 1, self.rc[i].at[:, 1 - self.y], self.r1[i], "y")
        else:
            self.send(i, 1, self.rc[i].at[:, :, 1 - self.x], self.r1[i], "x")

    def step_one(self, i):
        self.arrived(i, 1, self.r1[i])

        def one(z, carry):
            if self.order[i] == "y":
                mine = self.rc[i][z, self.y]
            else:
                mine = self.rc[i][z, :, self.x]
            self.r1[i][z] = self.add(mine, self.r1[i][z])
            return carry
        lax.fori_loop(0, 4, one, 0)
        if self.order[i] == "y":
            self.send(i, 2, self.r1[i].at[:, 1 - self.x], self.r2[i], "x")
        else:
            self.send(i, 2, self.r1[i].at[:, 1 - self.y], self.r2[i], "y")

    def step_two(self, i):
        self.arrived(i, 2, self.r2[i])
        pick = self.x if self.order[i] == "y" else self.y

        def one(z, carry):
            self.r2[i][z] = self.add(self.r1[i][z, pick], self.r2[i][z])
            return carry
        lax.fori_loop(0, 4, one, 0)
        for dz, to in ((1, "zp"), (3, "zm"), (2, "zo")):
            self.send(i, 2 + dz, self.r2[i].at[lax.rem(self.z + dz, 4)], self.r3[i].at[3 - dz], to)

    def step_z(self, i):
        total = self.r2[i][self.z].astype(f32)
        for dz in (1, 3, 2):
            self.arrived(i, 2 + dz, self.r3[i].at[3 - dz])
        for k in range(3):
            total = total + self.r3[i][k].astype(f32)
        out = self.outs[i]
        out[self.c, self.x] = total.astype(bf16)
        for slot, to in ((6, "x"), (7, "c"), (8, "xc")):
            self.send(i, slot, out.at[self.c, self.x], out.at[self.c, self.x], to)

    def step_end(self, i):
        out = self.outs[i]
        self.arrived(i, 6, out.at[self.c, 1 - self.x])
        self.arrived(i, 7, out.at[1 - self.c, self.x])
        self.arrived(i, 8, out.at[1 - self.c, 1 - self.x])

    def steps(self, i):
        return [functools.partial(f, i) for f in (self.step_core, self.step_one, self.step_two, self.step_z, self.step_end)]

    def finish(self):
        for i, slot in self.sent:
            block = self.r2[i].at[0]
            ref = {0: self.rc[i], 1: self.r1[i], 2: self.r2[i]}.get(slot, block)
            self.transfer(i, slot, ref, ref, "c").wait_send()

    @staticmethod
    def scratch(shapes):
        rc = [pltpu.VMEM((4, 2, 2, s[3], s[4] // 2), bf16) for s in shapes]
        r1 = [pltpu.VMEM((4, 2, s[3], s[4] // 2), bf16) for s in shapes]
        r2 = [pltpu.VMEM((4, s[3], s[4] // 2), bf16) for s in shapes]
        r3 = [pltpu.VMEM((3, s[3], s[4] // 2), bf16) for s in shapes]
        n = len(shapes)
        return rc + r1 + r2 + r3 + [pltpu.SemaphoreType.DMA((n, 9)), pltpu.SemaphoreType.DMA((n, 9))]


SMALL = (16, 128)


class SmallSum:
    HOPS = ("c", "x", "y", "zn", "zo")

    def __init__(self, acc, slots, ssem, rsem):
        self.acc, self.slots, self.ssem, self.rsem = acc, slots, ssem, rsem
        self.peers = peer_ids()
        w, z, y, x, c = coords()
        self.peers["zn"] = (2 * (z + 1 - 2 * (z % 2)) + y, 2 * x + c)

    def copy(self, k):
        return pltpu.make_async_remote_copy(
            src_ref=self.slots.at[5 + k], dst_ref=self.slots.at[k], send_sem=self.ssem.at[k], recv_sem=self.rsem.at[k],
            device_id=self.peers[self.HOPS[k]], device_id_type=MESH)

    def step(self, k):
        if k:
            self.copy(k - 1).wait()
            self.acc[...] = self.acc[...] + self.slots[k - 1]
        if k < 5:
            self.slots[5 + k] = self.acc[...]
            self.copy(k).start()

    def steps(self):
        return [functools.partial(self.step, k) for k in range(6)]


def none():
    pass


class Feed:
    def __init__(self, steps, share=1):
        self.steps = list(steps)
        self.share = share

    def __call__(self):
        for _ in range(self.share):
            if self.steps:
                self.steps.pop(0)()

    def rest(self):
        while self.steps:
            self.steps.pop(0)()


def forward_kernel(nbytes, vocab, split, *refs):
    bucket_ref, lengths_ref, ids_ref, rel_ref = refs[:4]
    scal_ref = Flags(bucket_ref, lengths_ref)
    n_in = 2 if split is None else 9
    given, refs = refs[4:4 + n_in], refs[4 + n_in:]
    fulls, outs = refs[:3], refs[3:14]
    stream_o, normed_o, emb_o, wcol_o, tot_o, vec_o, q_o, k_o, v_o, mixed_o, lse_o = outs
    (tt, wq, wk, wv, stream, normed, emb, wcol, tot, vec, q, k, v, mixed, lse, slabs, table, kaug, raug, strip, vt, base_ref, osem, wsem) = refs[14:38]
    done = []

    def out(src, dst):
        cp = pltpu.make_async_copy(src, dst, osem.at[len(done)])
        cp.start()
        done.append(cp)

    ntok = nbytes // 2
    d = q.shape[1]
    if split is not None:
        wide_t, own_t, own_p, own_f, own_d = refs[38:43]
        emb_ref, vecs_ref, sq, sk, sv, so, sg, su, sd = given
        rd = sd.shape[0]
        g = Gather([own_t, own_p, own_f, own_d], [tt] + list(fulls), split, *refs[43:46])
        r = own_t.shape[0]
        wide_t[...] = jnp.zeros_like(wide_t)
        wide_t[0:vocab, 0:r] = emb_ref[...].astype(f32)
        wide_t[vocab:vocab + 3, 0:r] = vecs_ref[...].astype(f32)
        own_t[...] = wide_t[...].T[0:r].astype(bf16)
        g.enter()
        g.start_direct(0)
        for m, part in enumerate((sq, sk, sv)):
            own_p[:, m * d:(m + 1) * d] = part[...]
        for m, part in enumerate((sg, su)):
            own_f[:, m * part.shape[1]:(m + 1) * part.shape[1]] = part[...]
        own_d[0:rd, :] = sd[...]
        own_d[rd:, :] = so[...]
        g.start(1)
        build_masks(scal_ref, kaug, raug, ntok)
        bias_rows(rel_ref, base_ref)
        relay, end = g.steps_direct(0)
        plans = [None] + [g.steps(i) for i in (1, 2, 3)]
        relay()
        for s in range(3):
            plans[1][s]()
        end()
        begin = [functools.partial(g.start, i) for i in (2, 3)]
        early = Feed(plans[1][3:6] + begin + plans[1][6:8] + [plans[i][s] for s in range(FEW) for i in (2, 3)], SHARE)
        late = [plans[i][s] for s in range(FEW, 8) for i in (2, 3)]
        per = -(-len(late) // 12)
        chunks = [late[j * per:(j + 1) * per] for j in range(12)]
    else:
        cp = pltpu.make_async_copy(given[0], tt, wsem.at[3])
        cp.start()
        build_masks(scal_ref, kaug, raug, ntok)
        bias_rows(rel_ref, base_ref)
        cp.wait()
        early = Feed([])
        chunks = [[]] * 12
    gbst_fwd_body(nbytes, vocab, scal_ref, ids_ref, tt, stream, normed, emb, wcol, tot, vec, slabs, table, early)
    early.rest()
    for src, dst in ((stream, stream_o), (normed, normed_o), (emb, emb_o), (wcol, wcol_o), (tot, tot_o), (vec, vec_o)):
        out(src, dst)
    loads = []
    for i, dst in enumerate((wq, wk, wv)):
        if split is not None and i == 0:
            plans[1][8]()
        cp = pltpu.make_async_copy((given[1] if split is None else fulls[0]).at[:, i * d:(i + 1) * d], dst, wsem.at[i])
        cp.start()
        loads.append(cp)
    for cp, w, dst, to in zip(loads, (wq, wk, wv), (q, k, v), (q_o, k_o, v_o)):
        cp.wait()
        for c in range(d // 256):
            cs = slice(c * 256, (c + 1) * 256)
            dst[:, cs] = nn(normed[...], w[:, cs]).astype(bf16)
        out(dst, to)

    def pair(p, carry):
        def hook(b):
            if b % 3 == 0:
                for j in range(6):
                    part = chunks[2 * j + b // 3]
                    if part:
                        @pl.when(p == j)
                        def _():
                            for step in part:
                                step()
        fwd_pair(p, q, k, v, base_ref, mixed, lse, kaug, raug, strip, vt, hook)
        return carry
    lax.fori_loop(0, d // 128, pair, 0)
    out(mixed, mixed_o)
    out(lse, lse_o)
    if split is not None:
        for i in (2, 3):
            plans[i][8]()
        g.finish()
    for cp in done:
        cp.wait()


FEW, SHARE = 3, 1


def forward_one(bucket, lengths, ids, rel, given, vocab, nbytes, wide, split):
    d = given[1].shape[0] if split is None else given[2].shape[1]
    hbm = pl.BlockSpec(memory_space=pltpu.HBM)
    vm = pl.BlockSpec(memory_space=pltpu.VMEM)
    sm = pl.BlockSpec(memory_space=pltpu.SMEM)
    pairs = d // 128
    sd = jax.ShapeDtypeStruct
    acts = [((TP, d), f32), ((TP, d), bf16), ((12 * ROWS, d), bf16), ((ROWS, 128), f32), ((8, 128), f32), ((8, d), f32),
            ((TP, d), bf16), ((TP, d), bf16), ((TP, d), bf16), ((TP, d), bf16), ((pairs, 8, 256), f32)]
    scratch = [pltpu.VMEM((d, VP), bf16)] + [pltpu.VMEM((d, d), bf16)] * 3 + [pltpu.VMEM(*a) for a in acts]
    scratch += [pltpu.VMEM((d // 128, TP, 128), f32), pltpu.VMEM((VP, d), bf16), pltpu.VMEM((TP, 128), bf16), pltpu.VMEM((NB, 256, 128), bf16),
                pltpu.VMEM((STRIP, 256), f32), pltpu.VMEM((128, TP), bf16), pltpu.VMEM((16, 512), f32), pltpu.SemaphoreType.DMA((11,)), pltpu.SemaphoreType.DMA((4,))]
    params = dict(vmem_limit_bytes=56 << 20)
    if split is not None:
        r, ff, rd = given[2].shape[0], given[6].shape[1], given[8].shape[0]
        scratch += [pltpu.VMEM((VP, 128), f32), pltpu.VMEM((r, VP), bf16), pltpu.VMEM((r, 3 * d), bf16), pltpu.VMEM((r, 2 * ff), bf16), pltpu.VMEM((rd + r, d), bf16)]
        scratch += [pltpu.SemaphoreType.DMA((4, Gather.SENDS)), pltpu.SemaphoreType.DMA((4, Gather.SLOTS)), pltpu.SemaphoreType.DMA((4,))]
        params.update(collective_id=1, has_side_effects=True)
        whole = [sd((wide * r, 3 * d), bf16), sd((wide * r, 2 * ff), bf16), sd((wide * (rd + r), d), bf16)]
    else:
        whole = [sd((16, 128), bf16)] * 3
    return pl.pallas_call(
        functools.partial(forward_kernel, nbytes, vocab, split),
        out_shape=tuple(whole) + tuple(sd(*a) for a in acts),
        in_specs=[sm, sm, vm, vm] + ([hbm] * 2 if split is None else [vm] * 9),
        out_specs=(hbm,) * 14,
        scratch_shapes=scratch,
        compiler_params=pltpu.CompilerParams(**params),
        name="forward_one",
    )(bucket, lengths, ids, rel, *given)


FCH = 256
FRB = 256
GELU = 0.7978845608028654


def flat(ref, cs=slice(None)):
    return ref[:, :, :, :, cs].reshape(ref.shape[0] * 4 * ref.shape[3], -1)


def norm_scale(x):
    return lax.rsqrt(jnp.mean(x * x, axis=1, keepdims=True) + EPS)


def row_block(b):
    return pl.ds(pl.multiple_of(b * FRB, FRB), FRB)


def store_product(dst, tr, rhs):
    rows = dst.shape[0] * 4 * dst.shape[3]
    parts = -(-rows // 1024)
    size = dst.shape[0] // parts
    wide = 256
    for m in range(parts):
        left = tr[m * rows // parts:(m + 1) * rows // parts, :]
        for c in range(dst.shape[4] // wide):
            cs = slice(c * wide, (c + 1) * wide)
            r = nn(left, rhs[:, cs]).astype(bf16)
            dst[m * size:(m + 1) * size, :, :, :, cs] = r.reshape((size,) + dst.shape[1:4] + (wide,))


def ff_phase(gu_h, do_h, mixed_h, stream_h, og_h, enc_o, g2, wo, wf, wd, stream, mid, gh_out, ggain2, sems, ready, poll):
    d = mid.shape[1]
    halves = len(wf)
    part = wf[0].shape[4] // 2

    def scoped(hid, gg, gu, tr, mixed, og, nff, dacc):
        ins = []
        ro, rd = wo.shape[3], wd.shape[3]
        ff = halves * part
        pairs = [(mixed_h, mixed)] + [(do_h.at[:, :, 2 * rd + x * ro:2 * rd + (x + 1) * ro], wo.at[:, :, x]) for x in range(2)]
        pairs += [(stream_h, stream)]
        for h in range(halves):
            at = h * part
            pairs += [(gu_h.at[:, :, :, :, at:at + part], wf[h].at[:, :, :, :, part:2 * part]), (gu_h.at[:, :, :, :, ff + at:ff + at + part], wf[h].at[:, :, :, :, 0:part])]
            if h == 0:
                pairs += [(do_h.at[:, :, x * rd:(x + 1) * rd], wd.at[:, :, x]) for x in range(2)]
        for n, (s, t) in enumerate(pairs):
            cp = pltpu.make_async_copy(s, t, sems.at[n])
            cp.start()
            ins.append(cp)
        for cp in ins[:4]:
            cp.wait()

        def first(b, carry):
            sl = row_block(b)
            middle = stream[sl, :] + nn(mixed[sl, :], flat(wo))
            dacc[sl, :] = middle
            nff[sl, :] = (middle * norm_scale(middle) * g2).astype(bf16)
            return carry
        lax.fori_loop(0, TP // FRB, first, 0)
        tr[0:d, :] = nff[...].T
        ntok = og_h.shape[0]
        og[...] = jnp.concatenate([og_h[...].astype(f32), jnp.zeros((TP - ntok, d), f32)], axis=0).astype(bf16)
        for cp in ins[4:8]:
            cp.wait()
        for h in range(halves):
            if h:
                for cp in ins[8:]:
                    cp.wait()

            for c in range(part // FCH):
                poll(h, c)
                cs = slice(c * FCH, (c + 1) * FCH)
                at = slice(h * part + c * FCH, h * part + (c + 1) * FCH)
                wuc, wgc = flat(wf[h], cs), flat(wf[h], slice(part + c * FCH, part + (c + 1) * FCH))
                wdc = wd[(h * part + c * FCH) // 512, c % 2].reshape(FCH, d)
                gate = nn(nff[...], wgc)
                up = nn(nff[...], wuc)
                gh = nt(og[...], wdc)
                sq = gate * gate
                th = jnp.tanh(gate * (GELU + (GELU * 0.044715) * sq))
                half = 0.5 + 0.5 * th
                act = gate * half
                hid[:, at] = (act * up).astype(bf16)
                dact = half + (0.5 * gate) * (1.0 - th * th) * (GELU + (3 * GELU * 0.044715) * sq)
                gg[:, cs] = (gh * up * dact).astype(bf16)
                gu[:, cs] = (gh * act).astype(bf16)
                dacc[...] += nn(hid[:, at], wdc)
                if h == 0 and c == 0:
                    mid[...] = nt(gg[:, cs], wgc)
                else:
                    mid[...] += nt(gg[:, cs], wgc)
                mid[...] += nt(gu[:, cs], wuc)
            store_product(wf[h].at[:, :, :, :, 0:part], tr.at[0:d], gu)
            store_product(wf[h].at[:, :, :, :, part:2 * part], tr.at[0:d], gg)
            ready("f%d" % h)

        tr[...] = hid[...].T
        store_product(wd, tr, og)
        ready("d")

        def last(b, carry):
            sl = row_block(b)
            nff[sl, :] = dacc[sl, :].astype(bf16)
            wo_all = flat(wo)
            middle = stream[sl, :] + nn(mixed[sl, :], wo_all)
            s2 = norm_scale(middle)
            back = mid[sl, :]
            t = back * g2
            xs = middle * s2
            grad = og[sl, :].astype(f32) + s2 * t - xs * (s2 * s2 * jnp.mean(middle * t, axis=1, keepdims=True))
            mid[sl, :] = grad
            low = grad.astype(bf16)
            gu[sl, 0:d] = low
            gh_out[sl, :] = nt(low, wo_all).astype(bf16)
            ggain2[...] += jnp.sum((back * xs).reshape(FRB // 8, 8, d), axis=0)
            return carry
        lax.fori_loop(0, TP // FRB, last, 0)
        cp = pltpu.make_async_copy(nff, enc_o, sems.at[0])
        cp.start()
        tr[0:d, :] = mixed[...].T
        store_product(wo, tr.at[0:d], gu)
        ready("o")
        cp.wait()
    act = lambda c: pltpu.VMEM((TP, c), bf16)
    pl.run_scoped(scoped, act(halves * part), act(part), act(part), pltpu.VMEM((halves * part, TP), bf16), act(d), act(d), act(d), pltpu.VMEM((TP, d), f32))


NAMES = ("t", "p0", "p1", "p2", "o", "f0", "f1", "d")
FIRST = {"t": "x", "p0": "x", "p1": "y", "p2": "x", "o": "x", "f0": "y", "f1": "x", "d": "y"}
STEPS = ("core", "one", "two", "z", "end")


def backward_kernel(nbytes, vocab, remote, *refs):
    n = len(NAMES)
    bucket_ref, lengths_ref, ids_ref, rel_ref, vec_ref, wcol_ref, tot_ref, lse_ref = refs[:8]
    scal_ref = Flags(bucket_ref, lengths_ref)
    q_h, k_h, v_h, normed_h, stream_h, mixed_h, og_h, emb_h, qkv_h, gu_h, do_h = refs[8:19]
    enc_o, outs, small_o = refs[19], refs[20:20 + n], refs[20 + n]
    refs = refs[21 + n:]
    stream, mid, g, ggain2, ggain, base_ref, fsem, lsem = refs[:8]
    refs = refs[1:]
    bias_rows(rel_ref, base_ref)
    if remote:
        terms = refs[7:7 + n]
        rest = refs[7 + n:]
        red = Reduce(terms, outs, tuple(FIRST[k] for k in NAMES), *[rest[k * n:(k + 1) * n] for k in range(4)], *rest[4 * n:4 * n + 2])
        small = SmallSum(*rest[4 * n + 2:4 * n + 6])
        st = {k: dict(zip(STEPS, red.steps(i))) for i, k in enumerate(NAMES)}
        st["s"] = {k: f for k, f in enumerate(small.steps())}
        red.enter()
    else:
        terms = outs
    term = dict(zip(NAMES, terms))

    def run(words):
        if remote:
            for word in words:
                name, step = word.split(".")
                st[name][int(step) if name == "s" else step]()

    def point(key):
        run(TABLE.get(key, ()))

    def ready(name):
        if remote:
            red.start(NAMES.index(name))
            point(name)

    def point_at(index, keys):
        for j, key in enumerate(keys):
            if remote and TABLE.get(key):
                @pl.when(index == j)
                def _():
                    point(key)

    def poll(h, c):
        point("c%d%d" % (h, c))
    ggain2[...] = jnp.zeros_like(ggain2)
    ff_phase(gu_h, do_h, mixed_h, stream_h, og_h, enc_o, vec_ref[2:3, :], term["o"], (term["f0"], term["f1"]), term["d"],
             stream, mid, g, ggain2, fsem, ready, poll)
    d = stream.shape[1]
    pairs = d // 128

    def scoped(q, k, v, nt_s, emb, wq, wk, wv):
        copies = []
        moves = ((q_h, q), (k_h, k), (v_h, v), (normed_h, nt_s), (emb_h, emb), *((qkv_h.at[:, m * d:(m + 1) * d], w) for m, w in enumerate((wq, wk, wv))))
        for m, (s, t) in enumerate(moves):
            cp = pltpu.make_async_copy(s, t, lsem.at[m])
            cp.start()
            copies.append(cp)
        for cp in copies[:4]:
            cp.wait()
        nt_s[...] = nt_s[...].T

        def attention(kaug, raug, strip, acc, kt, dk_s, dv_s, db):
            build_masks(scal_ref, kaug, raug, nbytes // 2)
            db[...] = jnp.zeros_like(db)
            def pair(p, carry):
                def hook(b):
                    if b % 3 == 0:
                        point_at(p, ["a%d%d" % (j, b // 3) for j in range(pairs)])
                bwd_pair(p, q, k, v, g, lse_ref, base_ref, db, kaug, raug, strip, acc, kt, dk_s, dv_s, hook)
                for j in range(pairs // 2):
                    @pl.when(p == 2 * j + 1)
                    def _():
                        dst = term["p%d" % j]
                        for m, src in enumerate((q, k, v)):
                            r = nn(nt_s[...], src[:, 256 * j:256 * (j + 1)]).astype(bf16)
                            dst[:, :, :, :, 256 * m:256 * (m + 1)] = r.reshape(dst.shape[:4] + (256,))
                        ready("p%d" % j)
                return carry
            lax.fori_loop(0, pairs, pair, 0)
            relt = lax.dot_general(db[...], bucket_hot(), (((1,), (0,)), ((), ())), precision=lax.Precision.HIGHEST, preferred_element_type=f32)
            row = lax.broadcasted_iota(jnp.int32, SMALL, 0)
            total = jnp.where(row == SMALL[0] - 1, tot_ref[0:1, :], relt)
            if remote:
                small.acc[...] = total
            else:
                small_o[...] = total
        strips = pltpu.VMEM((STRIP, 256), f32)
        pl.run_scoped(attention, pltpu.VMEM((TP, 128), bf16), pltpu.VMEM((NB, 256, 128), bf16), strips, strips, pltpu.VMEM((128, TP), bf16),
                      pltpu.VMEM((TP, 128), f32), pltpu.VMEM((TP, 128), f32), pltpu.VMEM((16, 512), f32))
        for cp in copies[4:]:
            cp.wait()

        def pooling(slabs, de):
            count = []

            def hook():
                point("h%d" % len(count))
                count.append(0)
            hook()
            ggain[...] = jnp.zeros_like(ggain)
            gain = vec_ref[1:2, :]

            def rows(b, carry):
                sl = row_block(b)
                gy = nt(q[sl, :], wq[...]) + nt(k[sl, :], wk[...]) + nt(v[sl, :], wv[...])
                x = stream[sl, :]
                s = norm_scale(x)
                t = gy * gain
                gs = mid[sl, :] + s * t - x * (s * s * s * jnp.mean(x * t, axis=1, keepdims=True))
                for c in range(d // 128):
                    slabs[c, sl, :] = gs[:, c * 128:(c + 1) * 128]
                ggain[...] += jnp.sum((gy * x * s).reshape(FRB // 8, 8, d), axis=0)
                return carry
            lax.fori_loop(0, TP // FRB, rows, 0)
            ggain[0:2, :] = jnp.concatenate([jnp.sum(ggain[...], axis=0, keepdims=True), jnp.sum(ggain2[...], axis=0, keepdims=True)], axis=0)
            hook()

            def put(gt):
                dst = term["t"]
                half = dst.shape[3]
                for zz in range(dst.shape[0]):
                    for yy in range(2):
                        for xx in range(2):
                            top = ((zz * 2 + yy) * 2 + xx) * half
                            dst[zz, yy, xx, :, 0:VR] = gt[top:top + half]
                            dst[zz, yy, xx, :, VR:VG] = jnp.zeros((half, VG - VR), bf16)
            gbst_bwd_body(nbytes, vocab, scal_ref, ids_ref, emb, wcol_ref, vec_ref, ggain, put, de, slabs, hook)
            if remote:
                ready("t")
        pl.run_scoped(pooling, pltpu.VMEM((d // 128, TP, 128), f32), pltpu.VMEM((12 * ROWS, d), bf16))
    act = pltpu.VMEM((TP, d), bf16)
    mat = pltpu.VMEM((d, d), bf16)
    pl.run_scoped(scoped, act, act, act, act, pltpu.VMEM((12 * ROWS, d), bf16), mat, mat, mat)
    if remote:
        point("end")
        small_o[...] = small.acc[...]
        red.finish()


TABLE = {
    "c13": ("f0.core",),
    "o": ("f1.core",),
    "a00": ("d.core", "o.core", "f0.one",),
    "a30": ("p0.core", "d.one", "f1.one",),
    "a31": ("o.one",),
    "a50": ("p1.core", "f0.two", "f1.two", "o.two",),
    "p2": ("p0.one",),
    "h0": ("p1.one",),
    "h1": ("p2.core", "s.0", "f0.z", "d.two", "p0.two",),
    "h2": ("s.1",),
    "h3": ("p1.two",),
    "h6": ("f1.z",),
    "h7": ("p2.one",),
    "h8": ("o.z",),
    "t": ("s.2",),
    "end": ("p2.two", "f0.end", "t.core", "s.3", "f1.end", "d.z", "o.end", "p0.z",
            "t.one", "p1.z", "t.two", "d.end", "s.4", "p2.z", "p0.end", "p1.end",
            "s.5", "t.z", "p2.end", "t.end",),
}


def backward_one(bucket, lengths, ids, rel, vec, wcol, tot, lse, acts, weights, vocab, nbytes, remote):
    d = acts[0].shape[1]
    hbm = pl.BlockSpec(memory_space=pltpu.HBM)
    vm = pl.BlockSpec(memory_space=pltpu.VMEM)
    sd = jax.ShapeDtypeStruct
    view = lambda r, c: (4, 2, 2, r // 16, c)
    qkv, gu, do = weights
    ff = gu.shape[1] // 2
    sm = pl.BlockSpec(memory_space=pltpu.SMEM)
    shapes = [view(d, VG)] + [view(d, d)] * 4 + [view(d, ff)] * 2 + [view(ff, d)]
    scratch = [pltpu.VMEM((TP, d), f32), pltpu.VMEM((TP, d), f32), pltpu.VMEM((TP, d), bf16), pltpu.VMEM((8, d), f32), pltpu.VMEM((8, d), f32),
               pltpu.VMEM((16, 512), f32), pltpu.SemaphoreType.DMA((11,)), pltpu.SemaphoreType.DMA((8,))]
    params = dict(vmem_limit_bytes=62 << 20)
    if remote:
        outs = [sd((2, 2, s[3], s[4] // 2), bf16) for s in shapes]
        scratch += [pltpu.VMEM(s, bf16) for s in shapes] + Reduce.scratch(shapes)
        scratch += [pltpu.VMEM(SMALL, f32), pltpu.VMEM((10,) + SMALL, f32), pltpu.SemaphoreType.DMA((5,)), pltpu.SemaphoreType.DMA((5,))]
        params.update(collective_id=2, has_side_effects=True)
    else:
        outs = [sd(s, bf16) for s in shapes]
    return pl.pallas_call(
        functools.partial(backward_kernel, nbytes, vocab, remote),
        out_shape=(sd((TP, d), bf16), *outs, sd(SMALL, f32)),
        in_specs=[sm, sm] + [vm] * 6 + [hbm] * 6 + [vm] + [hbm] * 4,
        out_specs=(hbm,) + (vm,) * (len(outs) + 1),
        scratch_shapes=scratch,
        compiler_params=pltpu.CompilerParams(**params),
        name="backward_one",
    )(bucket, lengths, ids, rel, vec, wcol, tot, lse, *acts, qkv, gu.reshape(view(*gu.shape)), do.reshape(4, 2, -1, d))


def finish_kernel(vocab, heads, buckets, *refs):
    ins, small_ref = dict(zip(NAMES, refs[:len(NAMES)])), refs[len(NAMES)]
    table_o, score_o, gain1_o, q_o, k_o, v_o, o_o, rel_o, gain2_o, gate_o, up_o, down_o, share_o = refs[len(NAMES) + 1:]

    def place(dst, src, left):
        half, width = src.shape[2], src.shape[3]
        for c in range(2):
            for x in range(2):
                dst[x * half:(x + 1) * half, left + c * width:left + (c + 1) * width] = src[c, x].astype(f32)
    place(o_o, ins["o"], 0)
    place(down_o, ins["d"], 0)
    for h in range(2):
        src = ins["f%d" % h]
        half, width = src.shape[2], src.shape[3]
        for c, dst in enumerate((up_o, gate_o)):
            for x in range(2):
                dst[x * half:(x + 1) * half, h * width:(h + 1) * width] = src[c, x].astype(f32)
    for j in range(3):
        src = ins["p%d" % j]
        half = src.shape[2]
        for piece in range(6):
            c, m = piece // 3, piece % 3
            dst = (q_o, k_o, v_o)[piece // 2]
            left = 256 * j + 128 * (piece % 2)
            for x in range(2):
                dst[x * half:(x + 1) * half, left:left + 128] = src[c, x, :, 128 * m:128 * (m + 1)].astype(f32)
    t = ins["t"]
    rows = jnp.concatenate([jnp.concatenate([t[c, x] for x in range(2)], axis=0) for c in range(2)], axis=1).astype(f32)
    turned = rows.T
    table_o[...] = turned[:vocab]
    score_o[...] = turned[vocab:vocab + 1]
    gain1_o[...] = turned[vocab + 1:vocab + 2]
    gain2_o[...] = turned[vocab + 2:vocab + 3]
    small = small_ref[...]
    rel_o[...] = small.T[:buckets, :heads]
    last = small[SMALL[0] - 1:SMALL[0], :]
    share_o[...] = last[:, 0:4] / last[:, 4:5]


def finish(outs, vocab, heads, buckets):
    vm = pl.BlockSpec(memory_space=pltpu.VMEM)
    sd = lambda *s: jax.ShapeDtypeStruct(s, f32)
    r = 2 * outs[1].shape[2]
    d = 2 * outs[1].shape[3]
    ff = 2 * outs[5].shape[3]
    return pl.pallas_call(
        functools.partial(finish_kernel, vocab, heads, buckets),
        out_shape=(sd(vocab, r), sd(1, r), sd(1, r), sd(r, d), sd(r, d), sd(r, d), sd(r, d), sd(buckets, heads), sd(1, r), sd(r, ff), sd(r, ff),
                   sd(2 * outs[7].shape[2], d), sd(1, 4)),
        in_specs=[vm] * len(outs),
        out_specs=(vm,) * 13,
        compiler_params=pltpu.CompilerParams(vmem_limit_bytes=32 << 20),
        name="finish",
    )(*outs)


def body(byte_ids, lengths, bucket, out_grad, embedding, score_weight, gain_attn, w_query, w_key, w_value, w_attn_out, rel_bias, gain_ff, w_gate, w_up, w_ff_out):
    vocab, width = embedding.shape
    wide = lax.axis_size("wide")
    ids = byte_ids[0]
    nbytes = ids.shape[0]
    idp = jnp.pad(ids.reshape(nbytes // 12, 12).T, ((0, 4), (0, ROWS - nbytes // 12)), constant_values=-1)
    vecs = jnp.stack([score_weight, gain_attn, gain_ff])
    shards = (w_query, w_key, w_value, w_attn_out, w_gate, w_up, w_ff_out)
    kernels = wide == 8 and lax.axis_size("narrow") == 4 and all(s.shape[0] % 32 == 0 for s in shards)
    if kernels:
        split, given = (True, True, True, False), (embedding, vecs) + shards
    else:
        columns = jnp.concatenate([embedding.T, vecs.T], axis=1)
        tt = jnp.pad(columns, ((0, 0), (0, VP - columns.shape[1])))
        tt, wq, wk, wv, wo, wg, wu, wd = (lax.all_gather(s, "wide", axis=0, tiled=True) for s in (tt,) + shards)
        split, given = None, (tt, jnp.concatenate([wq, wk, wv], axis=1))
    *weights, stream, normed, emb, wcol, tot, vec, q, k, v, mixed, lse = forward_one(bucket, lengths, idp, rel_bias, given, vocab, nbytes, wide, split)
    if not kernels:
        eight = lambda w: w.reshape(8, -1, w.shape[1])
        weights = (given[1], jnp.concatenate([wg, wu], axis=1), jnp.concatenate([eight(wd), eight(wo)], axis=1).reshape(-1, wo.shape[1]))
    encoded, *outs = backward_one(bucket, lengths, idp, rel_bias, vec, wcol, tot, lse, (q, k, v, normed, stream, mixed, out_grad[0], emb), weights, vocab, nbytes, kernels)
    encoded = encoded[:nbytes // 2][None]
    if kernels:
        done = finish(outs, vocab, rel_bias.shape[1], rel_bias.shape[0])
        line = lambda a: a.reshape(-1)
        return (encoded, done[0], line(done[1]), line(done[2]), *done[3:8], line(done[8]), *done[9:12], line(done[12]))
    small = outs[-1]
    t, p0, p1, p2, o, f0, f1, down = (a.reshape(-1, a.shape[-1]) for a in outs[:-1])
    part = lambda m: jnp.concatenate([p[:, 256 * m:256 * (m + 1)] for p in (p0, p1, p2)], axis=1)
    half = lambda m: jnp.concatenate([f[:, m * f.shape[1] // 2:(m + 1) * f.shape[1] // 2] for f in (f0, f1)], axis=1)
    grads = (t, part(0), part(1), part(2), o, half(1), half(0), down)
    sums = [lax.psum(lax.psum_scatter(g, "wide", scatter_dimension=0, tiled=True), "narrow").astype(f32) for g in grads]
    small = lax.psum(small, ("wide", "narrow"))
    g_rel, tot = small[:rel_bias.shape[1], :rel_bias.shape[0]].T, small[-1, :5]
    t = sums[0]
    return (encoded, t[:, :vocab].T, t[:, vocab], t[:, vocab + 1], *sums[1:5], g_rel, t[:, vocab + 2], *sums[5:], tot[:4] / tot[4])


def solution(mesh):
    both = ("wide", "narrow")
    rows = P("wide", None)
    vec = P("wide")
    placed = (P(both, None), P(both, None), P(both), P(both, None, None), P(None, "wide"), vec, vec, rows, rows, rows, rows, P(), vec, rows, rows, rows)
    outs = (P(both, None, None), P(None, "wide"), vec, vec, rows, rows, rows, rows, P(), vec, rows, rows, rows, P())
    return jax.shard_map(body, mesh=mesh, in_specs=placed, out_specs=outs, check_vma=False)
```
